32 devices in a mesh: groups: 2 (over x), paths: 16 (over z, y, core).
Axes of the slice: x: 2, y: 2, z: 4, core: 2. Of those that a mesh axis runs over, the one named last changes fastest.
Arguments:
- path_basis: bfloat16 [4096, 512], P(('groups', 'paths')), parts along dimension 0, may hold values from -6 to 6
- proxy_weight: bfloat16 [4096, 512], P(('groups', 'paths')), parts along dimension 0, may hold values from -0.25 to 0.25
- notional: bfloat16 [4096], P(('groups', 'paths')), parts along dimension 0, may hold values from -4 to 4
- set_of: int32 [4096], P('groups'), parts along dimension 0, may hold values from 0 to 511
- threshold_index: int32 [1024], P('groups'), parts along dimension 0, may hold values from 0 to 15
- threshold_levels: float32 [32], P('groups'), parts along dimension 0, may hold values from 0.5 to 20
- loss_rate: float32 [1024], P('groups'), parts along dimension 0, may hold values from 0.4 to 1
Outputs:
- expected_loss: float32 [2], P('groups'), parts along dimension 0
- basis_adjoint: float32 [4096, 512], P(('groups', 'paths')), parts along dimension 0
- weight_adjoint: float32 [4096, 512], P(('groups', 'paths')), parts along dimension 0
The draws below stay inside these ranges and needn't reach their ends.
There are 2 independent parts, one for each index of `groups`. The reference program is written for one: setup_inputs(seed, part) draws one part's arguments, and reference() takes and returns one part's arrays. A program takes and returns all parts, laid end to end along the dimension named above; each array names one. Nothing has to cross between parts.
Inputs may be any that keep to these rules, and one draw needn't show every extreme that they name: `set_of`: netting set of each trade; set sizes are uneven.
All inputs are finite; a program needn't handle non-finite values.
Results may differ from the reference program's by a relative error of at most 0.0041.
Values may be sent and summed in bfloat16 or wider, within the bound.
No kernel may reach another device: no remote copies, remote signals or barrier semaphores. Data moves between devices by JAX's collectives and lax.ppermute only.
A program may use at most 64 MiB of HBM per device.

```python
import math
import jax
import jax.numpy as jnp
import numpy as np
from jax import lax

FEATURES = 512
TRADES = 2048
SETS = 512
REGRESSORS = 32
LEVELS = 16
PATHS = 2048


def plant(array, rng, smallest, high):
    spot = [jax.random.randint(jax.random.fold_in(rng, axis), (), 0, length) for axis, length in enumerate(array.shape)]
    main_axis = array.shape.index(max(array.shape))
    next_to = spot[:main_axis] + [(spot[main_axis] + 1) % array.shape[main_axis]] + spot[main_axis + 1:]
    return array.at[tuple(spot)].set(smallest).at[tuple(next_to)].set(high)


def block_scale(key, extent, shards, smallest, high):
    def one(dim, parts):
        heights = jax.random.uniform(jax.random.fold_in(jax.random.fold_in(key, 6), dim), (parts,), jnp.float32, smallest / len(shards), high / len(shards))
        return jnp.repeat(jnp.exp(heights), extent[dim] // parts).reshape((-1,) + (1,) * (len(extent) - dim - 1))

    level = one(*shards[0])
    for cut in shards[1:]:
        level = level * one(*cut)
    return level


def rank_bounds(number_of, slope):
    portions = [(1 << 20) // math.isqrt(standing ** slope) + 1 for standing in range(1, number_of + 1)]
    deviation = 1 + sum(portions) // (1 << 30)
    return np.cumsum(np.array([max(1, weight // deviation) for weight in portions]))


def ranked(own_key, shape, count, lean):
    grid = rank_bounds(count, lean)
    pick = jax.random.randint(jax.random.fold_in(own_key, 1), shape, 0, int(grid[count - 1]))
    standing = jnp.searchsorted(jnp.asarray(grid, jnp.int32), pick, side="right")
    return jax.random.permutation(jax.random.fold_in(own_key, 2), count)[standing].astype(jnp.int32)


def gaussian(stream_key, dims, spread, most, cuts=(), kind=jnp.bfloat16):
    level = block_scale(stream_key, dims, cuts, -0.22, 0.18) if cuts else 1.0
    entries = jax.random.normal(stream_key, dims, jnp.float32) * spread * level
    return jnp.minimum(jnp.maximum(entries, -most), most).astype(kind)


def setup_inputs(seed: int = 0, part: int = 0) -> dict:
    key_list = jax.random.split(jax.random.key(seed), 8)
    part_keys = jax.random.split(jax.random.fold_in(key_list[7], part), 8)
    return {
        "path_basis": gaussian(part_keys[0], (PATHS, FEATURES), 1.0, 6.0, ((0, 16),)),
        "proxy_weight": gaussian(part_keys[1], (TRADES, FEATURES), FEATURES ** -0.5, 0.25, ((0, 16),)),
        "notional": jnp.clip(jax.random.uniform(part_keys[2], (TRADES,), jnp.float32, -4.0, 4.0) * block_scale(part_keys[2], (TRADES,), ((0, 16),), -0.4, 0.0), -4.0, 4.0).astype(jnp.bfloat16),
        "set_of": plant(ranked(part_keys[3], (TRADES,), SETS, 2), jax.random.fold_in(part_keys[3], 3), 0, SETS - 1).astype(jnp.int32),
        "threshold_index": plant(jax.random.randint(part_keys[4], (SETS,), 0, LEVELS), jax.random.fold_in(part_keys[4], 1), 0, LEVELS - 1).astype(jnp.int32),
        "threshold_levels": jnp.clip(jnp.exp(jax.random.uniform(part_keys[5], (LEVELS,), jnp.float32, math.log(0.5), math.log(20.0))), 0.5, 20.0),
        "loss_rate": jnp.clip(jax.random.uniform(part_keys[6], (SETS,), jnp.float32, 0.4, 1.0), 0.4, 1.0),
    }


RIDGE_SCALE = 0.01
PRECISE = lax.Precision.HIGHEST

def table_rows(labels, classes, target_type):
    return (labels[:, None] == jnp.arange(classes, dtype=jnp.int32)[None, :]).astype(target_type)

def contract_rows(former, latter):
    return lax.dot_general(former.astype(jnp.float32), latter.astype(jnp.float32), (((0,), (0,)), ((), ())), precision=PRECISE, preferred_element_type=jnp.float32)

def contract_cols(former, latter):
    return lax.dot_general(former.astype(jnp.float32), latter.astype(jnp.float32), (((1,), (1,)), ((), ())), precision=PRECISE, preferred_element_type=jnp.float32)

def matrix_product(former, latter):
    return jnp.dot(former.astype(jnp.float32), latter.astype(jnp.float32), precision=PRECISE, preferred_element_type=jnp.float32)

def spd_solve(matrix, target):
    lower_factor = jnp.linalg.cholesky(matrix)
    halfway = lax.linalg.triangular_solve(lower_factor, target, left_side=True, lower=True)
    return lax.linalg.triangular_solve(lower_factor, halfway, left_side=True, lower=True, transpose_a=True)

def reference(path_basis, proxy_weight, notional, set_of, threshold_index, threshold_levels, loss_rate):
    path_count = path_basis.shape[0]
    trade_count, feature_count = proxy_weight.shape
    set_total = loss_rate.shape[0]
    block_cols = math.gcd(256, trade_count)
    block_count = trade_count // block_cols
    weight_blocks = proxy_weight.reshape(block_count, block_cols, feature_count)
    notional_blocks = notional.astype(jnp.float32).reshape(block_count, block_cols)
    set_blocks = set_of.reshape(block_count, block_cols)

    def forward_step(running, pieces):
        weight_block, notional_block, set_block = pieces
        pre_act = lax.dot_general(path_basis.astype(jnp.float32), weight_block.astype(jnp.float32), (((1,), (1,)), ((), ())), preferred_element_type=jnp.float32)
        trade_value = (notional_block[None, :] * jax.nn.softplus(pre_act)).astype(jnp.bfloat16)
        return (running + jnp.dot(trade_value.astype(jnp.float32), table_rows(set_block, set_total, jnp.bfloat16).astype(jnp.float32), preferred_element_type=jnp.float32), None)
    exposure, _ = lax.scan(forward_step, jnp.zeros((path_count, set_total), jnp.float32), (weight_blocks, notional_blocks, set_blocks))
    thresholds = lax.optimization_barrier(jnp.sum(table_rows(threshold_index, threshold_levels.shape[0], jnp.float32) * threshold_levels[None, :], axis=1))
    design = jnp.concatenate([jnp.ones((path_count, 1), jnp.float32), path_basis[:, :REGRESSORS - 1].astype(jnp.float32)], axis=1)
    gram_matrix = contract_rows(design, design) + RIDGE_SCALE * path_count * jnp.eye(REGRESSORS, dtype=jnp.float32)
    coeffs = spd_solve(gram_matrix, contract_rows(design, exposure))
    fitted = matrix_product(design, coeffs)
    excess = fitted - thresholds[None, :]
    expected_loss = (jnp.sum(loss_rate[None, :] * jax.nn.softplus(excess)) / (path_count * set_total)).reshape(1)
    seed_adjoint = loss_rate[None, :] * jax.nn.sigmoid(excess)
    solve_adjoint = spd_solve(gram_matrix, contract_rows(design, seed_adjoint))
    adjoint_full = matrix_product(design, solve_adjoint)
    exposure_adjoint = adjoint_full.astype(jnp.bfloat16)
    design_adjoint = contract_cols(seed_adjoint - adjoint_full, coeffs) + contract_cols(exposure - fitted, solve_adjoint)

    def backward_step(running, pieces):
        weight_block, notional_block, set_block = pieces
        pre_trans = lax.dot_general(weight_block.astype(jnp.float32), path_basis.astype(jnp.float32), (((1,), (1,)), ((), ())), preferred_element_type=jnp.float32)
        spread_trans = lax.dot_general(table_rows(set_block, set_total, jnp.bfloat16).astype(jnp.float32), exposure_adjoint.astype(jnp.float32), (((1,), (1,)), ((), ())), preferred_element_type=jnp.float32)
        slope_trans = (notional_block[:, None] * jax.nn.sigmoid(pre_trans) * spread_trans).astype(jnp.bfloat16)
        running = running + lax.dot_general(slope_trans.astype(jnp.float32), weight_block.astype(jnp.float32), (((0,), (0,)), ((), ())), preferred_element_type=jnp.float32)
        return (running, jnp.dot(slope_trans.astype(jnp.float32), path_basis.astype(jnp.float32), preferred_element_type=jnp.float32))
    back_total, weight_rows = lax.scan(backward_step, jnp.zeros((path_count, feature_count), jnp.float32), (weight_blocks, notional_blocks, set_blocks))
    padding = jnp.zeros((path_count, feature_count - REGRESSORS + 1), jnp.float32)
    basis_adjoint = back_total + jnp.concatenate([design_adjoint[:, 1:], padding], axis=1)
    weight_adjoint = weight_rows.reshape(trade_count, feature_count) * (1.0 / math.sqrt(path_count))
    return (expected_loss, basis_adjoint, weight_adjoint)
```

```python
import math

import jax
import jax.numpy as jnp
from jax import lax
from jax.sharding import PartitionSpec as P

REGRESSORS = 32
RIDGE_SCALE = 0.01
PRECISE = lax.Precision.HIGHEST
F32 = jnp.float32
BF16 = jnp.bfloat16


def split_axis(size):
    inner = max(d for d in range(1, math.isqrt(size) + 1) if size % d == 0)
    return size // inner, inner


def dot_dims(a, b, ca, cb, precision=None):
    return lax.dot_general(
        a, b, (((ca,), (cb,)), ((), ())), precision=precision, preferred_element_type=F32
    )


def one_hot(labels, classes, target_type):
    return (labels[:, None] == jnp.arange(classes, dtype=jnp.int32)[None, :]).astype(target_type)


def spd_solve(matrix, target):
    lower_factor = jnp.linalg.cholesky(matrix)
    halfway = lax.linalg.triangular_solve(lower_factor, target, left_side=True, lower=True)
    return lax.linalg.triangular_solve(
        lower_factor, halfway, left_side=True, lower=True, transpose_a=True
    )


def shards(
    path_basis, proxy_weight, notional, set_of, threshold_index, threshold_levels, loss_rate
):
    n = lax.axis_size("paths")
    outer, inner = split_axis(n)
    me = lax.axis_index("paths")
    my_outer, my_inner = me // inner, me % inner
    path_rows, features = path_basis.shape
    trade_rows = proxy_weight.shape[0]
    paths_all = path_rows * n
    sets = loss_rate.shape[0]
    quarter = sets // inner

    def along_inner(x, k):
        pairs = [(o * inner + i, o * inner + (i + k) % inner) for o in range(outer) for i in range(inner)]
        return lax.ppermute(x, "paths", pairs)

    def along_outer(x, k):
        pairs = [(o * inner + i, ((o + k) % outer) * inner + i) for o in range(outer) for i in range(inner)]
        return lax.ppermute(x, "paths", pairs)

    weight_slots = [proxy_weight] + [along_outer(proxy_weight, k) for k in range(1, outer)]
    basis_slots = [path_basis] + [along_inner(path_basis, k) for k in range(1, inner)]
    design = jnp.concatenate(
        [jnp.ones((1, path_rows), BF16), path_basis[:, : REGRESSORS - 1].T], axis=0
    )
    small = jnp.concatenate([design, jnp.pad(notional[None, :], ((0, 15), (0, max(path_rows, trade_rows) - trade_rows)))], axis=0)
    small_slots = [small] + [along_outer(small, k) for k in range(1, outer)]
    design_outer = jnp.stack([s[:REGRESSORS] for s in small_slots])
    design_slots = [design_outer] + [along_inner(design_outer, k) for k in range(1, inner)]
    design_all = jnp.stack(design_slots, axis=2).transpose(1, 0, 2, 3).reshape(REGRESSORS, paths_all)
    design_group = design_all[:, : inner * path_rows]

    weights = jnp.concatenate(weight_slots, axis=0)
    basis = jnp.concatenate(basis_slots, axis=0)
    notional_group = jnp.concatenate([s[REGRESSORS, :trade_rows] for s in small_slots]).astype(F32)
    set_blocks = set_of.reshape(n, trade_rows)
    set_group = jnp.concatenate(
        [
            lax.dynamic_index_in_dim(set_blocks, ((my_outer + outer - k) % outer) * inner + my_inner, 0, False)
            for k in range(outer)
        ]
    )
    in_set = one_hot(set_group, sets, BF16)

    pre_act = dot_dims(basis, weights, 1, 1)
    trade_value = (notional_group[None, :] * jax.nn.softplus(pre_act)).astype(BF16)
    slope = jax.nn.sigmoid(pre_act)
    trade_moment = dot_dims(design_group, trade_value, 1, 0)
    moment = dot_dims(trade_moment, in_set.astype(F32), 1, 0, PRECISE)

    def piece(x, size, axis, index):
        return lax.dynamic_slice_in_dim(x, index * size, size, axis)

    mine = piece(moment, quarter, 1, my_inner)
    for k in range(1, inner):
        mine = mine + along_inner(piece(moment, quarter, 1, (my_inner + k) % inner), k)
    part = mine
    for k in range(1, outer):
        mine = mine + along_outer(part, k)

    thresholds = jnp.sum(
        one_hot(threshold_index, threshold_levels.shape[0], F32) * threshold_levels[None, :], axis=1
    )
    thresh = piece(thresholds, quarter, 0, my_inner)
    rate = piece(loss_rate, quarter, 0, my_inner)
    design_wide = design_all.astype(F32)
    gram = dot_dims(design_all, design_all, 1, 1) + RIDGE_SCALE * paths_all * jnp.eye(
        REGRESSORS, dtype=F32
    )
    coeffs = spd_solve(gram, mine)
    fitted = dot_dims(design_wide, coeffs, 0, 0, PRECISE)
    excess = fitted - thresh[None, :]
    seed = rate[None, :] * jax.nn.sigmoid(excess)
    loss = jnp.sum(rate[None, :] * jax.nn.softplus(excess)) / (paths_all * sets)
    adjoint = spd_solve(gram, dot_dims(design_wide, seed, 1, 0, PRECISE))

    adjoint_slots = jnp.stack([adjoint] + [along_inner(adjoint, k) for k in range(1, inner)])
    order = (my_inner + inner - jnp.arange(inner)) % inner
    adjoint_all = adjoint_slots[order].transpose(1, 0, 2).reshape(REGRESSORS, sets)

    adjoint_trade = dot_dims(adjoint_all, in_set.astype(F32), 1, 1, PRECISE)
    spread = dot_dims(design_group.astype(F32), adjoint_trade, 0, 0, PRECISE).astype(BF16)
    trade_adjoint = (notional_group[None, :] * slope * spread.astype(F32)).astype(BF16)

    group_rows = inner * path_rows
    residual = seed[:group_rows] - dot_dims(design_group.astype(F32), adjoint, 0, 0, PRECISE)
    design_part = (
        dot_dims(coeffs, residual, 1, 1, PRECISE)
        - dot_dims(adjoint, fitted[:group_rows], 1, 1, PRECISE)
        + dot_dims(adjoint_trade, trade_value.astype(F32), 1, 1, PRECISE)
    )
    design_part = design_part.at[0].set(loss)

    weight_part = dot_dims(trade_adjoint, basis, 0, 0) * (1.0 / math.sqrt(paths_all))
    weight_total = weight_part[:trade_rows]
    for k in range(1, outer):
        sent = weight_part[k * trade_rows : (k + 1) * trade_rows].astype(BF16)
        weight_total = weight_total + along_outer(sent, outer - k).astype(F32)
    basis_part = dot_dims(trade_adjoint, weights, 1, 0)
    basis_total = basis_part[:path_rows]
    design_total = design_part[:, :path_rows]
    for k in range(1, inner):
        rows = slice(k * path_rows, (k + 1) * path_rows)
        basis_total = basis_total + along_inner(basis_part[rows].astype(BF16), inner - k).astype(F32)
        design_total = design_total + along_inner(design_part[:, rows], inner - k)
    basis_adjoint = basis_total + jnp.pad(
        design_total[1:].T, ((0, 0), (0, features - REGRESSORS + 1))
    )
    return (design_total[0, :1], basis_adjoint, weight_total)


def solution(mesh):
    placed = (
        P(("groups", "paths"), None),
        P(("groups", "paths"), None),
        P(("groups", "paths")),
        P("groups"),
        P("groups"),
        P("groups"),
        P("groups"),
    )
    return jax.shard_map(
        shards,
        mesh=mesh,
        in_specs=placed,
        out_specs=(P("groups"), P(("groups", "paths"), None), P(("groups", "paths"), None)),
        check_vma=False,
    )
```

```python
import math
from functools import partial

import jax
import jax.numpy as jnp
from jax import lax
from jax.experimental import pallas as pl
from jax.experimental.pallas import tpu as pltpu
from jax.sharding import PartitionSpec as P

REGRESSORS = 32
RIDGE_SCALE = 0.01
PRECISE = lax.Precision.HIGHEST
F32 = jnp.float32
BF16 = jnp.bfloat16
LANES = 128
GROUP = 8
PAD_ROWS = 16
VMEM_BYTES = 48 * 1024 * 1024
CONSTANT = REGRESSORS - 1


def split_axis(size):
    inner = max(d for d in range(1, math.isqrt(size) + 1) if size % d == 0)
    return size // inner, inner


def dot(a, b, ca=1, cb=0, precision=None):
    return lax.dot_general(
        a, b, (((ca,), (cb,)), ((), ())), precision=precision, preferred_element_type=F32
    )


def three(x, axis):
    high = x.astype(BF16)
    rest = x - high.astype(F32)
    middle = rest.astype(BF16)
    low = (rest - middle.astype(F32)).astype(BF16)
    return jnp.concatenate([high, middle, low], axis=axis)


def lanes(shape):
    return lax.broadcasted_iota(jnp.int32, shape, len(shape) - 1)


def rows(shape):
    return lax.broadcasted_iota(jnp.int32, shape, len(shape) - 2)


def first_lanes(x, count):
    return jnp.where(lanes(x.shape) < count, x, 0.0)


def softplus(x):
    return jnp.maximum(x, 0.0) + jnp.log1p(jnp.exp(-jnp.abs(x)))


def sigmoid(x):
    small = jnp.exp(-jnp.abs(x))
    return jnp.where(x >= 0.0, 1.0, small) / (1.0 + small)


def fold_shape(per_device):
    folds = max(1, min(LANES // REGRESSORS, per_device // GROUP))
    return folds, per_device // folds


def fold(x, folds):
    block = x.shape[0] // folds
    total = first_lanes(x[:block], REGRESSORS)
    for q in range(1, folds):
        part = first_lanes(x[q * block : (q + 1) * block], REGRESSORS)
        total = total + pltpu.roll(part, q * REGRESSORS, 1)
    return total


def unfold(x, folds):
    parts = [first_lanes(x, REGRESSORS)]
    for q in range(1, folds):
        parts.append(first_lanes(pltpu.roll(x, LANES - q * REGRESSORS, 1), REGRESSORS))
    return jnp.concatenate(parts, axis=0)


def invert(matrix):
    size = matrix.shape[0]
    shape = (size, 2 * size)
    work = jnp.concatenate([matrix, jnp.eye(size, dtype=F32)], axis=1)
    row = rows(shape)
    col = lanes(shape)
    for k in range(size):
        column = jnp.sum(jnp.where(col == k, work, 0.0), axis=1, keepdims=True)
        pivot = jnp.sum(jnp.where(row == k, work, 0.0), axis=0, keepdims=True)
        pivot = pivot / jnp.sum(jnp.where(lanes(pivot.shape) == k, pivot, 0.0), axis=1, keepdims=True)
        work = jnp.where(row == k, pivot, work - column * pivot)
    return work[:, size:]


def prepare_kernel(ridge, per_device, design_ref, set_ref, x_ref, inverse_ref, member_ref):
    design = design_ref[...]
    count = design.shape[0]
    square = (count, count)
    gram = dot(design, design, 1, 1) + jnp.where(rows(square) == lanes(square), ridge, 0.0)
    inverse_ref[...] = invert(gram)
    sets, trades = member_ref.shape
    folds, fold_rows = fold_shape(per_device)
    block = sets // folds
    place = rows((sets, 1))
    within = place % block
    label = (within // fold_rows) * per_device + (place // block) * fold_rows + within % fold_rows
    member_ref[...] = jnp.where(set_ref[...] == label, 1.0, 0.0).astype(BF16)


def forward_kernel(folds, x_ref, w_ref, notional_ref, design_ref, member_ref, value_ref, moment_ref):
    blocks, block_rows, features = x_ref.shape
    weights = w_ref[...].reshape(-1, features)
    notional = notional_ref[...]
    for b in range(blocks):
        pre_act = dot(x_ref[b], weights, 1, 1)
        value_ref[b * block_rows : (b + 1) * block_rows] = (notional * softplus(pre_act)).astype(BF16)
    trade_moment = dot(design_ref[...], value_ref[...])
    wide = dot(member_ref[...], three(trade_moment, 0), 1, 1)
    wide = jnp.concatenate(
        [wide, jnp.zeros((wide.shape[0], LANES - wide.shape[1]), F32)], axis=1
    )
    moment = wide
    for k in range(1, 3):
        moment = moment + pltpu.roll(wide, LANES - k * REGRESSORS, 1)
    moment_ref[...] = fold(moment, folds)


def slope_kernel(x_ref, w_ref, notional_ref, slope_ref, design_ref):
    blocks, block_rows, features = x_ref.shape
    weights = w_ref[...].reshape(-1, features)
    notional = notional_ref[...]
    for b in range(blocks):
        here = slice(b * block_rows, (b + 1) * block_rows)
        slope_ref[here] = notional * sigmoid(dot(x_ref[b], weights, 1, 1))
        design = x_ref[b, :, :LANES].astype(F32)
        lane = lanes(design.shape)
        design = jnp.where(lane == CONSTANT, 1.0, jnp.where(lane < REGRESSORS, design, 0.0))
        wide = design
        for k in range(1, 3):
            wide = wide + pltpu.roll(design, k * REGRESSORS, 1)
        design_ref[here] = wide.astype(BF16)


def solve_kernel(folds, part_ref, inverse_ref, design_ref, thresh_ref, rate_ref, out_ref):
    devices = part_ref.shape[0]
    total = part_ref[0]
    for d in range(1, devices):
        total = total + part_ref[d]
    moment = unfold(total, folds)[:, :REGRESSORS]
    inverse = inverse_ref[...]
    design = design_ref[...].astype(F32)
    coeffs = dot(moment, inverse, precision=PRECISE)
    excess = dot(coeffs, design, precision=PRECISE) - thresh_ref[...]
    seed = rate_ref[...] * sigmoid(excess)
    adjoint = dot(dot(seed, design, 1, 1, PRECISE), inverse, precision=PRECISE)
    blank = jnp.zeros((coeffs.shape[0], LANES - REGRESSORS), F32)
    fold_rows = out_ref.shape[0] // 2
    out_ref[:fold_rows] = fold(jnp.concatenate([adjoint, blank], axis=1), folds)
    out_ref[fold_rows:] = fold(jnp.concatenate([coeffs, blank], axis=1), folds)


def weight_side_kernel(
    scale, folds, solved_ref, member_ref, design_ref, slope_ref, x_ref, adjoint_ref, slopes_ref, part_ref
):
    fold_rows = solved_ref.shape[1] // 2
    features = x_ref.shape[-1]
    folded = solved_ref[:, :fold_rows].reshape(-1, LANES)
    by_regressor = unfold(folded, folds).T[:REGRESSORS]
    blank = jnp.zeros((LANES - 3 * REGRESSORS, by_regressor.shape[1]), BF16)
    wide = jnp.concatenate([three(by_regressor, 0), blank], axis=0)
    adjoint = dot(wide, member_ref[...]).astype(BF16)
    adjoint_ref[...] = adjoint
    spread = dot(design_ref[...], adjoint).astype(BF16).astype(F32)
    slopes = (slope_ref[...] * spread).astype(BF16)
    slopes_ref[...] = slopes
    basis = x_ref[...].reshape(-1, features)
    part_ref[...] = (dot(slopes, basis, 0, 0) * scale).astype(BF16)


def basis_side_kernel(slopes_ref, w_ref, value_ref, adjoint_ref, part_ref):
    features = w_ref.shape[-1]
    part = dot(slopes_ref[...], w_ref[...].reshape(-1, features))
    wide = dot(value_ref[...], adjoint_ref[...], 1, 1)
    design = wide
    for k in range(1, 3):
        design = design + pltpu.roll(wide, LANES - k * REGRESSORS, 1)
    part_ref[:, :LANES] = (part[:, :LANES] + first_lanes(design, CONSTANT)).astype(BF16)
    part_ref[:, LANES:] = part[:, LANES:].astype(BF16)


def loss_kernel(
    folds, solved_ref, design_ref, own_ref, thresh_ref, rate_ref, loss_ref, own_adjoint_ref, total_ref
):
    fold_rows = solved_ref.shape[1] // 2
    adjoint = unfold(solved_ref[:, :fold_rows].reshape(-1, LANES), folds)[:, :REGRESSORS]
    coeffs = unfold(solved_ref[:, fold_rows:].reshape(-1, LANES), folds)[:, :REGRESSORS]
    thresh = thresh_ref[...]
    rate = rate_ref[...]
    split = three(coeffs, 1)

    def excess(design):
        return dot(split, jnp.concatenate([design] * 3, axis=0)) - thresh

    total_ref[...] = jnp.zeros(total_ref.shape, F32)

    def step(i, carry):
        here = pl.ds(pl.multiple_of(i * LANES, LANES), LANES)
        total_ref[...] += softplus(excess(design_ref[:, here]))
        return carry

    lax.fori_loop(0, design_ref.shape[1] // LANES, step, 0)
    paths_all = design_ref.shape[1]
    sets = coeffs.shape[0]
    weighted = jnp.sum(total_ref[...] * rate, axis=0, keepdims=True)
    loss = jnp.sum(weighted, axis=1, keepdims=True) / (paths_all * sets)
    loss_ref[...] = jnp.broadcast_to(loss, loss_ref.shape)

    own = own_ref[...]
    seed = rate * sigmoid(excess(own))
    cross = dot(adjoint, coeffs, 0, 0, PRECISE)
    cross = cross + dot(coeffs, adjoint, 0, 0, PRECISE)
    own_adjoint = dot(seed, coeffs, 0, 0, PRECISE) - dot(own.astype(F32), cross, 0, 0, PRECISE)
    blank = jnp.zeros((own_adjoint.shape[0], LANES - REGRESSORS), F32)
    own_adjoint_ref[...] = first_lanes(jnp.concatenate([own_adjoint, blank], axis=1), CONSTANT)


def sum_kernel(basis_ref, weight_ref, own_ref, basis_out_ref, weight_out_ref):
    basis = basis_ref[0].astype(F32)
    for k in range(1, basis_ref.shape[0]):
        basis = basis + basis_ref[k].astype(F32)
    basis_out_ref[:, :LANES] = basis[:, :LANES] + own_ref[...]
    basis_out_ref[:, LANES:] = basis[:, LANES:]
    weight = weight_ref[0].astype(F32)
    for k in range(1, weight_ref.shape[0]):
        weight = weight + weight_ref[k].astype(F32)
    weight_out_ref[...] = weight


def call(kernel, outs, *args, name, flops=0, scratch=()):
    size = sum(a.size * a.dtype.itemsize for a in args) + sum(
        math.prod(s) * jnp.dtype(d).itemsize for s, d in outs
    )
    return pl.pallas_call(
        kernel,
        out_shape=[jax.ShapeDtypeStruct(s, d) for s, d in outs],
        in_specs=[pl.BlockSpec(memory_space=pltpu.VMEM)] * len(args),
        out_specs=[pl.BlockSpec(memory_space=pltpu.VMEM)] * len(outs),
        scratch_shapes=scratch,
        compiler_params=pltpu.CompilerParams(vmem_limit_bytes=VMEM_BYTES),
        cost_estimate=pl.CostEstimate(flops=int(flops), bytes_accessed=int(size), transcendentals=0),
        name=name,
    )(*args)


def shards(
    path_basis, proxy_weight, notional, set_of, threshold_index, threshold_levels, loss_rate
):
    n = lax.axis_size("paths")
    outer, inner = split_axis(n)
    me = lax.axis_index("paths")
    my_outer, my_inner = me // inner, me % inner
    path_rows, features = path_basis.shape
    trade_rows = proxy_weight.shape[0]
    paths_all = path_rows * n
    sets = loss_rate.shape[0]
    per_device = sets // n
    folds, fold_rows = fold_shape(per_device)
    group_paths, group_trades = inner * path_rows, outer * trade_rows

    def swap(x, groups):
        return lax.all_to_all(x, "paths", 0, 0, axis_index_groups=groups, tiled=True)

    def spread_out(x, count, groups):
        return swap(jnp.broadcast_to(x[None], (count,) + x.shape), groups)

    everyone = [list(range(n))]
    along_inner = [[o * inner + i for i in range(inner)] for o in range(outer)]
    along_outer = [[o * inner + i for o in range(outer)] for i in range(inner)]

    width = max(path_rows, trade_rows)
    lead = path_basis[:, :REGRESSORS].T
    lead = jnp.where(jnp.arange(REGRESSORS)[:, None] == CONSTANT, jnp.ones((), BF16), lead)
    small = jnp.concatenate(
        [
            jnp.pad(lead, ((0, 0), (0, width - path_rows))),
            jnp.pad(notional[None, :], ((0, PAD_ROWS - 1), (0, width - trade_rows))),
        ],
        axis=0,
    )
    small_all = spread_out(small, n, everyone).reshape(outer, inner, -1, width)
    weights = spread_out(proxy_weight, outer, along_outer)
    basis = spread_out(path_basis, inner, along_inner)

    design_all = small_all[:, :, :REGRESSORS, :path_rows].transpose(2, 0, 1, 3)
    design_group = lax.dynamic_index_in_dim(design_all, my_outer, 1, False)
    design_group = design_group.reshape(REGRESSORS, group_paths)
    design_all = design_all.reshape(REGRESSORS, paths_all)
    notional_group = lax.dynamic_index_in_dim(small_all, my_inner, 1, False)
    notional_group = notional_group[:, REGRESSORS, :trade_rows].reshape(1, group_trades).astype(F32)
    set_group = lax.dynamic_index_in_dim(set_of.reshape(outer, inner, trade_rows), my_inner, 1, False)
    set_group = set_group.reshape(1, group_trades)

    level = threshold_index[:, None] == jnp.arange(threshold_levels.shape[0], dtype=jnp.int32)[None, :]
    thresholds = jnp.sum(jnp.where(level, threshold_levels[None, :], 0.0), axis=1)

    def own_sets(x):
        return lax.dynamic_slice_in_dim(x, me * per_device, per_device)[:, None]

    def packed_sets(x):
        return x.reshape(n, folds, fold_rows).transpose(1, 0, 2).reshape(sets, 1)

    inverse, member = call(
        partial(prepare_kernel, RIDGE_SCALE * paths_all, per_device),
        [((REGRESSORS, REGRESSORS), F32), ((sets, group_trades), BF16)],
        design_all, set_group, design_group,
        name="prepare",
    )
    value, moment = call(
        partial(forward_kernel, folds),
        [((group_paths, group_trades), BF16), ((n * fold_rows, LANES), F32)],
        basis, weights, notional_group, design_group, member,
        name="forward",
    )
    parts = swap(moment, everyone).reshape(n, fold_rows, LANES)
    slope, design_wide = call(
        slope_kernel,
        [((group_paths, group_trades), F32), ((group_paths, LANES), BF16)],
        basis, weights, notional_group,
        name="slope",
    )
    (solved,) = call(
        partial(solve_kernel, folds),
        [((2 * fold_rows, LANES), F32)],
        parts, inverse, design_all, own_sets(thresholds), own_sets(loss_rate),
        name="solve",
    )
    solved_all = spread_out(solved, n, everyone)
    scale = 1.0 / math.sqrt(paths_all)
    adjoint, slopes, weight_part = call(
        partial(weight_side_kernel, scale, folds),
        [
            ((LANES, group_trades), BF16),
            ((group_paths, group_trades), BF16),
            ((group_trades, features), BF16),
        ],
        solved_all, member, design_wide, slope, basis,
        name="weight_side",
    )
    weight_parts = swap(weight_part.reshape(outer, trade_rows, features), along_outer)
    (basis_part,) = call(
        basis_side_kernel,
        [((group_paths, features), BF16)],
        slopes, weights, value, adjoint,
        name="basis_side",
    )
    basis_parts = swap(basis_part.reshape(inner, path_rows, features), along_inner)
    loss, own_adjoint = call(
        partial(loss_kernel, folds),
        [((GROUP, LANES), F32), ((path_rows, LANES), F32)],
        solved_all, design_all, lead, packed_sets(thresholds), packed_sets(loss_rate),
        name="loss",
        scratch=[pltpu.VMEM((sets, LANES), F32)],
    )
    basis_adjoint, weight_adjoint = call(
        sum_kernel,
        [((path_rows, features), F32), ((trade_rows, features), F32)],
        basis_parts, weight_parts, own_adjoint,
        name="sums",
    )
    return (loss[0, :1], basis_adjoint, weight_adjoint)


def solution(mesh):
    placed = (
        P(("groups", "paths"), None),
        P(("groups", "paths"), None),
        P(("groups", "paths")),
        P("groups"),
        P("groups"),
        P("groups"),
        P("groups"),
    )
    return jax.shard_map(
        shards,
        mesh=mesh,
        in_specs=placed,
        out_specs=(P("groups"), P(("groups", "paths"), None), P(("groups", "paths"), None)),
        check_vma=False,
    )
```

```python
import math
from functools import partial

import jax
import jax.numpy as jnp
from jax import lax
from jax.experimental import pallas as pl
from jax.experimental.pallas import tpu as pltpu
from jax.sharding import PartitionSpec as P

REGRESSORS = 32
RIDGE_SCALE = 0.01
PRECISE = lax.Precision.HIGHEST
F32 = jnp.float32
BF16 = jnp.bfloat16
LANES = 128
PAD_ROWS = 16
CHUNK = 256
VMEM_BYTES = 48 * 1024 * 1024
LOG2_E = math.log2(math.e)
CONSTANT = REGRESSORS - 1


def split_bits(size):
    count = size.bit_length() - 1
    half = count // 2
    return list(range(1, half + 1)), list(range(count - 1, half, -1)) + [0]


def dot(a, b, ca=1, cb=0, precision=None):
    return lax.dot_general(
        a, b, (((ca,), (cb,)), ((), ())), precision=precision, preferred_element_type=F32
    )


def three(x, axis):
    high = x.astype(BF16)
    rest = x - high.astype(F32)
    middle = rest.astype(BF16)
    low = (rest - middle.astype(F32)).astype(BF16)
    return jnp.concatenate([high, middle, low], axis=axis)


def three_rows(x):
    blank = jnp.zeros((LANES - 3 * REGRESSORS, x.shape[1]), BF16)
    return jnp.concatenate([three(x, 0), blank], axis=0)


def lanes(shape):
    return lax.broadcasted_iota(jnp.int32, shape, len(shape) - 1)


def rows(shape):
    return lax.broadcasted_iota(jnp.int32, shape, len(shape) - 2)


def softplus(x):
    return jnp.maximum(x, 0.0) + jnp.log1p(jnp.exp(-jnp.abs(x)))


def sigmoid(x):
    small = jnp.exp(-jnp.abs(x))
    return jnp.where(x >= 0.0, 1.0, small) / (1.0 + small)


def each_chunk(size, step):
    count = size // CHUNK

    def body(i, carry):
        step(pl.ds(pl.multiple_of(i * CHUNK, CHUNK), CHUNK))
        return carry

    lax.fori_loop(0, count, body, 0, unroll=count <= 8)


def invert(matrix):
    size = matrix.shape[0]
    shape = (size, 2 * size)
    work = jnp.concatenate([matrix, jnp.eye(size, dtype=F32)], axis=1)
    row = rows(shape)
    col = lanes(shape)
    for k in range(size):
        column = jnp.sum(jnp.where(col == k, work, 0.0), axis=1, keepdims=True)
        pivot = jnp.sum(jnp.where(row == k, work, 0.0), axis=0, keepdims=True)
        pivot = pivot / jnp.sum(jnp.where(lanes(pivot.shape) == k, pivot, 0.0), axis=1, keepdims=True)
        work = jnp.where(row == k, pivot, work - column * pivot)
    return work[:, size:]


def member_kernel(set_ref, member_ref):
    label = rows((member_ref.shape[0], 1))
    member_ref[...] = jnp.where(set_ref[...] == label, 1.0, 0.0).astype(BF16)


def prepare_kernel(ridge, path_rows, small_ref, inverse_ref, design_ref, rows_ref):
    for d in range(small_ref.shape[0]):
        here = slice(d * path_rows, (d + 1) * path_rows)
        block = small_ref[d, :REGRESSORS, :path_rows]
        design_ref[:, here] = block
        turned = block.astype(F32).T
        blank = jnp.zeros((path_rows, LANES - 3 * REGRESSORS), F32)
        rows_ref[here] = jnp.concatenate([turned] * 3 + [blank], axis=1).astype(BF16)
    design = design_ref[...]
    square = (REGRESSORS, REGRESSORS)
    gram = dot(design, design, 1, 1) + jnp.where(rows(square) == lanes(square), ridge, 0.0)
    inverse_ref[...] = invert(gram)


def forward_kernel(paths, trades, *refs):
    x_refs, w_refs = refs[:paths], refs[paths : paths + trades]
    notional_ref, design_ref, member_ref, value_ref, moment_ref = refs[paths + trades :]
    weights = jnp.concatenate([w[...] for w in w_refs], axis=0)
    notional = notional_ref[...]
    start = 0
    for x in x_refs:
        pre_act = dot(x[...], weights, 1, 1)
        value_ref[start : start + x.shape[0]] = (notional * softplus(pre_act)).astype(BF16)
        start += x.shape[0]
    trade_moment = dot(design_ref[...], value_ref[...])
    parts = dot(three(trade_moment, 0), member_ref[...], 1, 1)
    moment_ref[...] = (
        parts[:REGRESSORS] + parts[REGRESSORS : 2 * REGRESSORS] + parts[2 * REGRESSORS :]
    )


def slope_kernel(paths, trades, *refs):
    x_refs, w_refs = refs[:paths], refs[paths : paths + trades]
    notional_ref, slope_ref = refs[paths + trades :]
    weights = jnp.concatenate([w[...] for w in w_refs], axis=0)
    notional = notional_ref[...]
    start = 0
    for x in x_refs:
        slope_ref[start : start + x.shape[0]] = notional * sigmoid(dot(x[...], weights, 1, 1))
        start += x.shape[0]


def solve_kernel(
    scale, paths, trades, moment_ref, inverse_ref, design_ref, rows_ref, thresh_ref, rate_ref,
    member_ref, slope_ref, *refs,
):
    x_refs = refs[:paths]
    coeffs_ref, adjoint_ref, traded_ref, slopes_ref = refs[paths : paths + 4]
    part_refs = refs[paths + 4 : paths + 4 + trades]
    turn_ref, total_ref = refs[paths + 4 + trades :]
    inverse = inverse_ref[...]
    coeffs = dot(inverse, moment_ref[...], precision=PRECISE)
    coeffs_ref[...] = coeffs
    is_constant = rows(coeffs.shape) == CONSTANT
    turn_ref[...] = three_rows(-LOG2_E * (coeffs - jnp.where(is_constant, thresh_ref[...], 0.0)))
    total_ref[...] = jnp.zeros(total_ref.shape, F32)

    def seeds(here):
        power = jnp.exp2(jnp.minimum(dot(rows_ref[here], turn_ref[...]), 126.0))
        seed = (1.0 / (1.0 + power)).astype(BF16)
        total_ref[...] += dot(design_ref[:, here], seed)

    each_chunk(rows_ref.shape[0], seeds)
    adjoint = dot(inverse, total_ref[...] * rate_ref[...], precision=PRECISE)
    adjoint_ref[...] = adjoint
    traded = dot(three_rows(adjoint), member_ref[...]).astype(BF16)
    traded_ref[...] = traded
    group = slopes_ref.shape[0]
    spread = dot(rows_ref[:group], traded).astype(BF16).astype(F32)
    slopes_ref[...] = (slope_ref[...] * spread).astype(BF16)
    basis = jnp.concatenate([x[...] for x in x_refs], axis=0)
    weight = (dot(slopes_ref[...], basis, 0, 0) * scale).astype(BF16)
    start = 0
    for part in part_refs:
        part[...] = weight[start : start + part.shape[0]]
        start += part.shape[0]


def basis_kernel(trades, slopes_ref, value_ref, traded_ref, *refs):
    w_refs, part_refs = refs[:trades], refs[trades:]
    weights = jnp.concatenate([w[...] for w in w_refs], axis=0)
    start = 0
    for part in part_refs:
        here = slice(start, start + part.shape[0])
        total = dot(slopes_ref[here], weights)
        wide = dot(value_ref[here], traded_ref[...], 1, 1)
        design = wide
        for k in range(1, 3):
            design = design + pltpu.roll(wide, LANES - k * REGRESSORS, 1)
        design = jnp.where(lanes(design.shape) < CONSTANT, design, 0.0)
        part[:, :LANES] = (total[:, :LANES] + design).astype(BF16)
        part[:, LANES:] = total[:, LANES:].astype(BF16)
        start += part.shape[0]


def loss_kernel(
    coeffs_ref, adjoint_ref, rows_ref, thresh_ref, rate_ref, loss_ref, own_ref, split_ref, total_ref
):
    coeffs = coeffs_ref[...]
    adjoint = adjoint_ref[...]
    thresh = thresh_ref[...]
    rate = rate_ref[...]
    split_ref[...] = three_rows(coeffs)
    total_ref[...] = jnp.zeros(total_ref.shape, F32)

    def losses(here):
        loss = softplus(dot(rows_ref[here], split_ref[...]) - thresh)
        total_ref[...] += jnp.sum(loss.reshape(-1, *total_ref.shape), axis=0)

    each_chunk(rows_ref.shape[0], losses)
    summed = jnp.sum(jnp.sum(total_ref[...] * rate, axis=0, keepdims=True), axis=1, keepdims=True)
    loss_ref[...] = jnp.broadcast_to(
        summed / (rows_ref.shape[0] * coeffs.shape[1]), loss_ref.shape
    )
    own = rows_ref[: own_ref.shape[0]]
    fitted = dot(own, split_ref[...])
    seed = rate * sigmoid(fitted - thresh)
    rest = seed - dot(own, three_rows(adjoint))
    design = dot(rest, coeffs, 1, 1, PRECISE) - dot(fitted, adjoint, 1, 1, PRECISE)
    blank = jnp.zeros((design.shape[0], LANES - REGRESSORS), F32)
    design = jnp.concatenate([design, blank], axis=1)
    own_ref[...] = jnp.where(lanes(design.shape) < CONSTANT, design, 0.0)


def sum_kernel(first, *refs):
    own_ref, terms = refs[0], refs[1:-2]
    basis_out_ref, weight_out_ref = refs[-2:]

    def total(parts):
        out = parts[0][...].astype(F32)
        for part in parts[1:]:
            out = out + part[...].astype(F32)
        return out

    basis = total(terms[:first])
    basis_out_ref[:, :LANES] = basis[:, :LANES] + own_ref[...]
    basis_out_ref[:, LANES:] = basis[:, LANES:]
    weight_out_ref[...] = total(terms[first:])


def call(kernel, outs, *args, name, flops=0, scratch=()):
    size = sum(a.size * a.dtype.itemsize for a in args) + sum(
        math.prod(s) * jnp.dtype(d).itemsize for s, d in outs
    )
    return pl.pallas_call(
        kernel,
        out_shape=[jax.ShapeDtypeStruct(s, d) for s, d in outs],
        in_specs=[pl.BlockSpec(memory_space=pltpu.VMEM)] * len(args),
        out_specs=[pl.BlockSpec(memory_space=pltpu.VMEM)] * len(outs),
        scratch_shapes=scratch,
        compiler_params=pltpu.CompilerParams(vmem_limit_bytes=VMEM_BYTES),
        cost_estimate=pl.CostEstimate(flops=int(flops), bytes_accessed=int(size), transcendentals=0),
        name=name,
    )(*args)


def shards(
    path_basis, proxy_weight, notional, set_of, threshold_index, threshold_levels, loss_rate
):
    n = lax.axis_size("paths")
    me = lax.axis_index("paths")
    inner_bits, outer_bits = split_bits(n)
    inner, outer = 1 << len(inner_bits), 1 << len(outer_bits)
    path_rows, features = path_basis.shape
    trade_rows = proxy_weight.shape[0]
    paths_all = path_rows * n
    sets = loss_rate.shape[0]
    group_paths, group_trades = inner * path_rows, outer * trade_rows

    def swap(x, bit):
        return lax.ppermute(x, "paths", [(d, d ^ (1 << bit)) for d in range(n)])

    def gather(x, bits):
        slots = [x]
        for bit in bits:
            slots = slots + [swap(s, bit) for s in slots]
        return slots

    def halve(slots, bits):
        slots = [[s] for s in slots]
        for bit in reversed(bits):
            count = len(slots) // 2
            for k in reversed(range(count)):
                gone = slots[count + k]
                if len(gone) > 1:
                    gone = [sum(g.astype(F32) for g in gone).astype(BF16)]
                slots[k].append(swap(gone[0], bit))
            slots = slots[:count]
        return slots[0]

    weights = gather(proxy_weight, outer_bits)
    basis = gather(path_basis, inner_bits)

    width = max(path_rows, trade_rows)
    lead = path_basis[:, :REGRESSORS].T
    lead = jnp.where(jnp.arange(REGRESSORS)[:, None] == CONSTANT, jnp.ones((), BF16), lead)
    small = jnp.concatenate(
        [
            jnp.pad(lead, ((0, 0), (0, width - path_rows))),
            jnp.pad(notional[None, :], ((0, PAD_ROWS - 1), (0, width - trade_rows))),
        ],
        axis=0,
    )[None]
    for bit in inner_bits + outer_bits:
        small = jnp.concatenate([small, swap(small, bit)], axis=0)
    design_group = jnp.concatenate([small[k, :REGRESSORS, :path_rows] for k in range(inner)], axis=1)
    notional_group = small[::inner, REGRESSORS, :trade_rows].reshape(1, group_trades).astype(F32)
    set_blocks = set_of.reshape(n, trade_rows)
    set_group = []
    for k in range(outer):
        mask = sum(((k >> j) & 1) << bit for j, bit in enumerate(outer_bits))
        set_group.append(lax.dynamic_index_in_dim(set_blocks, me ^ mask, 0))
    set_group = jnp.concatenate(set_group, axis=1)

    level = threshold_index[:, None] == jnp.arange(threshold_levels.shape[0], dtype=jnp.int32)[None, :]
    thresh = jnp.sum(jnp.where(level, threshold_levels[None, :], 0.0), axis=1)[None, :]
    rate = loss_rate[None, :]

    (member,) = call(member_kernel, [((sets, group_trades), BF16)], set_group, name="member")
    value, moment = call(
        partial(forward_kernel, inner, outer),
        [((group_paths, group_trades), BF16), ((REGRESSORS, sets), F32)],
        *basis, *weights, notional_group, design_group, member,
        name="forward",
    )
    for bit in inner_bits + outer_bits:
        moment = moment + swap(moment, bit)
    (slope,) = call(
        partial(slope_kernel, inner, outer),
        [((group_paths, group_trades), F32)],
        *basis, *weights, notional_group,
        name="slope",
    )
    inverse, design_all, design_rows = call(
        partial(prepare_kernel, RIDGE_SCALE * paths_all, path_rows),
        [((REGRESSORS, REGRESSORS), F32), ((REGRESSORS, paths_all), BF16), ((paths_all, LANES), BF16)],
        small,
        name="prepare",
    )
    coeffs, adjoint, traded, slopes, *weight_parts = call(
        partial(solve_kernel, 1.0 / math.sqrt(paths_all), inner, outer),
        [
            ((REGRESSORS, sets), F32),
            ((REGRESSORS, sets), F32),
            ((LANES, group_trades), BF16),
            ((group_paths, group_trades), BF16),
        ]
        + [((trade_rows, features), BF16)] * outer,
        moment, inverse, design_all, design_rows, thresh, rate, member, slope, *basis,
        name="solve",
        scratch=[pltpu.VMEM((LANES, sets), BF16), pltpu.VMEM((REGRESSORS, sets), F32)],
    )
    weight_terms = halve(weight_parts, outer_bits)
    basis_parts = call(
        partial(basis_kernel, outer),
        [((path_rows, features), BF16)] * inner,
        slopes, value, traded, *weights,
        name="basis_side",
    )
    basis_terms = halve(basis_parts, inner_bits)
    loss, own_adjoint = call(
        loss_kernel,
        [((8, LANES), F32), ((path_rows, LANES), F32)],
        coeffs, adjoint, design_rows, thresh, rate,
        name="loss",
        scratch=[pltpu.VMEM((LANES, sets), BF16), pltpu.VMEM((8, sets), F32)],
    )
    basis_adjoint, weight_adjoint = call(
        partial(sum_kernel, len(basis_terms)),
        [((path_rows, features), F32), ((trade_rows, features), F32)],
        own_adjoint, *basis_terms, *weight_terms,
        name="sums",
    )
    return (loss[0, :1], basis_adjoint, weight_adjoint)


def solution(mesh):
    placed = (
        P(("groups", "paths"), None),
        P(("groups", "paths"), None),
        P(("groups", "paths")),
        P("groups"),
        P("groups"),
        P("groups"),
        P("groups"),
    )
    return jax.shard_map(
        shards,
        mesh=mesh,
        in_specs=placed,
        out_specs=(P("groups"), P(("groups", "paths"), None), P(("groups", "paths"), None)),
        check_vma=False,
    )
```

```python
import math
from functools import partial

import jax
import jax.numpy as jnp
from jax import lax
from jax.experimental import pallas as pl
from jax.experimental.pallas import tpu as pltpu
from jax.sharding import PartitionSpec as P

REGRESSORS = 32
RIDGE_SCALE = 0.01
PRECISE = lax.Precision.HIGHEST
F32 = jnp.float32
BF16 = jnp.bfloat16
LANES = 128
PAD_ROWS = 16
CHUNK = 256
VMEM_BYTES = 48 * 1024 * 1024
LOG2_E = math.log2(math.e)
CONSTANT = REGRESSORS - 1


def split_bits(size):
    count = size.bit_length() - 1
    half = count // 2
    return list(range(1, half + 1)), list(range(count - 1, half, -1)) + [0]


def dot(a, b, ca=1, cb=0, precision=None):
    return lax.dot_general(
        a, b, (((ca,), (cb,)), ((), ())), precision=precision, preferred_element_type=F32
    )


def three(x, axis):
    high = x.astype(BF16)
    rest = x - high.astype(F32)
    middle = rest.astype(BF16)
    low = (rest - middle.astype(F32)).astype(BF16)
    return jnp.concatenate([high, middle, low], axis=axis)


def three_rows(x):
    blank = jnp.zeros((LANES - 3 * REGRESSORS, x.shape[1]), BF16)
    return jnp.concatenate([three(x, 0), blank], axis=0)


def lanes(shape):
    return lax.broadcasted_iota(jnp.int32, shape, len(shape) - 1)


def rows(shape):
    return lax.broadcasted_iota(jnp.int32, shape, len(shape) - 2)


def softplus(x):
    return jnp.maximum(x, 0.0) + jnp.log1p(jnp.exp(-jnp.abs(x)))


def sigmoid(x):
    small = jnp.exp(-jnp.abs(x))
    return jnp.where(x >= 0.0, 1.0, small) / (1.0 + small)


def each_chunk(size, step):
    count = size // CHUNK

    def body(i, carry):
        step(pl.ds(pl.multiple_of(i * CHUNK, CHUNK), CHUNK))
        return carry

    lax.fori_loop(0, count, body, 0, unroll=count <= 8)


def invert(matrix):
    size = matrix.shape[0]
    work = jnp.concatenate([matrix, jnp.eye(size, dtype=F32)], axis=1)
    row = rows((size, 2 * size))
    for k in range(size):
        pivot = work[k : k + 1] / work[k : k + 1, k : k + 1]
        work = jnp.where(row == k, pivot, work - work[:, k : k + 1] * pivot)
    return work[:, size:]


def tables_kernel(
    trade_masks, inner, me_ref, level_ref, set_ref, index_ref, rate_ref,
    member_ref, thresh_out_ref, rate_out_ref,
):
    me = me_ref[0]
    place = (me >> 1) & (inner - 1)
    size = member_ref.shape[0] // inner
    trades = set_ref.shape[-1]
    for m in range(inner):
        here = slice(m * size, (m + 1) * size)
        label = (place ^ m) * size + rows((size, 1))
        for j, mask in enumerate(trade_masks):
            member_ref[here, j * trades : (j + 1) * trades] = jnp.where(
                set_ref[me ^ mask] == label, 1.0, 0.0
            ).astype(BF16)
        index = index_ref[place ^ m]
        thresh = jnp.zeros(index.shape, F32)
        for k in range(level_ref.shape[0]):
            thresh = jnp.where(index == k, level_ref[k], thresh)
        thresh_out_ref[:, here] = thresh
        rate_out_ref[:, here] = rate_ref[place ^ m]


def design_kernel(path_rows, small_ref, design_ref, rows_ref):
    for d in range(small_ref.shape[0]):
        here = slice(d * path_rows, (d + 1) * path_rows)
        block = small_ref[d, :REGRESSORS, :path_rows]
        design_ref[:, here] = block
        turned = block.astype(F32).T
        blank = jnp.zeros((path_rows, LANES - 3 * REGRESSORS), F32)
        rows_ref[here] = jnp.concatenate([turned] * 3 + [blank], axis=1).astype(BF16)


def inverse_kernel(ridge, path_rows, small_ref, inverse_ref):
    square = (REGRESSORS, REGRESSORS)
    gram = jnp.where(rows(square) == lanes(square), ridge, 0.0)
    for d in range(small_ref.shape[0]):
        block = small_ref[d, :REGRESSORS, :path_rows]
        gram = gram + dot(block, block, 1, 1)
    inverse_ref[...] = invert(gram)


def forward_kernel(paths, trades, *refs):
    x_refs, w_refs = refs[:paths], refs[paths : paths + trades]
    notional_ref, design_ref, member_ref, value_ref, *moment_refs = refs[paths + trades :]
    weights = jnp.concatenate([w[...] for w in w_refs], axis=0)
    notional = notional_ref[...]
    start = 0
    for x in x_refs:
        pre_act = dot(x[...], weights, 1, 1)
        value_ref[start : start + x.shape[0]] = (notional * softplus(pre_act)).astype(BF16)
        start += x.shape[0]
    trade_moment = dot(design_ref[...], value_ref[...])
    parts = dot(three(trade_moment, 0), member_ref[...], 1, 1)
    moment = parts[:REGRESSORS] + parts[REGRESSORS : 2 * REGRESSORS] + parts[2 * REGRESSORS :]
    size = moment.shape[1] // len(moment_refs)
    for m, moment_ref in enumerate(moment_refs):
        moment_ref[...] = moment[:, m * size : (m + 1) * size]


def slope_kernel(paths, trades, *refs):
    x_refs, w_refs = refs[:paths], refs[paths : paths + trades]
    notional_ref, slope_ref = refs[paths + trades :]
    weights = jnp.concatenate([w[...] for w in w_refs], axis=0)
    notional = notional_ref[...]
    start = 0
    for x in x_refs:
        slope_ref[start : start + x.shape[0]] = notional * sigmoid(dot(x[...], weights, 1, 1))
        start += x.shape[0]


def solve_kernel(
    terms, inverse_ref, design_ref, rows_ref, thresh_ref, rate_ref, *refs
):
    solved_ref, turn_ref, total_ref = refs[terms:]
    moment = refs[0][...]
    for ref in refs[1:terms]:
        moment = moment + ref[...]
    size = moment.shape[1]
    inverse = inverse_ref[...]
    coeffs = dot(inverse, moment, precision=PRECISE)
    solved_ref[REGRESSORS:] = coeffs
    is_constant = rows(coeffs.shape) == CONSTANT
    shifted = coeffs - jnp.where(is_constant, thresh_ref[:, :size], 0.0)
    turn_ref[...] = three_rows(-LOG2_E * shifted)
    total_ref[...] = jnp.zeros(total_ref.shape, F32)

    def seeds(here):
        power = jnp.exp2(jnp.minimum(dot(rows_ref[here], turn_ref[...]), 126.0))
        seed = (1.0 / (1.0 + power)).astype(BF16)
        total_ref[...] += dot(design_ref[:, here], seed)

    each_chunk(rows_ref.shape[0], seeds)
    solved_ref[:REGRESSORS] = dot(inverse, total_ref[...] * rate_ref[:, :size], precision=PRECISE)


def joined(refs, part):
    here = slice(part * REGRESSORS, (part + 1) * REGRESSORS)
    return jnp.concatenate([ref[here] for ref in refs], axis=1)


def backward_kernel(scale, paths, trades, member_ref, rows_ref, slope_ref, value_ref, *refs):
    solved_refs, refs = refs[:paths], refs[paths:]
    x_refs, refs = refs[:paths], refs[paths:]
    w_refs, refs = refs[:trades], refs[trades:]
    weight_refs, basis_refs, slopes_ref = refs[:trades], refs[trades:-1], refs[-1]
    traded = dot(three_rows(joined(solved_refs, 0)), member_ref[...]).astype(BF16)
    group = slopes_ref.shape[0]
    spread = dot(rows_ref[:group], traded).astype(BF16).astype(F32)
    slopes_ref[...] = (slope_ref[...] * spread).astype(BF16)
    basis = jnp.concatenate([x[...] for x in x_refs], axis=0)
    weight = (dot(slopes_ref[...], basis, 0, 0) * scale).astype(BF16)
    start = 0
    for part in weight_refs:
        part[...] = weight[start : start + part.shape[0]]
        start += part.shape[0]
    weights = jnp.concatenate([w[...] for w in w_refs], axis=0)
    start = 0
    for part in basis_refs:
        here = slice(start, start + part.shape[0])
        total = dot(slopes_ref[here], weights)
        wide = dot(value_ref[here], traded, 1, 1)
        design = wide
        for k in range(1, 3):
            design = design + pltpu.roll(wide, LANES - k * REGRESSORS, 1)
        design = jnp.where(lanes(design.shape) < CONSTANT, design, 0.0)
        part[:, :LANES] = (total[:, :LANES] + design).astype(BF16)
        part[:, LANES:] = total[:, LANES:].astype(BF16)
        start += part.shape[0]


def loss_kernel(rows_ref, thresh_ref, rate_ref, *refs):
    solved_refs, (loss_ref, own_ref, split_ref, total_ref) = refs[:-4], refs[-4:]
    adjoint = joined(solved_refs, 0)
    coeffs = joined(solved_refs, 1)
    thresh = thresh_ref[...]
    rate = rate_ref[...]
    split_ref[...] = three_rows(coeffs)
    total_ref[...] = jnp.zeros(total_ref.shape, F32)

    def losses(here):
        loss = softplus(dot(rows_ref[here], split_ref[...]) - thresh)
        total_ref[...] += jnp.sum(loss.reshape(-1, *total_ref.shape), axis=0)

    each_chunk(rows_ref.shape[0], losses)
    summed = jnp.sum(jnp.sum(total_ref[...] * rate, axis=0, keepdims=True), axis=1, keepdims=True)
    loss_ref[...] = jnp.broadcast_to(
        summed / (rows_ref.shape[0] * coeffs.shape[1]), loss_ref.shape
    )
    own = rows_ref[: own_ref.shape[0]]
    fitted = dot(own, split_ref[...])
    seed = rate * sigmoid(fitted - thresh)
    rest = seed - dot(own, three_rows(adjoint))
    design = dot(rest, coeffs, 1, 1, PRECISE) - dot(fitted, adjoint, 1, 1, PRECISE)
    blank = jnp.zeros((design.shape[0], LANES - REGRESSORS), F32)
    design = jnp.concatenate([design, blank], axis=1)
    own_ref[...] = jnp.where(lanes(design.shape) < CONSTANT, design, 0.0)


def total(refs):
    out = refs[0][...].astype(F32)
    for ref in refs[1:]:
        out = out + ref[...].astype(F32)
    return out


def weight_sum_kernel(*refs):
    refs[-1][...] = total(refs[:-1])


def basis_sum_kernel(own_ref, *refs):
    basis = total(refs[:-1])
    refs[-1][:, :LANES] = basis[:, :LANES] + own_ref[...]
    refs[-1][:, LANES:] = basis[:, LANES:]


def call(kernel, outs, *args, name, flops=0, scratch=(), scalars=0):
    size = sum(a.size * a.dtype.itemsize for a in args) + sum(
        math.prod(s) * jnp.dtype(d).itemsize for s, d in outs
    )
    return pl.pallas_call(
        kernel,
        out_shape=[jax.ShapeDtypeStruct(s, d) for s, d in outs],
        in_specs=[pl.BlockSpec(memory_space=pltpu.SMEM)] * scalars
        + [pl.BlockSpec(memory_space=pltpu.VMEM)] * (len(args) - scalars),
        out_specs=[pl.BlockSpec(memory_space=pltpu.VMEM)] * len(outs),
        scratch_shapes=scratch,
        compiler_params=pltpu.CompilerParams(vmem_limit_bytes=VMEM_BYTES),
        cost_estimate=pl.CostEstimate(flops=int(flops), bytes_accessed=int(size), transcendentals=0),
        name=name,
    )(*args)


def shards(
    path_basis, proxy_weight, notional, set_of, threshold_index, threshold_levels, loss_rate
):
    n = lax.axis_size("paths")
    me = lax.axis_index("paths")
    inner_bits, outer_bits = split_bits(n)
    inner, outer = 1 << len(inner_bits), 1 << len(outer_bits)
    path_rows, features = path_basis.shape
    trade_rows = proxy_weight.shape[0]
    paths_all = path_rows * n
    sets = loss_rate.shape[0]
    quarter = sets // inner
    group_paths, group_trades = inner * path_rows, outer * trade_rows

    def swap(x, mask):
        return lax.ppermute(x, "paths", [(d, d ^ mask) for d in range(n)])

    def masks(bits):
        return [
            sum(((m >> j) & 1) << bit for j, bit in enumerate(bits)) for m in range(1 << len(bits))
        ]

    def after(x, *others):
        return lax.optimization_barrier((x, *others))[0]

    def direct(slots, bits):
        return [swap(x, mask) for x, mask in zip(slots[1:], masks(bits)[1:])]

    def halve(slots, bits):
        slots = [[s] for s in slots]
        for bit in reversed(bits):
            count = len(slots) // 2
            last = None
            for k in reversed(range(count)):
                gone = slots[count + k]
                gone = gone[0] if len(gone) == 1 else sum(g.astype(F32) for g in gone).astype(BF16)
                if last is not None:
                    gone = after(gone, last)
                last = swap(gone, 1 << bit)
                slots[k].append(last)
            slots = slots[:count]
        return slots[0]

    basis = [path_basis]
    weights = [proxy_weight]
    for j, bit in enumerate(outer_bits):
        if j == 1:
            break
        weights = weights + [swap(w, 1 << bit) for w in weights]
    for bit in inner_bits:
        basis = basis + [swap(x, 1 << bit) for x in basis]
    for bit in outer_bits[1:]:
        weights = weights + [swap(w if k else after(w, basis[1]), 1 << bit) for k, w in enumerate(weights)]

    width = max(path_rows, trade_rows)
    lead = path_basis[:, :REGRESSORS].T
    lead = jnp.where(jnp.arange(REGRESSORS)[:, None] == CONSTANT, jnp.ones((), BF16), lead)
    small = jnp.concatenate(
        [
            jnp.pad(lead, ((0, 0), (0, width - path_rows))),
            jnp.pad(notional[None, :], ((0, PAD_ROWS - 1), (0, width - trade_rows))),
        ],
        axis=0,
    )[None]
    for j, bit in enumerate(inner_bits + outer_bits):
        small = jnp.concatenate([small, swap(small, 1 << bit)], axis=0)
        if j == 0:
            small = after(small, basis[1])
        if j == 1:
            small = after(small, weights[1])
    design_group = jnp.concatenate([small[k, :REGRESSORS, :path_rows] for k in range(inner)], axis=1)
    notional_group = small[::inner, REGRESSORS, :trade_rows].reshape(1, group_trades).astype(F32)
    member, thresh, rate = call(
        partial(tables_kernel, masks(outer_bits), inner),
        [((sets, group_trades), BF16), ((1, sets), F32), ((1, sets), F32)],
        me.astype(jnp.int32).reshape(1),
        threshold_levels,
        set_of.reshape(n, 1, trade_rows),
        threshold_index.reshape(inner, 1, quarter),
        loss_rate.reshape(inner, 1, quarter),
        name="tables",
        scalars=2,
    )
    value, *moments = call(
        partial(forward_kernel, inner, outer),
        [((group_paths, group_trades), BF16)] + [((REGRESSORS, quarter), F32)] * inner,
        *basis, *weights, notional_group, design_group, member,
        name="forward",
    )
    moment = sum(direct(moments, inner_bits), moments[0])
    (inverse,) = call(
        partial(inverse_kernel, RIDGE_SCALE * paths_all, path_rows),
        [((REGRESSORS, REGRESSORS), F32)],
        small,
        name="inverse",
    )
    moment = after(moment, inverse)
    moments = [moment] + direct([moment] * outer, outer_bits)
    design_all, design_rows = call(
        partial(design_kernel, path_rows),
        [((REGRESSORS, paths_all), BF16), ((paths_all, LANES), BF16)],
        small,
        name="design",
    )
    (solved,) = call(
        partial(solve_kernel, outer),
        [((2 * REGRESSORS, quarter), F32)],
        inverse, design_all, design_rows, thresh, rate, *moments,
        name="solve",
        scratch=[pltpu.VMEM((LANES, quarter), BF16), pltpu.VMEM((REGRESSORS, quarter), F32)],
    )
    solved = [solved] + direct([solved] * inner, inner_bits)
    (slope,) = call(
        partial(slope_kernel, inner, outer),
        [((group_paths, group_trades), F32)],
        *basis, *weights, notional_group,
        name="slope",
    )
    parts = call(
        partial(backward_kernel, 1.0 / math.sqrt(paths_all), inner, outer),
        [((trade_rows, features), BF16)] * outer + [((path_rows, features), BF16)] * inner,
        member, design_rows, slope, value, *solved, *basis, *weights,
        name="backward",
        scratch=[pltpu.VMEM((group_paths, group_trades), BF16)],
    )
    weight_terms = halve(parts[:outer], outer_bits)
    basis_terms = halve(parts[outer:], inner_bits)
    loss, own_adjoint = call(
        loss_kernel,
        [((8, LANES), F32), ((path_rows, LANES), F32)],
        design_rows, thresh, rate, *solved,
        name="loss",
        scratch=[pltpu.VMEM((LANES, sets), BF16), pltpu.VMEM((8, sets), F32)],
    )
    (weight_adjoint,) = call(
        weight_sum_kernel, [((trade_rows, features), F32)], *weight_terms, name="weight_sum"
    )
    (basis_adjoint,) = call(
        basis_sum_kernel, [((path_rows, features), F32)], own_adjoint, *basis_terms, name="basis_sum"
    )
    return (loss[0, :1], basis_adjoint, weight_adjoint)


def solution(mesh):
    placed = (
        P(("groups", "paths"), None),
        P(("groups", "paths"), None),
        P(("groups", "paths")),
        P("groups"),
        P("groups"),
        P("groups"),
        P("groups"),
    )
    return jax.shard_map(
        shards,
        mesh=mesh,
        in_specs=placed,
        out_specs=(P("groups"), P(("groups", "paths"), None), P(("groups", "paths"), None)),
        check_vma=False,
    )
```

```python
import math
from functools import partial

import jax
import jax.numpy as jnp
from jax import lax
from jax.experimental import pallas as pl
from jax.experimental.pallas import tpu as pltpu
from jax.sharding import PartitionSpec as P

REGRESSORS = 32
RIDGE_SCALE = 0.01
PRECISE = lax.Precision.HIGHEST
F32 = jnp.float32
BF16 = jnp.bfloat16
LANES = 128
PAD_ROWS = 16
CHUNK = 256
VMEM_BYTES = 48 * 1024 * 1024
LOG2_E = math.log2(math.e)
CONSTANT = REGRESSORS - 1


def split_bits(size):
    count = size.bit_length() - 1
    half = count // 2
    return list(range(1, half + 1)), list(range(count - 1, half, -1)) + [0]


def dot(a, b, ca=1, cb=0, precision=None):
    return lax.dot_general(
        a, b, (((ca,), (cb,)), ((), ())), precision=precision, preferred_element_type=F32
    )


def three(x, axis):
    high = x.astype(BF16)
    rest = x - high.astype(F32)
    middle = rest.astype(BF16)
    low = (rest - middle.astype(F32)).astype(BF16)
    return jnp.concatenate([high, middle, low], axis=axis)


def three_rows(x):
    blank = jnp.zeros((LANES - 3 * REGRESSORS, x.shape[1]), BF16)
    return jnp.concatenate([three(x, 0), blank], axis=0)


def lanes(shape):
    return lax.broadcasted_iota(jnp.int32, shape, len(shape) - 1)


def rows(shape):
    return lax.broadcasted_iota(jnp.int32, shape, len(shape) - 2)


def softplus(x):
    return jnp.maximum(x, 0.0) + jnp.log1p(jnp.exp(-jnp.abs(x)))


def sigmoid(x):
    small = jnp.exp(-jnp.abs(x))
    return jnp.where(x >= 0.0, 1.0, small) / (1.0 + small)


def each_chunk(size, step):
    count = size // CHUNK

    def body(i, carry):
        step(pl.ds(pl.multiple_of(i * CHUNK, CHUNK), CHUNK))
        return carry

    lax.fori_loop(0, count, body, 0, unroll=count <= 8)


def eliminate(work, columns):
    row = rows(work.shape)
    for k in columns:
        pivot = work[k : k + 1] / work[k : k + 1, k : k + 1]
        work = jnp.where(row == k, pivot, work - work[:, k : k + 1] * pivot)
    return work


def pack_kernel(x_ref, w_ref, notional_ref, wide_ref, lead_ref):
    trades = w_ref.shape[0]
    wide_ref[:trades] = w_ref[...]
    row = jnp.broadcast_to(notional_ref[...], (PAD_ROWS, notional_ref.shape[1]))
    wide_ref[trades:] = jnp.zeros((PAD_ROWS, wide_ref.shape[1]), BF16)
    wide_ref[trades:, : notional_ref.shape[1]] = row
    turned = x_ref[:, :LANES].astype(F32).T[:REGRESSORS]
    lead_ref[0] = jnp.where(rows(turned.shape) == CONSTANT, 1.0, turned).astype(BF16)


def tables_kernel(
    trade_masks, inner, me_ref, level_ref, set_ref, index_ref, rate_ref,
    member_ref, thresh_out_ref, rate_out_ref,
):
    me = me_ref[0]
    place = (me >> 1) & (inner - 1)
    size = member_ref.shape[0] // inner
    trades = set_ref.shape[-1]
    for m in range(inner):
        here = slice(m * size, (m + 1) * size)
        label = (place ^ m) * size + rows((size, 1))
        for j, mask in enumerate(trade_masks):
            member_ref[here, j * trades : (j + 1) * trades] = jnp.where(
                set_ref[me ^ mask] == label, 1.0, 0.0
            ).astype(BF16)
        index = index_ref[place ^ m]
        thresh = jnp.zeros(index.shape, F32)
        for k in range(level_ref.shape[0]):
            thresh = jnp.where(index == k, level_ref[k], thresh)
        thresh_out_ref[:, here] = thresh
        rate_out_ref[:, here] = rate_ref[place ^ m]


def design_kernel(order, path_rows, small_ref, design_ref, rows_ref):
    for k, d in enumerate(order):
        here = slice(k * path_rows, (k + 1) * path_rows)
        block = small_ref[d]
        design_ref[:, here] = block
        turned = block.astype(F32).T
        blank = jnp.zeros((path_rows, LANES - 3 * REGRESSORS), F32)
        rows_ref[here] = jnp.concatenate([turned] * 3 + [blank], axis=1).astype(BF16)


def inverse_begin_kernel(ridge, small_ref, work_ref):
    square = (REGRESSORS, REGRESSORS)
    gram = jnp.where(rows(square) == lanes(square), ridge, 0.0)
    for d in range(small_ref.shape[0]):
        gram = gram + dot(small_ref[d], small_ref[d], 1, 1)
    work = jnp.concatenate([gram, jnp.eye(REGRESSORS, dtype=F32)], axis=1)
    work_ref[...] = eliminate(work, range(REGRESSORS // 2))


def inverse_end_kernel(work_ref, inverse_ref):
    work = eliminate(work_ref[...], range(REGRESSORS // 2, REGRESSORS))
    inverse_ref[...] = work[:, REGRESSORS:]


def trade_blocks(refs):
    trades = refs[0].shape[0] - PAD_ROWS
    weights = jnp.concatenate([ref[:trades] for ref in refs], axis=0)
    notional = [ref[trades:].astype(F32)[:1, :trades] for ref in refs]
    return weights, jnp.concatenate(notional, axis=1)


def forward_kernel(paths, trades, *refs):
    x_refs, w_refs = refs[:paths], refs[paths : paths + trades]
    member_ref, value_ref, *moment_refs = refs[paths + trades :]
    weights, notional = trade_blocks(w_refs)
    start = 0
    trade_moment = None
    for x in x_refs:
        pre_act = dot(x[...], weights, 1, 1)
        value = (notional * softplus(pre_act)).astype(BF16)
        value_ref[start : start + x.shape[0]] = value
        start += x.shape[0]
        design = x[:, :LANES].astype(F32)
        lane = lanes(design.shape)
        design = jnp.where(lane == CONSTANT, 1.0, design).astype(BF16)
        part = dot(design, value, 0, 0)[:REGRESSORS]
        trade_moment = part if trade_moment is None else trade_moment + part
    parts = dot(three(trade_moment, 0), member_ref[...], 1, 1)
    moment = parts[:REGRESSORS] + parts[REGRESSORS : 2 * REGRESSORS] + parts[2 * REGRESSORS :]
    size = moment.shape[1] // len(moment_refs)
    for m, moment_ref in enumerate(moment_refs):
        moment_ref[...] = moment[:, m * size : (m + 1) * size]


def slope_kernel(paths, trades, *refs):
    x_refs, w_refs = refs[:paths], refs[paths : paths + trades]
    slope_ref = refs[-1]
    weights, notional = trade_blocks(w_refs)
    start = 0
    for x in x_refs:
        slope_ref[start : start + x.shape[0]] = notional * sigmoid(dot(x[...], weights, 1, 1))
        start += x.shape[0]


def solve_kernel(
    terms, inverse_ref, design_ref, rows_ref, thresh_ref, rate_ref, *refs
):
    solved_ref, turn_ref, total_ref = refs[terms:]
    moment = refs[0][...]
    for ref in refs[1:terms]:
        moment = moment + ref[...]
    size = moment.shape[1]
    inverse = inverse_ref[...]
    coeffs = dot(inverse, moment, precision=PRECISE)
    solved_ref[REGRESSORS:] = coeffs
    is_constant = rows(coeffs.shape) == CONSTANT
    shifted = coeffs - jnp.where(is_constant, thresh_ref[:, :size], 0.0)
    turn_ref[...] = three_rows(-LOG2_E * shifted)
    total_ref[...] = jnp.zeros(total_ref.shape, F32)

    def seeds(here):
        power = jnp.exp2(jnp.minimum(dot(rows_ref[here], turn_ref[...]), 126.0))
        seed = (1.0 / (1.0 + power)).astype(BF16)
        total_ref[...] += dot(design_ref[:, here], seed)

    each_chunk(rows_ref.shape[0], seeds)
    solved_ref[:REGRESSORS] = dot(inverse, total_ref[...] * rate_ref[:, :size], precision=PRECISE)


def joined(refs, part):
    here = slice(part * REGRESSORS, (part + 1) * REGRESSORS)
    return jnp.concatenate([ref[here] for ref in refs], axis=1)


def backward_kernel(scale, paths, trades, member_ref, rows_ref, slope_ref, value_ref, *refs):
    solved_refs, refs = refs[:paths], refs[paths:]
    x_refs, refs = refs[:paths], refs[paths:]
    w_refs, refs = refs[:trades], refs[trades:]
    weight_refs, basis_refs, slopes_ref = refs[:trades], refs[trades:-1], refs[-1]
    traded = dot(three_rows(joined(solved_refs, 0)), member_ref[...]).astype(BF16)
    group = slopes_ref.shape[0]
    spread = dot(rows_ref[:group], traded).astype(BF16).astype(F32)
    slopes_ref[...] = (slope_ref[...] * spread).astype(BF16)
    basis = jnp.concatenate([x[...] for x in x_refs], axis=0)
    weight = (dot(slopes_ref[...], basis, 0, 0) * scale).astype(BF16)
    start = 0
    for part in weight_refs:
        part[...] = weight[start : start + part.shape[0]]
        start += part.shape[0]
    weights, _ = trade_blocks(w_refs)
    start = 0
    for part in basis_refs:
        here = slice(start, start + part.shape[0])
        total = dot(slopes_ref[here], weights)
        wide = dot(value_ref[here], traded, 1, 1)
        design = wide
        for k in range(1, 3):
            design = design + pltpu.roll(wide, LANES - k * REGRESSORS, 1)
        design = jnp.where(lanes(design.shape) < CONSTANT, design, 0.0)
        part[:, :LANES] = (total[:, :LANES] + design).astype(BF16)
        part[:, LANES:] = total[:, LANES:].astype(BF16)
        start += part.shape[0]


def loss_kernel(rows_ref, thresh_ref, rate_ref, *refs):
    solved_refs, (loss_ref, own_ref, split_ref, total_ref) = refs[:-4], refs[-4:]
    adjoint = joined(solved_refs, 0)
    coeffs = joined(solved_refs, 1)
    thresh = thresh_ref[...]
    rate = rate_ref[...]
    split_ref[...] = three_rows(coeffs)
    total_ref[...] = jnp.zeros(total_ref.shape, F32)

    def losses(here):
        loss = softplus(dot(rows_ref[here], split_ref[...]) - thresh)
        total_ref[...] += jnp.sum(loss.reshape(-1, *total_ref.shape), axis=0)

    each_chunk(rows_ref.shape[0], losses)
    summed = jnp.sum(jnp.sum(total_ref[...] * rate, axis=0, keepdims=True), axis=1, keepdims=True)
    loss_ref[...] = jnp.broadcast_to(
        summed / (rows_ref.shape[0] * coeffs.shape[1]), loss_ref.shape
    )
    own = rows_ref[: own_ref.shape[0]]
    fitted = dot(own, split_ref[...])
    seed = rate * sigmoid(fitted - thresh)
    rest = seed - dot(own, three_rows(adjoint))
    design = dot(rest, coeffs, 1, 1, PRECISE) - dot(fitted, adjoint, 1, 1, PRECISE)
    blank = jnp.zeros((design.shape[0], LANES - REGRESSORS), F32)
    design = jnp.concatenate([design, blank], axis=1)
    own_ref[...] = jnp.where(lanes(design.shape) < CONSTANT, design, 0.0)


def total(refs):
    out = refs[0][...].astype(F32)
    for ref in refs[1:]:
        out = out + ref[...].astype(F32)
    return out


def weight_sum_kernel(*refs):
    refs[-1][...] = total(refs[:-1])


def basis_sum_kernel(own_ref, *refs):
    basis = total(refs[:-1])
    refs[-1][:, :LANES] = basis[:, :LANES] + own_ref[...]
    refs[-1][:, LANES:] = basis[:, LANES:]


def call(kernel, outs, *args, name, flops=0, scratch=(), scalars=0):
    size = sum(a.size * a.dtype.itemsize for a in args) + sum(
        math.prod(s) * jnp.dtype(d).itemsize for s, d in outs
    )
    return pl.pallas_call(
        kernel,
        out_shape=[jax.ShapeDtypeStruct(s, d) for s, d in outs],
        in_specs=[pl.BlockSpec(memory_space=pltpu.SMEM)] * scalars
        + [pl.BlockSpec(memory_space=pltpu.VMEM)] * (len(args) - scalars),
        out_specs=[pl.BlockSpec(memory_space=pltpu.VMEM)] * len(outs),
        scratch_shapes=scratch,
        compiler_params=pltpu.CompilerParams(vmem_limit_bytes=VMEM_BYTES),
        cost_estimate=pl.CostEstimate(flops=int(flops), bytes_accessed=int(size), transcendentals=0),
        name=name,
    )(*args)


def shards(
    path_basis, proxy_weight, notional, set_of, threshold_index, threshold_levels, loss_rate
):
    n = lax.axis_size("paths")
    me = lax.axis_index("paths")
    inner_bits, outer_bits = split_bits(n)
    inner, outer = 1 << len(inner_bits), 1 << len(outer_bits)
    path_rows, features = path_basis.shape
    trade_rows = proxy_weight.shape[0]
    paths_all = path_rows * n
    sets = loss_rate.shape[0]
    quarter = sets // inner
    group_paths, group_trades = inner * path_rows, outer * trade_rows

    def swap(x, mask):
        return lax.ppermute(x, "paths", [(d, d ^ mask) for d in range(n)])

    def masks(bits):
        return [
            sum(((m >> j) & 1) << bit for j, bit in enumerate(bits)) for m in range(1 << len(bits))
        ]

    def after(x, *others):
        return lax.optimization_barrier((x, *others))[0]

    def direct(slots, bits):
        return [swap(x, mask) for x, mask in zip(slots[1:], masks(bits)[1:])]

    def halve(slots, bits):
        slots = [[s] for s in slots]
        for bit in reversed(bits):
            count = len(slots) // 2
            last = None
            for k in reversed(range(count)):
                gone = slots[count + k]
                gone = gone[0] if len(gone) == 1 else sum(g.astype(F32) for g in gone).astype(BF16)
                if last is not None:
                    gone = after(gone, last)
                last = swap(gone, 1 << bit)
                slots[k].append(last)
            slots = slots[:count]
        return slots[0]

    wide, small = call(
        pack_kernel,
        [((trade_rows + PAD_ROWS, features), BF16), ((1, REGRESSORS, path_rows), BF16)],
        path_basis, proxy_weight, notional[None, :],
        name="pack",
    )
    small_bits = outer_bits[:-1] + inner_bits + outer_bits[-1:]
    first_bit = outer_bits[0]
    weights = [wide, swap(wide, 1 << first_bit)]
    basis = [path_basis] + direct([path_basis] * inner, inner_bits)
    for bit in outer_bits[1:]:
        weights = weights + [swap(w, 1 << bit) for w in weights]
    for j, bit in enumerate(small_bits):
        if j == 2:
            small = after(small, weights[1])
        small = jnp.concatenate([small, swap(small, 1 << bit)], axis=0)
    small_masks = masks(small_bits)
    first_masks = masks(inner_bits)
    order = [small_masks.index(mask) for mask in first_masks]
    order += [k for k in range(n) if small_masks[k] not in first_masks]
    member, thresh, rate = call(
        partial(tables_kernel, masks(outer_bits), inner),
        [((sets, group_trades), BF16), ((1, sets), F32), ((1, sets), F32)],
        me.astype(jnp.int32).reshape(1),
        threshold_levels,
        set_of.reshape(n, 1, trade_rows),
        threshold_index.reshape(inner, 1, quarter),
        loss_rate.reshape(inner, 1, quarter),
        name="tables",
        scalars=2,
    )
    value, *moments = call(
        partial(forward_kernel, inner, outer),
        [((group_paths, group_trades), BF16)] + [((REGRESSORS, quarter), F32)] * inner,
        *basis, *weights, member,
        name="forward",
    )
    moment = sum(direct(moments, inner_bits), moments[0])
    (work,) = call(
        partial(inverse_begin_kernel, RIDGE_SCALE * paths_all),
        [((REGRESSORS, 2 * REGRESSORS), F32)],
        small,
        name="inverse_begin",
    )
    moment = after(moment, work)
    for bit in outer_bits[:0:-1]:
        moment = moment + swap(moment, 1 << bit)
    moments = [moment, swap(moment, 1 << first_bit)]
    (inverse,) = call(
        inverse_end_kernel, [((REGRESSORS, REGRESSORS), F32)], work, name="inverse_end"
    )
    design_all, design_rows = call(
        partial(design_kernel, order, path_rows),
        [((REGRESSORS, paths_all), BF16), ((paths_all, LANES), BF16)],
        small,
        name="design",
    )
    (solved,) = call(
        partial(solve_kernel, len(moments)),
        [((2 * REGRESSORS, quarter), F32)],
        inverse, design_all, design_rows, thresh, rate, *moments,
        name="solve",
        scratch=[pltpu.VMEM((LANES, quarter), BF16), pltpu.VMEM((REGRESSORS, quarter), F32)],
    )
    solved = [solved] + direct([solved] * inner, inner_bits)
    (slope,) = call(
        partial(slope_kernel, inner, outer),
        [((group_paths, group_trades), F32)],
        *basis, *weights,
        name="slope",
    )
    parts = call(
        partial(backward_kernel, 1.0 / math.sqrt(paths_all), inner, outer),
        [((trade_rows, features), BF16)] * outer + [((path_rows, features), BF16)] * inner,
        member, design_rows, slope, value, *solved, *basis, *weights,
        name="backward",
        scratch=[pltpu.VMEM((group_paths, group_trades), BF16)],
    )
    weight_terms = halve(parts[:outer], outer_bits)
    basis_terms = [parts[outer]] + direct(parts[outer:], inner_bits)
    loss, own_adjoint = call(
        loss_kernel,
        [((8, LANES), F32), ((path_rows, LANES), F32)],
        design_rows, thresh, rate, *solved,
        name="loss",
        scratch=[pltpu.VMEM((LANES, sets), BF16), pltpu.VMEM((8, sets), F32)],
    )
    (weight_adjoint,) = call(
        weight_sum_kernel, [((trade_rows, features), F32)], *weight_terms, name="weight_sum"
    )
    (basis_adjoint,) = call(
        basis_sum_kernel, [((path_rows, features), F32)], own_adjoint, *basis_terms, name="basis_sum"
    )
    return (loss[0, :1], basis_adjoint, weight_adjoint)


def solution(mesh):
    placed = (
        P(("groups", "paths"), None),
        P(("groups", "paths"), None),
        P(("groups", "paths")),
        P("groups"),
        P("groups"),
        P("groups"),
        P("groups"),
    )
    return jax.shard_map(
        shards,
        mesh=mesh,
        in_specs=placed,
        out_specs=(P("groups"), P(("groups", "paths"), None), P(("groups", "paths"), None)),
        check_vma=False,
    )
```

```python
import math
from functools import partial

import jax
import jax.numpy as jnp
from jax import lax
from jax.experimental import pallas as pl
from jax.experimental.pallas import tpu as pltpu
from jax.sharding import PartitionSpec as P

REGRESSORS = 32
RIDGE_SCALE = 0.01
PRECISE = lax.Precision.HIGHEST
F32 = jnp.float32
BF16 = jnp.bfloat16
LANES = 128
PAD_ROWS = 16
CHUNK = 256
VMEM_BYTES = 48 * 1024 * 1024
LOG2_E = math.log2(math.e)
CONSTANT = REGRESSORS - 1


def split_bits(size):
    count = size.bit_length() - 1
    half = count // 2
    return list(range(1, half + 1)), list(range(count - 1, half, -1)) + [0]


def dot(a, b, ca=1, cb=0, precision=None):
    return lax.dot_general(
        a, b, (((ca,), (cb,)), ((), ())), precision=precision, preferred_element_type=F32
    )


def three(x, axis):
    high = x.astype(BF16)
    rest = x - high.astype(F32)
    middle = rest.astype(BF16)
    low = (rest - middle.astype(F32)).astype(BF16)
    return jnp.concatenate([high, middle, low], axis=axis)


def three_rows(x):
    blank = jnp.zeros((LANES - 3 * REGRESSORS, x.shape[1]), BF16)
    return jnp.concatenate([three(x, 0), blank], axis=0)


def lanes(shape):
    return lax.broadcasted_iota(jnp.int32, shape, len(shape) - 1)


def rows(shape):
    return lax.broadcasted_iota(jnp.int32, shape, len(shape) - 2)


def softplus(x):
    return jnp.maximum(x, 0.0) + jnp.log1p(jnp.exp(-jnp.abs(x)))


def sigmoid(x):
    small = jnp.exp(-jnp.abs(x))
    return jnp.where(x >= 0.0, 1.0, small) / (1.0 + small)


def each_chunk(size, step):
    count = size // CHUNK

    def body(i, carry):
        step(pl.ds(pl.multiple_of(i * CHUNK, CHUNK), CHUNK))
        return carry

    lax.fori_loop(0, count, body, 0, unroll=count <= 8)


def eliminate(work, columns):
    row = rows(work.shape)
    for k in columns:
        pivot = work[k : k + 1] / work[k : k + 1, k : k + 1]
        work = jnp.where(row == k, pivot, work - work[:, k : k + 1] * pivot)
    return work


def lead_kernel(*refs):
    x_refs, lead_ref = refs[:-1], refs[-1]
    start = 0
    for x in x_refs:
        turned = x[:, :LANES].astype(F32).T[:REGRESSORS]
        turned = jnp.where(rows(turned.shape) == CONSTANT, 1.0, turned)
        lead_ref[0, :, start : start + x.shape[0]] = turned.astype(BF16)
        start += x.shape[0]


def tables_kernel(
    trade_masks, inner, me_ref, level_ref, set_ref, index_ref, rate_ref, x_ref, w_ref,
    member_ref, thresh_out_ref, rate_out_ref, x_out_ref, w_out_ref,
):
    x_out_ref[...] = x_ref[...]
    w_out_ref[...] = w_ref[...]
    me = me_ref[0]
    place = (me >> 1) & (inner - 1)
    size = member_ref.shape[0] // inner
    trades = set_ref.shape[-1]
    for m in range(inner):
        here = slice(m * size, (m + 1) * size)
        label = (place ^ m) * size + rows((size, 1))
        for j, mask in enumerate(trade_masks):
            member_ref[here, j * trades : (j + 1) * trades] = jnp.where(
                set_ref[me ^ mask] == label, 1.0, 0.0
            ).astype(BF16)
        index = index_ref[place ^ m]
        thresh = jnp.zeros(index.shape, F32)
        for k in range(level_ref.shape[0]):
            thresh = jnp.where(index == k, level_ref[k], thresh)
        thresh_out_ref[:, here] = thresh
        rate_out_ref[:, here] = rate_ref[place ^ m]


def design_kernel(small_ref, design_ref, rows_ref):
    size = small_ref.shape[2]
    for d in range(small_ref.shape[0]):
        here = slice(d * size, (d + 1) * size)
        block = small_ref[d]
        design_ref[:, here] = block
        turned = block.astype(F32).T
        blank = jnp.zeros((size, LANES - 3 * REGRESSORS), F32)
        rows_ref[here] = jnp.concatenate([turned] * 3 + [blank], axis=1).astype(BF16)


def inverse_begin_kernel(ridge, small_ref, work_ref):
    square = (REGRESSORS, REGRESSORS)
    gram = jnp.where(rows(square) == lanes(square), ridge, 0.0)
    for d in range(small_ref.shape[0]):
        gram = gram + dot(small_ref[d], small_ref[d], 1, 1)
    work = jnp.concatenate([gram, jnp.eye(REGRESSORS, dtype=F32)], axis=1)
    work_ref[...] = eliminate(work, range(REGRESSORS // 2))


def inverse_end_kernel(work_ref, inverse_ref):
    work = eliminate(work_ref[...], range(REGRESSORS // 2, REGRESSORS))
    inverse_ref[...] = work[:, REGRESSORS:]


def forward_kernel(paths, trades, *refs):
    x_refs, w_refs = refs[:paths], refs[paths : paths + trades]
    notional_ref, member_ref, value_ref, *moment_refs = refs[paths + trades :]
    weights = jnp.concatenate([w[...] for w in w_refs], axis=0)
    notional = notional_ref[...]
    start = 0
    trade_moment = None
    for x in x_refs:
        pre_act = dot(x[...], weights, 1, 1)
        value = (notional * softplus(pre_act)).astype(BF16)
        value_ref[start : start + x.shape[0]] = value
        start += x.shape[0]
        design = x[:, :LANES].astype(F32)
        lane = lanes(design.shape)
        design = jnp.where(lane == CONSTANT, 1.0, design).astype(BF16)
        part = dot(design, value, 0, 0)[:REGRESSORS]
        trade_moment = part if trade_moment is None else trade_moment + part
    parts = dot(three(trade_moment, 0), member_ref[...], 1, 1)
    moment = parts[:REGRESSORS] + parts[REGRESSORS : 2 * REGRESSORS] + parts[2 * REGRESSORS :]
    size = moment.shape[1] // len(moment_refs)
    for m, moment_ref in enumerate(moment_refs):
        moment_ref[...] = moment[:, m * size : (m + 1) * size]


def slope_kernel(paths, trades, *refs):
    x_refs, w_refs = refs[:paths], refs[paths : paths + trades]
    notional_ref, slope_ref = refs[paths + trades :]
    weights = jnp.concatenate([w[...] for w in w_refs], axis=0)
    notional = notional_ref[...]
    start = 0
    for x in x_refs:
        slope_ref[start : start + x.shape[0]] = notional * sigmoid(dot(x[...], weights, 1, 1))
        start += x.shape[0]


def solve_kernel(
    terms, inverse_ref, design_ref, rows_ref, thresh_ref, rate_ref, *refs
):
    solved_ref, turn_ref, total_ref = refs[terms:]
    moment = refs[0][...]
    for ref in refs[1:terms]:
        moment = moment + ref[...]
    size = moment.shape[1]
    inverse = inverse_ref[...]
    coeffs = dot(inverse, moment, precision=PRECISE)
    solved_ref[REGRESSORS:] = coeffs
    is_constant = rows(coeffs.shape) == CONSTANT
    shifted = coeffs - jnp.where(is_constant, thresh_ref[:, :size], 0.0)
    turn_ref[...] = three_rows(-LOG2_E * shifted)
    total_ref[...] = jnp.zeros(total_ref.shape, F32)

    def seeds(here):
        power = jnp.exp2(jnp.minimum(dot(rows_ref[here], turn_ref[...]), 126.0))
        seed = (1.0 / (1.0 + power)).astype(BF16)
        total_ref[...] += dot(design_ref[:, here], seed)

    each_chunk(rows_ref.shape[0], seeds)
    solved_ref[:REGRESSORS] = dot(inverse, total_ref[...] * rate_ref[:, :size], precision=PRECISE)


def joined(refs, part):
    here = slice(part * REGRESSORS, (part + 1) * REGRESSORS)
    return jnp.concatenate([ref[here] for ref in refs], axis=1)


def weight_side_kernel(scale, paths, member_ref, rows_ref, slope_ref, *refs):
    solved_refs, x_refs = refs[:paths], refs[paths : 2 * paths]
    traded_ref, slopes_ref, *weight_refs = refs[2 * paths :]
    traded = dot(three_rows(joined(solved_refs, 0)), member_ref[...]).astype(BF16)
    traded_ref[...] = traded
    group = slopes_ref.shape[0]
    spread = dot(rows_ref[:group], traded).astype(BF16).astype(F32)
    slopes_ref[...] = (slope_ref[...] * spread).astype(BF16)
    basis = jnp.concatenate([x[...] for x in x_refs], axis=0)
    weight = (dot(slopes_ref[...], basis, 0, 0) * scale).astype(BF16)
    start = 0
    for part in weight_refs:
        part[...] = weight[start : start + part.shape[0]]
        start += part.shape[0]


def basis_side_kernel(trades, value_ref, traded_ref, slopes_ref, *refs):
    w_refs, basis_refs = refs[:trades], refs[trades:]
    weights = jnp.concatenate([w[...] for w in w_refs], axis=0)
    start = 0
    for part in basis_refs:
        here = slice(start, start + part.shape[0])
        total = dot(slopes_ref[here], weights)
        wide = dot(value_ref[here], traded_ref[...], 1, 1)
        design = wide
        for k in range(1, 3):
            design = design + pltpu.roll(wide, LANES - k * REGRESSORS, 1)
        design = jnp.where(lanes(design.shape) < CONSTANT, design, 0.0)
        part[:, :LANES] = (total[:, :LANES] + design).astype(BF16)
        part[:, LANES:] = total[:, LANES:].astype(BF16)
        start += part.shape[0]


def loss_kernel(rows_ref, thresh_ref, rate_ref, *refs):
    solved_refs, (loss_ref, own_ref, split_ref, total_ref) = refs[:-4], refs[-4:]
    adjoint = joined(solved_refs, 0)
    coeffs = joined(solved_refs, 1)
    thresh = thresh_ref[...]
    rate = rate_ref[...]
    split_ref[...] = three_rows(coeffs)
    total_ref[...] = jnp.zeros(total_ref.shape, F32)

    def losses(here):
        loss = softplus(dot(rows_ref[here], split_ref[...]) - thresh)
        total_ref[...] += jnp.sum(loss.reshape(-1, *total_ref.shape), axis=0)

    each_chunk(rows_ref.shape[0], losses)
    summed = jnp.sum(jnp.sum(total_ref[...] * rate, axis=0, keepdims=True), axis=1, keepdims=True)
    loss_ref[...] = jnp.broadcast_to(
        summed / (rows_ref.shape[0] * coeffs.shape[1]), loss_ref.shape
    )
    own = rows_ref[: own_ref.shape[0]]
    fitted = dot(own, split_ref[...])
    seed = rate * sigmoid(fitted - thresh)
    rest = seed - dot(own, three_rows(adjoint))
    design = dot(rest, coeffs, 1, 1, PRECISE) - dot(fitted, adjoint, 1, 1, PRECISE)
    blank = jnp.zeros((design.shape[0], LANES - REGRESSORS), F32)
    design = jnp.concatenate([design, blank], axis=1)
    own_ref[...] = jnp.where(lanes(design.shape) < CONSTANT, design, 0.0)


def total(refs):
    out = refs[0][...].astype(F32)
    for ref in refs[1:]:
        out = out + ref[...].astype(F32)
    return out


def weight_sum_kernel(*refs):
    refs[-1][...] = total(refs[:-1])


def basis_sum_kernel(own_ref, *refs):
    basis = total(refs[:-1])
    refs[-1][:, :LANES] = basis[:, :LANES] + own_ref[...]
    refs[-1][:, LANES:] = basis[:, LANES:]


def call(kernel, outs, *args, name, flops=0, scratch=(), scalars=0):
    size = sum(a.size * a.dtype.itemsize for a in args) + sum(
        math.prod(s) * jnp.dtype(d).itemsize for s, d in outs
    )
    return pl.pallas_call(
        kernel,
        out_shape=[jax.ShapeDtypeStruct(s, d) for s, d in outs],
        in_specs=[pl.BlockSpec(memory_space=pltpu.SMEM)] * scalars
        + [pl.BlockSpec(memory_space=pltpu.VMEM)] * (len(args) - scalars),
        out_specs=[pl.BlockSpec(memory_space=pltpu.VMEM)] * len(outs),
        scratch_shapes=scratch,
        compiler_params=pltpu.CompilerParams(vmem_limit_bytes=VMEM_BYTES),
        cost_estimate=pl.CostEstimate(flops=int(flops), bytes_accessed=int(size), transcendentals=0),
        name=name,
    )(*args)


def shards(
    path_basis, proxy_weight, notional, set_of, threshold_index, threshold_levels, loss_rate
):
    n = lax.axis_size("paths")
    me = lax.axis_index("paths")
    inner_bits, outer_bits = split_bits(n)
    inner, outer = 1 << len(inner_bits), 1 << len(outer_bits)
    path_rows, features = path_basis.shape
    trade_rows = proxy_weight.shape[0]
    paths_all = path_rows * n
    sets = loss_rate.shape[0]
    quarter = sets // inner
    group_paths, group_trades = inner * path_rows, outer * trade_rows

    def swap(x, mask):
        return lax.ppermute(x, "paths", [(d, d ^ mask) for d in range(n)])

    def masks(bits):
        return [
            sum(((m >> j) & 1) << bit for j, bit in enumerate(bits)) for m in range(1 << len(bits))
        ]

    def after(x, *others):
        return lax.optimization_barrier((x, *others))[0]

    def direct(slots, bits):
        return [swap(x, mask) for x, mask in zip(slots[1:], masks(bits)[1:])]

    first_bit = outer_bits[0]
    weights = [proxy_weight, swap(proxy_weight, 1 << first_bit)]
    basis = [path_basis] + direct([path_basis] * inner, inner_bits)
    notionals = notional
    for bit in outer_bits:
        notionals = jnp.concatenate([notionals, swap(notionals, 1 << bit)])
    for bit in outer_bits[1:]:
        weights = weights + [swap(w, 1 << bit) for w in weights]
    notionals = notionals.astype(F32)[None, :]

    member, thresh, rate, basis[0], weights[0] = call(
        partial(tables_kernel, masks(outer_bits), inner),
        [
            ((sets, group_trades), BF16),
            ((1, sets), F32),
            ((1, sets), F32),
            (path_basis.shape, BF16),
            (proxy_weight.shape, BF16),
        ],
        me.astype(jnp.int32).reshape(1),
        threshold_levels,
        set_of.reshape(n, 1, trade_rows),
        threshold_index.reshape(inner, 1, quarter),
        loss_rate.reshape(inner, 1, quarter),
        path_basis,
        proxy_weight,
        name="tables",
        scalars=2,
    )
    (small,) = call(lead_kernel, [((1, REGRESSORS, group_paths), BF16)], *basis, name="lead")
    small = after(small, weights[1])
    for bit in outer_bits:
        small = jnp.concatenate([small, swap(small, 1 << bit)], axis=0)
    value, *moments = call(
        partial(forward_kernel, inner, outer),
        [((group_paths, group_trades), BF16)] + [((REGRESSORS, quarter), F32)] * inner,
        *basis, *weights, notionals, member,
        name="forward",
    )
    moment = sum(direct(moments, inner_bits), moments[0])
    (work,) = call(
        partial(inverse_begin_kernel, RIDGE_SCALE * paths_all),
        [((REGRESSORS, 2 * REGRESSORS), F32)],
        small,
        name="inverse_begin",
    )
    moment = after(moment, work)
    for bit in outer_bits[:0:-1]:
        moment = moment + swap(moment, 1 << bit)
    moments = [moment, swap(moment, 1 << first_bit)]
    (inverse,) = call(
        inverse_end_kernel, [((REGRESSORS, REGRESSORS), F32)], work, name="inverse_end"
    )
    design_all, design_rows = call(
        design_kernel,
        [((REGRESSORS, paths_all), BF16), ((paths_all, LANES), BF16)],
        small,
        name="design",
    )
    (solved,) = call(
        partial(solve_kernel, len(moments)),
        [((2 * REGRESSORS, quarter), F32)],
        inverse, design_all, design_rows, thresh, rate, *moments,
        name="solve",
        scratch=[pltpu.VMEM((LANES, quarter), BF16), pltpu.VMEM((REGRESSORS, quarter), F32)],
    )
    solved = [solved] + direct([solved] * inner, inner_bits)
    (slope,) = call(
        partial(slope_kernel, inner, outer),
        [((group_paths, group_trades), F32)],
        *basis, *weights, notionals,
        name="slope",
    )
    traded, slopes, *weight_parts = call(
        partial(weight_side_kernel, 1.0 / math.sqrt(paths_all), inner),
        [((LANES, group_trades), BF16), ((group_paths, group_trades), BF16)]
        + [((trade_rows, features), BF16)] * outer,
        member, design_rows, slope, *solved, *basis,
        name="weight_side",
    )
    terms = [[part] for part in weight_parts]
    for bit in reversed(outer_bits):
        count = len(terms) // 2
        arrived = None
        for k in reversed(range(count)):
            gone = terms[count + k]
            gone = gone[0] if len(gone) == 1 else sum(g.astype(F32) for g in gone).astype(BF16)
            if arrived is not None:
                gone = after(gone, arrived)
            arrived = swap(gone, 1 << bit)
            terms[k].append(arrived)
        terms = terms[:count]
        if bit == outer_bits[-1]:
            slopes = after(slopes, terms[-1][-1])
    weight_terms = terms[0]
    basis_parts = call(
        partial(basis_side_kernel, outer),
        [((path_rows, features), BF16)] * inner,
        value, traded, slopes, *weights,
        name="basis_side",
    )
    basis_terms = [basis_parts[0]] + direct(basis_parts, inner_bits)
    loss, own_adjoint = call(
        loss_kernel,
        [((8, LANES), F32), ((path_rows, LANES), F32)],
        design_rows, thresh, rate, *solved,
        name="loss",
        scratch=[pltpu.VMEM((LANES, sets), BF16), pltpu.VMEM((8, sets), F32)],
    )
    (weight_adjoint,) = call(
        weight_sum_kernel, [((trade_rows, features), F32)], *weight_terms, name="weight_sum"
    )
    (basis_adjoint,) = call(
        basis_sum_kernel, [((path_rows, features), F32)], own_adjoint, *basis_terms, name="basis_sum"
    )
    return (loss[0, :1], basis_adjoint, weight_adjoint)


def solution(mesh):
    placed = (
        P(("groups", "paths"), None),
        P(("groups", "paths"), None),
        P(("groups", "paths")),
        P("groups"),
        P("groups"),
        P("groups"),
        P("groups"),
    )
    return jax.shard_map(
        shards,
        mesh=mesh,
        in_specs=placed,
        out_specs=(P("groups"), P(("groups", "paths"), None), P(("groups", "paths"), None)),
        check_vma=False,
    )
```

```python
import math
from functools import partial

import jax
import jax.numpy as jnp
from jax import lax
from jax.experimental import pallas as pl
from jax.experimental.pallas import tpu as pltpu
from jax.sharding import PartitionSpec as P

REGRESSORS = 32
RIDGE_SCALE = 0.01
PRECISE = lax.Precision.HIGHEST
F32 = jnp.float32
BF16 = jnp.bfloat16
LANES = 128
PAD_ROWS = 16
CHUNK = 256
VMEM_BYTES = 48 * 1024 * 1024
LOG2_E = math.log2(math.e)
CONSTANT = REGRESSORS - 1


def split_bits(size):
    count = size.bit_length() - 1
    half = count // 2
    return list(range(1, half + 1)), list(range(count - 1, half, -1)) + [0]


def dot(a, b, ca=1, cb=0, precision=None):
    return lax.dot_general(
        a, b, (((ca,), (cb,)), ((), ())), precision=precision, preferred_element_type=F32
    )


def three(x, axis):
    high = x.astype(BF16)
    rest = x - high.astype(F32)
    middle = rest.astype(BF16)
    low = (rest - middle.astype(F32)).astype(BF16)
    return jnp.concatenate([high, middle, low], axis=axis)


def three_rows(x):
    blank = jnp.zeros((LANES - 3 * REGRESSORS, x.shape[1]), BF16)
    return jnp.concatenate([three(x, 0), blank], axis=0)


def lanes(shape):
    return lax.broadcasted_iota(jnp.int32, shape, len(shape) - 1)


def rows(shape):
    return lax.broadcasted_iota(jnp.int32, shape, len(shape) - 2)


def softplus(x):
    return jnp.maximum(x, 0.0) + jnp.log1p(jnp.exp(-jnp.abs(x)))


def sigmoid(x):
    small = jnp.exp(-jnp.abs(x))
    return jnp.where(x >= 0.0, 1.0, small) / (1.0 + small)


def each_chunk(size, step):
    count = size // CHUNK

    def body(i, carry):
        step(pl.ds(pl.multiple_of(i * CHUNK, CHUNK), CHUNK))
        return carry

    lax.fori_loop(0, count, body, 0, unroll=count <= 8)


def eliminate(work, columns):
    row = rows(work.shape)
    for k in columns:
        pivot = work[k : k + 1] / work[k : k + 1, k : k + 1]
        work = jnp.where(row == k, pivot, work - work[:, k : k + 1] * pivot)
    return work


def pack_kernel(x_ref, w_ref, notional_ref, wide_ref, own_ref, sems):
    trades = w_ref.shape[0]
    weights = pltpu.make_async_copy(w_ref, wide_ref.at[pl.ds(0, trades)], sems.at[0])
    basis = pltpu.make_async_copy(x_ref, own_ref, sems.at[1])
    weights.start()
    basis.start()
    wide_ref[trades:] = jnp.zeros((PAD_ROWS, wide_ref.shape[1]), BF16)
    wide_ref[trades:, :trades] = jnp.broadcast_to(notional_ref[...], (PAD_ROWS, trades))
    weights.wait()
    basis.wait()


def trade_blocks(refs):
    trades = refs[0].shape[0] - PAD_ROWS
    weights = jnp.concatenate([ref[:trades] for ref in refs], axis=0)
    notional = [ref[trades:].astype(F32)[:1, :trades] for ref in refs]
    return weights, jnp.concatenate(notional, axis=1)


def lead_kernel(*refs):
    x_refs, lead_ref = refs[:-1], refs[-1]
    start = 0
    for x in x_refs:
        turned = x[:, :LANES].astype(F32).T[:REGRESSORS]
        turned = jnp.where(rows(turned.shape) == CONSTANT, 1.0, turned)
        lead_ref[0, :, start : start + x.shape[0]] = turned.astype(BF16)
        start += x.shape[0]


def tables_kernel(
    trade_masks, inner, me_ref, level_ref, set_ref, index_ref, rate_ref,
    member_ref, thresh_out_ref, rate_out_ref,
):
    me = me_ref[0]
    place = (me >> 1) & (inner - 1)
    size = member_ref.shape[0] // inner
    trades = set_ref.shape[-1]
    for m in range(inner):
        here = slice(m * size, (m + 1) * size)
        label = (place ^ m) * size + rows((size, 1))
        for j, mask in enumerate(trade_masks):
            member_ref[here, j * trades : (j + 1) * trades] = jnp.where(
                set_ref[me ^ mask] == label, 1.0, 0.0
            ).astype(BF16)
        index = index_ref[place ^ m]
        thresh = jnp.zeros(index.shape, F32)
        for k in range(level_ref.shape[0]):
            thresh = jnp.where(index == k, level_ref[k], thresh)
        thresh_out_ref[:, here] = thresh
        rate_out_ref[:, here] = rate_ref[place ^ m]


def design_kernel(small_ref, design_ref, rows_ref):
    size = small_ref.shape[2]
    for d in range(small_ref.shape[0]):
        here = slice(d * size, (d + 1) * size)
        block = small_ref[d]
        design_ref[:, here] = block
        turned = block.astype(F32).T
        blank = jnp.zeros((size, LANES - 3 * REGRESSORS), F32)
        rows_ref[here] = jnp.concatenate([turned] * 3 + [blank], axis=1).astype(BF16)


def inverse_begin_kernel(ridge, small_ref, work_ref):
    square = (REGRESSORS, REGRESSORS)
    gram = jnp.where(rows(square) == lanes(square), ridge, 0.0)
    for d in range(small_ref.shape[0]):
        gram = gram + dot(small_ref[d], small_ref[d], 1, 1)
    work = jnp.concatenate([gram, jnp.eye(REGRESSORS, dtype=F32)], axis=1)
    work_ref[...] = eliminate(work, range(REGRESSORS // 2))


def inverse_end_kernel(work_ref, inverse_ref):
    work = eliminate(work_ref[...], range(REGRESSORS // 2, REGRESSORS))
    inverse_ref[...] = work[:, REGRESSORS:]


def forward_kernel(paths, trades, *refs):
    x_refs, w_refs = refs[:paths], refs[paths : paths + trades]
    lead_ref, member_ref, value_ref, *moment_refs = refs[paths + trades :]
    weights, notional = trade_blocks(w_refs)
    start = 0
    for x in x_refs:
        pre_act = dot(x[...], weights, 1, 1)
        value_ref[start : start + x.shape[0]] = (notional * softplus(pre_act)).astype(BF16)
        start += x.shape[0]
    trade_moment = dot(lead_ref[0], value_ref[...])
    parts = dot(three(trade_moment, 0), member_ref[...], 1, 1)
    moment = parts[:REGRESSORS] + parts[REGRESSORS : 2 * REGRESSORS] + parts[2 * REGRESSORS :]
    size = moment.shape[1] // len(moment_refs)
    for m, moment_ref in enumerate(moment_refs):
        moment_ref[...] = moment[:, m * size : (m + 1) * size]


def slope_kernel(paths, trades, *refs):
    x_refs, w_refs = refs[:paths], refs[paths : paths + trades]
    slope_ref = refs[-1]
    weights, notional = trade_blocks(w_refs)
    start = 0
    for x in x_refs:
        slope_ref[start : start + x.shape[0]] = notional * sigmoid(dot(x[...], weights, 1, 1))
        start += x.shape[0]


def solve_kernel(
    terms, inverse_ref, design_ref, rows_ref, thresh_ref, rate_ref, *refs
):
    solved_ref, turn_ref, total_ref = refs[terms:]
    moment = refs[0][...]
    for ref in refs[1:terms]:
        moment = moment + ref[...]
    size = moment.shape[1]
    inverse = inverse_ref[...]
    coeffs = dot(inverse, moment, precision=PRECISE)
    solved_ref[REGRESSORS:] = coeffs
    is_constant = rows(coeffs.shape) == CONSTANT
    shifted = coeffs - jnp.where(is_constant, thresh_ref[:, :size], 0.0)
    turn_ref[...] = three_rows(-LOG2_E * shifted)
    total_ref[...] = jnp.zeros(total_ref.shape, F32)

    def seeds(here):
        power = jnp.exp2(jnp.minimum(dot(rows_ref[here], turn_ref[...]), 126.0))
        seed = (1.0 / (1.0 + power)).astype(BF16)
        total_ref[...] += dot(design_ref[:, here], seed)

    each_chunk(rows_ref.shape[0], seeds)
    solved_ref[:REGRESSORS] = dot(inverse, total_ref[...] * rate_ref[:, :size], precision=PRECISE)


def joined(refs, part):
    here = slice(part * REGRESSORS, (part + 1) * REGRESSORS)
    return jnp.concatenate([ref[here] for ref in refs], axis=1)


def backward_kernel(scale, paths, trades, member_ref, rows_ref, slope_ref, value_ref, *refs):
    solved_refs, refs = refs[:paths], refs[paths:]
    x_refs, refs = refs[:paths], refs[paths:]
    w_refs, refs = refs[:trades], refs[trades:]
    weight_refs, basis_refs, slopes_ref = refs[:trades], refs[trades:-1], refs[-1]
    traded = dot(three_rows(joined(solved_refs, 0)), member_ref[...]).astype(BF16)
    group = slopes_ref.shape[0]
    spread = dot(rows_ref[:group], traded).astype(BF16).astype(F32)
    slopes_ref[...] = (slope_ref[...] * spread).astype(BF16)
    basis = jnp.concatenate([x[...] for x in x_refs], axis=0)
    weight = (dot(slopes_ref[...], basis, 0, 0) * scale).astype(BF16)
    start = 0
    for part in weight_refs:
        part[...] = weight[start : start + part.shape[0]]
        start += part.shape[0]
    weights, _ = trade_blocks(w_refs)
    start = 0
    for part in basis_refs:
        here = slice(start, start + part.shape[0])
        total = dot(slopes_ref[here], weights)
        wide = dot(value_ref[here], traded, 1, 1)
        design = wide
        for k in range(1, 3):
            design = design + pltpu.roll(wide, LANES - k * REGRESSORS, 1)
        design = jnp.where(lanes(design.shape) < CONSTANT, design, 0.0)
        part[:, :LANES] = (total[:, :LANES] + design).astype(BF16)
        part[:, LANES:] = total[:, LANES:].astype(BF16)
        start += part.shape[0]


def loss_kernel(rows_ref, thresh_ref, rate_ref, *refs):
    solved_refs, (loss_ref, own_ref, split_ref, total_ref) = refs[:-4], refs[-4:]
    adjoint = joined(solved_refs, 0)
    coeffs = joined(solved_refs, 1)
    thresh = thresh_ref[...]
    rate = rate_ref[...]
    split_ref[...] = three_rows(coeffs)
    total_ref[...] = jnp.zeros(total_ref.shape, F32)

    def losses(here):
        loss = softplus(dot(rows_ref[here], split_ref[...]) - thresh)
        total_ref[...] += jnp.sum(loss.reshape(-1, *total_ref.shape), axis=0)

    each_chunk(rows_ref.shape[0], losses)
    summed = jnp.sum(jnp.sum(total_ref[...] * rate, axis=0, keepdims=True), axis=1, keepdims=True)
    loss_ref[...] = jnp.broadcast_to(
        summed / (rows_ref.shape[0] * coeffs.shape[1]), loss_ref.shape
    )
    own = rows_ref[: own_ref.shape[0]]
    fitted = dot(own, split_ref[...])
    seed = rate * sigmoid(fitted - thresh)
    rest = seed - dot(own, three_rows(adjoint))
    design = dot(rest, coeffs, 1, 1, PRECISE) - dot(fitted, adjoint, 1, 1, PRECISE)
    blank = jnp.zeros((design.shape[0], LANES - REGRESSORS), F32)
    design = jnp.concatenate([design, blank], axis=1)
    own_ref[...] = jnp.where(lanes(design.shape) < CONSTANT, design, 0.0)


def total(refs):
    out = refs[0][...].astype(F32)
    for ref in refs[1:]:
        out = out + ref[...].astype(F32)
    return out


def weight_sum_kernel(*refs):
    refs[-1][...] = total(refs[:-1])


def basis_sum_kernel(own_ref, *refs):
    basis = total(refs[:-1])
    refs[-1][:, :LANES] = basis[:, :LANES] + own_ref[...]
    refs[-1][:, LANES:] = basis[:, LANES:]


def call(kernel, outs, *args, name, flops=0, scratch=(), scalars=0, far=0):
    size = sum(a.size * a.dtype.itemsize for a in args) + sum(
        math.prod(s) * jnp.dtype(d).itemsize for s, d in outs
    )
    return pl.pallas_call(
        kernel,
        out_shape=[jax.ShapeDtypeStruct(s, d) for s, d in outs],
        in_specs=[pl.BlockSpec(memory_space=pltpu.SMEM)] * scalars
        + [pl.BlockSpec(memory_space=pl.ANY)] * far
        + [pl.BlockSpec(memory_space=pltpu.VMEM)] * (len(args) - scalars - far),
        out_specs=[pl.BlockSpec(memory_space=pltpu.VMEM)] * len(outs),
        scratch_shapes=scratch,
        compiler_params=pltpu.CompilerParams(vmem_limit_bytes=VMEM_BYTES),
        cost_estimate=pl.CostEstimate(flops=int(flops), bytes_accessed=int(size), transcendentals=0),
        name=name,
    )(*args)


def shards(
    path_basis, proxy_weight, notional, set_of, threshold_index, threshold_levels, loss_rate
):
    n = lax.axis_size("paths")
    me = lax.axis_index("paths")
    inner_bits, outer_bits = split_bits(n)
    inner, outer = 1 << len(inner_bits), 1 << len(outer_bits)
    path_rows, features = path_basis.shape
    trade_rows = proxy_weight.shape[0]
    paths_all = path_rows * n
    sets = loss_rate.shape[0]
    quarter = sets // inner
    group_paths, group_trades = inner * path_rows, outer * trade_rows

    def swap(x, mask):
        return lax.ppermute(x, "paths", [(d, d ^ mask) for d in range(n)])

    def masks(bits):
        return [
            sum(((m >> j) & 1) << bit for j, bit in enumerate(bits)) for m in range(1 << len(bits))
        ]

    def after(x, *others):
        return lax.optimization_barrier((x, *others))[0]

    def direct(slots, bits):
        sent = [swap(x, mask) for x, mask in zip(slots[:0:-1], masks(bits)[:0:-1])]
        return sent[::-1]

    first_bit = outer_bits[0]
    wide, own = call(
        pack_kernel,
        [((trade_rows + PAD_ROWS, features), BF16), (path_basis.shape, BF16)],
        path_basis, proxy_weight, notional[None, :],
        name="pack",
        scratch=[pltpu.SemaphoreType.DMA((2,))],
        far=2,
    )
    weights = [wide, swap(wide, 1 << first_bit)]
    basis = [own] + direct([path_basis] * inner, inner_bits)
    for bit in outer_bits[1:]:
        weights = weights + [swap(w, 1 << bit) for w in weights]

    member, thresh, rate = call(
        partial(tables_kernel, masks(outer_bits), inner),
        [((sets, group_trades), BF16), ((1, sets), F32), ((1, sets), F32)],
        me.astype(jnp.int32).reshape(1),
        threshold_levels,
        set_of.reshape(n, 1, trade_rows),
        threshold_index.reshape(inner, 1, quarter),
        loss_rate.reshape(inner, 1, quarter),
        name="tables",
        scalars=2,
    )
    (lead,) = call(lead_kernel, [((1, REGRESSORS, group_paths), BF16)], *basis, name="lead")
    value, *moments = call(
        partial(forward_kernel, inner, outer),
        [((group_paths, group_trades), BF16)] + [((REGRESSORS, quarter), F32)] * inner,
        *basis, *weights, lead, member,
        name="forward",
    )
    small = after(lead, weights[1])
    small = jnp.concatenate([small, swap(small, 1 << first_bit)], axis=0)
    for bit in outer_bits[1:]:
        small = after(small, value)
        small = jnp.concatenate([small, swap(small, 1 << bit)], axis=0)
    moment = sum(direct(moments, inner_bits), moments[0])
    (work,) = call(
        partial(inverse_begin_kernel, RIDGE_SCALE * paths_all),
        [((REGRESSORS, 2 * REGRESSORS), F32)],
        small,
        name="inverse_begin",
    )
    moment = after(moment, work)
    for bit in outer_bits[:0:-1]:
        moment = moment + swap(moment, 1 << bit)
    moments = [moment, swap(moment, 1 << first_bit)]
    (inverse,) = call(
        inverse_end_kernel, [((REGRESSORS, REGRESSORS), F32)], work, name="inverse_end"
    )
    design_all, design_rows = call(
        design_kernel,
        [((REGRESSORS, paths_all), BF16), ((paths_all, LANES), BF16)],
        small,
        name="design",
    )
    (solved,) = call(
        partial(solve_kernel, len(moments)),
        [((2 * REGRESSORS, quarter), F32)],
        inverse, design_all, design_rows, thresh, rate, *moments,
        name="solve",
        scratch=[pltpu.VMEM((LANES, quarter), BF16), pltpu.VMEM((REGRESSORS, quarter), F32)],
    )
    solved = [solved] + direct([solved] * inner, inner_bits)
    (slope,) = call(
        partial(slope_kernel, inner, outer),
        [((group_paths, group_trades), F32)],
        *basis, *weights,
        name="slope",
    )
    parts = call(
        partial(backward_kernel, 1.0 / math.sqrt(paths_all), inner, outer),
        [((trade_rows, features), BF16)] * outer + [((path_rows, features), BF16)] * inner,
        member, design_rows, slope, value, *solved, *basis, *weights,
        name="backward",
        scratch=[pltpu.VMEM((group_paths, group_trades), BF16)],
    )
    terms = [[part] for part in parts[:outer]]
    for bit in reversed(outer_bits):
        count = len(terms) // 2
        arrived = None
        for k in reversed(range(count)):
            gone = terms[count + k]
            gone = gone[0] if len(gone) == 1 else sum(g.astype(F32) for g in gone).astype(BF16)
            if arrived is not None:
                gone = after(gone, arrived)
            arrived = swap(gone, 1 << bit)
            terms[k].append(arrived)
        terms = terms[:count]
    weight_terms = terms[0]
    basis_parts = parts[outer:]
    basis_terms = [basis_parts[0]] + direct(basis_parts, inner_bits)
    loss, own_adjoint = call(
        loss_kernel,
        [((8, LANES), F32), ((path_rows, LANES), F32)],
        design_rows, thresh, rate, *solved,
        name="loss",
        scratch=[pltpu.VMEM((LANES, sets), BF16), pltpu.VMEM((8, sets), F32)],
    )
    (weight_adjoint,) = call(
        weight_sum_kernel, [((trade_rows, features), F32)], *weight_terms, name="weight_sum"
    )
    (basis_adjoint,) = call(
        basis_sum_kernel, [((path_rows, features), F32)], own_adjoint, *basis_terms, name="basis_sum"
    )
    return (loss[0, :1], basis_adjoint, weight_adjoint)


def solution(mesh):
    placed = (
        P(("groups", "paths"), None),
        P(("groups", "paths"), None),
        P(("groups", "paths")),
        P("groups"),
        P("groups"),
        P("groups"),
        P("groups"),
    )
    return jax.shard_map(
        shards,
        mesh=mesh,
        in_specs=placed,
        out_specs=(P("groups"), P(("groups", "paths"), None), P(("groups", "paths"), None)),
        check_vma=False,
    )
```

```python
import math
from functools import partial

import jax
import jax.numpy as jnp
from jax import lax
from jax.experimental import pallas as pl
from jax.experimental.pallas import tpu as pltpu
from jax.sharding import PartitionSpec as P

REGRESSORS = 32
RIDGE_SCALE = 0.01
PRECISE = lax.Precision.HIGHEST
F32 = jnp.float32
BF16 = jnp.bfloat16
LANES = 128
PAD_ROWS = 16
CHUNK = 256
VMEM_BYTES = 48 * 1024 * 1024
LOG2_E = math.log2(math.e)
CONSTANT = REGRESSORS - 1


def split_bits(size):
    count = size.bit_length() - 1
    half = count // 2
    return list(range(1, half + 1)), list(range(count - 1, half, -1)) + [0]


def dot(a, b, ca=1, cb=0, precision=None):
    return lax.dot_general(
        a, b, (((ca,), (cb,)), ((), ())), precision=precision, preferred_element_type=F32
    )


def three(x, axis):
    high = x.astype(BF16)
    rest = x - high.astype(F32)
    middle = rest.astype(BF16)
    low = (rest - middle.astype(F32)).astype(BF16)
    return jnp.concatenate([high, middle, low], axis=axis)


def three_rows(x):
    blank = jnp.zeros((LANES - 3 * REGRESSORS, x.shape[1]), BF16)
    return jnp.concatenate([three(x, 0), blank], axis=0)


def lanes(shape):
    return lax.broadcasted_iota(jnp.int32, shape, len(shape) - 1)


def rows(shape):
    return lax.broadcasted_iota(jnp.int32, shape, len(shape) - 2)


def softplus(x):
    return jnp.maximum(x, 0.0) + jnp.log1p(jnp.exp(-jnp.abs(x)))


def sigmoid(x):
    small = jnp.exp(-jnp.abs(x))
    return jnp.where(x >= 0.0, 1.0, small) / (1.0 + small)


def each_chunk(size, step):
    count = size // CHUNK

    def body(i, carry):
        step(pl.ds(pl.multiple_of(i * CHUNK, CHUNK), CHUNK))
        return carry

    lax.fori_loop(0, count, body, 0, unroll=count <= 8)


def eliminate(work, columns):
    row = rows(work.shape)
    for k in columns:
        pivot = work[k : k + 1] / work[k : k + 1, k : k + 1]
        work = jnp.where(row == k, pivot, work - work[:, k : k + 1] * pivot)
    return work


def pack_kernel(x_ref, w_ref, notional_ref, wide_ref, own_ref, sems):
    trades = w_ref.shape[0]
    weights = pltpu.make_async_copy(w_ref, wide_ref.at[pl.ds(0, trades)], sems.at[0])
    basis = pltpu.make_async_copy(x_ref, own_ref, sems.at[1])
    weights.start()
    basis.start()
    wide_ref[trades:] = jnp.zeros((PAD_ROWS, wide_ref.shape[1]), BF16)
    wide_ref[trades:, :trades] = jnp.broadcast_to(notional_ref[...], (PAD_ROWS, trades))
    weights.wait()
    basis.wait()


def trade_blocks(refs):
    trades = refs[0].shape[0] - PAD_ROWS
    weights = jnp.concatenate([ref[:trades] for ref in refs], axis=0)
    notional = [ref[trades:].astype(F32)[:1, :trades] for ref in refs]
    return weights, jnp.concatenate(notional, axis=1)


def lead_kernel(*refs):
    x_refs, lead_ref = refs[:-1], refs[-1]
    start = 0
    for x in x_refs:
        turned = x[:, :LANES].astype(F32).T[:REGRESSORS]
        turned = jnp.where(rows(turned.shape) == CONSTANT, 1.0, turned)
        lead_ref[0, :, start : start + x.shape[0]] = turned.astype(BF16)
        start += x.shape[0]


def tables_kernel(
    trade_masks, inner, me_ref, level_ref, set_ref, index_ref, rate_ref,
    member_ref, thresh_out_ref, rate_out_ref,
):
    me = me_ref[0]
    place = (me >> 1) & (inner - 1)
    size = member_ref.shape[0] // inner
    trades = set_ref.shape[-1]
    for m in range(inner):
        here = slice(m * size, (m + 1) * size)
        label = (place ^ m) * size + rows((size, 1))
        for j, mask in enumerate(trade_masks):
            member_ref[here, j * trades : (j + 1) * trades] = jnp.where(
                set_ref[me ^ mask] == label, 1.0, 0.0
            ).astype(BF16)
        index = index_ref[place ^ m]
        thresh = jnp.zeros(index.shape, F32)
        for k in range(level_ref.shape[0]):
            thresh = jnp.where(index == k, level_ref[k], thresh)
        thresh_out_ref[:, here] = thresh
        rate_out_ref[:, here] = rate_ref[place ^ m]


def design_kernel(small_ref, design_ref, rows_ref):
    size = small_ref.shape[2]
    for d in range(small_ref.shape[0]):
        here = slice(d * size, (d + 1) * size)
        block = small_ref[d]
        design_ref[:, here] = block
        turned = block.astype(F32).T
        blank = jnp.zeros((size, LANES - 3 * REGRESSORS), F32)
        rows_ref[here] = jnp.concatenate([turned] * 3 + [blank], axis=1).astype(BF16)


def inverse_begin_kernel(ridge, small_ref, work_ref):
    square = (REGRESSORS, REGRESSORS)
    gram = jnp.where(rows(square) == lanes(square), ridge, 0.0)
    for d in range(small_ref.shape[0]):
        gram = gram + dot(small_ref[d], small_ref[d], 1, 1)
    work = jnp.concatenate([gram, jnp.eye(REGRESSORS, dtype=F32)], axis=1)
    work_ref[...] = eliminate(work, range(REGRESSORS // 2))


def inverse_end_kernel(work_ref, inverse_ref):
    work = eliminate(work_ref[...], range(REGRESSORS // 2, REGRESSORS))
    inverse_ref[...] = work[:, REGRESSORS:]


def forward_kernel(paths, trades, *refs):
    x_refs, w_refs = refs[:paths], refs[paths : paths + trades]
    lead_ref, member_ref, value_ref, *moment_refs = refs[paths + trades :]
    weights, notional = trade_blocks(w_refs)
    start = 0
    for x in x_refs:
        pre_act = dot(x[...], weights, 1, 1)
        value_ref[start : start + x.shape[0]] = (notional * softplus(pre_act)).astype(BF16)
        start += x.shape[0]
    trade_moment = dot(lead_ref[0], value_ref[...])
    parts = dot(three(trade_moment, 0), member_ref[...], 1, 1)
    moment = parts[:REGRESSORS] + parts[REGRESSORS : 2 * REGRESSORS] + parts[2 * REGRESSORS :]
    size = moment.shape[1] // len(moment_refs)
    for m, moment_ref in enumerate(moment_refs):
        moment_ref[...] = moment[:, m * size : (m + 1) * size]


def slope_kernel(paths, trades, *refs):
    x_refs, w_refs = refs[:paths], refs[paths : paths + trades]
    slope_ref = refs[-1]
    weights, notional = trade_blocks(w_refs)
    start = 0
    for x in x_refs:
        slope_ref[start : start + x.shape[0]] = notional * sigmoid(dot(x[...], weights, 1, 1))
        start += x.shape[0]


def solve_kernel(
    terms, inverse_ref, design_ref, rows_ref, thresh_ref, rate_ref, *refs
):
    solved_ref, turn_ref, total_ref = refs[terms:]
    moment = refs[0][...]
    for ref in refs[1:terms]:
        moment = moment + ref[...]
    size = moment.shape[1]
    inverse = inverse_ref[...]
    coeffs = dot(inverse, moment, precision=PRECISE)
    solved_ref[REGRESSORS:] = coeffs
    is_constant = rows(coeffs.shape) == CONSTANT
    shifted = coeffs - jnp.where(is_constant, thresh_ref[:, :size], 0.0)
    turn_ref[...] = three_rows(-LOG2_E * shifted)
    total_ref[...] = jnp.zeros(total_ref.shape, F32)

    def seeds(here):
        power = jnp.exp2(jnp.minimum(dot(rows_ref[here], turn_ref[...]), 126.0))
        seed = (1.0 / (1.0 + power)).astype(BF16)
        total_ref[...] += dot(design_ref[:, here], seed)

    each_chunk(rows_ref.shape[0], seeds)
    solved_ref[:REGRESSORS] = dot(inverse, total_ref[...] * rate_ref[:, :size], precision=PRECISE)


def joined(refs, part):
    here = slice(part * REGRESSORS, (part + 1) * REGRESSORS)
    return jnp.concatenate([ref[here] for ref in refs], axis=1)


def backward_kernel(scale, paths, trades, member_ref, rows_ref, slope_ref, value_ref, *refs):
    solved_refs, refs = refs[:paths], refs[paths:]
    x_refs, refs = refs[:paths], refs[paths:]
    w_refs, refs = refs[:trades], refs[trades:]
    weight_refs, basis_refs, slopes_ref = refs[:trades], refs[trades:-1], refs[-1]
    traded = dot(three_rows(joined(solved_refs, 0)), member_ref[...]).astype(BF16)
    group = slopes_ref.shape[0]
    spread = dot(rows_ref[:group], traded).astype(BF16).astype(F32)
    slopes_ref[...] = (slope_ref[...] * spread).astype(BF16)
    basis = jnp.concatenate([x[...] for x in x_refs], axis=0)
    weight = (dot(slopes_ref[...], basis, 0, 0) * scale).astype(BF16)
    start = 0
    for part in weight_refs:
        part[...] = weight[start : start + part.shape[0]]
        start += part.shape[0]
    weights, _ = trade_blocks(w_refs)
    start = 0
    for part in basis_refs:
        here = slice(start, start + part.shape[0])
        total = dot(slopes_ref[here], weights)
        wide = dot(value_ref[here], traded, 1, 1)
        design = wide
        for k in range(1, 3):
            design = design + pltpu.roll(wide, LANES - k * REGRESSORS, 1)
        design = jnp.where(lanes(design.shape) < CONSTANT, design, 0.0)
        part[:, :LANES] = (total[:, :LANES] + design).astype(BF16)
        part[:, LANES:] = total[:, LANES:].astype(BF16)
        start += part.shape[0]


def loss_kernel(rows_ref, thresh_ref, rate_ref, *refs):
    solved_refs, (loss_ref, own_ref, split_ref, total_ref) = refs[:-4], refs[-4:]
    adjoint = joined(solved_refs, 0)
    coeffs = joined(solved_refs, 1)
    thresh = thresh_ref[...]
    rate = rate_ref[...]
    split_ref[...] = three_rows(coeffs)
    total_ref[...] = jnp.zeros(total_ref.shape, F32)

    def losses(here):
        loss = softplus(dot(rows_ref[here], split_ref[...]) - thresh)
        total_ref[...] += jnp.sum(loss.reshape(-1, *total_ref.shape), axis=0)

    each_chunk(rows_ref.shape[0], losses)
    summed = jnp.sum(jnp.sum(total_ref[...] * rate, axis=0, keepdims=True), axis=1, keepdims=True)
    loss_ref[...] = jnp.broadcast_to(
        summed / (rows_ref.shape[0] * coeffs.shape[1]), loss_ref.shape
    )
    own = rows_ref[: own_ref.shape[0]]
    fitted = dot(own, split_ref[...])
    seed = rate * sigmoid(fitted - thresh)
    rest = seed - dot(own, three_rows(adjoint))
    design = dot(rest, coeffs, 1, 1, PRECISE) - dot(fitted, adjoint, 1, 1, PRECISE)
    blank = jnp.zeros((design.shape[0], LANES - REGRESSORS), F32)
    design = jnp.concatenate([design, blank], axis=1)
    own_ref[...] = jnp.where(lanes(design.shape) < CONSTANT, design, 0.0)


def total(refs):
    out = refs[0][...].astype(F32)
    for ref in refs[1:]:
        out = out + ref[...].astype(F32)
    return out


def sum_kernel(first, own_ref, *refs):
    basis_ref, weight_ref = refs[-2:]
    basis = total(refs[:first])
    basis_ref[:, :LANES] = basis[:, :LANES] + own_ref[...]
    basis_ref[:, LANES:] = basis[:, LANES:]
    weight_ref[...] = total(refs[first:-2])


def call(kernel, outs, *args, name, flops=0, scratch=(), scalars=0, far=0):
    size = sum(a.size * a.dtype.itemsize for a in args) + sum(
        math.prod(s) * jnp.dtype(d).itemsize for s, d in outs
    )
    return pl.pallas_call(
        kernel,
        out_shape=[jax.ShapeDtypeStruct(s, d) for s, d in outs],
        in_specs=[pl.BlockSpec(memory_space=pltpu.SMEM)] * scalars
        + [pl.BlockSpec(memory_space=pltpu.HBM)] * far
        + [pl.BlockSpec(memory_space=pltpu.VMEM)] * (len(args) - scalars - far),
        out_specs=[pl.BlockSpec(memory_space=pltpu.VMEM)] * len(outs),
        scratch_shapes=scratch,
        compiler_params=pltpu.CompilerParams(vmem_limit_bytes=VMEM_BYTES),
        cost_estimate=pl.CostEstimate(flops=int(flops), bytes_accessed=int(size), transcendentals=0),
        name=name,
    )(*args)


def shards(
    path_basis, proxy_weight, notional, set_of, threshold_index, threshold_levels, loss_rate
):
    n = lax.axis_size("paths")
    me = lax.axis_index("paths")
    inner_bits, outer_bits = split_bits(n)
    inner, outer = 1 << len(inner_bits), 1 << len(outer_bits)
    path_rows, features = path_basis.shape
    trade_rows = proxy_weight.shape[0]
    paths_all = path_rows * n
    sets = loss_rate.shape[0]
    quarter = sets // inner
    group_paths, group_trades = inner * path_rows, outer * trade_rows

    def swap(x, mask):
        return lax.ppermute(x, "paths", [(d, d ^ mask) for d in range(n)])

    def masks(bits):
        return [
            sum(((m >> j) & 1) << bit for j, bit in enumerate(bits)) for m in range(1 << len(bits))
        ]

    def after(x, *others):
        return lax.optimization_barrier((x, *others))[0]

    def direct(slots, bits):
        sent = [swap(x, mask) for x, mask in zip(slots[:0:-1], masks(bits)[:0:-1])]
        return sent[::-1]

    first_bit = outer_bits[0]
    wide, own = call(
        pack_kernel,
        [((trade_rows + PAD_ROWS, features), BF16), (path_basis.shape, BF16)],
        path_basis, proxy_weight, notional[None, :],
        name="pack",
        scratch=[pltpu.SemaphoreType.DMA((2,))],
        far=2,
    )
    weights = [wide, swap(wide, 1 << first_bit)]
    basis = [own] + direct([path_basis] * inner, inner_bits)
    member, thresh, rate = call(
        partial(tables_kernel, masks(outer_bits), inner),
        [((sets, group_trades), BF16), ((1, sets), F32), ((1, sets), F32)],
        me.astype(jnp.int32).reshape(1),
        threshold_levels,
        set_of.reshape(n, 1, trade_rows),
        threshold_index.reshape(inner, 1, quarter),
        loss_rate.reshape(inner, 1, quarter),
        name="tables",
        scalars=2,
    )
    for bit in outer_bits[1:]:
        weights = weights + [
            swap(after(w, member) if k else w, 1 << bit) for k, w in enumerate(weights)
        ]
    (lead,) = call(lead_kernel, [((1, REGRESSORS, group_paths), BF16)], *basis, name="lead")
    value, *moments = call(
        partial(forward_kernel, inner, outer),
        [((group_paths, group_trades), BF16)] + [((REGRESSORS, quarter), F32)] * inner,
        *basis, *weights, lead, member,
        name="forward",
    )
    small = after(lead, value)
    for bit in outer_bits:
        small = jnp.concatenate([small, swap(small, 1 << bit)], axis=0)
    moment = sum(direct(moments, inner_bits), moments[0])
    (work,) = call(
        partial(inverse_begin_kernel, RIDGE_SCALE * paths_all),
        [((REGRESSORS, 2 * REGRESSORS), F32)],
        small,
        name="inverse_begin",
    )
    moment = after(moment, work)
    for bit in outer_bits[:0:-1]:
        moment = moment + swap(moment, 1 << bit)
    moments = [moment, swap(moment, 1 << first_bit)]
    (inverse,) = call(
        inverse_end_kernel, [((REGRESSORS, REGRESSORS), F32)], work, name="inverse_end"
    )
    design_all, design_rows = call(
        design_kernel,
        [((REGRESSORS, paths_all), BF16), ((paths_all, LANES), BF16)],
        small,
        name="design",
    )
    (solved,) = call(
        partial(solve_kernel, len(moments)),
        [((2 * REGRESSORS, quarter), F32)],
        inverse, design_all, design_rows, thresh, rate, *moments,
        name="solve",
        scratch=[pltpu.VMEM((LANES, quarter), BF16), pltpu.VMEM((REGRESSORS, quarter), F32)],
    )
    solved = [solved] + direct([solved] * inner, inner_bits)
    (slope,) = call(
        partial(slope_kernel, inner, outer),
        [((group_paths, group_trades), F32)],
        *basis, *weights,
        name="slope",
    )
    parts = call(
        partial(backward_kernel, 1.0 / math.sqrt(paths_all), inner, outer),
        [((trade_rows, features), BF16)] * outer + [((path_rows, features), BF16)] * inner,
        member, design_rows, slope, value, *solved, *basis, *weights,
        name="backward",
        scratch=[pltpu.VMEM((group_paths, group_trades), BF16)],
    )
    terms = [[part] for part in parts[:outer]]
    for bit in reversed(outer_bits):
        count = len(terms) // 2
        arrived = None
        for k in reversed(range(count)):
            gone = terms[count + k]
            gone = gone[0] if len(gone) == 1 else sum(g.astype(F32) for g in gone).astype(BF16)
            if arrived is not None:
                gone = after(gone, arrived)
            arrived = swap(gone, 1 << bit)
            terms[k].append(arrived)
            if bit == outer_bits[-1] and k == count - 1:
                basis_parts = list(parts[outer:])
                basis_parts[1] = after(basis_parts[1], arrived)
        terms = terms[:count]
    weight_terms = terms[0]
    basis_terms = [basis_parts[0]] + direct(basis_parts, inner_bits)
    loss, own_adjoint = call(
        loss_kernel,
        [((8, LANES), F32), ((path_rows, LANES), F32)],
        design_rows, thresh, rate, *solved,
        name="loss",
        scratch=[pltpu.VMEM((LANES, sets), BF16), pltpu.VMEM((8, sets), F32)],
    )
    basis_adjoint, weight_adjoint = call(
        partial(sum_kernel, len(basis_terms)),
        [((path_rows, features), F32), ((trade_rows, features), F32)],
        own_adjoint, *basis_terms, *weight_terms,
        name="sums",
    )
    return (loss[0, :1], basis_adjoint, weight_adjoint)


def solution(mesh):
    placed = (
        P(("groups", "paths"), None),
        P(("groups", "paths"), None),
        P(("groups", "paths")),
        P("groups"),
        P("groups"),
        P("groups"),
        P("groups"),
    )
    return jax.shard_map(
        shards,
        mesh=mesh,
        in_specs=placed,
        out_specs=(P("groups"), P(("groups", "paths"), None), P(("groups", "paths"), None)),
        check_vma=False,
    )
```

```python
import math
from functools import partial

import jax
import jax.numpy as jnp
from jax import lax
from jax.experimental import pallas as pl
from jax.experimental.pallas import tpu as pltpu
from jax.sharding import PartitionSpec as P

REGRESSORS = 32
RIDGE_SCALE = 0.01
PRECISE = lax.Precision.HIGHEST
F32 = jnp.float32
BF16 = jnp.bfloat16
LANES = 128
CHUNK = 256
VMEM_BYTES = 48 * 1024 * 1024
LOG2_E = math.log2(math.e)
CONSTANT = REGRESSORS - 1


def split_bits(size):
    count = size.bit_length() - 1
    half = count // 2
    return list(range(1, half + 1)), list(range(count - 1, half, -1)) + [0]


def dot(a, b, ca=1, cb=0, precision=None):
    return lax.dot_general(
        a, b, (((ca,), (cb,)), ((), ())), precision=precision, preferred_element_type=F32
    )


def three(x, axis):
    high = x.astype(BF16)
    rest = x - high.astype(F32)
    middle = rest.astype(BF16)
    low = (rest - middle.astype(F32)).astype(BF16)
    return jnp.concatenate([high, middle, low], axis=axis)


def three_rows(x):
    blank = jnp.zeros((LANES - 3 * REGRESSORS, x.shape[1]), BF16)
    return jnp.concatenate([three(x, 0), blank], axis=0)


def lanes(shape):
    return lax.broadcasted_iota(jnp.int32, shape, len(shape) - 1)


def rows(shape):
    return lax.broadcasted_iota(jnp.int32, shape, len(shape) - 2)


def softplus(x):
    return jnp.maximum(x, 0.0) + jnp.log1p(jnp.exp(-jnp.abs(x)))


def sigmoid(x):
    small = jnp.exp(-jnp.abs(x))
    return jnp.where(x >= 0.0, 1.0, small) / (1.0 + small)


def each_chunk(size, step):
    count = size // CHUNK

    def body(i, carry):
        step(pl.ds(pl.multiple_of(i * CHUNK, CHUNK), CHUNK))
        return carry

    lax.fori_loop(0, count, body, 0, unroll=count <= 8)


def invert(matrix):
    size = matrix.shape[0]
    work = jnp.concatenate([matrix, jnp.eye(size, dtype=F32)], axis=1)
    row = rows(work.shape)
    for k in range(0, size, 2):
        left, right = work[:, k : k + 1], work[:, k + 1 : k + 2]
        upper, lower = work[k : k + 1], work[k + 1 : k + 2]
        a, b, c, d = left[k : k + 1], right[k : k + 1], left[k + 1 : k + 2], right[k + 1 : k + 2]
        scale = 1.0 / (a * d - b * c)
        upper, lower = (d * upper - b * lower) * scale, (a * lower - c * upper) * scale
        work = work - left * upper - right * lower
        work = jnp.where(row == k, upper, jnp.where(row == k + 1, lower, work))
    return work[:, size:]


def lead_kernel(*refs):
    x_refs, lead_ref = refs[:-1], refs[-1]
    start = 0
    for x in x_refs:
        turned = x[:, :LANES].astype(F32).T[:REGRESSORS]
        turned = jnp.where(rows(turned.shape) == CONSTANT, 1.0, turned)
        lead_ref[:, start : start + x.shape[0]] = turned.astype(BF16)
        start += x.shape[0]


def tables_kernel(
    trade_masks, inner, me_ref, level_ref, set_ref, index_ref, rate_ref,
    member_ref, thresh_out_ref, rate_out_ref,
):
    me = me_ref[0]
    place = (me >> 1) & (inner - 1)
    size = member_ref.shape[0] // inner
    trades = set_ref.shape[-1]
    for m in range(inner):
        here = slice(m * size, (m + 1) * size)
        label = (place ^ m) * size + rows((size, 1))
        for j, mask in enumerate(trade_masks):
            member_ref[here, j * trades : (j + 1) * trades] = jnp.where(
                set_ref[me ^ mask] == label, 1.0, 0.0
            ).astype(BF16)
        index = index_ref[place ^ m]
        thresh = jnp.zeros(index.shape, F32)
        for k in range(level_ref.shape[0]):
            thresh = jnp.where(index == k, level_ref[k], thresh)
        thresh_out_ref[:, here] = thresh
        rate_out_ref[:, here] = rate_ref[place ^ m]


def design_kernel(*refs):
    lead_refs, (design_ref, rows_ref) = refs[:-2], refs[-2:]
    size = lead_refs[0].shape[1]
    for d, lead_ref in enumerate(lead_refs):
        here = slice(d * size, (d + 1) * size)
        design_ref[:, here] = lead_ref[...]
        turned = lead_ref[...].astype(F32).T
        blank = jnp.zeros((size, LANES - 3 * REGRESSORS), F32)
        rows_ref[here] = jnp.concatenate([turned] * 3 + [blank], axis=1).astype(BF16)


def inverse_kernel(ridge, *refs):
    square = (REGRESSORS, REGRESSORS)
    gram = jnp.where(rows(square) == lanes(square), ridge, 0.0)
    for lead_ref in refs[:-1]:
        gram = gram + dot(lead_ref[...], lead_ref[...], 1, 1)
    refs[-1][...] = invert(gram)


def joined_weights(refs):
    return jnp.concatenate([ref[...] for ref in refs], axis=0)


def joined_notionals(refs):
    return jnp.concatenate([ref[...].astype(F32) for ref in refs], axis=1)


def forward_kernel(paths, trades, *refs):
    x_refs, refs = refs[:paths], refs[paths:]
    weights, notional = joined_weights(refs[:trades]), joined_notionals(refs[trades : 2 * trades])
    lead_ref, member_ref, value_ref, *moment_refs = refs[2 * trades :]
    start = 0
    for x in x_refs:
        pre_act = dot(x[...], weights, 1, 1)
        value_ref[start : start + x.shape[0]] = (notional * softplus(pre_act)).astype(BF16)
        start += x.shape[0]
    trade_moment = dot(lead_ref[...], value_ref[...])
    parts = dot(three(trade_moment, 0), member_ref[...], 1, 1)
    moment = parts[:REGRESSORS] + parts[REGRESSORS : 2 * REGRESSORS] + parts[2 * REGRESSORS :]
    size = moment.shape[1] // len(moment_refs)
    for m, moment_ref in enumerate(moment_refs):
        moment_ref[...] = moment[:, m * size : (m + 1) * size]


def slope_kernel(paths, trades, *refs):
    x_refs, refs, slope_ref = refs[:paths], refs[paths:], refs[-1]
    weights, notional = joined_weights(refs[:trades]), joined_notionals(refs[trades : 2 * trades])
    start = 0
    for x in x_refs:
        slope_ref[start : start + x.shape[0]] = notional * sigmoid(dot(x[...], weights, 1, 1))
        start += x.shape[0]


def solve_kernel(
    terms, inverse_ref, design_ref, rows_ref, thresh_ref, rate_ref, *refs
):
    solved_ref, turn_ref, total_ref = refs[terms:]
    moment = refs[0][...]
    for ref in refs[1:terms]:
        moment = moment + ref[...]
    size = moment.shape[1]
    inverse = inverse_ref[...]
    coeffs = dot(inverse, moment, precision=PRECISE)
    solved_ref[REGRESSORS:] = coeffs
    is_constant = rows(coeffs.shape) == CONSTANT
    shifted = coeffs - jnp.where(is_constant, thresh_ref[:, :size], 0.0)
    turn_ref[...] = three_rows(-LOG2_E * shifted)
    total_ref[...] = jnp.zeros(total_ref.shape, F32)

    def seeds(here):
        power = jnp.exp2(jnp.minimum(dot(rows_ref[here], turn_ref[...]), 126.0))
        seed = (1.0 / (1.0 + power)).astype(BF16)
        total_ref[...] += dot(design_ref[:, here], seed)

    each_chunk(rows_ref.shape[0], seeds)
    solved_ref[:REGRESSORS] = dot(inverse, total_ref[...] * rate_ref[:, :size], precision=PRECISE)


def joined(refs, part):
    here = slice(part * REGRESSORS, (part + 1) * REGRESSORS)
    return jnp.concatenate([ref[here] for ref in refs], axis=1)


def backward_kernel(scale, paths, trades, member_ref, rows_ref, slope_ref, value_ref, *refs):
    solved_refs, refs = refs[:paths], refs[paths:]
    x_refs, refs = refs[:paths], refs[paths:]
    w_refs, refs = refs[:trades], refs[trades:]
    weight_refs, basis_refs, slopes_ref = refs[:trades], refs[trades:-1], refs[-1]
    traded = dot(three_rows(joined(solved_refs, 0)), member_ref[...]).astype(BF16)
    group = slopes_ref.shape[0]
    spread = dot(rows_ref[:group], traded).astype(BF16).astype(F32)
    slopes_ref[...] = (slope_ref[...] * spread).astype(BF16)
    basis = jnp.concatenate([x[...] for x in x_refs], axis=0)
    weight = (dot(slopes_ref[...], basis, 0, 0) * scale).astype(BF16)
    start = 0
    for part in weight_refs:
        part[...] = weight[start : start + part.shape[0]]
        start += part.shape[0]
    weights = joined_weights(w_refs)
    start = 0
    for part in basis_refs:
        here = slice(start, start + part.shape[0])
        total = dot(slopes_ref[here], weights)
        wide = dot(value_ref[here], traded, 1, 1)
        design = wide
        for k in range(1, 3):
            design = design + pltpu.roll(wide, LANES - k * REGRESSORS, 1)
        design = jnp.where(lanes(design.shape) < CONSTANT, design, 0.0)
        part[:, :LANES] = (total[:, :LANES] + design).astype(BF16)
        part[:, LANES:] = total[:, LANES:].astype(BF16)
        start += part.shape[0]


def loss_kernel(rows_ref, thresh_ref, rate_ref, *refs):
    solved_refs, (loss_ref, own_ref, split_ref, total_ref) = refs[:-4], refs[-4:]
    adjoint = joined(solved_refs, 0)
    coeffs = joined(solved_refs, 1)
    thresh = thresh_ref[...]
    rate = rate_ref[...]
    split_ref[...] = three_rows(coeffs)
    total_ref[...] = jnp.zeros(total_ref.shape, F32)

    def losses(here):
        loss = softplus(dot(rows_ref[here], split_ref[...]) - thresh)
        total_ref[...] += jnp.sum(loss.reshape(-1, *total_ref.shape), axis=0)

    each_chunk(rows_ref.shape[0], losses)
    summed = jnp.sum(jnp.sum(total_ref[...] * rate, axis=0, keepdims=True), axis=1, keepdims=True)
    loss_ref[...] = jnp.broadcast_to(
        summed / (rows_ref.shape[0] * coeffs.shape[1]), loss_ref.shape
    )
    own = rows_ref[: own_ref.shape[0]]
    fitted = dot(own, split_ref[...])
    seed = rate * sigmoid(fitted - thresh)
    rest = seed - dot(own, three_rows(adjoint))
    design = dot(rest, coeffs, 1, 1, PRECISE) - dot(fitted, adjoint, 1, 1, PRECISE)
    blank = jnp.zeros((design.shape[0], LANES - REGRESSORS), F32)
    design = jnp.concatenate([design, blank], axis=1)
    own_ref[...] = jnp.where(lanes(design.shape) < CONSTANT, design, 0.0)


def total(refs):
    out = refs[0][...].astype(F32)
    for ref in refs[1:]:
        out = out + ref[...].astype(F32)
    return out


def sum_kernel(first, own_ref, *refs):
    basis_ref, weight_ref = refs[-2:]
    basis = total(refs[:first])
    basis_ref[:, :LANES] = basis[:, :LANES] + own_ref[...]
    basis_ref[:, LANES:] = basis[:, LANES:]
    weight_ref[...] = total(refs[first:-2])


def call(kernel, outs, *args, name, flops=0, scratch=(), scalars=0):
    size = sum(a.size * a.dtype.itemsize for a in args) + sum(
        math.prod(s) * jnp.dtype(d).itemsize for s, d in outs
    )
    return pl.pallas_call(
        kernel,
        out_shape=[jax.ShapeDtypeStruct(s, d) for s, d in outs],
        in_specs=[pl.BlockSpec(memory_space=pltpu.SMEM)] * scalars
        + [pl.BlockSpec(memory_space=pltpu.VMEM)] * (len(args) - scalars),
        out_specs=[pl.BlockSpec(memory_space=pltpu.VMEM)] * len(outs),
        scratch_shapes=scratch,
        compiler_params=pltpu.CompilerParams(vmem_limit_bytes=VMEM_BYTES),
        cost_estimate=pl.CostEstimate(flops=int(flops), bytes_accessed=int(size), transcendentals=0),
        name=name,
    )(*args)


def shards(
    path_basis, proxy_weight, notional, set_of, threshold_index, threshold_levels, loss_rate
):
    n = lax.axis_size("paths")
    me = lax.axis_index("paths")
    inner_bits, outer_bits = split_bits(n)
    inner, outer = 1 << len(inner_bits), 1 << len(outer_bits)
    path_rows, features = path_basis.shape
    trade_rows = proxy_weight.shape[0]
    paths_all = path_rows * n
    sets = loss_rate.shape[0]
    quarter = sets // inner
    group_paths, group_trades = inner * path_rows, outer * trade_rows

    def swap(x, mask):
        return lax.ppermute(x, "paths", [(d, d ^ mask) for d in range(n)])

    def masks(bits):
        return [
            sum(((m >> j) & 1) << bit for j, bit in enumerate(bits)) for m in range(1 << len(bits))
        ]

    def after(x, *others):
        return lax.optimization_barrier((x, *others))[0]

    def direct(slots, bits):
        sent = [swap(x, mask) for x, mask in zip(slots[:0:-1], masks(bits)[:0:-1])]
        return sent[::-1]

    first_bit = outer_bits[0]
    weights = [proxy_weight, swap(proxy_weight, 1 << first_bit)]
    basis = [path_basis] + direct([path_basis] * inner, inner_bits)
    notionals = [notional, swap(notional, 1 << first_bit)]

    member, thresh, rate = call(
        partial(tables_kernel, masks(outer_bits), inner),
        [((sets, group_trades), BF16), ((1, sets), F32), ((1, sets), F32)],
        me.astype(jnp.int32).reshape(1),
        threshold_levels,
        set_of.reshape(n, 1, trade_rows),
        threshold_index.reshape(inner, 1, quarter),
        loss_rate.reshape(inner, 1, quarter),
        name="tables",
        scalars=2,
    )
    for bit in outer_bits[1:]:
        weights = weights + [
            swap(w if k else after(w, member), 1 << bit) for k, w in enumerate(weights)
        ]
        notionals = notionals + [swap(x, 1 << bit) for x in notionals]
    notionals = [x[None, :] for x in notionals]
    (lead,) = call(lead_kernel, [((REGRESSORS, group_paths), BF16)], *basis, name="lead")
    leads = [lead] + direct([lead] * outer, outer_bits)
    value, *moments = call(
        partial(forward_kernel, inner, outer),
        [((group_paths, group_trades), BF16)] + [((REGRESSORS, quarter), F32)] * inner,
        *basis, *weights, *notionals, lead, member,
        name="forward",
    )
    moment = sum(direct(moments, inner_bits), moments[0])
    for bit in outer_bits[:0:-1]:
        moment = moment + swap(moment, 1 << bit)
    moments = [moment, swap(moment, 1 << first_bit)]
    (inverse,) = call(
        partial(inverse_kernel, RIDGE_SCALE * paths_all),
        [((REGRESSORS, REGRESSORS), F32)],
        *leads,
        name="inverse",
    )
    design_all, design_rows = call(
        design_kernel,
        [((REGRESSORS, paths_all), BF16), ((paths_all, LANES), BF16)],
        *leads,
        name="design",
    )
    (solved,) = call(
        partial(solve_kernel, len(moments)),
        [((2 * REGRESSORS, quarter), F32)],
        inverse, design_all, design_rows, thresh, rate, *moments,
        name="solve",
        scratch=[pltpu.VMEM((LANES, quarter), BF16), pltpu.VMEM((REGRESSORS, quarter), F32)],
    )
    solved = [solved] + direct([solved] * inner, inner_bits)
    (slope,) = call(
        partial(slope_kernel, inner, outer),
        [((group_paths, group_trades), F32)],
        *basis, *weights, *notionals,
        name="slope",
    )
    parts = call(
        partial(backward_kernel, 1.0 / math.sqrt(paths_all), inner, outer),
        [((trade_rows, features), BF16)] * outer + [((path_rows, features), BF16)] * inner,
        member, design_rows, slope, value, *solved, *basis, *weights,
        name="backward",
        scratch=[pltpu.VMEM((group_paths, group_trades), BF16)],
    )
    terms = [[part] for part in parts[:outer]]
    for bit in reversed(outer_bits):
        count = len(terms) // 2
        arrived = None
        for k in reversed(range(count)):
            gone = terms[count + k]
            gone = gone[0] if len(gone) == 1 else sum(g.astype(F32) for g in gone).astype(BF16)
            if arrived is not None:
                gone = after(gone, arrived)
            arrived = swap(gone, 1 << bit)
            terms[k].append(arrived)
            if bit == outer_bits[-1] and k == count - 1:
                basis_parts = list(parts[outer:])
                basis_parts[1] = after(basis_parts[1], arrived)
        terms = terms[:count]
    weight_terms = terms[0]
    basis_terms = [basis_parts[0]] + direct(basis_parts, inner_bits)
    loss, own_adjoint = call(
        loss_kernel,
        [((8, LANES), F32), ((path_rows, LANES), F32)],
        design_rows, thresh, rate, *solved,
        name="loss",
        scratch=[pltpu.VMEM((LANES, sets), BF16), pltpu.VMEM((8, sets), F32)],
    )
    basis_adjoint, weight_adjoint = call(
        partial(sum_kernel, len(basis_terms)),
        [((path_rows, features), F32), ((trade_rows, features), F32)],
        own_adjoint, *basis_terms, *weight_terms,
        name="sums",
    )
    return (loss[0, :1], basis_adjoint, weight_adjoint)


def solution(mesh):
    placed = (
        P(("groups", "paths"), None),
        P(("groups", "paths"), None),
        P(("groups", "paths")),
        P("groups"),
        P("groups"),
        P("groups"),
        P("groups"),
    )
    return jax.shard_map(
        shards,
        mesh=mesh,
        in_specs=placed,
        out_specs=(P("groups"), P(("groups", "paths"), None), P(("groups", "paths"), None)),
        check_vma=False,
    )
```

```python
import math
from functools import partial

import jax
import jax.numpy as jnp
from jax import lax
from jax.experimental import pallas as pl
from jax.experimental.pallas import tpu as pltpu
from jax.sharding import PartitionSpec as P

REGRESSORS = 32
RIDGE_SCALE = 0.01
PRECISE = lax.Precision.HIGHEST
F32 = jnp.float32
BF16 = jnp.bfloat16
LANES = 128
SUBLANES = 8
CHUNK = 256
VMEM_BYTES = 48 * 1024 * 1024
LOG2_E = math.log2(math.e)
SHARES = 2
CONSTANT = REGRESSORS - 1


def split_bits(size):
    count = size.bit_length() - 1
    half = count // 2
    return list(range(1, half + 1)), list(range(count - 1, half, -1)) + [0]


def dot(a, b, ca=1, cb=0, precision=None):
    return lax.dot_general(
        a, b, (((ca,), (cb,)), ((), ())), precision=precision, preferred_element_type=F32
    )


def three(x, axis):
    high = x.astype(BF16)
    rest = x - high.astype(F32)
    middle = rest.astype(BF16)
    low = (rest - middle.astype(F32)).astype(BF16)
    return jnp.concatenate([high, middle, low], axis=axis)


def three_rows(x):
    blank = jnp.zeros((LANES - 3 * REGRESSORS, x.shape[1]), BF16)
    return jnp.concatenate([three(x, 0), blank], axis=0)


def lanes(shape):
    return lax.broadcasted_iota(jnp.int32, shape, len(shape) - 1)


def rows(shape):
    return lax.broadcasted_iota(jnp.int32, shape, len(shape) - 2)


def softplus(x):
    return jnp.maximum(x, 0.0) + jnp.log1p(jnp.exp(-jnp.abs(x)))


def sigmoid(x):
    small = jnp.exp(-jnp.abs(x))
    return jnp.where(x >= 0.0, 1.0, small) / (1.0 + small)


def each_chunk(size, step):
    count = size // CHUNK

    def body(i, carry):
        step(pl.ds(pl.multiple_of(i * CHUNK, CHUNK), CHUNK))
        return carry

    lax.fori_loop(0, count, body, 0, unroll=count <= 8)


def invert(matrix):
    size = matrix.shape[0]
    work = jnp.concatenate([matrix, jnp.eye(size, dtype=F32)], axis=1)
    shape = (SUBLANES, 2 * size)
    blocks = [work[i : i + SUBLANES] for i in range(0, size, SUBLANES)]
    row = rows(shape)

    def one_row(block, k):
        return jnp.broadcast_to(block[k : k + 1], shape)

    for k in range(0, size, 2):
        left = [jnp.broadcast_to(block[:, k : k + 1], shape) for block in blocks]
        right = [jnp.broadcast_to(block[:, k + 1 : k + 2], shape) for block in blocks]
        at, here = k // SUBLANES, k % SUBLANES
        a, b = one_row(left[at], here), one_row(right[at], here)
        c, d = one_row(left[at], here + 1), one_row(right[at], here + 1)
        upper, lower = one_row(blocks[at], here), one_row(blocks[at], here + 1)
        scale = 1.0 / (a * d - b * c)
        upper, lower = (d * upper - b * lower) * scale, (a * lower - c * upper) * scale
        blocks = [w - x * upper - y * lower for w, x, y in zip(blocks, left, right)]
        kept = jnp.where(row == here + 1, lower, blocks[at])
        blocks[at] = jnp.where(row == here, upper, kept)
    return jnp.concatenate(blocks, axis=0)[:, size:]


def lead_kernel(*refs):
    x_refs, lead_ref = refs[:-1], refs[-1]
    start = 0
    for x in x_refs:
        turned = x[:, :LANES].astype(F32).T[:REGRESSORS]
        turned = jnp.where(rows(turned.shape) == CONSTANT, 1.0, turned)
        lead_ref[:, start : start + x.shape[0]] = turned.astype(BF16)
        start += x.shape[0]


def tables_kernel(
    trade_masks, me_ref, level_ref, set_ref, index_ref, rate_ref, x_ref, w_ref,
    member_ref, thresh_out_ref, rate_out_ref, x_out_ref, w_out_ref,
):
    x_out_ref[...] = x_ref[...]
    w_out_ref[...] = w_ref[...]
    me = me_ref[0]
    shares = index_ref.shape[0]
    place = me & (shares - 1)
    size = member_ref.shape[0] // shares
    trades = set_ref.shape[-1]
    for m in range(shares):
        here = slice(m * size, (m + 1) * size)
        label = (place ^ m) * size + rows((size, 1))
        for j, mask in enumerate(trade_masks):
            member_ref[here, j * trades : (j + 1) * trades] = jnp.where(
                set_ref[me ^ mask] == label, 1.0, 0.0
            ).astype(BF16)
        index = index_ref[place ^ m]
        thresh = jnp.zeros(index.shape, F32)
        for k in range(level_ref.shape[0]):
            thresh = jnp.where(index == k, level_ref[k], thresh)
        thresh_out_ref[:, here] = thresh
        rate_out_ref[:, here] = rate_ref[place ^ m]


def design_kernel(*refs):
    lead_refs, (design_ref, rows_ref) = refs[:-2], refs[-2:]
    size = lead_refs[0].shape[1]
    for d, lead_ref in enumerate(lead_refs):
        here = slice(d * size, (d + 1) * size)
        design_ref[:, here] = lead_ref[...]
        turned = lead_ref[...].astype(F32).T
        blank = jnp.zeros((size, LANES - 3 * REGRESSORS), F32)
        rows_ref[here] = jnp.concatenate([turned] * 3 + [blank], axis=1).astype(BF16)


def inverse_kernel(ridge, *refs):
    square = (REGRESSORS, REGRESSORS)
    gram = jnp.where(rows(square) == lanes(square), ridge, 0.0)
    for lead_ref in refs[:-1]:
        gram = gram + dot(lead_ref[...], lead_ref[...], 1, 1)
    refs[-1][...] = invert(gram)


def joined_weights(refs):
    return jnp.concatenate([ref[...] for ref in refs], axis=0)


def joined_notionals(refs):
    return jnp.concatenate([ref[...].astype(F32) for ref in refs], axis=1)


def forward_kernel(paths, trades, *refs):
    x_refs, refs = refs[:paths], refs[paths:]
    weights, notional = joined_weights(refs[:trades]), joined_notionals(refs[trades : 2 * trades])
    lead_ref, member_ref, value_ref, *moment_refs = refs[2 * trades :]
    start = 0
    for x in x_refs:
        pre_act = dot(x[...], weights, 1, 1)
        value_ref[start : start + x.shape[0]] = (notional * softplus(pre_act)).astype(BF16)
        start += x.shape[0]
    trade_moment = dot(lead_ref[...], value_ref[...])
    parts = dot(three(trade_moment, 0), member_ref[...], 1, 1)
    moment = parts[:REGRESSORS] + parts[REGRESSORS : 2 * REGRESSORS] + parts[2 * REGRESSORS :]
    size = moment.shape[1] // len(moment_refs)
    for m, moment_ref in enumerate(moment_refs):
        moment_ref[...] = moment[:, m * size : (m + 1) * size]


def slope_kernel(paths, trades, *refs):
    x_refs, refs, slope_ref = refs[:paths], refs[paths:], refs[-1]
    weights, notional = joined_weights(refs[:trades]), joined_notionals(refs[trades : 2 * trades])
    start = 0
    for x in x_refs:
        slope_ref[start : start + x.shape[0]] = notional * sigmoid(dot(x[...], weights, 1, 1))
        start += x.shape[0]


def solve_kernel(
    terms, inverse_ref, design_ref, rows_ref, thresh_ref, rate_ref, *refs
):
    solved_ref, turn_ref, total_ref = refs[terms:]
    moment = refs[0][...]
    for ref in refs[1:terms]:
        moment = moment + ref[...]
    size = moment.shape[1]
    inverse = inverse_ref[...]
    coeffs = dot(inverse, moment, precision=PRECISE)
    solved_ref[REGRESSORS:] = coeffs
    is_constant = rows(coeffs.shape) == CONSTANT
    shifted = coeffs - jnp.where(is_constant, thresh_ref[:, :size], 0.0)
    turn_ref[...] = three_rows(-LOG2_E * shifted)
    total_ref[...] = jnp.zeros(total_ref.shape, F32)

    def seeds(here):
        power = jnp.exp2(jnp.minimum(dot(rows_ref[here], turn_ref[...]), 126.0))
        seed = (1.0 / (1.0 + power)).astype(BF16)
        total_ref[...] += dot(design_ref[:, here], seed)

    each_chunk(rows_ref.shape[0], seeds)
    solved_ref[:REGRESSORS] = dot(inverse, total_ref[...] * rate_ref[:, :size], precision=PRECISE)


def joined(refs, part):
    here = slice(part * REGRESSORS, (part + 1) * REGRESSORS)
    return jnp.concatenate([ref[here] for ref in refs], axis=1)


def backward_kernel(scale, shares, paths, trades, member_ref, rows_ref, slope_ref, value_ref, *refs):
    solved_refs, refs = refs[:shares], refs[shares:]
    x_refs, refs = refs[:paths], refs[paths:]
    w_refs, refs = refs[:trades], refs[trades:]
    weight_refs, basis_refs, slopes_ref = refs[:trades], refs[trades:-1], refs[-1]
    traded = dot(three_rows(joined(solved_refs, 0)), member_ref[...]).astype(BF16)
    group = slopes_ref.shape[0]
    spread = dot(rows_ref[:group], traded).astype(BF16).astype(F32)
    slopes_ref[...] = (slope_ref[...] * spread).astype(BF16)
    basis = jnp.concatenate([x[...] for x in x_refs], axis=0)
    weight = (dot(slopes_ref[...], basis, 0, 0) * scale).astype(BF16)
    start = 0
    for part in weight_refs:
        part[...] = weight[start : start + part.shape[0]]
        start += part.shape[0]
    weights = joined_weights(w_refs)
    start = 0
    for part in basis_refs:
        here = slice(start, start + part.shape[0])
        total = dot(slopes_ref[here], weights)
        wide = dot(value_ref[here], traded, 1, 1)
        design = wide
        for k in range(1, 3):
            design = design + pltpu.roll(wide, LANES - k * REGRESSORS, 1)
        design = jnp.where(lanes(design.shape) < CONSTANT, design, 0.0)
        part[:, :LANES] = (total[:, :LANES] + design).astype(BF16)
        part[:, LANES:] = total[:, LANES:].astype(BF16)
        start += part.shape[0]


def loss_kernel(rows_ref, thresh_ref, rate_ref, *refs):
    solved_refs, (loss_ref, own_ref, split_ref, total_ref) = refs[:-4], refs[-4:]
    adjoint = joined(solved_refs, 0)
    coeffs = joined(solved_refs, 1)
    thresh = thresh_ref[...]
    rate = rate_ref[...]
    split_ref[...] = three_rows(coeffs)
    total_ref[...] = jnp.zeros(total_ref.shape, F32)

    def losses(here):
        loss = softplus(dot(rows_ref[here], split_ref[...]) - thresh)
        total_ref[...] += jnp.sum(loss.reshape(-1, *total_ref.shape), axis=0)

    each_chunk(rows_ref.shape[0], losses)
    summed = jnp.sum(jnp.sum(total_ref[...] * rate, axis=0, keepdims=True), axis=1, keepdims=True)
    loss_ref[...] = jnp.broadcast_to(
        summed / (rows_ref.shape[0] * coeffs.shape[1]), loss_ref.shape
    )
    own = rows_ref[: own_ref.shape[0]]
    fitted = dot(own, split_ref[...])
    seed = rate * sigmoid(fitted - thresh)
    rest = seed - dot(own, three_rows(adjoint))
    design = dot(rest, coeffs, 1, 1, PRECISE) - dot(fitted, adjoint, 1, 1, PRECISE)
    blank = jnp.zeros((design.shape[0], LANES - REGRESSORS), F32)
    design = jnp.concatenate([design, blank], axis=1)
    own_ref[...] = jnp.where(lanes(design.shape) < CONSTANT, design, 0.0)


def total(refs):
    out = refs[0][...].astype(F32)
    for ref in refs[1:]:
        out = out + ref[...].astype(F32)
    return out


def sum_kernel(first, own_ref, *refs):
    basis_ref, weight_ref = refs[-2:]
    basis = total(refs[:first])
    basis_ref[:, :LANES] = basis[:, :LANES] + own_ref[...]
    basis_ref[:, LANES:] = basis[:, LANES:]
    weight_ref[...] = total(refs[first:-2])


def call(kernel, outs, *args, name, flops=0, scratch=(), scalars=0):
    size = sum(a.size * a.dtype.itemsize for a in args) + sum(
        math.prod(s) * jnp.dtype(d).itemsize for s, d in outs
    )
    return pl.pallas_call(
        kernel,
        out_shape=[jax.ShapeDtypeStruct(s, d) for s, d in outs],
        in_specs=[pl.BlockSpec(memory_space=pltpu.SMEM)] * scalars
        + [pl.BlockSpec(memory_space=pltpu.VMEM)] * (len(args) - scalars),
        out_specs=[pl.BlockSpec(memory_space=pltpu.VMEM)] * len(outs),
        scratch_shapes=scratch,
        compiler_params=pltpu.CompilerParams(vmem_limit_bytes=VMEM_BYTES),
        cost_estimate=pl.CostEstimate(flops=int(flops), bytes_accessed=int(size), transcendentals=0),
        name=name,
    )(*args)


def shards(
    path_basis, proxy_weight, notional, set_of, threshold_index, threshold_levels, loss_rate
):
    n = lax.axis_size("paths")
    me = lax.axis_index("paths")
    inner_bits, outer_bits = split_bits(n)
    inner, outer = 1 << len(inner_bits), 1 << len(outer_bits)
    path_rows, features = path_basis.shape
    trade_rows = proxy_weight.shape[0]
    paths_all = path_rows * n
    sets = loss_rate.shape[0]
    share = sets // SHARES
    group_paths, group_trades = inner * path_rows, outer * trade_rows

    def swap(x, mask):
        return lax.ppermute(x, "paths", [(d, d ^ mask) for d in range(n)])

    def masks(bits):
        return [
            sum(((m >> j) & 1) << bit for j, bit in enumerate(bits)) for m in range(1 << len(bits))
        ]

    def after(x, *others):
        return lax.optimization_barrier((x, *others))[0]

    def direct(slots, bits):
        return [swap(x, mask) for x, mask in zip(slots[1:], masks(bits)[1:])]

    first_bit = outer_bits[0]
    weights = [proxy_weight, swap(proxy_weight, 1 << first_bit)]
    basis = [path_basis] + direct([path_basis] * inner, inner_bits)
    notionals = [notional, swap(notional, 1 << first_bit)]

    member, thresh, rate, basis[0], own_weight = call(
        partial(tables_kernel, masks(outer_bits)),
        [
            ((sets, group_trades), BF16),
            ((1, sets), F32),
            ((1, sets), F32),
            (path_basis.shape, BF16),
            (proxy_weight.shape, BF16),
        ],
        me.astype(jnp.int32).reshape(1),
        threshold_levels,
        set_of.reshape(n, 1, trade_rows),
        threshold_index.reshape(SHARES, 1, share),
        loss_rate.reshape(SHARES, 1, share),
        path_basis,
        proxy_weight,
        name="tables",
        scalars=2,
    )
    for bit in outer_bits[1:]:
        weights = weights + [
            swap(w if k else after(w, member), 1 << bit) for k, w in enumerate(weights)
        ]
        notionals = notionals + [swap(x, 1 << bit) for x in notionals]
    weights[0] = own_weight
    notionals = [x[None, :] for x in notionals]
    (lead,) = call(lead_kernel, [((REGRESSORS, group_paths), BF16)], *basis, name="lead")
    leads = [lead] + direct([lead] * outer, outer_bits)
    value, *moments = call(
        partial(forward_kernel, inner, outer),
        [((group_paths, group_trades), BF16)] + [((REGRESSORS, share), F32)] * SHARES,
        *basis, *weights, *notionals, lead, member,
        name="forward",
    )
    moment = moments[0] + swap(moments[1], SHARES - 1)
    for bit in inner_bits + outer_bits[-2:0:-1]:
        moment = moment + swap(moment, 1 << bit)
    moments = [moment, swap(moment, 1 << first_bit)]
    (inverse,) = call(
        partial(inverse_kernel, RIDGE_SCALE * paths_all),
        [((REGRESSORS, REGRESSORS), F32)],
        *leads,
        name="inverse",
    )
    design_all, design_rows = call(
        design_kernel,
        [((REGRESSORS, paths_all), BF16), ((paths_all, LANES), BF16)],
        *leads,
        name="design",
    )
    (solved,) = call(
        partial(solve_kernel, len(moments)),
        [((2 * REGRESSORS, share), F32)],
        inverse, design_all, design_rows, thresh, rate, *moments,
        name="solve",
        scratch=[pltpu.VMEM((LANES, share), BF16), pltpu.VMEM((REGRESSORS, share), F32)],
    )
    solved = [solved, swap(solved, SHARES - 1)]
    (slope,) = call(
        partial(slope_kernel, inner, outer),
        [((group_paths, group_trades), F32)],
        *basis, *weights, *notionals,
        name="slope",
    )
    parts = call(
        partial(backward_kernel, 1.0 / math.sqrt(paths_all), SHARES, inner, outer),
        [((trade_rows, features), BF16)] * outer + [((path_rows, features), BF16)] * inner,
        member, design_rows, slope, value, *solved, *basis, *weights,
        name="backward",
        scratch=[pltpu.VMEM((group_paths, group_trades), BF16)],
    )
    terms = [[part] for part in parts[:outer]]
    for bit in reversed(outer_bits):
        count = len(terms) // 2
        arrived = None
        for k in reversed(range(count)):
            gone = terms[count + k]
            gone = gone[0] if len(gone) == 1 else sum(g.astype(F32) for g in gone).astype(BF16)
            if arrived is not None:
                gone = after(gone, arrived)
            arrived = swap(gone, 1 << bit)
            terms[k].append(arrived)
            if bit == outer_bits[-1] and k == count - 1:
                basis_parts = list(parts[outer:])
                basis_parts[1] = after(basis_parts[1], arrived)
        terms = terms[:count]
    weight_terms = terms[0]
    basis_terms = [basis_parts[0]] + direct(basis_parts, inner_bits)
    loss, own_adjoint = call(
        loss_kernel,
        [((8, LANES), F32), ((path_rows, LANES), F32)],
        design_rows, thresh, rate, *solved,
        name="loss",
        scratch=[pltpu.VMEM((LANES, sets), BF16), pltpu.VMEM((8, sets), F32)],
    )
    basis_adjoint, weight_adjoint = call(
        partial(sum_kernel, len(basis_terms)),
        [((path_rows, features), F32), ((trade_rows, features), F32)],
        own_adjoint, *basis_terms, *weight_terms,
        name="sums",
    )
    return (loss[0, :1], basis_adjoint, weight_adjoint)


def solution(mesh):
    placed = (
        P(("groups", "paths"), None),
        P(("groups", "paths"), None),
        P(("groups", "paths")),
        P("groups"),
        P("groups"),
        P("groups"),
        P("groups"),
    )
    return jax.shard_map(
        shards,
        mesh=mesh,
        in_specs=placed,
        out_specs=(P("groups"), P(("groups", "paths"), None), P(("groups", "paths"), None)),
        check_vma=False,
    )
```

```python
import math
from functools import partial

import jax
import jax.numpy as jnp
from jax import lax
from jax.experimental import pallas as pl
from jax.experimental.pallas import tpu as pltpu
from jax.sharding import PartitionSpec as P

REGRESSORS = 32
RIDGE_SCALE = 0.01
PRECISE = lax.Precision.HIGHEST
F32 = jnp.float32
BF16 = jnp.bfloat16
LANES = 128
SUBLANES = 8
CHUNK = 256
CHUNKS = 2
VMEM_BYTES = 48 * 1024 * 1024
LOG2_E = math.log2(math.e)
SHARES = 2
CONSTANT = REGRESSORS - 1


def split_bits(size):
    count = size.bit_length() - 1
    half = count // 2
    return list(range(1, half + 1)), list(range(count - 1, half, -1)) + [0]


def dot(a, b, ca=1, cb=0, precision=None):
    return lax.dot_general(
        a, b, (((ca,), (cb,)), ((), ())), precision=precision, preferred_element_type=F32
    )


def three(x, axis):
    high = x.astype(BF16)
    rest = x - high.astype(F32)
    middle = rest.astype(BF16)
    low = (rest - middle.astype(F32)).astype(BF16)
    return jnp.concatenate([high, middle, low], axis=axis)


def three_rows(x):
    blank = jnp.zeros((LANES - 3 * REGRESSORS, x.shape[1]), BF16)
    return jnp.concatenate([three(x, 0), blank], axis=0)


def lanes(shape):
    return lax.broadcasted_iota(jnp.int32, shape, len(shape) - 1)


def rows(shape):
    return lax.broadcasted_iota(jnp.int32, shape, len(shape) - 2)


def softplus(x):
    return jnp.maximum(x, 0.0) + jnp.log1p(jnp.exp(-jnp.abs(x)))


def sigmoid(x):
    small = jnp.exp(-jnp.abs(x))
    return jnp.where(x >= 0.0, 1.0, small) / (1.0 + small)


def each_chunk(size, step):
    count = size // CHUNK

    def body(i, carry):
        step(pl.ds(pl.multiple_of(i * CHUNK, CHUNK), CHUNK))
        return carry

    lax.fori_loop(0, count, body, 0, unroll=count <= 8)


def invert(matrix):
    size = matrix.shape[0]
    work = jnp.concatenate([matrix, jnp.eye(size, dtype=F32)], axis=1)
    shape = (SUBLANES, 2 * size)
    blocks = [work[i : i + SUBLANES] for i in range(0, size, SUBLANES)]
    row = rows(shape)

    def one_row(block, k):
        return jnp.broadcast_to(block[k : k + 1], shape)

    for k in range(0, size, 2):
        left = [jnp.broadcast_to(block[:, k : k + 1], shape) for block in blocks]
        right = [jnp.broadcast_to(block[:, k + 1 : k + 2], shape) for block in blocks]
        at, here = k // SUBLANES, k % SUBLANES
        a, b = one_row(left[at], here), one_row(right[at], here)
        c, d = one_row(left[at], here + 1), one_row(right[at], here + 1)
        upper, lower = one_row(blocks[at], here), one_row(blocks[at], here + 1)
        scale = 1.0 / (a * d - b * c)
        upper, lower = (d * upper - b * lower) * scale, (a * lower - c * upper) * scale
        blocks = [w - x * upper - y * lower for w, x, y in zip(blocks, left, right)]
        kept = jnp.where(row == here + 1, lower, blocks[at])
        blocks[at] = jnp.where(row == here, upper, kept)
    return jnp.concatenate(blocks, axis=0)[:, size:]


def lead_kernel(*refs):
    x_refs, lead_ref = refs[:-1], refs[-1]
    start = 0
    for x in x_refs:
        turned = x[:, :LANES].astype(F32).T[:REGRESSORS]
        turned = jnp.where(rows(turned.shape) == CONSTANT, 1.0, turned)
        lead_ref[:, start : start + x.shape[0]] = turned.astype(BF16)
        start += x.shape[0]


def tables_kernel(
    trade_masks, me_ref, level_ref, set_ref, index_ref, rate_ref, x_ref, w_ref,
    member_ref, thresh_out_ref, rate_out_ref, x_out_ref, w_out_ref,
):
    x_out_ref[...] = x_ref[...]
    w_out_ref[...] = w_ref[...]
    me = me_ref[0]
    shares = index_ref.shape[0]
    place = me & (shares - 1)
    size = member_ref.shape[0] // shares
    trades = set_ref.shape[-1]
    for m in range(shares):
        here = slice(m * size, (m + 1) * size)
        label = (place ^ m) * size + rows((size, 1))
        for j, mask in enumerate(trade_masks):
            member_ref[here, j * trades : (j + 1) * trades] = jnp.where(
                set_ref[me ^ mask] == label, 1.0, 0.0
            ).astype(BF16)
        index = index_ref[place ^ m]
        thresh = jnp.zeros(index.shape, F32)
        for k in range(level_ref.shape[0]):
            thresh = jnp.where(index == k, level_ref[k], thresh)
        thresh_out_ref[:, here] = thresh
        rate_out_ref[:, here] = rate_ref[place ^ m]


def design_kernel(small_ref, design_ref, rows_ref):
    size = small_ref.shape[2]
    for d in range(small_ref.shape[0]):
        here = slice(d * size, (d + 1) * size)
        design_ref[:, here] = small_ref[d]
        turned = small_ref[d].astype(F32).T
        blank = jnp.zeros((size, LANES - 3 * REGRESSORS), F32)
        rows_ref[here] = jnp.concatenate([turned] * 3 + [blank], axis=1).astype(BF16)


def inverse_kernel(ridge, small_ref, inverse_ref):
    square = (REGRESSORS, REGRESSORS)
    gram = jnp.where(rows(square) == lanes(square), ridge, 0.0)
    for d in range(small_ref.shape[0]):
        gram = gram + dot(small_ref[d], small_ref[d], 1, 1)
    inverse_ref[...] = invert(gram)


def joined_weights(refs):
    return jnp.concatenate([ref[...] for ref in refs], axis=0)


def joined_notionals(refs):
    return jnp.concatenate([ref[...].astype(F32) for ref in refs], axis=1)


def forward_kernel(paths, trades, *refs):
    x_refs, refs = refs[:paths], refs[paths:]
    weights, notional = joined_weights(refs[:trades]), joined_notionals(refs[trades : 2 * trades])
    lead_ref, member_ref, value_ref, *moment_refs = refs[2 * trades :]
    start = 0
    for x in x_refs:
        pre_act = dot(x[...], weights, 1, 1)
        value_ref[start : start + x.shape[0]] = (notional * softplus(pre_act)).astype(BF16)
        start += x.shape[0]
    trade_moment = dot(lead_ref[...], value_ref[...])
    parts = dot(three(trade_moment, 0), member_ref[...], 1, 1)
    moment = parts[:REGRESSORS] + parts[REGRESSORS : 2 * REGRESSORS] + parts[2 * REGRESSORS :]
    size = moment.shape[1] // len(moment_refs)
    for m, moment_ref in enumerate(moment_refs):
        moment_ref[...] = moment[:, m * size : (m + 1) * size]


def slope_kernel(paths, trades, *refs):
    x_refs, refs, slope_ref = refs[:paths], refs[paths:], refs[-1]
    weights, notional = joined_weights(refs[:trades]), joined_notionals(refs[trades : 2 * trades])
    start = 0
    for x in x_refs:
        slope_ref[start : start + x.shape[0]] = notional * sigmoid(dot(x[...], weights, 1, 1))
        start += x.shape[0]


def solve_kernel(
    terms, inverse_ref, design_ref, rows_ref, thresh_ref, rate_ref, *refs
):
    solved_ref, turn_ref, total_ref = refs[terms:]
    moment = refs[0][...]
    for ref in refs[1:terms]:
        moment = moment + ref[...]
    size = moment.shape[1]
    inverse = inverse_ref[...]
    coeffs = dot(inverse, moment, precision=PRECISE)
    solved_ref[REGRESSORS:] = coeffs
    is_constant = rows(coeffs.shape) == CONSTANT
    shifted = coeffs - jnp.where(is_constant, thresh_ref[:, :size], 0.0)
    turn_ref[...] = three_rows(-LOG2_E * shifted)
    total_ref[...] = jnp.zeros(total_ref.shape, F32)

    def seeds(here):
        power = jnp.exp2(jnp.minimum(dot(rows_ref[here], turn_ref[...]), 126.0))
        seed = (1.0 / (1.0 + power)).astype(BF16)
        total_ref[...] += dot(design_ref[:, here], seed)

    each_chunk(rows_ref.shape[0], seeds)
    solved_ref[:REGRESSORS] = dot(inverse, total_ref[...] * rate_ref[:, :size], precision=PRECISE)


def joined(refs, part):
    here = slice(part * REGRESSORS, (part + 1) * REGRESSORS)
    return jnp.concatenate([ref[here] for ref in refs], axis=1)


def backward_kernel(
    scale, shares, paths, trades, member_ref, rows_ref, slope_ref, value_ref, *refs
):
    solved_refs, refs = refs[:shares], refs[shares:]
    x_refs, refs = refs[:paths], refs[paths:]
    w_refs, refs = refs[:trades], refs[trades:]
    weight_refs, basis_refs, slopes_ref = refs[:trades], refs[trades:-1], refs[-1]
    traded = dot(three_rows(joined(solved_refs, 0)), member_ref[...]).astype(BF16)
    group = slopes_ref.shape[0]
    spread = dot(rows_ref[:group], traded).astype(BF16).astype(F32)
    slopes_ref[...] = (slope_ref[...] * spread).astype(BF16)
    basis = jnp.concatenate([x[...] for x in x_refs], axis=0)
    weight = (dot(slopes_ref[...], basis, 0, 0) * scale).astype(BF16)
    start = 0
    for part in weight_refs:
        part[...] = weight[start : start + part.shape[0]]
        start += part.shape[0]
    weights = joined_weights(w_refs)
    start = 0
    for part in basis_refs:
        here = slice(start, start + part.shape[0])
        total = dot(slopes_ref[here], weights)
        wide = dot(value_ref[here], traded, 1, 1)
        design = wide
        for k in range(1, 3):
            design = design + pltpu.roll(wide, LANES - k * REGRESSORS, 1)
        design = jnp.where(lanes(design.shape) < CONSTANT, design, 0.0)
        part[:, :LANES] = (total[:, :LANES] + design).astype(BF16)
        part[:, LANES:] = total[:, LANES:].astype(BF16)
        start += part.shape[0]


def loss_kernel(rows_ref, thresh_ref, rate_ref, *refs):
    solved_refs, (loss_ref, own_ref, split_ref, total_ref) = refs[:-4], refs[-4:]
    adjoint = joined(solved_refs, 0)
    coeffs = joined(solved_refs, 1)
    thresh = thresh_ref[...]
    rate = rate_ref[...]
    split_ref[...] = three_rows(coeffs)
    total_ref[...] = jnp.zeros(total_ref.shape, F32)

    def losses(here):
        loss = softplus(dot(rows_ref[here], split_ref[...]) - thresh)
        total_ref[...] += jnp.sum(loss.reshape(-1, *total_ref.shape), axis=0)

    each_chunk(rows_ref.shape[0], losses)
    summed = jnp.sum(jnp.sum(total_ref[...] * rate, axis=0, keepdims=True), axis=1, keepdims=True)
    loss_ref[...] = jnp.broadcast_to(
        summed / (rows_ref.shape[0] * coeffs.shape[1]), loss_ref.shape
    )
    own = rows_ref[: own_ref.shape[0]]
    fitted = dot(own, split_ref[...])
    seed = rate * sigmoid(fitted - thresh)
    rest = seed - dot(own, three_rows(adjoint))
    design = dot(rest, coeffs, 1, 1, PRECISE) - dot(fitted, adjoint, 1, 1, PRECISE)
    blank = jnp.zeros((design.shape[0], LANES - REGRESSORS), F32)
    design = jnp.concatenate([design, blank], axis=1)
    own_ref[...] = jnp.where(lanes(design.shape) < CONSTANT, design, 0.0)


def total(refs):
    out = refs[0][...].astype(F32)
    for ref in refs[1:]:
        out = out + ref[...].astype(F32)
    return out


def sum_kernel(whole, pieces, own_ref, *refs):
    basis_ref, weight_ref = refs[-2:]
    chunks, last = refs[whole : whole + pieces * CHUNKS], refs[whole + pieces * CHUNKS : -2]
    basis = total(refs[:whole])
    size = basis.shape[0] // CHUNKS
    for k in range(CHUNKS):
        here = slice(k * size, (k + 1) * size)
        part = basis[here] + total(chunks[k * pieces : (k + 1) * pieces])
        basis_ref[here, :LANES] = part[:, :LANES] + own_ref[here]
        basis_ref[here, LANES:] = part[:, LANES:]
    weight_ref[...] = total(last)


def call(kernel, outs, *args, name, flops=0, scratch=(), scalars=0):
    size = sum(a.size * a.dtype.itemsize for a in args) + sum(
        math.prod(s) * jnp.dtype(d).itemsize for s, d in outs
    )
    return pl.pallas_call(
        kernel,
        out_shape=[jax.ShapeDtypeStruct(s, d) for s, d in outs],
        in_specs=[pl.BlockSpec(memory_space=pltpu.SMEM)] * scalars
        + [pl.BlockSpec(memory_space=pltpu.VMEM)] * (len(args) - scalars),
        out_specs=[pl.BlockSpec(memory_space=pltpu.VMEM)] * len(outs),
        scratch_shapes=scratch,
        compiler_params=pltpu.CompilerParams(vmem_limit_bytes=VMEM_BYTES),
        cost_estimate=pl.CostEstimate(flops=int(flops), bytes_accessed=int(size), transcendentals=0),
        name=name,
    )(*args)


def shards(
    path_basis, proxy_weight, notional, set_of, threshold_index, threshold_levels, loss_rate
):
    n = lax.axis_size("paths")
    me = lax.axis_index("paths")
    inner_bits, outer_bits = split_bits(n)
    inner, outer = 1 << len(inner_bits), 1 << len(outer_bits)
    path_rows, features = path_basis.shape
    trade_rows = proxy_weight.shape[0]
    paths_all = path_rows * n
    sets = loss_rate.shape[0]
    share = sets // SHARES
    group_paths, group_trades = inner * path_rows, outer * trade_rows

    def swap(x, mask):
        return lax.ppermute(x, "paths", [(d, d ^ mask) for d in range(n)])

    def masks(bits):
        return [
            sum(((m >> j) & 1) << bit for j, bit in enumerate(bits)) for m in range(1 << len(bits))
        ]

    def after(x, *others):
        return lax.optimization_barrier((x, *others))[0]

    def direct(slots, bits):
        return [swap(x, mask) for x, mask in zip(slots[1:], masks(bits)[1:])]

    first_bit = outer_bits[0]
    weights = [proxy_weight, swap(proxy_weight, 1 << first_bit)]
    basis = [path_basis] + direct([path_basis] * inner, inner_bits)
    notionals = [notional, swap(notional, 1 << first_bit)]

    member, thresh, rate, basis[0], own_weight = call(
        partial(tables_kernel, masks(outer_bits)),
        [
            ((sets, group_trades), BF16),
            ((1, sets), F32),
            ((1, sets), F32),
            (path_basis.shape, BF16),
            (proxy_weight.shape, BF16),
        ],
        me.astype(jnp.int32).reshape(1),
        threshold_levels,
        set_of.reshape(n, 1, trade_rows),
        threshold_index.reshape(SHARES, 1, share),
        loss_rate.reshape(SHARES, 1, share),
        path_basis,
        proxy_weight,
        name="tables",
        scalars=2,
    )
    for bit in outer_bits[1:]:
        weights = weights + [
            swap(w if k else after(w, member), 1 << bit) for k, w in enumerate(weights)
        ]
        notionals = notionals + [swap(x, 1 << bit) for x in notionals]
    weights[0] = own_weight
    notionals = [x[None, :] for x in notionals]
    (lead,) = call(lead_kernel, [((REGRESSORS, group_paths), BF16)], *basis, name="lead")
    value, *moments = call(
        partial(forward_kernel, inner, outer),
        [((group_paths, group_trades), BF16)] + [((REGRESSORS, share), F32)] * SHARES,
        *basis, *weights, *notionals, lead, member,
        name="forward",
    )
    small = lead[None]
    for bit in outer_bits:
        small = jnp.concatenate([small, swap(small, 1 << bit)], axis=0)
    moment = moments[0] + swap(moments[1], SHARES - 1)
    for bit in inner_bits + outer_bits[-2:0:-1]:
        moment = moment + swap(moment, 1 << bit)
    moments = [moment, swap(moment, 1 << first_bit)]
    (inverse,) = call(
        partial(inverse_kernel, RIDGE_SCALE * paths_all),
        [((REGRESSORS, REGRESSORS), F32)],
        small,
        name="inverse",
    )
    design_all, design_rows = call(
        design_kernel,
        [((REGRESSORS, paths_all), BF16), ((paths_all, LANES), BF16)],
        small,
        name="design",
    )
    (solved,) = call(
        partial(solve_kernel, len(moments)),
        [((2 * REGRESSORS, share), F32)],
        inverse, design_all, design_rows, thresh, rate, *moments,
        name="solve",
        scratch=[pltpu.VMEM((LANES, share), BF16), pltpu.VMEM((REGRESSORS, share), F32)],
    )
    solved = [solved, swap(solved, SHARES - 1)]
    (slope,) = call(
        partial(slope_kernel, inner, outer),
        [((group_paths, group_trades), F32)],
        *basis, *weights, *notionals,
        name="slope",
    )
    heights = [path_rows] * 2 + [path_rows // CHUNKS] * (CHUNKS * (inner - 2))
    parts = call(
        partial(backward_kernel, 1.0 / math.sqrt(paths_all), SHARES, inner, outer),
        [((trade_rows, features), BF16)] * outer + [((h, features), BF16) for h in heights],
        member, design_rows, slope, value, *solved, *basis, *weights,
        name="backward",
        scratch=[pltpu.VMEM((group_paths, group_trades), BF16)],
    )

    def rounded_sum(terms):
        return terms[0] if len(terms) == 1 else sum(t.astype(F32) for t in terms).astype(BF16)

    terms = [[part] for part in parts[:outer]]
    core_step = None
    for bit in reversed(outer_bits):
        count = len(terms) // 2
        arrived = None
        for k in reversed(range(count)):
            gone = rounded_sum(terms[count + k])
            if arrived is not None:
                gone = after(gone, arrived)
            arrived = swap(gone, 1 << bit)
            terms[k].append(arrived)
            core_step = arrived if core_step is None else core_step
        terms = terms[:count]
    weight_terms = terms[0]
    own, first, *rest = parts[outer:]
    pieces = [[[piece] for piece in rest[m * CHUNKS : (m + 1) * CHUNKS]] for m in range(inner - 2)]
    pieces = [None, None] + pieces
    whole_terms, piece_terms = [own], [[] for _ in range(CHUNKS)]
    for j, bit in enumerate(inner_bits):
        for m in reversed(range(2, inner)):
            if (m >> j) & 1 and m % (1 << j) == 0:
                for k in range(CHUNKS):
                    gone = rounded_sum(pieces[m][k])
                    if j == 0:
                        gone = after(gone, core_step)
                    arrived = swap(gone, 1 << bit)
                    target = piece_terms[k] if m == 1 << j else pieces[m - (1 << j)][k]
                    target.append(arrived)
        if j == 0:
            whole_terms.append(swap(after(first, core_step), 1 << bit))
    piece_terms = [t for terms in piece_terms for t in terms]
    loss, own_adjoint = call(
        loss_kernel,
        [((8, LANES), F32), ((path_rows, LANES), F32)],
        design_rows, thresh, rate, *solved,
        name="loss",
        scratch=[pltpu.VMEM((LANES, sets), BF16), pltpu.VMEM((8, sets), F32)],
    )
    basis_adjoint, weight_adjoint = call(
        partial(sum_kernel, len(whole_terms), len(piece_terms) // CHUNKS),
        [((path_rows, features), F32), ((trade_rows, features), F32)],
        own_adjoint, *whole_terms, *piece_terms, *weight_terms,
        name="sums",
    )
    return (loss[0, :1], basis_adjoint, weight_adjoint)


def solution(mesh):
    placed = (
        P(("groups", "paths"), None),
        P(("groups", "paths"), None),
        P(("groups", "paths")),
        P("groups"),
        P("groups"),
        P("groups"),
        P("groups"),
    )
    return jax.shard_map(
        shards,
        mesh=mesh,
        in_specs=placed,
        out_specs=(P("groups"), P(("groups", "paths"), None), P(("groups", "paths"), None)),
        check_vma=False,
    )
```

```python
import math
from functools import partial

import jax
import jax.numpy as jnp
from jax import lax
from jax.experimental import pallas as pl
from jax.experimental.pallas import tpu as pltpu
from jax.sharding import PartitionSpec as P

REGRESSORS = 32
RIDGE_SCALE = 0.01
PRECISE = lax.Precision.HIGHEST
F32 = jnp.float32
BF16 = jnp.bfloat16
LANES = 128
SUBLANES = 8
CHUNK = 256
VMEM_BYTES = 48 * 1024 * 1024
LOG2_E = math.log2(math.e)
SHARES = 2
CONSTANT = REGRESSORS - 1


def split_bits(size):
    count = size.bit_length() - 1
    half = count // 2
    return list(range(1, half + 1)), list(range(count - 1, half, -1)) + [0]


def dot(a, b, ca=1, cb=0, precision=None):
    return lax.dot_general(
        a, b, (((ca,), (cb,)), ((), ())), precision=precision, preferred_element_type=F32
    )


def three(x, axis):
    high = x.astype(BF16)
    rest = x - high.astype(F32)
    middle = rest.astype(BF16)
    low = (rest - middle.astype(F32)).astype(BF16)
    return jnp.concatenate([high, middle, low], axis=axis)


def three_rows(x):
    blank = jnp.zeros((LANES - 3 * REGRESSORS, x.shape[1]), BF16)
    return jnp.concatenate([three(x, 0), blank], axis=0)


def lanes(shape):
    return lax.broadcasted_iota(jnp.int32, shape, len(shape) - 1)


def rows(shape):
    return lax.broadcasted_iota(jnp.int32, shape, len(shape) - 2)


def softplus(x):
    return jnp.maximum(x, 0.0) + jnp.log1p(jnp.exp(-jnp.abs(x)))


def sigmoid(x):
    small = jnp.exp(-jnp.abs(x))
    return jnp.where(x >= 0.0, 1.0, small) / (1.0 + small)


def each_chunk(size, step):
    count = size // CHUNK

    def body(i, carry):
        step(pl.ds(pl.multiple_of(i * CHUNK, CHUNK), CHUNK))
        return carry

    lax.fori_loop(0, count, body, 0, unroll=count <= 8)


def invert(matrix):
    size = matrix.shape[0]
    work = jnp.concatenate([matrix, jnp.eye(size, dtype=F32)], axis=1)
    shape = (SUBLANES, 2 * size)
    blocks = [work[i : i + SUBLANES] for i in range(0, size, SUBLANES)]
    row = rows(shape)

    def one_row(block, k):
        return jnp.broadcast_to(block[k : k + 1], shape)

    for k in range(0, size, 2):
        left = [jnp.broadcast_to(block[:, k : k + 1], shape) for block in blocks]
        right = [jnp.broadcast_to(block[:, k + 1 : k + 2], shape) for block in blocks]
        at, here = k // SUBLANES, k % SUBLANES
        a, b = one_row(left[at], here), one_row(right[at], here)
        c, d = one_row(left[at], here + 1), one_row(right[at], here + 1)
        upper, lower = one_row(blocks[at], here), one_row(blocks[at], here + 1)
        scale = 1.0 / (a * d - b * c)
        upper, lower = (d * upper - b * lower) * scale, (a * lower - c * upper) * scale
        blocks = [w - x * upper - y * lower for w, x, y in zip(blocks, left, right)]
        kept = jnp.where(row == here + 1, lower, blocks[at])
        blocks[at] = jnp.where(row == here, upper, kept)
    return jnp.concatenate(blocks, axis=0)[:, size:]


def lead_kernel(*refs):
    x_refs, lead_ref = refs[:-1], refs[-1]
    start = 0
    for x in x_refs:
        turned = x[:, :LANES].astype(F32).T[:REGRESSORS]
        turned = jnp.where(rows(turned.shape) == CONSTANT, 1.0, turned)
        lead_ref[:, start : start + x.shape[0]] = turned.astype(BF16)
        start += x.shape[0]


def tables_kernel(
    trade_masks, me_ref, level_ref, set_ref, index_ref, rate_ref, x_ref, w_ref,
    member_ref, thresh_out_ref, rate_out_ref, x_out_ref, w_out_ref,
):
    x_out_ref[...] = x_ref[...]
    w_out_ref[...] = w_ref[...]
    me = me_ref[0]
    shares = index_ref.shape[0]
    place = me & (shares - 1)
    size = member_ref.shape[0] // shares
    trades = set_ref.shape[-1]
    for m in range(shares):
        here = slice(m * size, (m + 1) * size)
        label = (place ^ m) * size + rows((size, 1))
        for j, mask in enumerate(trade_masks):
            member_ref[here, j * trades : (j + 1) * trades] = jnp.where(
                set_ref[me ^ mask] == label, 1.0, 0.0
            ).astype(BF16)
        index = index_ref[place ^ m]
        thresh = jnp.zeros(index.shape, F32)
        for k in range(level_ref.shape[0]):
            thresh = jnp.where(index == k, level_ref[k], thresh)
        thresh_out_ref[:, here] = thresh
        rate_out_ref[:, here] = rate_ref[place ^ m]


def design_kernel(small_ref, design_ref, rows_ref):
    size = small_ref.shape[2]
    for d in range(small_ref.shape[0]):
        here = slice(d * size, (d + 1) * size)
        design_ref[:, here] = small_ref[d]
        turned = small_ref[d].astype(F32).T
        blank = jnp.zeros((size, LANES - 3 * REGRESSORS), F32)
        rows_ref[here] = jnp.concatenate([turned] * 3 + [blank], axis=1).astype(BF16)


def inverse_kernel(ridge, small_ref, inverse_ref):
    square = (REGRESSORS, REGRESSORS)
    gram = jnp.where(rows(square) == lanes(square), ridge, 0.0)
    for d in range(small_ref.shape[0]):
        gram = gram + dot(small_ref[d], small_ref[d], 1, 1)
    inverse_ref[...] = invert(gram)


def joined_weights(refs):
    return jnp.concatenate([ref[...] for ref in refs], axis=0)


def joined_notionals(refs):
    return jnp.concatenate([ref[...].astype(F32) for ref in refs], axis=1)


def forward_kernel(paths, trades, *refs):
    x_refs, refs = refs[:paths], refs[paths:]
    weights, notional = joined_weights(refs[:trades]), joined_notionals(refs[trades : 2 * trades])
    lead_ref, member_ref, value_ref, *moment_refs = refs[2 * trades :]
    start = 0
    for x in x_refs:
        pre_act = dot(x[...], weights, 1, 1)
        value_ref[start : start + x.shape[0]] = (notional * softplus(pre_act)).astype(BF16)
        start += x.shape[0]
    trade_moment = dot(lead_ref[...], value_ref[...])
    parts = dot(three(trade_moment, 0), member_ref[...], 1, 1)
    moment = parts[:REGRESSORS] + parts[REGRESSORS : 2 * REGRESSORS] + parts[2 * REGRESSORS :]
    size = moment.shape[1] // len(moment_refs)
    for m, moment_ref in enumerate(moment_refs):
        moment_ref[...] = moment[:, m * size : (m + 1) * size]


def slope_kernel(paths, trades, *refs):
    x_refs, refs, slope_ref = refs[:paths], refs[paths:], refs[-1]
    weights, notional = joined_weights(refs[:trades]), joined_notionals(refs[trades : 2 * trades])
    start = 0
    for x in x_refs:
        slope_ref[start : start + x.shape[0]] = notional * sigmoid(dot(x[...], weights, 1, 1))
        start += x.shape[0]


def solve_kernel(
    terms, inverse_ref, design_ref, rows_ref, thresh_ref, rate_ref, *refs
):
    solved_ref, turn_ref, total_ref = refs[terms:]
    moment = refs[0][...]
    for ref in refs[1:terms]:
        moment = moment + ref[...]
    size = moment.shape[1]
    inverse = inverse_ref[...]
    coeffs = dot(inverse, moment, precision=PRECISE)
    solved_ref[REGRESSORS:] = coeffs
    is_constant = rows(coeffs.shape) == CONSTANT
    shifted = coeffs - jnp.where(is_constant, thresh_ref[:, :size], 0.0)
    turn_ref[...] = three_rows(-LOG2_E * shifted)
    total_ref[...] = jnp.zeros(total_ref.shape, F32)

    def seeds(here):
        power = jnp.exp2(jnp.minimum(dot(rows_ref[here], turn_ref[...]), 126.0))
        seed = (1.0 / (1.0 + power)).astype(BF16)
        total_ref[...] += dot(design_ref[:, here], seed)

    each_chunk(rows_ref.shape[0], seeds)
    solved_ref[:REGRESSORS] = dot(inverse, total_ref[...] * rate_ref[:, :size], precision=PRECISE)


def joined(refs, part):
    here = slice(part * REGRESSORS, (part + 1) * REGRESSORS)
    return jnp.concatenate([ref[here] for ref in refs], axis=1)


def backward_kernel(scale, shares, paths, trades, member_ref, rows_ref, slope_ref, value_ref, *refs):
    solved_refs, refs = refs[:shares], refs[shares:]
    x_refs, refs = refs[:paths], refs[paths:]
    w_refs, refs = refs[:trades], refs[trades:]
    weight_refs, basis_refs, slopes_ref = refs[:trades], refs[trades:-1], refs[-1]
    traded = dot(three_rows(joined(solved_refs, 0)), member_ref[...]).astype(BF16)
    group = slopes_ref.shape[0]
    spread = dot(rows_ref[:group], traded).astype(BF16).astype(F32)
    slopes_ref[...] = (slope_ref[...] * spread).astype(BF16)
    basis = jnp.concatenate([x[...] for x in x_refs], axis=0)
    weight = (dot(slopes_ref[...], basis, 0, 0) * scale).astype(BF16)
    start = 0
    for part in weight_refs:
        part[...] = weight[start : start + part.shape[0]]
        start += part.shape[0]
    weights = joined_weights(w_refs)
    start = 0
    for part in basis_refs:
        here = slice(start, start + part.shape[0])
        total = dot(slopes_ref[here], weights)
        wide = dot(value_ref[here], traded, 1, 1)
        design = wide
        for k in range(1, 3):
            design = design + pltpu.roll(wide, LANES - k * REGRESSORS, 1)
        design = jnp.where(lanes(design.shape) < CONSTANT, design, 0.0)
        part[:, :LANES] = (total[:, :LANES] + design).astype(BF16)
        part[:, LANES:] = total[:, LANES:].astype(BF16)
        start += part.shape[0]


def loss_kernel(rows_ref, thresh_ref, rate_ref, *refs):
    solved_refs, (loss_ref, own_ref, split_ref, total_ref) = refs[:-4], refs[-4:]
    adjoint = joined(solved_refs, 0)
    coeffs = joined(solved_refs, 1)
    thresh = thresh_ref[...]
    rate = rate_ref[...]
    split_ref[...] = three_rows(coeffs)
    total_ref[...] = jnp.zeros(total_ref.shape, F32)

    def losses(here):
        loss = softplus(dot(rows_ref[here], split_ref[...]) - thresh)
        total_ref[...] += jnp.sum(loss.reshape(-1, *total_ref.shape), axis=0)

    each_chunk(rows_ref.shape[0], losses)
    summed = jnp.sum(jnp.sum(total_ref[...] * rate, axis=0, keepdims=True), axis=1, keepdims=True)
    loss_ref[...] = jnp.broadcast_to(
        summed / (rows_ref.shape[0] * coeffs.shape[1]), loss_ref.shape
    )
    own = rows_ref[: own_ref.shape[0]]
    fitted = dot(own, split_ref[...])
    seed = rate * sigmoid(fitted - thresh)
    rest = seed - dot(own, three_rows(adjoint))
    design = dot(rest, coeffs, 1, 1, PRECISE) - dot(fitted, adjoint, 1, 1, PRECISE)
    blank = jnp.zeros((design.shape[0], LANES - REGRESSORS), F32)
    design = jnp.concatenate([design, blank], axis=1)
    own_ref[...] = jnp.where(lanes(design.shape) < CONSTANT, design, 0.0)


def total(refs):
    out = refs[0][...].astype(F32)
    for ref in refs[1:]:
        out = out + ref[...].astype(F32)
    return out


def sum_kernel(first, own_ref, *refs):
    basis_ref, weight_ref = refs[-2:]
    basis = total(refs[:first])
    basis_ref[:, :LANES] = basis[:, :LANES] + own_ref[...]
    basis_ref[:, LANES:] = basis[:, LANES:]
    weight_ref[...] = total(refs[first:-2])


def call(kernel, outs, *args, name, flops=0, scratch=(), scalars=0):
    size = sum(a.size * a.dtype.itemsize for a in args) + sum(
        math.prod(s) * jnp.dtype(d).itemsize for s, d in outs
    )
    return pl.pallas_call(
        kernel,
        out_shape=[jax.ShapeDtypeStruct(s, d) for s, d in outs],
        in_specs=[pl.BlockSpec(memory_space=pltpu.SMEM)] * scalars
        + [pl.BlockSpec(memory_space=pltpu.VMEM)] * (len(args) - scalars),
        out_specs=[pl.BlockSpec(memory_space=pltpu.VMEM)] * len(outs),
        scratch_shapes=scratch,
        compiler_params=pltpu.CompilerParams(vmem_limit_bytes=VMEM_BYTES),
        cost_estimate=pl.CostEstimate(flops=int(flops), bytes_accessed=int(size), transcendentals=0),
        name=name,
    )(*args)


def shards(
    path_basis, proxy_weight, notional, set_of, threshold_index, threshold_levels, loss_rate
):
    n = lax.axis_size("paths")
    me = lax.axis_index("paths")
    inner_bits, outer_bits = split_bits(n)
    inner, outer = 1 << len(inner_bits), 1 << len(outer_bits)
    path_rows, features = path_basis.shape
    trade_rows = proxy_weight.shape[0]
    paths_all = path_rows * n
    sets = loss_rate.shape[0]
    share = sets // SHARES
    group_paths, group_trades = inner * path_rows, outer * trade_rows

    def swap(x, mask):
        return lax.ppermute(x, "paths", [(d, d ^ mask) for d in range(n)])

    def masks(bits):
        return [
            sum(((m >> j) & 1) << bit for j, bit in enumerate(bits)) for m in range(1 << len(bits))
        ]

    def after(x, *others):
        return lax.optimization_barrier((x, *others))[0]

    def direct(slots, bits):
        return [swap(x, mask) for x, mask in zip(slots[1:], masks(bits)[1:])]

    first_bit = outer_bits[0]
    weights = [proxy_weight, swap(proxy_weight, 1 << first_bit)]
    basis = [path_basis] + direct([path_basis] * inner, inner_bits)
    notionals = [notional, swap(notional, 1 << first_bit)]

    member, thresh, rate, basis[0], own_weight = call(
        partial(tables_kernel, masks(outer_bits)),
        [
            ((sets, group_trades), BF16),
            ((1, sets), F32),
            ((1, sets), F32),
            (path_basis.shape, BF16),
            (proxy_weight.shape, BF16),
        ],
        me.astype(jnp.int32).reshape(1),
        threshold_levels,
        set_of.reshape(n, 1, trade_rows),
        threshold_index.reshape(SHARES, 1, share),
        loss_rate.reshape(SHARES, 1, share),
        path_basis,
        proxy_weight,
        name="tables",
        scalars=2,
    )
    for bit in outer_bits[1:]:
        weights = weights + [
            swap(w if k else after(w, member), 1 << bit) for k, w in enumerate(weights)
        ]
        notionals = notionals + [swap(x, 1 << bit) for x in notionals]
    weights[0] = own_weight
    notionals = [x[None, :] for x in notionals]
    (lead,) = call(lead_kernel, [((REGRESSORS, group_paths), BF16)], *basis, name="lead")
    value, *moments = call(
        partial(forward_kernel, inner, outer),
        [((group_paths, group_trades), BF16)] + [((REGRESSORS, share), F32)] * SHARES,
        *basis, *weights, *notionals, lead, member,
        name="forward",
    )
    moment = moments[0] + swap(moments[1], SHARES - 1)
    small = after(lead, moment)[None]
    steps = inner_bits + outer_bits[-2:0:-1]
    for k in range(max(len(steps), outer_bits.index(0) + 1)):
        if k < len(outer_bits):
            if k > 0:
                small = after(small, moment)
            small = jnp.concatenate([small, swap(small, 1 << outer_bits[k])], axis=0)
        if k < len(steps):
            moment = moment + swap(moment, 1 << steps[k])
    moments = [moment, swap(moment, 1 << first_bit)]
    (inverse,) = call(
        partial(inverse_kernel, RIDGE_SCALE * paths_all),
        [((REGRESSORS, REGRESSORS), F32)],
        small,
        name="inverse",
    )
    design_all, design_rows = call(
        design_kernel,
        [((REGRESSORS, paths_all), BF16), ((paths_all, LANES), BF16)],
        small,
        name="design",
    )
    (solved,) = call(
        partial(solve_kernel, len(moments)),
        [((2 * REGRESSORS, share), F32)],
        inverse, design_all, design_rows, thresh, rate, *moments,
        name="solve",
        scratch=[pltpu.VMEM((LANES, share), BF16), pltpu.VMEM((REGRESSORS, share), F32)],
    )
    solved = [solved, swap(solved, SHARES - 1)]
    (slope,) = call(
        partial(slope_kernel, inner, outer),
        [((group_paths, group_trades), F32)],
        *basis, *weights, *notionals,
        name="slope",
    )
    parts = call(
        partial(backward_kernel, 1.0 / math.sqrt(paths_all), SHARES, inner, outer),
        [((trade_rows, features), BF16)] * outer + [((path_rows, features), BF16)] * inner,
        member, design_rows, slope, value, *solved, *basis, *weights,
        name="backward",
        scratch=[pltpu.VMEM((group_paths, group_trades), BF16)],
    )
    terms = [[part] for part in parts[:outer]]
    for bit in reversed(outer_bits):
        count = len(terms) // 2
        arrived = None
        for k in reversed(range(count)):
            gone = terms[count + k]
            gone = gone[0] if len(gone) == 1 else sum(g.astype(F32) for g in gone).astype(BF16)
            if arrived is not None:
                gone = after(gone, arrived)
            arrived = swap(gone, 1 << bit)
            terms[k].append(arrived)
            if bit == outer_bits[-1] and k == count - 1:
                basis_parts = list(parts[outer:])
                basis_parts[1] = after(basis_parts[1], arrived)
        terms = terms[:count]
    weight_terms = terms[0]
    basis_terms = [basis_parts[0]] + direct(basis_parts, inner_bits)
    loss, own_adjoint = call(
        loss_kernel,
        [((8, LANES), F32), ((path_rows, LANES), F32)],
        design_rows, thresh, rate, *solved,
        name="loss",
        scratch=[pltpu.VMEM((LANES, sets), BF16), pltpu.VMEM((8, sets), F32)],
    )
    basis_adjoint, weight_adjoint = call(
        partial(sum_kernel, len(basis_terms)),
        [((path_rows, features), F32), ((trade_rows, features), F32)],
        own_adjoint, *basis_terms, *weight_terms,
        name="sums",
    )
    return (loss[0, :1], basis_adjoint, weight_adjoint)


def solution(mesh):
    placed = (
        P(("groups", "paths"), None),
        P(("groups", "paths"), None),
        P(("groups", "paths")),
        P("groups"),
        P("groups"),
        P("groups"),
        P("groups"),
    )
    return jax.shard_map(
        shards,
        mesh=mesh,
        in_specs=placed,
        out_specs=(P("groups"), P(("groups", "paths"), None), P(("groups", "paths"), None)),
        check_vma=False,
    )
```

```python
import math
from functools import partial

import jax
import jax.numpy as jnp
from jax import lax
from jax.experimental import pallas as pl
from jax.experimental.pallas import tpu as pltpu
from jax.sharding import PartitionSpec as P

REGRESSORS = 32
RIDGE_SCALE = 0.01
PRECISE = lax.Precision.HIGHEST
F32 = jnp.float32
BF16 = jnp.bfloat16
LANES = 128
SUBLANES = 8
CHUNK = 256
VMEM_BYTES = 48 * 1024 * 1024
LOG2_E = math.log2(math.e)
SHARES = 2
CONSTANT = REGRESSORS - 1


def split_bits(size):
    count = size.bit_length() - 1
    half = count // 2
    return list(range(1, half + 1)), list(range(count - 1, half, -1)) + [0]


def dot(a, b, ca=1, cb=0, precision=None):
    return lax.dot_general(
        a, b, (((ca,), (cb,)), ((), ())), precision=precision, preferred_element_type=F32
    )


def three(x, axis):
    high = x.astype(BF16)
    rest = x - high.astype(F32)
    middle = rest.astype(BF16)
    low = (rest - middle.astype(F32)).astype(BF16)
    return jnp.concatenate([high, middle, low], axis=axis)


def three_rows(x):
    blank = jnp.zeros((LANES - 3 * REGRESSORS, x.shape[1]), BF16)
    return jnp.concatenate([three(x, 0), blank], axis=0)


def lanes(shape):
    return lax.broadcasted_iota(jnp.int32, shape, len(shape) - 1)


def rows(shape):
    return lax.broadcasted_iota(jnp.int32, shape, len(shape) - 2)


def softplus(x):
    return jnp.maximum(x, 0.0) + jnp.log1p(jnp.exp(-jnp.abs(x)))


def sigmoid(x):
    small = jnp.exp(-jnp.abs(x))
    return jnp.where(x >= 0.0, 1.0, small) / (1.0 + small)


def each_chunk(size, step):
    count = size // CHUNK

    def body(i, carry):
        step(pl.ds(pl.multiple_of(i * CHUNK, CHUNK), CHUNK))
        return carry

    lax.fori_loop(0, count, body, 0, unroll=count <= 8)


def invert(matrix):
    size = matrix.shape[0]
    work = jnp.concatenate([matrix, jnp.eye(size, dtype=F32)], axis=1)
    shape = (SUBLANES, 2 * size)
    blocks = [work[i : i + SUBLANES] for i in range(0, size, SUBLANES)]
    row = rows(shape)

    def one_row(block, k):
        return jnp.broadcast_to(block[k : k + 1], shape)

    for k in range(0, size, 4):
        at, here = k // SUBLANES, k % SUBLANES
        columns = [
            [jnp.broadcast_to(block[:, k + j : k + j + 1], shape) for block in blocks]
            for j in range(4)
        ]
        p = [[one_row(columns[j][at], here + i) for j in range(4)] for i in range(4)]
        r = [one_row(blocks[at], here + i) for i in range(4)]
        for i in range(4):
            scale = 1.0 / p[i][i]
            r[i] = r[i] * scale
            p[i] = [entry * scale for entry in p[i]]
            for m in range(4):
                if m != i:
                    r[m] = r[m] - p[m][i] * r[i]
                    p[m] = [x - p[m][i] * y if j > i else x for j, (x, y) in enumerate(zip(p[m], p[i]))]
        for i, block in enumerate(blocks):
            for j in range(4):
                block = block - columns[j][i] * r[j]
            if i == at:
                for j in range(4):
                    block = jnp.where(row == here + j, r[j], block)
            blocks[i] = block
    return jnp.concatenate(blocks, axis=0)[:, size:]


def lead_kernel(*refs):
    x_refs, lead_ref = refs[:-1], refs[-1]
    start = 0
    for x in x_refs:
        turned = x[:, :LANES].astype(F32).T[:REGRESSORS]
        turned = jnp.where(rows(turned.shape) == CONSTANT, 1.0, turned)
        lead_ref[:, start : start + x.shape[0]] = turned.astype(BF16)
        start += x.shape[0]


def tables_kernel(
    trade_masks, me_ref, level_ref, set_ref, index_ref, rate_ref, x_ref, w_ref,
    member_ref, thresh_out_ref, rate_out_ref, x_out_ref, w_out_ref,
):
    x_out_ref[...] = x_ref[...]
    w_out_ref[...] = w_ref[...]
    me = me_ref[0]
    shares = index_ref.shape[0]
    place = me & (shares - 1)
    size = member_ref.shape[0] // shares
    trades = set_ref.shape[-1]
    for m in range(shares):
        here = slice(m * size, (m + 1) * size)
        label = (place ^ m) * size + rows((size, 1))
        for j, mask in enumerate(trade_masks):
            member_ref[here, j * trades : (j + 1) * trades] = jnp.where(
                set_ref[me ^ mask] == label, 1.0, 0.0
            ).astype(BF16)
        index = index_ref[place ^ m]
        thresh = jnp.zeros(index.shape, F32)
        for k in range(level_ref.shape[0]):
            thresh = jnp.where(index == k, level_ref[k], thresh)
        thresh_out_ref[:, here] = thresh
        rate_out_ref[:, here] = rate_ref[place ^ m]


def design_kernel(small_ref, design_ref, rows_ref):
    size = small_ref.shape[2]
    for d in range(small_ref.shape[0]):
        here = slice(d * size, (d + 1) * size)
        design_ref[:, here] = small_ref[d]
        turned = small_ref[d].astype(F32).T
        blank = jnp.zeros((size, LANES - 3 * REGRESSORS), F32)
        rows_ref[here] = jnp.concatenate([turned] * 3 + [blank], axis=1).astype(BF16)


def inverse_kernel(ridge, small_ref, inverse_ref):
    square = (REGRESSORS, REGRESSORS)
    gram = jnp.where(rows(square) == lanes(square), ridge, 0.0)
    for d in range(small_ref.shape[0]):
        gram = gram + dot(small_ref[d], small_ref[d], 1, 1)
    inverse_ref[...] = invert(gram)


def joined_weights(refs):
    return jnp.concatenate([ref[...] for ref in refs], axis=0)


def joined_notionals(refs):
    return jnp.concatenate([ref[...].astype(F32) for ref in refs], axis=1)


def forward_kernel(paths, trades, *refs):
    x_refs, refs = refs[:paths], refs[paths:]
    weights, notional = joined_weights(refs[:trades]), joined_notionals(refs[trades : 2 * trades])
    lead_ref, member_ref, value_ref, *moment_refs = refs[2 * trades :]
    start = 0
    for x in x_refs:
        pre_act = dot(x[...], weights, 1, 1)
        value_ref[start : start + x.shape[0]] = (notional * softplus(pre_act)).astype(BF16)
        start += x.shape[0]
    trade_moment = dot(lead_ref[...], value_ref[...])
    parts = dot(three(trade_moment, 0), member_ref[...], 1, 1)
    moment = parts[:REGRESSORS] + parts[REGRESSORS : 2 * REGRESSORS] + parts[2 * REGRESSORS :]
    size = moment.shape[1] // len(moment_refs)
    for m, moment_ref in enumerate(moment_refs):
        moment_ref[...] = moment[:, m * size : (m + 1) * size]


def slope_kernel(paths, trades, *refs):
    x_refs, refs, slope_ref = refs[:paths], refs[paths:], refs[-1]
    weights, notional = joined_weights(refs[:trades]), joined_notionals(refs[trades : 2 * trades])
    start = 0
    for x in x_refs:
        slope_ref[start : start + x.shape[0]] = notional * sigmoid(dot(x[...], weights, 1, 1))
        start += x.shape[0]


def solve_kernel(
    terms, inverse_ref, design_ref, rows_ref, thresh_ref, rate_ref, *refs
):
    solved_ref, turn_ref, total_ref = refs[terms:]
    moment = refs[0][...]
    for ref in refs[1:terms]:
        moment = moment + ref[...]
    size = moment.shape[1]
    inverse = inverse_ref[...]
    coeffs = dot(inverse, moment, precision=PRECISE)
    solved_ref[REGRESSORS:] = coeffs
    is_constant = rows(coeffs.shape) == CONSTANT
    shifted = coeffs - jnp.where(is_constant, thresh_ref[:, :size], 0.0)
    turn_ref[...] = three_rows(-LOG2_E * shifted)
    total_ref[...] = jnp.zeros(total_ref.shape, F32)

    def seeds(here):
        power = jnp.exp2(jnp.minimum(dot(rows_ref[here], turn_ref[...]), 126.0))
        below = 1.0 + power
        seed = pl.reciprocal(below, approx=True)
        seed = (seed * (2.0 - below * seed)).astype(BF16)
        total_ref[...] += dot(design_ref[:, here], seed)

    each_chunk(rows_ref.shape[0], seeds)
    solved_ref[:REGRESSORS] = dot(inverse, total_ref[...] * rate_ref[:, :size], precision=PRECISE)


def joined(refs, part):
    here = slice(part * REGRESSORS, (part + 1) * REGRESSORS)
    return jnp.concatenate([ref[here] for ref in refs], axis=1)


def backward_kernel(scale, shares, paths, trades, member_ref, rows_ref, slope_ref, value_ref, *refs):
    solved_refs, refs = refs[:shares], refs[shares:]
    x_refs, refs = refs[:paths], refs[paths:]
    w_refs, refs = refs[:trades], refs[trades:]
    weight_refs, basis_refs, slopes_ref = refs[:trades], refs[trades:-1], refs[-1]
    traded = dot(three_rows(joined(solved_refs, 0)), member_ref[...]).astype(BF16)
    group = slopes_ref.shape[0]
    spread = dot(rows_ref[:group], traded).astype(BF16).astype(F32)
    slopes_ref[...] = (slope_ref[...] * spread).astype(BF16)
    basis = jnp.concatenate([x[...] for x in x_refs], axis=0)
    weight = (dot(slopes_ref[...], basis, 0, 0) * scale).astype(BF16)
    start = 0
    for part in weight_refs:
        part[...] = weight[start : start + part.shape[0]]
        start += part.shape[0]
    weights = joined_weights(w_refs)
    start = 0
    for part in basis_refs:
        here = slice(start, start + part.shape[0])
        total = dot(slopes_ref[here], weights)
        wide = dot(value_ref[here], traded, 1, 1)
        design = wide
        for k in range(1, 3):
            design = design + pltpu.roll(wide, LANES - k * REGRESSORS, 1)
        design = jnp.where(lanes(design.shape) < CONSTANT, design, 0.0)
        part[:, :LANES] = (total[:, :LANES] + design).astype(BF16)
        part[:, LANES:] = total[:, LANES:].astype(BF16)
        start += part.shape[0]


def loss_kernel(rows_ref, thresh_ref, rate_ref, *refs):
    solved_refs, (loss_ref, own_ref, split_ref, total_ref) = refs[:-4], refs[-4:]
    adjoint = joined(solved_refs, 0)
    coeffs = joined(solved_refs, 1)
    thresh = thresh_ref[...]
    rate = rate_ref[...]
    split_ref[...] = three_rows(coeffs)
    total_ref[...] = jnp.zeros(total_ref.shape, F32)

    def losses(here):
        loss = softplus(dot(rows_ref[here], split_ref[...]) - thresh)
        total_ref[...] += jnp.sum(loss.reshape(-1, *total_ref.shape), axis=0)

    each_chunk(rows_ref.shape[0], losses)
    summed = jnp.sum(jnp.sum(total_ref[...] * rate, axis=0, keepdims=True), axis=1, keepdims=True)
    loss_ref[...] = jnp.broadcast_to(
        summed / (rows_ref.shape[0] * coeffs.shape[1]), loss_ref.shape
    )
    own = rows_ref[: own_ref.shape[0]]
    fitted = dot(own, split_ref[...])
    seed = rate * sigmoid(fitted - thresh)
    rest = seed - dot(own, three_rows(adjoint))
    design = dot(rest, coeffs, 1, 1, PRECISE) - dot(fitted, adjoint, 1, 1, PRECISE)
    blank = jnp.zeros((design.shape[0], LANES - REGRESSORS), F32)
    design = jnp.concatenate([design, blank], axis=1)
    own_ref[...] = jnp.where(lanes(design.shape) < CONSTANT, design, 0.0)


def total(refs):
    out = refs[0][...].astype(F32)
    for ref in refs[1:]:
        out = out + ref[...].astype(F32)
    return out


def sum_kernel(first, own_ref, *refs):
    basis_ref, weight_ref = refs[-2:]
    basis = total(refs[:first])
    basis_ref[:, :LANES] = basis[:, :LANES] + own_ref[...]
    basis_ref[:, LANES:] = basis[:, LANES:]
    weight_ref[...] = total(refs[first:-2])


def call(kernel, outs, *args, name, flops=0, scratch=(), scalars=0):
    size = sum(a.size * a.dtype.itemsize for a in args) + sum(
        math.prod(s) * jnp.dtype(d).itemsize for s, d in outs
    )
    return pl.pallas_call(
        kernel,
        out_shape=[jax.ShapeDtypeStruct(s, d) for s, d in outs],
        in_specs=[pl.BlockSpec(memory_space=pltpu.SMEM)] * scalars
        + [pl.BlockSpec(memory_space=pltpu.VMEM)] * (len(args) - scalars),
        out_specs=[pl.BlockSpec(memory_space=pltpu.VMEM)] * len(outs),
        scratch_shapes=scratch,
        compiler_params=pltpu.CompilerParams(vmem_limit_bytes=VMEM_BYTES),
        cost_estimate=pl.CostEstimate(flops=int(flops), bytes_accessed=int(size), transcendentals=0),
        name=name,
    )(*args)


def shards(
    path_basis, proxy_weight, notional, set_of, threshold_index, threshold_levels, loss_rate
):
    n = lax.axis_size("paths")
    me = lax.axis_index("paths")
    inner_bits, outer_bits = split_bits(n)
    inner, outer = 1 << len(inner_bits), 1 << len(outer_bits)
    path_rows, features = path_basis.shape
    trade_rows = proxy_weight.shape[0]
    paths_all = path_rows * n
    sets = loss_rate.shape[0]
    share = sets // SHARES
    group_paths, group_trades = inner * path_rows, outer * trade_rows

    def swap(x, mask):
        return lax.ppermute(x, "paths", [(d, d ^ mask) for d in range(n)])

    def masks(bits):
        return [
            sum(((m >> j) & 1) << bit for j, bit in enumerate(bits)) for m in range(1 << len(bits))
        ]

    def after(x, *others):
        return lax.optimization_barrier((x, *others))[0]

    def direct(slots, bits):
        return [swap(x, mask) for x, mask in zip(slots[1:], masks(bits)[1:])]

    first_bit = outer_bits[0]
    weights = [proxy_weight, swap(proxy_weight, 1 << first_bit)]
    basis = [path_basis] + direct([path_basis] * inner, inner_bits)
    notionals = [notional, swap(notional, 1 << first_bit)]

    member, thresh, rate, basis[0], own_weight = call(
        partial(tables_kernel, masks(outer_bits)),
        [
            ((sets, group_trades), BF16),
            ((1, sets), F32),
            ((1, sets), F32),
            (path_basis.shape, BF16),
            (proxy_weight.shape, BF16),
        ],
        me.astype(jnp.int32).reshape(1),
        threshold_levels,
        set_of.reshape(n, 1, trade_rows),
        threshold_index.reshape(SHARES, 1, share),
        loss_rate.reshape(SHARES, 1, share),
        path_basis,
        proxy_weight,
        name="tables",
        scalars=2,
    )
    for bit in outer_bits[1:]:
        weights = weights + [
            swap(w if k else after(w, member), 1 << bit) for k, w in enumerate(weights)
        ]
        notionals = notionals + [swap(x, 1 << bit) for x in notionals]
    weights[0] = own_weight
    notionals = [x[None, :] for x in notionals]
    (lead,) = call(lead_kernel, [((REGRESSORS, group_paths), BF16)], *basis, name="lead")
    value, *moments = call(
        partial(forward_kernel, inner, outer),
        [((group_paths, group_trades), BF16)] + [((REGRESSORS, share), F32)] * SHARES,
        *basis, *weights, *notionals, lead, member,
        name="forward",
    )
    moment = moments[0] + swap(moments[1], SHARES - 1)
    small = after(lead, moment)[None]
    small = jnp.concatenate([small, swap(small, 1 << first_bit)], axis=0)
    moment = sum(direct([moment] * inner, inner_bits), moment)
    for bit in outer_bits[1:]:
        small = after(small, moment)
        small = jnp.concatenate([small, swap(small, 1 << bit)], axis=0)
    for bit in outer_bits[-2:0:-1]:
        moment = moment + swap(moment, 1 << bit)
    moments = [moment, swap(moment, 1 << first_bit)]
    (inverse,) = call(
        partial(inverse_kernel, RIDGE_SCALE * paths_all),
        [((REGRESSORS, REGRESSORS), F32)],
        small,
        name="inverse",
    )
    design_all, design_rows = call(
        design_kernel,
        [((REGRESSORS, paths_all), BF16), ((paths_all, LANES), BF16)],
        small,
        name="design",
    )
    (solved,) = call(
        partial(solve_kernel, len(moments)),
        [((2 * REGRESSORS, share), F32)],
        inverse, design_all, design_rows, thresh, rate, *moments,
        name="solve",
        scratch=[pltpu.VMEM((LANES, share), BF16), pltpu.VMEM((REGRESSORS, share), F32)],
    )
    solved = [solved, swap(solved, SHARES - 1)]
    (slope,) = call(
        partial(slope_kernel, inner, outer),
        [((group_paths, group_trades), F32)],
        *basis, *weights, *notionals,
        name="slope",
    )
    parts = call(
        partial(backward_kernel, 1.0 / math.sqrt(paths_all), SHARES, inner, outer),
        [((trade_rows, features), BF16)] * outer + [((path_rows, features), BF16)] * inner,
        member, design_rows, slope, value, *solved, *basis, *weights,
        name="backward",
        scratch=[pltpu.VMEM((group_paths, group_trades), BF16)],
    )
    terms = [[part] for part in parts[:outer]]
    for bit in reversed(outer_bits):
        count = len(terms) // 2
        arrived = None
        for k in reversed(range(count)):
            gone = terms[count + k]
            gone = gone[0] if len(gone) == 1 else sum(g.astype(F32) for g in gone).astype(BF16)
            if arrived is not None:
                gone = after(gone, arrived)
            arrived = swap(gone, 1 << bit)
            terms[k].append(arrived)
            if bit == outer_bits[-1] and k == count - 1:
                basis_parts = list(parts[outer:])
                basis_parts[1] = after(basis_parts[1], arrived)
        terms = terms[:count]
    weight_terms = terms[0]
    basis_terms = [basis_parts[0]] + direct(basis_parts, inner_bits)
    loss, own_adjoint = call(
        loss_kernel,
        [((8, LANES), F32), ((path_rows, LANES), F32)],
        design_rows, thresh, rate, *solved,
        name="loss",
        scratch=[pltpu.VMEM((LANES, sets), BF16), pltpu.VMEM((8, sets), F32)],
    )
    basis_adjoint, weight_adjoint = call(
        partial(sum_kernel, len(basis_terms)),
        [((path_rows, features), F32), ((trade_rows, features), F32)],
        own_adjoint, *basis_terms, *weight_terms,
        name="sums",
    )
    return (loss[0, :1], basis_adjoint, weight_adjoint)


def solution(mesh):
    placed = (
        P(("groups", "paths"), None),
        P(("groups", "paths"), None),
        P(("groups", "paths")),
        P("groups"),
        P("groups"),
        P("groups"),
        P("groups"),
    )
    return jax.shard_map(
        shards,
        mesh=mesh,
        in_specs=placed,
        out_specs=(P("groups"), P(("groups", "paths"), None), P(("groups", "paths"), None)),
        check_vma=False,
    )
```

```python
import math
from functools import partial

import jax
import jax.numpy as jnp
from jax import lax
from jax.experimental import pallas as pl
from jax.experimental.pallas import tpu as pltpu
from jax.sharding import PartitionSpec as P

REGRESSORS = 32
RIDGE_SCALE = 0.01
PRECISE = lax.Precision.HIGHEST
F32 = jnp.float32
BF16 = jnp.bfloat16
LANES = 128
SUBLANES = 8
CHUNK = 256
VMEM_BYTES = 48 * 1024 * 1024
LOG2_E = math.log2(math.e)
SHARES = 2
CONSTANT = REGRESSORS - 1


def split_bits(size):
    count = size.bit_length() - 1
    half = count // 2
    return list(range(1, half + 1)), list(range(count - 1, half, -1)) + [0]


def dot(a, b, ca=1, cb=0, precision=None):
    return lax.dot_general(
        a, b, (((ca,), (cb,)), ((), ())), precision=precision, preferred_element_type=F32
    )


def three(x, axis):
    high = x.astype(BF16)
    rest = x - high.astype(F32)
    middle = rest.astype(BF16)
    low = (rest - middle.astype(F32)).astype(BF16)
    return jnp.concatenate([high, middle, low], axis=axis)


def three_rows(x):
    blank = jnp.zeros((LANES - 3 * REGRESSORS, x.shape[1]), BF16)
    return jnp.concatenate([three(x, 0), blank], axis=0)


def lanes(shape):
    return lax.broadcasted_iota(jnp.int32, shape, len(shape) - 1)


def rows(shape):
    return lax.broadcasted_iota(jnp.int32, shape, len(shape) - 2)


def softplus(x):
    return jnp.maximum(x, 0.0) + jnp.log1p(jnp.exp(-jnp.abs(x)))


def sigmoid(x):
    small = jnp.exp(-jnp.abs(x))
    return jnp.where(x >= 0.0, 1.0, small) / (1.0 + small)


def each_chunk(size, step):
    count = size // CHUNK

    def body(i, carry):
        step(pl.ds(pl.multiple_of(i * CHUNK, CHUNK), CHUNK))
        return carry

    lax.fori_loop(0, count, body, 0, unroll=count <= 8)


def invert(matrix):
    size = matrix.shape[0]
    work = jnp.concatenate([matrix, jnp.eye(size, dtype=F32)], axis=1)
    shape = (SUBLANES, 2 * size)
    blocks = [work[i : i + SUBLANES] for i in range(0, size, SUBLANES)]
    row = rows(shape)

    def one_row(block, k):
        return jnp.broadcast_to(block[k : k + 1], shape)

    for k in range(0, size, 4):
        at, here = k // SUBLANES, k % SUBLANES
        columns = [
            [jnp.broadcast_to(block[:, k + j : k + j + 1], shape) for block in blocks]
            for j in range(4)
        ]
        p = [[one_row(columns[j][at], here + i) for j in range(4)] for i in range(4)]
        r = [one_row(blocks[at], here + i) for i in range(4)]
        for i in range(4):
            scale = 1.0 / p[i][i]
            r[i] = r[i] * scale
            p[i] = [entry * scale for entry in p[i]]
            for m in range(4):
                if m != i:
                    r[m] = r[m] - p[m][i] * r[i]
                    p[m] = [x - p[m][i] * y if j > i else x for j, (x, y) in enumerate(zip(p[m], p[i]))]
        for i, block in enumerate(blocks):
            for j in range(4):
                block = block - columns[j][i] * r[j]
            if i == at:
                for j in range(4):
                    block = jnp.where(row == here + j, r[j], block)
            blocks[i] = block
    return jnp.concatenate(blocks, axis=0)[:, size:]


def lead_kernel(*refs):
    x_refs, lead_ref = refs[:-1], refs[-1]
    start = 0
    for x in x_refs:
        turned = x[:, :LANES].astype(F32).T[:REGRESSORS]
        turned = jnp.where(rows(turned.shape) == CONSTANT, 1.0, turned)
        lead_ref[:, start : start + x.shape[0]] = turned.astype(BF16)
        start += x.shape[0]


def tables_kernel(
    trade_masks, me_ref, level_ref, set_ref, index_ref, rate_ref, x_ref, w_ref,
    member_ref, thresh_out_ref, rate_out_ref, x_out_ref, w_out_ref,
):
    x_out_ref[...] = x_ref[...]
    w_out_ref[...] = w_ref[...]
    me = me_ref[0]
    shares = index_ref.shape[0]
    place = me & (shares - 1)
    size = member_ref.shape[0] // shares
    trades = set_ref.shape[-1]
    for m in range(shares):
        here = slice(m * size, (m + 1) * size)
        label = (place ^ m) * size + rows((size, 1))
        for j, mask in enumerate(trade_masks):
            member_ref[here, j * trades : (j + 1) * trades] = jnp.where(
                set_ref[me ^ mask] == label, 1.0, 0.0
            ).astype(BF16)
        index = index_ref[place ^ m]
        thresh = jnp.zeros(index.shape, F32)
        for k in range(level_ref.shape[0]):
            thresh = jnp.where(index == k, level_ref[k], thresh)
        thresh_out_ref[:, here] = thresh
        rate_out_ref[:, here] = rate_ref[place ^ m]


def design_kernel(small_ref, design_ref, rows_ref):
    size = small_ref.shape[2]
    for d in range(small_ref.shape[0]):
        here = slice(d * size, (d + 1) * size)
        design_ref[:, here] = small_ref[d]
        turned = small_ref[d].astype(F32).T
        blank = jnp.zeros((size, LANES - 3 * REGRESSORS), F32)
        rows_ref[here] = jnp.concatenate([turned] * 3 + [blank], axis=1).astype(BF16)


def inverse_kernel(ridge, small_ref, inverse_ref):
    square = (REGRESSORS, REGRESSORS)
    gram = jnp.where(rows(square) == lanes(square), ridge, 0.0)
    for d in range(small_ref.shape[0]):
        gram = gram + dot(small_ref[d], small_ref[d], 1, 1)
    inverse_ref[...] = invert(gram)


def joined_weights(refs):
    return jnp.concatenate([ref[...] for ref in refs], axis=0)


def joined_notionals(refs):
    return jnp.concatenate([ref[...].astype(F32) for ref in refs], axis=1)


def forward_kernel(paths, trades, *refs):
    x_refs, refs = refs[:paths], refs[paths:]
    weights, notional = joined_weights(refs[:trades]), joined_notionals(refs[trades : 2 * trades])
    lead_ref, member_ref, value_ref, *moment_refs = refs[2 * trades :]
    start = 0
    for x in x_refs:
        pre_act = dot(x[...], weights, 1, 1)
        value_ref[start : start + x.shape[0]] = (notional * softplus(pre_act)).astype(BF16)
        start += x.shape[0]
    trade_moment = dot(lead_ref[...], value_ref[...])
    parts = dot(three(trade_moment, 0), member_ref[...], 1, 1)
    moment = parts[:REGRESSORS] + parts[REGRESSORS : 2 * REGRESSORS] + parts[2 * REGRESSORS :]
    size = moment.shape[1] // len(moment_refs)
    for m, moment_ref in enumerate(moment_refs):
        moment_ref[...] = moment[:, m * size : (m + 1) * size]


def slope_kernel(paths, trades, *refs):
    x_refs, refs, slope_ref = refs[:paths], refs[paths:], refs[-1]
    weights, notional = joined_weights(refs[:trades]), joined_notionals(refs[trades : 2 * trades])
    start = 0
    for x in x_refs:
        slope_ref[start : start + x.shape[0]] = notional * sigmoid(dot(x[...], weights, 1, 1))
        start += x.shape[0]


def solve_kernel(
    terms, inverse_ref, design_ref, rows_ref, thresh_ref, rate_ref, *refs
):
    solved_ref, turn_ref, total_ref = refs[terms:]
    moment = refs[0][...]
    for ref in refs[1:terms]:
        moment = moment + ref[...]
    size = moment.shape[1]
    inverse = inverse_ref[...]
    coeffs = dot(inverse, moment, precision=PRECISE)
    solved_ref[REGRESSORS:] = coeffs
    is_constant = rows(coeffs.shape) == CONSTANT
    shifted = coeffs - jnp.where(is_constant, thresh_ref[:, :size], 0.0)
    turn_ref[...] = three_rows(-LOG2_E * shifted)
    total_ref[...] = jnp.zeros(total_ref.shape, F32)

    def seeds(here):
        power = jnp.exp2(jnp.minimum(dot(rows_ref[here], turn_ref[...]), 126.0))
        below = 1.0 + power
        seed = pl.reciprocal(below, approx=True)
        seed = (seed * (2.0 - below * seed)).astype(BF16)
        total_ref[...] += dot(design_ref[:, here], seed)

    each_chunk(rows_ref.shape[0], seeds)
    solved_ref[:REGRESSORS] = dot(inverse, total_ref[...] * rate_ref[:, :size], precision=PRECISE)


def joined(refs, part):
    here = slice(part * REGRESSORS, (part + 1) * REGRESSORS)
    return jnp.concatenate([ref[here] for ref in refs], axis=1)


def weight_side_kernel(scale, shares, paths, member_ref, rows_ref, slope_ref, *refs):
    solved_refs, refs = refs[:shares], refs[shares:]
    x_refs, (traded_ref, slopes_ref, *weight_refs) = refs[:paths], refs[paths:]
    traded = dot(three_rows(joined(solved_refs, 0)), member_ref[...]).astype(BF16)
    traded_ref[...] = traded
    group = slopes_ref.shape[0]
    spread = dot(rows_ref[:group], traded).astype(BF16).astype(F32)
    slopes_ref[...] = (slope_ref[...] * spread).astype(BF16)
    basis = jnp.concatenate([x[...] for x in x_refs], axis=0)
    weight = (dot(slopes_ref[...], basis, 0, 0) * scale).astype(BF16)
    start = 0
    for part in weight_refs:
        part[...] = weight[start : start + part.shape[0]]
        start += part.shape[0]


def basis_side_kernel(trades, value_ref, traded_ref, slopes_ref, *refs):
    w_refs, basis_refs = refs[:trades], refs[trades:]
    weights = joined_weights(w_refs)
    start = 0
    for part in basis_refs:
        here = slice(start, start + part.shape[0])
        total = dot(slopes_ref[here], weights)
        wide = dot(value_ref[here], traded_ref[...], 1, 1)
        design = wide
        for k in range(1, 3):
            design = design + pltpu.roll(wide, LANES - k * REGRESSORS, 1)
        design = jnp.where(lanes(design.shape) < CONSTANT, design, 0.0)
        part[:, :LANES] = (total[:, :LANES] + design).astype(BF16)
        part[:, LANES:] = total[:, LANES:].astype(BF16)
        start += part.shape[0]


def loss_kernel(rows_ref, thresh_ref, rate_ref, *refs):
    solved_refs, (loss_ref, own_ref, split_ref, total_ref) = refs[:-4], refs[-4:]
    adjoint = joined(solved_refs, 0)
    coeffs = joined(solved_refs, 1)
    thresh = thresh_ref[...]
    rate = rate_ref[...]
    split_ref[...] = three_rows(coeffs)
    total_ref[...] = jnp.zeros(total_ref.shape, F32)

    def losses(here):
        loss = softplus(dot(rows_ref[here], split_ref[...]) - thresh)
        total_ref[...] += jnp.sum(loss.reshape(-1, *total_ref.shape), axis=0)

    each_chunk(rows_ref.shape[0], losses)
    summed = jnp.sum(jnp.sum(total_ref[...] * rate, axis=0, keepdims=True), axis=1, keepdims=True)
    loss_ref[...] = jnp.broadcast_to(
        summed / (rows_ref.shape[0] * coeffs.shape[1]), loss_ref.shape
    )
    own = rows_ref[: own_ref.shape[0]]
    fitted = dot(own, split_ref[...])
    seed = rate * sigmoid(fitted - thresh)
    rest = seed - dot(own, three_rows(adjoint))
    design = dot(rest, coeffs, 1, 1, PRECISE) - dot(fitted, adjoint, 1, 1, PRECISE)
    blank = jnp.zeros((design.shape[0], LANES - REGRESSORS), F32)
    design = jnp.concatenate([design, blank], axis=1)
    own_ref[...] = jnp.where(lanes(design.shape) < CONSTANT, design, 0.0)


def total(refs):
    out = refs[0][...].astype(F32)
    for ref in refs[1:]:
        out = out + ref[...].astype(F32)
    return out


def sum_kernel(first, own_ref, *refs):
    basis_ref, weight_ref = refs[-2:]
    basis = total(refs[:first])
    basis_ref[:, :LANES] = basis[:, :LANES] + own_ref[...]
    basis_ref[:, LANES:] = basis[:, LANES:]
    weight_ref[...] = total(refs[first:-2])


def call(kernel, outs, *args, name, flops=0, scratch=(), scalars=0):
    size = sum(a.size * a.dtype.itemsize for a in args) + sum(
        math.prod(s) * jnp.dtype(d).itemsize for s, d in outs
    )
    return pl.pallas_call(
        kernel,
        out_shape=[jax.ShapeDtypeStruct(s, d) for s, d in outs],
        in_specs=[pl.BlockSpec(memory_space=pltpu.SMEM)] * scalars
        + [pl.BlockSpec(memory_space=pltpu.VMEM)] * (len(args) - scalars),
        out_specs=[pl.BlockSpec(memory_space=pltpu.VMEM)] * len(outs),
        scratch_shapes=scratch,
        compiler_params=pltpu.CompilerParams(vmem_limit_bytes=VMEM_BYTES),
        cost_estimate=pl.CostEstimate(flops=int(flops), bytes_accessed=int(size), transcendentals=0),
        name=name,
    )(*args)


def shards(
    path_basis, proxy_weight, notional, set_of, threshold_index, threshold_levels, loss_rate
):
    n = lax.axis_size("paths")
    me = lax.axis_index("paths")
    inner_bits, outer_bits = split_bits(n)
    inner, outer = 1 << len(inner_bits), 1 << len(outer_bits)
    path_rows, features = path_basis.shape
    trade_rows = proxy_weight.shape[0]
    paths_all = path_rows * n
    sets = loss_rate.shape[0]
    share = sets // SHARES
    group_paths, group_trades = inner * path_rows, outer * trade_rows

    def swap(x, mask):
        return lax.ppermute(x, "paths", [(d, d ^ mask) for d in range(n)])

    def masks(bits):
        return [
            sum(((m >> j) & 1) << bit for j, bit in enumerate(bits)) for m in range(1 << len(bits))
        ]

    def after(x, *others):
        return lax.optimization_barrier((x, *others))[0]

    def direct(slots, bits):
        return [swap(x, mask) for x, mask in zip(slots[1:], masks(bits)[1:])]

    first_bit = outer_bits[0]
    weights = [proxy_weight, swap(proxy_weight, 1 << first_bit)]
    basis = [path_basis] + direct([path_basis] * inner, inner_bits)
    notionals = [notional, swap(notional, 1 << first_bit)]

    member, thresh, rate, basis[0], own_weight = call(
        partial(tables_kernel, masks(outer_bits)),
        [
            ((sets, group_trades), BF16),
            ((1, sets), F32),
            ((1, sets), F32),
            (path_basis.shape, BF16),
            (proxy_weight.shape, BF16),
        ],
        me.astype(jnp.int32).reshape(1),
        threshold_levels,
        set_of.reshape(n, 1, trade_rows),
        threshold_index.reshape(SHARES, 1, share),
        loss_rate.reshape(SHARES, 1, share),
        path_basis,
        proxy_weight,
        name="tables",
        scalars=2,
    )
    for bit in outer_bits[1:]:
        weights = weights + [
            swap(w if k else after(w, member), 1 << bit) for k, w in enumerate(weights)
        ]
        notionals = notionals + [swap(x, 1 << bit) for x in notionals]
    weights[0] = own_weight
    notionals = [x[None, :] for x in notionals]
    (lead,) = call(lead_kernel, [((REGRESSORS, group_paths), BF16)], *basis, name="lead")
    value, *moments = call(
        partial(forward_kernel, inner, outer),
        [((group_paths, group_trades), BF16)] + [((REGRESSORS, share), F32)] * SHARES,
        *basis, *weights, *notionals, lead, member,
        name="forward",
    )
    moment = moments[0] + swap(moments[1], SHARES - 1)
    small = lead[None]
    for bit in outer_bits:
        small = jnp.concatenate([small, swap(small, 1 << bit)], axis=0)
    moment = sum(direct([moment] * inner, inner_bits), moment)
    for bit in outer_bits[-2:0:-1]:
        moment = moment + swap(moment, 1 << bit)
    moments = [moment, swap(moment, 1 << first_bit)]
    (inverse,) = call(
        partial(inverse_kernel, RIDGE_SCALE * paths_all),
        [((REGRESSORS, REGRESSORS), F32)],
        small,
        name="inverse",
    )
    design_all, design_rows = call(
        design_kernel,
        [((REGRESSORS, paths_all), BF16), ((paths_all, LANES), BF16)],
        small,
        name="design",
    )
    (solved,) = call(
        partial(solve_kernel, len(moments)),
        [((2 * REGRESSORS, share), F32)],
        inverse, design_all, design_rows, thresh, rate, *moments,
        name="solve",
        scratch=[pltpu.VMEM((LANES, share), BF16), pltpu.VMEM((REGRESSORS, share), F32)],
    )
    solved = [solved, swap(solved, SHARES - 1)]
    (slope,) = call(
        partial(slope_kernel, inner, outer),
        [((group_paths, group_trades), F32)],
        *basis, *weights, *notionals,
        name="slope",
    )
    traded, slopes, *weight_parts = call(
        partial(weight_side_kernel, 1.0 / math.sqrt(paths_all), SHARES, inner),
        [((LANES, group_trades), BF16), ((group_paths, group_trades), BF16)]
        + [((trade_rows, features), BF16)] * outer,
        member, design_rows, slope, *solved, *basis,
        name="weight_side",
    )
    basis_parts = list(
        call(
            partial(basis_side_kernel, outer),
            [((path_rows, features), BF16)] * inner,
            value, traded, slopes, *weights,
            name="basis_side",
        )
    )
    terms = [[part] for part in weight_parts]
    for bit in reversed(outer_bits):
        count = len(terms) // 2
        arrived = None
        for k in reversed(range(count)):
            gone = terms[count + k]
            gone = gone[0] if len(gone) == 1 else sum(g.astype(F32) for g in gone).astype(BF16)
            if arrived is not None:
                gone = after(gone, arrived)
            arrived = swap(gone, 1 << bit)
            terms[k].append(arrived)
            if bit == outer_bits[-1] and k == count - 1:
                basis_parts[1] = after(basis_parts[1], arrived)
        terms = terms[:count]
    weight_terms = terms[0]
    basis_terms = [basis_parts[0]] + direct(basis_parts, inner_bits)
    loss, own_adjoint = call(
        loss_kernel,
        [((8, LANES), F32), ((path_rows, LANES), F32)],
        design_rows, thresh, rate, *solved,
        name="loss",
        scratch=[pltpu.VMEM((LANES, sets), BF16), pltpu.VMEM((8, sets), F32)],
    )
    basis_adjoint, weight_adjoint = call(
        partial(sum_kernel, len(basis_terms)),
        [((path_rows, features), F32), ((trade_rows, features), F32)],
        own_adjoint, *basis_terms, *weight_terms,
        name="sums",
    )
    return (loss[0, :1], basis_adjoint, weight_adjoint)


def solution(mesh):
    placed = (
        P(("groups", "paths"), None),
        P(("groups", "paths"), None),
        P(("groups", "paths")),
        P("groups"),
        P("groups"),
        P("groups"),
        P("groups"),
    )
    return jax.shard_map(
        shards,
        mesh=mesh,
        in_specs=placed,
        out_specs=(P("groups"), P(("groups", "paths"), None), P(("groups", "paths"), None)),
        check_vma=False,
    )
```

```python
import math
from functools import partial

import jax
import jax.numpy as jnp
from jax import lax
from jax.experimental import pallas as pl
from jax.experimental.pallas import tpu as pltpu
from jax.sharding import PartitionSpec as P

REGRESSORS = 32
RIDGE_SCALE = 0.01
PRECISE = lax.Precision.HIGHEST
F32 = jnp.float32
BF16 = jnp.bfloat16
LANES = 128
SUBLANES = 8
CHUNK = 256
VMEM_BYTES = 48 * 1024 * 1024
LOG2_E = math.log2(math.e)
SHARES = 2
CONSTANT = REGRESSORS - 1


def split_bits(size):
    count = size.bit_length() - 1
    half = count // 2
    return list(range(1, half + 1)), list(range(count - 1, half, -1)) + [0]


def dot(a, b, ca=1, cb=0, precision=None):
    return lax.dot_general(
        a, b, (((ca,), (cb,)), ((), ())), precision=precision, preferred_element_type=F32
    )


def three(x, axis):
    high = x.astype(BF16)
    rest = x - high.astype(F32)
    middle = rest.astype(BF16)
    low = (rest - middle.astype(F32)).astype(BF16)
    return jnp.concatenate([high, middle, low], axis=axis)


def three_rows(x):
    blank = jnp.zeros((LANES - 3 * REGRESSORS, x.shape[1]), BF16)
    return jnp.concatenate([three(x, 0), blank], axis=0)


def lanes(shape):
    return lax.broadcasted_iota(jnp.int32, shape, len(shape) - 1)


def rows(shape):
    return lax.broadcasted_iota(jnp.int32, shape, len(shape) - 2)


def softplus(x):
    return jnp.maximum(x, 0.0) + jnp.log1p(jnp.exp(-jnp.abs(x)))


def sigmoid(x):
    small = jnp.exp(-jnp.abs(x))
    return jnp.where(x >= 0.0, 1.0, small) / (1.0 + small)


def each_chunk(size, step):
    count = size // CHUNK

    def body(i, carry):
        step(pl.ds(pl.multiple_of(i * CHUNK, CHUNK), CHUNK))
        return carry

    lax.fori_loop(0, count, body, 0, unroll=count <= 8)


def invert(matrix):
    size = matrix.shape[0]
    work = jnp.concatenate([matrix, jnp.eye(size, dtype=F32)], axis=1)
    shape = (SUBLANES, 2 * size)
    blocks = [work[i : i + SUBLANES] for i in range(0, size, SUBLANES)]
    row = rows(shape)

    def one_row(block, k):
        return jnp.broadcast_to(block[k : k + 1], shape)

    for k in range(0, size, 4):
        at, here = k // SUBLANES, k % SUBLANES
        columns = [
            [jnp.broadcast_to(block[:, k + j : k + j + 1], shape) for block in blocks]
            for j in range(4)
        ]
        p = [[one_row(columns[j][at], here + i) for j in range(4)] for i in range(4)]
        r = [one_row(blocks[at], here + i) for i in range(4)]
        for i in range(4):
            scale = 1.0 / p[i][i]
            r[i] = r[i] * scale
            p[i] = [entry * scale for entry in p[i]]
            for m in range(4):
                if m != i:
                    r[m] = r[m] - p[m][i] * r[i]
                    p[m] = [x - p[m][i] * y if j > i else x for j, (x, y) in enumerate(zip(p[m], p[i]))]
        for i, block in enumerate(blocks):
            for j in range(4):
                block = block - columns[j][i] * r[j]
            if i == at:
                for j in range(4):
                    block = jnp.where(row == here + j, r[j], block)
            blocks[i] = block
    return jnp.concatenate(blocks, axis=0)[:, size:]


def regressors(x):
    turned = x[:, :LANES].astype(F32).T[:REGRESSORS]
    return jnp.where(rows(turned.shape) == CONSTANT, 1.0, turned).astype(BF16)


def lead_kernel(*refs):
    x_refs, lead_ref = refs[:-1], refs[-1]
    start = 0
    for x in x_refs:
        lead_ref[:, start : start + x.shape[0]] = regressors(x)
        start += x.shape[0]


def tables_kernel(
    trade_masks, me_ref, level_ref, set_ref, index_ref, rate_ref, x_ref, w_ref,
    member_ref, thresh_out_ref, rate_out_ref, x_out_ref, w_out_ref, lead_ref,
):
    x_out_ref[...] = x_ref[...]
    lead_ref[...] = regressors(x_ref)
    w_out_ref[...] = w_ref[...]
    me = me_ref[0]
    shares = index_ref.shape[0]
    place = me & (shares - 1)
    size = member_ref.shape[0] // shares
    trades = set_ref.shape[-1]
    for m in range(shares):
        here = slice(m * size, (m + 1) * size)
        label = (place ^ m) * size + rows((size, 1))
        for j, mask in enumerate(trade_masks):
            member_ref[here, j * trades : (j + 1) * trades] = jnp.where(
                set_ref[me ^ mask] == label, 1.0, 0.0
            ).astype(BF16)
        index = index_ref[place ^ m]
        thresh = jnp.zeros(index.shape, F32)
        for k in range(level_ref.shape[0]):
            thresh = jnp.where(index == k, level_ref[k], thresh)
        thresh_out_ref[:, here] = thresh
        rate_out_ref[:, here] = rate_ref[place ^ m]


def design_kernel(small_ref, design_ref, rows_ref):
    size = small_ref.shape[2]
    for d in range(small_ref.shape[0]):
        here = slice(d * size, (d + 1) * size)
        design_ref[:, here] = small_ref[d]
        turned = small_ref[d].astype(F32).T
        blank = jnp.zeros((size, LANES - 3 * REGRESSORS), F32)
        rows_ref[here] = jnp.concatenate([turned] * 3 + [blank], axis=1).astype(BF16)


def inverse_kernel(ridge, small_ref, inverse_ref):
    square = (REGRESSORS, REGRESSORS)
    gram = jnp.where(rows(square) == lanes(square), ridge, 0.0)
    for d in range(small_ref.shape[0]):
        gram = gram + dot(small_ref[d], small_ref[d], 1, 1)
    inverse_ref[...] = invert(gram)


def joined_weights(refs):
    return jnp.concatenate([ref[...] for ref in refs], axis=0)


def joined_notionals(refs):
    return jnp.concatenate([ref[...].astype(F32) for ref in refs], axis=1)


def forward_kernel(paths, trades, *refs):
    x_refs, refs = refs[:paths], refs[paths:]
    weights, notional = joined_weights(refs[:trades]), joined_notionals(refs[trades : 2 * trades])
    lead_ref, member_ref, value_ref, *moment_refs = refs[2 * trades :]
    start = 0
    for x in x_refs:
        pre_act = dot(x[...], weights, 1, 1)
        value_ref[start : start + x.shape[0]] = (notional * softplus(pre_act)).astype(BF16)
        start += x.shape[0]
    trade_moment = dot(lead_ref[...], value_ref[...])
    parts = dot(three(trade_moment, 0), member_ref[...], 1, 1)
    moment = parts[:REGRESSORS] + parts[REGRESSORS : 2 * REGRESSORS] + parts[2 * REGRESSORS :]
    size = moment.shape[1] // len(moment_refs)
    for m, moment_ref in enumerate(moment_refs):
        moment_ref[...] = moment[:, m * size : (m + 1) * size]


def slope_kernel(paths, trades, *refs):
    x_refs, refs, slope_ref = refs[:paths], refs[paths:], refs[-1]
    weights, notional = joined_weights(refs[:trades]), joined_notionals(refs[trades : 2 * trades])
    start = 0
    for x in x_refs:
        slope_ref[start : start + x.shape[0]] = notional * sigmoid(dot(x[...], weights, 1, 1))
        start += x.shape[0]


def solve_kernel(
    terms, inverse_ref, design_ref, rows_ref, thresh_ref, rate_ref, *refs
):
    solved_ref, turn_ref, total_ref = refs[terms:]
    moment = refs[0][...]
    for ref in refs[1:terms]:
        moment = moment + ref[...]
    size = moment.shape[1]
    inverse = inverse_ref[...]
    coeffs = dot(inverse, moment, precision=PRECISE)
    solved_ref[REGRESSORS:] = coeffs
    is_constant = rows(coeffs.shape) == CONSTANT
    shifted = coeffs - jnp.where(is_constant, thresh_ref[:, :size], 0.0)
    turn_ref[...] = three_rows(-LOG2_E * shifted)
    total_ref[...] = jnp.zeros(total_ref.shape, F32)

    def seeds(here):
        power = jnp.exp2(jnp.minimum(dot(rows_ref[here], turn_ref[...]), 126.0))
        below = 1.0 + power
        seed = pl.reciprocal(below, approx=True)
        seed = (seed * (2.0 - below * seed)).astype(BF16)
        total_ref[...] += dot(design_ref[:, here], seed)

    each_chunk(rows_ref.shape[0], seeds)
    solved_ref[:REGRESSORS] = dot(inverse, total_ref[...] * rate_ref[:, :size], precision=PRECISE)


def joined(refs, part):
    here = slice(part * REGRESSORS, (part + 1) * REGRESSORS)
    return jnp.concatenate([ref[here] for ref in refs], axis=1)


def weight_side_kernel(scale, shares, paths, member_ref, rows_ref, slope_ref, *refs):
    solved_refs, refs = refs[:shares], refs[shares:]
    x_refs, (traded_ref, slopes_ref, *weight_refs) = refs[:paths], refs[paths:]
    traded = dot(three_rows(joined(solved_refs, 0)), member_ref[...]).astype(BF16)
    traded_ref[...] = traded
    group = slopes_ref.shape[0]
    spread = dot(rows_ref[:group], traded).astype(BF16).astype(F32)
    slopes_ref[...] = (slope_ref[...] * spread).astype(BF16)
    basis = jnp.concatenate([x[...] for x in x_refs], axis=0)
    weight = (dot(slopes_ref[...], basis, 0, 0) * scale).astype(BF16)
    start = 0
    for part in weight_refs:
        part[...] = weight[start : start + part.shape[0]]
        start += part.shape[0]


def basis_side_kernel(trades, value_ref, traded_ref, slopes_ref, *refs):
    w_refs, basis_refs = refs[:trades], refs[trades:]
    weights = joined_weights(w_refs)
    start = 0
    for part in basis_refs:
        here = slice(start, start + part.shape[0])
        total = dot(slopes_ref[here], weights)
        wide = dot(value_ref[here], traded_ref[...], 1, 1)
        design = wide
        for k in range(1, 3):
            design = design + pltpu.roll(wide, LANES - k * REGRESSORS, 1)
        design = jnp.where(lanes(design.shape) < CONSTANT, design, 0.0)
        part[:, :LANES] = (total[:, :LANES] + design).astype(BF16)
        part[:, LANES:] = total[:, LANES:].astype(BF16)
        start += part.shape[0]


def loss_kernel(rows_ref, thresh_ref, rate_ref, *refs):
    solved_refs, (loss_ref, own_ref, split_ref, total_ref) = refs[:-4], refs[-4:]
    adjoint = joined(solved_refs, 0)
    coeffs = joined(solved_refs, 1)
    thresh = thresh_ref[...]
    rate = rate_ref[...]
    split_ref[...] = three_rows(coeffs)
    total_ref[...] = jnp.zeros(total_ref.shape, F32)

    def losses(here):
        loss = softplus(dot(rows_ref[here], split_ref[...]) - thresh)
        total_ref[...] += jnp.sum(loss.reshape(-1, *total_ref.shape), axis=0)

    each_chunk(rows_ref.shape[0], losses)
    summed = jnp.sum(jnp.sum(total_ref[...] * rate, axis=0, keepdims=True), axis=1, keepdims=True)
    loss_ref[...] = jnp.broadcast_to(
        summed / (rows_ref.shape[0] * coeffs.shape[1]), loss_ref.shape
    )
    own = rows_ref[: own_ref.shape[0]]
    fitted = dot(own, split_ref[...])
    seed = rate * sigmoid(fitted - thresh)
    rest = seed - dot(own, three_rows(adjoint))
    design = dot(rest, coeffs, 1, 1, PRECISE) - dot(fitted, adjoint, 1, 1, PRECISE)
    blank = jnp.zeros((design.shape[0], LANES - REGRESSORS), F32)
    design = jnp.concatenate([design, blank], axis=1)
    own_ref[...] = jnp.where(lanes(design.shape) < CONSTANT, design, 0.0)


def total(refs):
    out = refs[0][...].astype(F32)
    for ref in refs[1:]:
        out = out + ref[...].astype(F32)
    return out


def sum_kernel(first, own_ref, *refs):
    basis_ref, weight_ref = refs[-2:]
    basis = total(refs[:first])
    basis_ref[:, :LANES] = basis[:, :LANES] + own_ref[...]
    basis_ref[:, LANES:] = basis[:, LANES:]
    weight_ref[...] = total(refs[first:-2])


def call(kernel, outs, *args, name, flops=0, scratch=(), scalars=0):
    size = sum(a.size * a.dtype.itemsize for a in args) + sum(
        math.prod(s) * jnp.dtype(d).itemsize for s, d in outs
    )
    return pl.pallas_call(
        kernel,
        out_shape=[jax.ShapeDtypeStruct(s, d) for s, d in outs],
        in_specs=[pl.BlockSpec(memory_space=pltpu.SMEM)] * scalars
        + [pl.BlockSpec(memory_space=pltpu.VMEM)] * (len(args) - scalars),
        out_specs=[pl.BlockSpec(memory_space=pltpu.VMEM)] * len(outs),
        scratch_shapes=scratch,
        compiler_params=pltpu.CompilerParams(vmem_limit_bytes=VMEM_BYTES),
        cost_estimate=pl.CostEstimate(flops=int(flops), bytes_accessed=int(size), transcendentals=0),
        name=name,
    )(*args)


def shards(
    path_basis, proxy_weight, notional, set_of, threshold_index, threshold_levels, loss_rate
):
    n = lax.axis_size("paths")
    me = lax.axis_index("paths")
    inner_bits, outer_bits = split_bits(n)
    inner, outer = 1 << len(inner_bits), 1 << len(outer_bits)
    path_rows, features = path_basis.shape
    trade_rows = proxy_weight.shape[0]
    paths_all = path_rows * n
    sets = loss_rate.shape[0]
    share = sets // SHARES
    group_paths, group_trades = inner * path_rows, outer * trade_rows

    def swap(x, mask):
        return lax.ppermute(x, "paths", [(d, d ^ mask) for d in range(n)])

    def masks(bits):
        return [
            sum(((m >> j) & 1) << bit for j, bit in enumerate(bits)) for m in range(1 << len(bits))
        ]

    def after(x, *others):
        return lax.optimization_barrier((x, *others))[0]

    def direct(slots, bits):
        return [swap(x, mask) for x, mask in zip(slots[1:], masks(bits)[1:])]

    first_bit = outer_bits[0]
    weights = [proxy_weight, swap(proxy_weight, 1 << first_bit)]
    basis = [path_basis] + direct([path_basis] * inner, inner_bits)
    notionals = [notional, swap(notional, 1 << first_bit)]

    member, thresh, rate, basis[0], own_weight, own_lead = call(
        partial(tables_kernel, masks(outer_bits)),
        [
            ((sets, group_trades), BF16),
            ((1, sets), F32),
            ((1, sets), F32),
            (path_basis.shape, BF16),
            (proxy_weight.shape, BF16),
            ((REGRESSORS, path_rows), BF16),
        ],
        me.astype(jnp.int32).reshape(1),
        threshold_levels,
        set_of.reshape(n, 1, trade_rows),
        threshold_index.reshape(SHARES, 1, share),
        loss_rate.reshape(SHARES, 1, share),
        path_basis,
        proxy_weight,
        name="tables",
        scalars=2,
    )
    for bit in outer_bits[1:]:
        weights = weights + [
            swap(w if k else after(w, member), 1 << bit) for k, w in enumerate(weights)
        ]
        notionals = notionals + [swap(x, 1 << bit) for x in notionals]
    weights[0] = own_weight
    notionals = [x[None, :] for x in notionals]
    (lead,) = call(lead_kernel, [((REGRESSORS, group_paths), BF16)], *basis, name="lead")
    value, *moments = call(
        partial(forward_kernel, inner, outer),
        [((group_paths, group_trades), BF16)] + [((REGRESSORS, share), F32)] * SHARES,
        *basis, *weights, *notionals, lead, member,
        name="forward",
    )
    beside = [own_lead]
    for bit in outer_bits[:-1]:
        beside = beside + [swap(x, 1 << bit) for x in beside]
    beside = beside[1:]
    moment = moments[0] + swap(after(moments[1], *beside), SHARES - 1)
    message = jnp.concatenate([moment] + [x.astype(F32) for x in beside], axis=1)
    arrived = [message] + direct([message] * inner, inner_bits)
    moment = sum(x[:, :share] for x in arrived)
    small = [lead]
    for k in range(len(beside)):
        start = share + k * path_rows
        group = [x[:, start : start + path_rows].astype(BF16) for x in arrived]
        small.append(jnp.concatenate(group, axis=1))
    small = jnp.stack(small)
    small = jnp.concatenate([small, swap(small, SHARES - 1)], axis=0)
    for bit in outer_bits[-2:0:-1]:
        moment = moment + swap(moment, 1 << bit)
    moments = [moment, swap(moment, 1 << first_bit)]
    (inverse,) = call(
        partial(inverse_kernel, RIDGE_SCALE * paths_all),
        [((REGRESSORS, REGRESSORS), F32)],
        small,
        name="inverse",
    )
    design_all, design_rows = call(
        design_kernel,
        [((REGRESSORS, paths_all), BF16), ((paths_all, LANES), BF16)],
        small,
        name="design",
    )
    (solved,) = call(
        partial(solve_kernel, len(moments)),
        [((2 * REGRESSORS, share), F32)],
        inverse, design_all, design_rows, thresh, rate, *moments,
        name="solve",
        scratch=[pltpu.VMEM((LANES, share), BF16), pltpu.VMEM((REGRESSORS, share), F32)],
    )
    solved = [solved, swap(solved, SHARES - 1)]
    (slope,) = call(
        partial(slope_kernel, inner, outer),
        [((group_paths, group_trades), F32)],
        *basis, *weights, *notionals,
        name="slope",
    )
    traded, slopes, *weight_parts = call(
        partial(weight_side_kernel, 1.0 / math.sqrt(paths_all), SHARES, inner),
        [((LANES, group_trades), BF16), ((group_paths, group_trades), BF16)]
        + [((trade_rows, features), BF16)] * outer,
        member, design_rows, slope, *solved, *basis,
        name="weight_side",
    )
    basis_parts = list(
        call(
            partial(basis_side_kernel, outer),
            [((path_rows, features), BF16)] * inner,
            value, traded, slopes, *weights,
            name="basis_side",
        )
    )
    terms = [[part] for part in weight_parts]
    for bit in reversed(outer_bits):
        count = len(terms) // 2
        arrived = None
        for k in reversed(range(count)):
            gone = terms[count + k]
            gone = gone[0] if len(gone) == 1 else sum(g.astype(F32) for g in gone).astype(BF16)
            if arrived is not None:
                gone = after(gone, arrived)
            arrived = swap(gone, 1 << bit)
            terms[k].append(arrived)
            if bit == outer_bits[-1] and k == count - 1:
                basis_parts[1] = after(basis_parts[1], arrived)
        terms = terms[:count]
    weight_terms = terms[0]
    basis_terms = [basis_parts[0]] + direct(basis_parts, inner_bits)
    loss, own_adjoint = call(
        loss_kernel,
        [((8, LANES), F32), ((path_rows, LANES), F32)],
        design_rows, thresh, rate, *solved,
        name="loss",
        scratch=[pltpu.VMEM((LANES, sets), BF16), pltpu.VMEM((8, sets), F32)],
    )
    basis_adjoint, weight_adjoint = call(
        partial(sum_kernel, len(basis_terms)),
        [((path_rows, features), F32), ((trade_rows, features), F32)],
        own_adjoint, *basis_terms, *weight_terms,
        name="sums",
    )
    return (loss[0, :1], basis_adjoint, weight_adjoint)


def solution(mesh):
    placed = (
        P(("groups", "paths"), None),
        P(("groups", "paths"), None),
        P(("groups", "paths")),
        P("groups"),
        P("groups"),
        P("groups"),
        P("groups"),
    )
    return jax.shard_map(
        shards,
        mesh=mesh,
        in_specs=placed,
        out_specs=(P("groups"), P(("groups", "paths"), None), P(("groups", "paths"), None)),
        check_vma=False,
    )
```

```python
import math
from functools import partial

import jax
import jax.numpy as jnp
from jax import lax
from jax.experimental import pallas as pl
from jax.experimental.pallas import tpu as pltpu
from jax.sharding import PartitionSpec as P

REGRESSORS = 32
RIDGE_SCALE = 0.01
PRECISE = lax.Precision.HIGHEST
F32 = jnp.float32
BF16 = jnp.bfloat16
LANES = 128
SUBLANES = 8
CHUNK = 256
VMEM_BYTES = 48 * 1024 * 1024
LOG2_E = math.log2(math.e)
SHARES = 2
CONSTANT = REGRESSORS - 1


def split_bits(size):
    count = size.bit_length() - 1
    half = count // 2
    return list(range(1, half + 1)), list(range(count - 1, half, -1)) + [0]


def dot(a, b, ca=1, cb=0, precision=None):
    return lax.dot_general(
        a, b, (((ca,), (cb,)), ((), ())), precision=precision, preferred_element_type=F32
    )


def three(x, axis):
    high = x.astype(BF16)
    rest = x - high.astype(F32)
    middle = rest.astype(BF16)
    low = (rest - middle.astype(F32)).astype(BF16)
    return jnp.concatenate([high, middle, low], axis=axis)


def three_rows(x):
    blank = jnp.zeros((LANES - 3 * REGRESSORS, x.shape[1]), BF16)
    return jnp.concatenate([three(x, 0), blank], axis=0)


def lanes(shape):
    return lax.broadcasted_iota(jnp.int32, shape, len(shape) - 1)


def rows(shape):
    return lax.broadcasted_iota(jnp.int32, shape, len(shape) - 2)


def softplus(x):
    return jnp.maximum(x, 0.0) + jnp.log1p(jnp.exp(-jnp.abs(x)))


def sigmoid(x):
    small = jnp.exp(-jnp.abs(x))
    return jnp.where(x >= 0.0, 1.0, small) / (1.0 + small)


def each_chunk(size, step):
    count = size // CHUNK

    def body(i, carry):
        step(pl.ds(pl.multiple_of(i * CHUNK, CHUNK), CHUNK))
        return carry

    lax.fori_loop(0, count, body, 0, unroll=count <= 8)


def invert(matrix):
    size = matrix.shape[0]
    work = jnp.concatenate([matrix, jnp.eye(size, dtype=F32)], axis=1)
    shape = (SUBLANES, 2 * size)
    blocks = [work[i : i + SUBLANES] for i in range(0, size, SUBLANES)]
    row = rows(shape)

    def one_row(block, k):
        return jnp.broadcast_to(block[k : k + 1], shape)

    for k in range(0, size, 4):
        at, here = k // SUBLANES, k % SUBLANES
        columns = [
            [jnp.broadcast_to(block[:, k + j : k + j + 1], shape) for block in blocks]
            for j in range(4)
        ]
        p = [[one_row(columns[j][at], here + i) for j in range(4)] for i in range(4)]
        r = [one_row(blocks[at], here + i) for i in range(4)]
        for i in range(4):
            scale = 1.0 / p[i][i]
            r[i] = r[i] * scale
            p[i] = [entry * scale for entry in p[i]]
            for m in range(4):
                if m != i:
                    r[m] = r[m] - p[m][i] * r[i]
                    p[m] = [x - p[m][i] * y if j > i else x for j, (x, y) in enumerate(zip(p[m], p[i]))]
        for i, block in enumerate(blocks):
            for j in range(4):
                block = block - columns[j][i] * r[j]
            if i == at:
                for j in range(4):
                    block = jnp.where(row == here + j, r[j], block)
            blocks[i] = block
    return jnp.concatenate(blocks, axis=0)[:, size:]


def lead_kernel(*refs):
    x_refs, lead_ref = refs[:-1], refs[-1]
    start = 0
    for x in x_refs:
        turned = x[:, :LANES].astype(F32).T[:REGRESSORS]
        turned = jnp.where(rows(turned.shape) == CONSTANT, 1.0, turned)
        lead_ref[:, start : start + x.shape[0]] = turned.astype(BF16)
        start += x.shape[0]


def tables_kernel(
    trade_masks, me_ref, level_ref, set_ref, index_ref, rate_ref, x_ref, w_ref,
    member_ref, thresh_out_ref, rate_out_ref, x_out_ref, w_out_ref,
):
    x_out_ref[...] = x_ref[...]
    w_out_ref[...] = w_ref[...]
    me = me_ref[0]
    shares = index_ref.shape[0]
    place = me & (shares - 1)
    size = member_ref.shape[0] // shares
    trades = set_ref.shape[-1]
    for m in range(shares):
        here = slice(m * size, (m + 1) * size)
        label = (place ^ m) * size + rows((size, 1))
        for j, mask in enumerate(trade_masks):
            member_ref[here, j * trades : (j + 1) * trades] = jnp.where(
                set_ref[me ^ mask] == label, 1.0, 0.0
            ).astype(BF16)
        index = index_ref[place ^ m]
        thresh = jnp.zeros(index.shape, F32)
        for k in range(level_ref.shape[0]):
            thresh = jnp.where(index == k, level_ref[k], thresh)
        thresh_out_ref[:, here] = thresh
        rate_out_ref[:, here] = rate_ref[place ^ m]


def design_kernel(small_ref, design_ref, rows_ref):
    size = small_ref.shape[2]
    for d in range(small_ref.shape[0]):
        here = slice(d * size, (d + 1) * size)
        design_ref[:, here] = small_ref[d]
        turned = small_ref[d].astype(F32).T
        blank = jnp.zeros((size, LANES - 3 * REGRESSORS), F32)
        rows_ref[here] = jnp.concatenate([turned] * 3 + [blank], axis=1).astype(BF16)


def inverse_kernel(ridge, small_ref, inverse_ref):
    square = (REGRESSORS, REGRESSORS)
    gram = jnp.where(rows(square) == lanes(square), ridge, 0.0)
    for d in range(small_ref.shape[0]):
        gram = gram + dot(small_ref[d], small_ref[d], 1, 1)
    inverse_ref[...] = invert(gram)


def joined_weights(refs):
    return jnp.concatenate([ref[...] for ref in refs], axis=0)


def joined_notionals(refs):
    return jnp.concatenate([ref[...].astype(F32) for ref in refs], axis=1)


def forward_kernel(paths, trades, *refs):
    x_refs, refs = refs[:paths], refs[paths:]
    weights, notional = joined_weights(refs[:trades]), joined_notionals(refs[trades : 2 * trades])
    lead_ref, member_ref, value_ref, *moment_refs = refs[2 * trades :]
    start = 0
    for x in x_refs:
        pre_act = dot(x[...], weights, 1, 1)
        value_ref[start : start + x.shape[0]] = (notional * softplus(pre_act)).astype(BF16)
        start += x.shape[0]
    trade_moment = dot(lead_ref[...], value_ref[...])
    parts = dot(three(trade_moment, 0), member_ref[...], 1, 1)
    moment = parts[:REGRESSORS] + parts[REGRESSORS : 2 * REGRESSORS] + parts[2 * REGRESSORS :]
    size = moment.shape[1] // len(moment_refs)
    for m, moment_ref in enumerate(moment_refs):
        moment_ref[...] = moment[:, m * size : (m + 1) * size]


def slope_kernel(paths, trades, *refs):
    x_refs, refs, slope_ref = refs[:paths], refs[paths:], refs[-1]
    weights, notional = joined_weights(refs[:trades]), joined_notionals(refs[trades : 2 * trades])
    start = 0
    for x in x_refs:
        slope_ref[start : start + x.shape[0]] = notional * sigmoid(dot(x[...], weights, 1, 1))
        start += x.shape[0]


def solve_kernel(
    terms, inverse_ref, design_ref, rows_ref, thresh_ref, rate_ref, *refs
):
    solved_ref, turn_ref, total_ref = refs[terms:]
    moment = refs[0][...]
    for ref in refs[1:terms]:
        moment = moment + ref[...]
    size = moment.shape[1]
    inverse = inverse_ref[...]
    coeffs = dot(inverse, moment, precision=PRECISE)
    solved_ref[REGRESSORS:] = coeffs
    is_constant = rows(coeffs.shape) == CONSTANT
    shifted = coeffs - jnp.where(is_constant, thresh_ref[:, :size], 0.0)
    turn_ref[...] = three_rows(-LOG2_E * shifted)
    total_ref[...] = jnp.zeros(total_ref.shape, F32)

    def seeds(here):
        power = jnp.exp2(jnp.minimum(dot(rows_ref[here], turn_ref[...]), 126.0))
        below = 1.0 + power
        seed = pl.reciprocal(below, approx=True)
        seed = (seed * (2.0 - below * seed)).astype(BF16)
        total_ref[...] += dot(design_ref[:, here], seed)

    each_chunk(rows_ref.shape[0], seeds)
    solved_ref[:REGRESSORS] = dot(inverse, total_ref[...] * rate_ref[:, :size], precision=PRECISE)


def joined(refs, part):
    here = slice(part * REGRESSORS, (part + 1) * REGRESSORS)
    return jnp.concatenate([ref[here] for ref in refs], axis=1)


def weight_side_kernel(scale, shares, paths, member_ref, rows_ref, slope_ref, *refs):
    solved_refs, refs = refs[:shares], refs[shares:]
    x_refs, (traded_ref, slopes_ref, *weight_refs) = refs[:paths], refs[paths:]
    traded = dot(three_rows(joined(solved_refs, 0)), member_ref[...]).astype(BF16)
    traded_ref[...] = traded
    group = slopes_ref.shape[0]
    spread = dot(rows_ref[:group], traded).astype(BF16).astype(F32)
    slopes_ref[...] = (slope_ref[...] * spread).astype(BF16)
    basis = jnp.concatenate([x[...] for x in x_refs], axis=0)
    weight = (dot(slopes_ref[...], basis, 0, 0) * scale).astype(BF16)
    start = 0
    for part in weight_refs:
        part[...] = weight[start : start + part.shape[0]]
        start += part.shape[0]


def basis_side_kernel(trades, value_ref, traded_ref, slopes_ref, *refs):
    w_refs, basis_refs = refs[:trades], refs[trades:]
    weights = joined_weights(w_refs)
    start = 0
    for part in basis_refs:
        here = slice(start, start + part.shape[0])
        total = dot(slopes_ref[here], weights)
        wide = dot(value_ref[here], traded_ref[...], 1, 1)
        design = wide
        for k in range(1, 3):
            design = design + pltpu.roll(wide, LANES - k * REGRESSORS, 1)
        design = jnp.where(lanes(design.shape) < CONSTANT, design, 0.0)
        part[:, :LANES] = (total[:, :LANES] + design).astype(BF16)
        part[:, LANES:] = total[:, LANES:].astype(BF16)
        start += part.shape[0]


def loss_kernel(rows_ref, thresh_ref, rate_ref, *refs):
    solved_refs, (loss_ref, own_ref, split_ref, total_ref) = refs[:-4], refs[-4:]
    adjoint = joined(solved_refs, 0)
    coeffs = joined(solved_refs, 1)
    thresh = thresh_ref[...]
    rate = rate_ref[...]
    split_ref[...] = three_rows(coeffs)
    total_ref[...] = jnp.zeros(total_ref.shape, F32)

    def losses(here):
        loss = softplus(dot(rows_ref[here], split_ref[...]) - thresh)
        total_ref[...] += jnp.sum(loss.reshape(-1, *total_ref.shape), axis=0)

    each_chunk(rows_ref.shape[0], losses)
    summed = jnp.sum(jnp.sum(total_ref[...] * rate, axis=0, keepdims=True), axis=1, keepdims=True)
    loss_ref[...] = jnp.broadcast_to(
        summed / (rows_ref.shape[0] * coeffs.shape[1]), loss_ref.shape
    )
    own = rows_ref[: own_ref.shape[0]]
    fitted = dot(own, split_ref[...])
    seed = rate * sigmoid(fitted - thresh)
    rest = seed - dot(own, three_rows(adjoint))
    design = dot(rest, coeffs, 1, 1, PRECISE) - dot(fitted, adjoint, 1, 1, PRECISE)
    blank = jnp.zeros((design.shape[0], LANES - REGRESSORS), F32)
    design = jnp.concatenate([design, blank], axis=1)
    own_ref[...] = jnp.where(lanes(design.shape) < CONSTANT, design, 0.0)


def total(refs):
    out = refs[0][...].astype(F32)
    for ref in refs[1:]:
        out = out + ref[...].astype(F32)
    return out


def sum_kernel(first, own_ref, *refs):
    basis_ref, weight_ref = refs[-2:]
    basis = total(refs[:first])
    basis_ref[:, :LANES] = basis[:, :LANES] + own_ref[...]
    basis_ref[:, LANES:] = basis[:, LANES:]
    weight_ref[...] = total(refs[first:-2])


def call(kernel, outs, *args, name, flops=0, scratch=(), scalars=0):
    size = sum(a.size * a.dtype.itemsize for a in args) + sum(
        math.prod(s) * jnp.dtype(d).itemsize for s, d in outs
    )
    return pl.pallas_call(
        kernel,
        out_shape=[jax.ShapeDtypeStruct(s, d) for s, d in outs],
        in_specs=[pl.BlockSpec(memory_space=pltpu.SMEM)] * scalars
        + [pl.BlockSpec(memory_space=pltpu.VMEM)] * (len(args) - scalars),
        out_specs=[pl.BlockSpec(memory_space=pltpu.VMEM)] * len(outs),
        scratch_shapes=scratch,
        compiler_params=pltpu.CompilerParams(vmem_limit_bytes=VMEM_BYTES),
        cost_estimate=pl.CostEstimate(flops=int(flops), bytes_accessed=int(size), transcendentals=0),
        name=name,
    )(*args)


def shards(
    path_basis, proxy_weight, notional, set_of, threshold_index, threshold_levels, loss_rate
):
    n = lax.axis_size("paths")
    me = lax.axis_index("paths")
    inner_bits, outer_bits = split_bits(n)
    inner, outer = 1 << len(inner_bits), 1 << len(outer_bits)
    path_rows, features = path_basis.shape
    trade_rows = proxy_weight.shape[0]
    paths_all = path_rows * n
    sets = loss_rate.shape[0]
    share = sets // SHARES
    group_paths, group_trades = inner * path_rows, outer * trade_rows

    def swap(x, mask):
        return lax.ppermute(x, "paths", [(d, d ^ mask) for d in range(n)])

    def masks(bits):
        return [
            sum(((m >> j) & 1) << bit for j, bit in enumerate(bits)) for m in range(1 << len(bits))
        ]

    def after(x, *others):
        return lax.optimization_barrier((x, *others))[0]

    def direct(slots, bits):
        return [swap(x, mask) for x, mask in zip(slots[1:], masks(bits)[1:])]

    first_bit = outer_bits[0]
    weights = [proxy_weight, swap(proxy_weight, 1 << first_bit)]
    basis = [path_basis] + direct([path_basis] * inner, inner_bits)
    notionals = [notional, swap(notional, 1 << first_bit)]

    member, thresh, rate, basis[0], own_weight = call(
        partial(tables_kernel, masks(outer_bits)),
        [
            ((sets, group_trades), BF16),
            ((1, sets), F32),
            ((1, sets), F32),
            (path_basis.shape, BF16),
            (proxy_weight.shape, BF16),
        ],
        me.astype(jnp.int32).reshape(1),
        threshold_levels,
        set_of.reshape(n, 1, trade_rows),
        threshold_index.reshape(SHARES, 1, share),
        loss_rate.reshape(SHARES, 1, share),
        path_basis,
        proxy_weight,
        name="tables",
        scalars=2,
    )
    for bit in outer_bits[1:]:
        weights = weights + [
            swap(w if k else after(w, member), 1 << bit) for k, w in enumerate(weights)
        ]
        notionals = notionals + [swap(x, 1 << bit) for x in notionals]
    weights[0] = own_weight
    notionals = [x[None, :] for x in notionals]
    (lead,) = call(lead_kernel, [((REGRESSORS, group_paths), BF16)], *basis, name="lead")
    value, *moments = call(
        partial(forward_kernel, inner, outer),
        [((group_paths, group_trades), BF16)] + [((REGRESSORS, share), F32)] * SHARES,
        *basis, *weights, *notionals, lead, member,
        name="forward",
    )
    moment = moments[0] + swap(moments[1], SHARES - 1)
    lead = after(lead, moment)
    leads = [lead] + direct([lead] * outer, outer_bits)
    for bit in outer_bits[:-1]:
        there = swap(moment, 1 << bit)
        moment = moment + there
    small = jnp.stack(leads)
    moments = [moment] + direct([moment] * inner, inner_bits)
    (inverse,) = call(
        partial(inverse_kernel, RIDGE_SCALE * paths_all),
        [((REGRESSORS, REGRESSORS), F32)],
        small,
        name="inverse",
    )
    design_all, design_rows = call(
        design_kernel,
        [((REGRESSORS, paths_all), BF16), ((paths_all, LANES), BF16)],
        small,
        name="design",
    )
    (solved,) = call(
        partial(solve_kernel, len(moments)),
        [((2 * REGRESSORS, share), F32)],
        inverse, design_all, design_rows, thresh, rate, *moments,
        name="solve",
        scratch=[pltpu.VMEM((LANES, share), BF16), pltpu.VMEM((REGRESSORS, share), F32)],
    )
    solved = [solved, swap(solved, SHARES - 1)]
    (slope,) = call(
        partial(slope_kernel, inner, outer),
        [((group_paths, group_trades), F32)],
        *basis, *weights, *notionals,
        name="slope",
    )
    traded, slopes, *weight_parts = call(
        partial(weight_side_kernel, 1.0 / math.sqrt(paths_all), SHARES, inner),
        [((LANES, group_trades), BF16), ((group_paths, group_trades), BF16)]
        + [((trade_rows, features), BF16)] * outer,
        member, design_rows, slope, *solved, *basis,
        name="weight_side",
    )
    basis_parts = list(
        call(
            partial(basis_side_kernel, outer),
            [((path_rows, features), BF16)] * inner,
            value, traded, slopes, *weights,
            name="basis_side",
        )
    )
    terms = [[part] for part in weight_parts]
    for bit in reversed(outer_bits):
        count = len(terms) // 2
        arrived = None
        for k in reversed(range(count)):
            gone = terms[count + k]
            gone = gone[0] if len(gone) == 1 else sum(g.astype(F32) for g in gone).astype(BF16)
            if arrived is not None:
                gone = after(gone, arrived)
            arrived = swap(gone, 1 << bit)
            terms[k].append(arrived)
            if bit == outer_bits[-1] and k == count - 1:
                basis_parts[1] = after(basis_parts[1], arrived)
        terms = terms[:count]
    weight_terms = terms[0]
    basis_terms = [basis_parts[0]] + direct(basis_parts, inner_bits)
    loss, own_adjoint = call(
        loss_kernel,
        [((8, LANES), F32), ((path_rows, LANES), F32)],
        design_rows, thresh, rate, *solved,
        name="loss",
        scratch=[pltpu.VMEM((LANES, sets), BF16), pltpu.VMEM((8, sets), F32)],
    )
    basis_adjoint, weight_adjoint = call(
        partial(sum_kernel, len(basis_terms)),
        [((path_rows, features), F32), ((trade_rows, features), F32)],
        own_adjoint, *basis_terms, *weight_terms,
        name="sums",
    )
    return (loss[0, :1], basis_adjoint, weight_adjoint)


def solution(mesh):
    placed = (
        P(("groups", "paths"), None),
        P(("groups", "paths"), None),
        P(("groups", "paths")),
        P("groups"),
        P("groups"),
        P("groups"),
        P("groups"),
    )
    return jax.shard_map(
        shards,
        mesh=mesh,
        in_specs=placed,
        out_specs=(P("groups"), P(("groups", "paths"), None), P(("groups", "paths"), None)),
        check_vma=False,
    )
```

```python
import math
from functools import partial

import jax
import jax.numpy as jnp
from jax import lax
from jax.experimental import pallas as pl
from jax.experimental.pallas import tpu as pltpu
from jax.sharding import PartitionSpec as P

REGRESSORS = 32
RIDGE_SCALE = 0.01
PRECISE = lax.Precision.HIGHEST
F32 = jnp.float32
BF16 = jnp.bfloat16
LANES = 128
SUBLANES = 8
CHUNK = 256
VMEM_BYTES = 48 * 1024 * 1024
LOG2_E = math.log2(math.e)
SHARES = 2
CONSTANT = REGRESSORS - 1


def split_bits(size):
    count = size.bit_length() - 1
    half = count // 2
    return list(range(1, half + 1)), list(range(count - 1, half, -1)) + [0]


def dot(a, b, ca=1, cb=0, precision=None):
    return lax.dot_general(
        a, b, (((ca,), (cb,)), ((), ())), precision=precision, preferred_element_type=F32
    )


def three(x, axis):
    high = x.astype(BF16)
    rest = x - high.astype(F32)
    middle = rest.astype(BF16)
    low = (rest - middle.astype(F32)).astype(BF16)
    return jnp.concatenate([high, middle, low], axis=axis)


def three_rows(x):
    blank = jnp.zeros((LANES - 3 * REGRESSORS, x.shape[1]), BF16)
    return jnp.concatenate([three(x, 0), blank], axis=0)


def lanes(shape):
    return lax.broadcasted_iota(jnp.int32, shape, len(shape) - 1)


def rows(shape):
    return lax.broadcasted_iota(jnp.int32, shape, len(shape) - 2)


def softplus(x):
    return jnp.maximum(x, 0.0) + jnp.log1p(jnp.exp(-jnp.abs(x)))


def sigmoid(x):
    small = jnp.exp(-jnp.abs(x))
    return jnp.where(x >= 0.0, 1.0, small) / (1.0 + small)


def each_chunk(size, step, first):
    count = size // CHUNK

    def body(i, carry):
        return step(carry, pl.ds(pl.multiple_of(i * CHUNK, CHUNK), CHUNK))

    return lax.fori_loop(0, count, body, first, unroll=count <= 8)


def invert(matrix):
    size = matrix.shape[0]
    work = jnp.concatenate([matrix, jnp.eye(size, dtype=F32)], axis=1)
    shape = (SUBLANES, 2 * size)
    blocks = [work[i : i + SUBLANES] for i in range(0, size, SUBLANES)]
    row = rows(shape)

    def one_row(block, k):
        return jnp.broadcast_to(block[k : k + 1], shape)

    for k in range(0, size, 4):
        at, here = k // SUBLANES, k % SUBLANES
        columns = [
            [jnp.broadcast_to(block[:, k + j : k + j + 1], shape) for block in blocks]
            for j in range(4)
        ]
        p = [[one_row(columns[j][at], here + i) for j in range(4)] for i in range(4)]
        r = [one_row(blocks[at], here + i) for i in range(4)]
        for i in range(4):
            scale = 1.0 / p[i][i]
            r[i] = r[i] * scale
            p[i] = [entry * scale for entry in p[i]]
            for m in range(4):
                if m != i:
                    r[m] = r[m] - p[m][i] * r[i]
                    p[m] = [x - p[m][i] * y if j > i else x for j, (x, y) in enumerate(zip(p[m], p[i]))]
        for i, block in enumerate(blocks):
            for j in range(4):
                block = block - columns[j][i] * r[j]
            if i == at:
                for j in range(4):
                    block = jnp.where(row == here + j, r[j], block)
            blocks[i] = block
    return jnp.concatenate(blocks, axis=0)[:, size:]


def lead_kernel(*refs):
    x_refs, lead_ref = refs[:-1], refs[-1]
    start = 0
    for x in x_refs:
        turned = x[:, :LANES].astype(F32).T[:REGRESSORS]
        turned = jnp.where(rows(turned.shape) == CONSTANT, 1.0, turned)
        lead_ref[:, start : start + x.shape[0]] = turned.astype(BF16)
        start += x.shape[0]


def tables_kernel(
    trade_masks, me_ref, level_ref, set_ref, index_ref, rate_ref, x_ref, w_ref,
    member_ref, thresh_out_ref, rate_out_ref, x_out_ref, w_out_ref,
):
    x_out_ref[...] = x_ref[...]
    w_out_ref[...] = w_ref[...]
    me = me_ref[0]
    shares = index_ref.shape[0]
    place = me & (shares - 1)
    size = member_ref.shape[0] // shares
    trades = set_ref.shape[-1]
    for m in range(shares):
        here = slice(m * size, (m + 1) * size)
        label = (place ^ m) * size + rows((size, 1))
        for j, mask in enumerate(trade_masks):
            member_ref[here, j * trades : (j + 1) * trades] = jnp.where(
                set_ref[me ^ mask] == label, 1.0, 0.0
            ).astype(BF16)
        index = index_ref[place ^ m]
        thresh = jnp.zeros(index.shape, F32)
        for k in range(level_ref.shape[0]):
            thresh = jnp.where(index == k, level_ref[k], thresh)
        thresh_out_ref[:, here] = thresh
        rate_out_ref[:, here] = rate_ref[place ^ m]


def design_kernel(small_ref, design_ref, rows_ref):
    size = small_ref.shape[2]
    for d in range(small_ref.shape[0]):
        here = slice(d * size, (d + 1) * size)
        design_ref[:, here] = small_ref[d]
        turned = small_ref[d].astype(F32).T
        blank = jnp.zeros((size, LANES - 3 * REGRESSORS), F32)
        rows_ref[here] = jnp.concatenate([turned] * 3 + [blank], axis=1).astype(BF16)


def inverse_kernel(ridge, small_ref, inverse_ref):
    square = (REGRESSORS, REGRESSORS)
    gram = jnp.where(rows(square) == lanes(square), ridge, 0.0)
    for d in range(small_ref.shape[0]):
        gram = gram + dot(small_ref[d], small_ref[d], 1, 1)
    inverse_ref[...] = invert(gram)


def joined_weights(refs):
    return jnp.concatenate([ref[...] for ref in refs], axis=0)


def joined_notionals(refs):
    return jnp.concatenate([ref[...].astype(F32) for ref in refs], axis=1)


def forward_kernel(paths, trades, *refs):
    x_refs, refs = refs[:paths], refs[paths:]
    weights, notional = joined_weights(refs[:trades]), joined_notionals(refs[trades : 2 * trades])
    lead_ref, member_ref, value_ref, *moment_refs = refs[2 * trades :]
    start = 0
    for x in x_refs:
        pre_act = dot(x[...], weights, 1, 1)
        value_ref[start : start + x.shape[0]] = (notional * softplus(pre_act)).astype(BF16)
        start += x.shape[0]
    trade_moment = dot(lead_ref[...], value_ref[...])
    parts = dot(three(trade_moment, 0), member_ref[...], 1, 1)
    moment = parts[:REGRESSORS] + parts[REGRESSORS : 2 * REGRESSORS] + parts[2 * REGRESSORS :]
    size = moment.shape[1] // len(moment_refs)
    for m, moment_ref in enumerate(moment_refs):
        moment_ref[...] = moment[:, m * size : (m + 1) * size]


def slope_kernel(paths, trades, *refs):
    x_refs, refs, slope_ref = refs[:paths], refs[paths:], refs[-1]
    weights, notional = joined_weights(refs[:trades]), joined_notionals(refs[trades : 2 * trades])
    start = 0
    for x in x_refs:
        slope_ref[start : start + x.shape[0]] = notional * sigmoid(dot(x[...], weights, 1, 1))
        start += x.shape[0]


def solve_kernel(
    terms, inverse_ref, design_ref, rows_ref, thresh_ref, rate_ref, *refs
):
    solved_ref, turn_ref = refs[terms:]
    moment = refs[0][...]
    for ref in refs[1:terms]:
        moment = moment + ref[...]
    size = moment.shape[1]
    inverse = inverse_ref[...]
    coeffs = dot(inverse, moment, precision=PRECISE)
    solved_ref[REGRESSORS:] = coeffs
    is_constant = rows(coeffs.shape) == CONSTANT
    shifted = coeffs - jnp.where(is_constant, thresh_ref[:, :size], 0.0)
    turn_ref[...] = three_rows(-LOG2_E * shifted)

    def seeds(total, here):
        power = jnp.exp2(jnp.minimum(dot(rows_ref[here], turn_ref[...]), 126.0))
        below = 1.0 + power
        seed = pl.reciprocal(below, approx=True)
        seed = (seed * (2.0 - below * seed)).astype(BF16)
        return total + dot(design_ref[:, here], seed)

    total = each_chunk(rows_ref.shape[0], seeds, jnp.zeros((REGRESSORS, size), F32))
    solved_ref[:REGRESSORS] = dot(inverse, total * rate_ref[:, :size], precision=PRECISE)


def joined(refs, part):
    here = slice(part * REGRESSORS, (part + 1) * REGRESSORS)
    return jnp.concatenate([ref[here] for ref in refs], axis=1)


def weight_side_kernel(scale, shares, paths, member_ref, rows_ref, slope_ref, *refs):
    solved_refs, refs = refs[:shares], refs[shares:]
    x_refs, (traded_ref, slopes_ref, *weight_refs) = refs[:paths], refs[paths:]
    traded = dot(three_rows(joined(solved_refs, 0)), member_ref[...]).astype(BF16)
    traded_ref[...] = traded
    group = slopes_ref.shape[0]
    spread = dot(rows_ref[:group], traded).astype(BF16).astype(F32)
    slopes_ref[...] = (slope_ref[...] * spread).astype(BF16)
    basis = jnp.concatenate([x[...] for x in x_refs], axis=0)
    weight = (dot(slopes_ref[...], basis, 0, 0) * scale).astype(BF16)
    start = 0
    for part in weight_refs:
        part[...] = weight[start : start + part.shape[0]]
        start += part.shape[0]


def basis_side_kernel(trades, value_ref, traded_ref, slopes_ref, *refs):
    w_refs, basis_refs = refs[:trades], refs[trades:]
    weights = joined_weights(w_refs)
    start = 0
    for part in basis_refs:
        here = slice(start, start + part.shape[0])
        total = dot(slopes_ref[here], weights)
        wide = dot(value_ref[here], traded_ref[...], 1, 1)
        design = wide
        for k in range(1, 3):
            design = design + pltpu.roll(wide, LANES - k * REGRESSORS, 1)
        design = jnp.where(lanes(design.shape) < CONSTANT, design, 0.0)
        part[:, :LANES] = (total[:, :LANES] + design).astype(BF16)
        part[:, LANES:] = total[:, LANES:].astype(BF16)
        start += part.shape[0]


def loss_kernel(rows_ref, thresh_ref, rate_ref, *refs):
    solved_refs, (loss_ref, own_ref, split_ref) = refs[:-3], refs[-3:]
    adjoint = joined(solved_refs, 0)
    coeffs = joined(solved_refs, 1)
    thresh = thresh_ref[...]
    rate = rate_ref[...]
    split_ref[...] = three_rows(coeffs)

    def losses(total, here):
        loss = softplus(dot(rows_ref[here], split_ref[...]) - thresh)
        return total + jnp.sum(loss.reshape(-1, *total.shape), axis=0)

    total = each_chunk(rows_ref.shape[0], losses, jnp.zeros((SUBLANES, coeffs.shape[1]), F32))
    summed = jnp.sum(jnp.sum(total * rate, axis=0, keepdims=True), axis=1, keepdims=True)
    loss_ref[...] = jnp.broadcast_to(
        summed / (rows_ref.shape[0] * coeffs.shape[1]), loss_ref.shape
    )
    own = rows_ref[: own_ref.shape[0]]
    fitted = dot(own, split_ref[...])
    seed = rate * sigmoid(fitted - thresh)
    rest = seed - dot(own, three_rows(adjoint))
    design = dot(rest, coeffs, 1, 1, PRECISE) - dot(fitted, adjoint, 1, 1, PRECISE)
    blank = jnp.zeros((design.shape[0], LANES - REGRESSORS), F32)
    design = jnp.concatenate([design, blank], axis=1)
    own_ref[...] = jnp.where(lanes(design.shape) < CONSTANT, design, 0.0)


def total(refs):
    out = refs[0][...].astype(F32)
    for ref in refs[1:]:
        out = out + ref[...].astype(F32)
    return out


def sum_kernel(first, own_ref, *refs):
    basis_ref, weight_ref = refs[-2:]
    basis = total(refs[:first])
    basis_ref[:, :LANES] = basis[:, :LANES] + own_ref[...]
    basis_ref[:, LANES:] = basis[:, LANES:]
    weight_ref[...] = total(refs[first:-2])


def call(kernel, outs, *args, name, flops=0, scratch=(), scalars=0):
    size = sum(a.size * a.dtype.itemsize for a in args) + sum(
        math.prod(s) * jnp.dtype(d).itemsize for s, d in outs
    )
    return pl.pallas_call(
        kernel,
        out_shape=[jax.ShapeDtypeStruct(s, d) for s, d in outs],
        in_specs=[pl.BlockSpec(memory_space=pltpu.SMEM)] * scalars
        + [pl.BlockSpec(memory_space=pltpu.VMEM)] * (len(args) - scalars),
        out_specs=[pl.BlockSpec(memory_space=pltpu.VMEM)] * len(outs),
        scratch_shapes=scratch,
        compiler_params=pltpu.CompilerParams(vmem_limit_bytes=VMEM_BYTES),
        cost_estimate=pl.CostEstimate(flops=int(flops), bytes_accessed=int(size), transcendentals=0),
        name=name,
    )(*args)


def shards(
    path_basis, proxy_weight, notional, set_of, threshold_index, threshold_levels, loss_rate
):
    n = lax.axis_size("paths")
    me = lax.axis_index("paths")
    inner_bits, outer_bits = split_bits(n)
    inner, outer = 1 << len(inner_bits), 1 << len(outer_bits)
    path_rows, features = path_basis.shape
    trade_rows = proxy_weight.shape[0]
    paths_all = path_rows * n
    sets = loss_rate.shape[0]
    share = sets // SHARES
    group_paths, group_trades = inner * path_rows, outer * trade_rows

    def swap(x, mask):
        return lax.ppermute(x, "paths", [(d, d ^ mask) for d in range(n)])

    def masks(bits):
        return [
            sum(((m >> j) & 1) << bit for j, bit in enumerate(bits)) for m in range(1 << len(bits))
        ]

    def after(x, *others):
        return lax.optimization_barrier((x, *others))[0]

    def direct(slots, masks):
        return [swap(x, mask) for x, mask in zip(slots[1:], masks[1:])]

    outer_masks = masks(outer_bits)
    inner_masks = [0] + masks(inner_bits)[:0:-1]
    first_bit = outer_bits[0]
    weights = [proxy_weight, swap(proxy_weight, 1 << first_bit)]
    basis = [path_basis] + direct([path_basis] * inner, inner_masks)
    notionals = [notional, swap(notional, 1 << first_bit)]

    member, thresh, rate, basis[0], own_weight = call(
        partial(tables_kernel, outer_masks),
        [
            ((sets, group_trades), BF16),
            ((1, sets), F32),
            ((1, sets), F32),
            (path_basis.shape, BF16),
            (proxy_weight.shape, BF16),
        ],
        me.astype(jnp.int32).reshape(1),
        threshold_levels,
        set_of.reshape(n, 1, trade_rows),
        threshold_index.reshape(SHARES, 1, share),
        loss_rate.reshape(SHARES, 1, share),
        path_basis,
        proxy_weight,
        name="tables",
        scalars=2,
    )
    for bit in outer_bits[1:]:
        weights = weights + [
            swap(w if k else after(w, member), 1 << bit) for k, w in enumerate(weights)
        ]
        notionals = notionals + [swap(x, 1 << bit) for x in notionals]
    weights[0] = own_weight
    notionals = [x[None, :] for x in notionals]
    (lead,) = call(lead_kernel, [((REGRESSORS, group_paths), BF16)], *basis, name="lead")
    value, *moments = call(
        partial(forward_kernel, inner, outer),
        [((group_paths, group_trades), BF16)] + [((REGRESSORS, share), F32)] * SHARES,
        *basis, *weights, *notionals, lead, member,
        name="forward",
    )
    moment = moments[0] + swap(moments[1], SHARES - 1)
    lead = after(lead, moment)
    leads = [lead] + direct([lead] * outer, outer_masks)
    for bit in outer_bits[:-1]:
        there = swap(moment, 1 << bit)
        moment = moment + there
    small = jnp.stack(leads)
    moments = [moment] + direct([moment] * inner, inner_masks)
    (inverse,) = call(
        partial(inverse_kernel, RIDGE_SCALE * paths_all),
        [((REGRESSORS, REGRESSORS), F32)],
        small,
        name="inverse",
    )
    design_all, design_rows = call(
        design_kernel,
        [((REGRESSORS, paths_all), BF16), ((paths_all, LANES), BF16)],
        small,
        name="design",
    )
    (solved,) = call(
        partial(solve_kernel, len(moments)),
        [((2 * REGRESSORS, share), F32)],
        inverse, design_all, design_rows, thresh, rate, *moments,
        name="solve",
        scratch=[pltpu.VMEM((LANES, share), BF16)],
    )
    solved = [solved, swap(solved, SHARES - 1)]
    (slope,) = call(
        partial(slope_kernel, inner, outer),
        [((group_paths, group_trades), F32)],
        *basis, *weights, *notionals,
        name="slope",
    )
    traded, slopes, *weight_parts = call(
        partial(weight_side_kernel, 1.0 / math.sqrt(paths_all), SHARES, inner),
        [((LANES, group_trades), BF16), ((group_paths, group_trades), BF16)]
        + [((trade_rows, features), BF16)] * outer,
        member, design_rows, slope, *solved, *basis,
        name="weight_side",
    )
    basis_parts = list(
        call(
            partial(basis_side_kernel, outer),
            [((path_rows, features), BF16)] * inner,
            value, traded, slopes, *weights,
            name="basis_side",
        )
    )
    terms = [[part] for part in weight_parts]
    for bit in reversed(outer_bits):
        count = len(terms) // 2
        arrived = None
        for k in reversed(range(count)):
            gone = terms[count + k]
            gone = gone[0] if len(gone) == 1 else sum(g.astype(F32) for g in gone).astype(BF16)
            if arrived is not None:
                gone = after(gone, arrived)
            arrived = swap(gone, 1 << bit)
            terms[k].append(arrived)
            if bit == outer_bits[-1] and k == count - 1:
                basis_parts[-1] = after(basis_parts[-1], arrived)
        terms = terms[:count]
    weight_terms = terms[0]
    basis_terms = [basis_parts[0]] + direct(basis_parts, inner_masks)
    loss, own_adjoint = call(
        loss_kernel,
        [((8, LANES), F32), ((path_rows, LANES), F32)],
        design_rows, thresh, rate, *solved,
        name="loss",
        scratch=[pltpu.VMEM((LANES, sets), BF16)],
    )
    basis_adjoint, weight_adjoint = call(
        partial(sum_kernel, len(basis_terms)),
        [((path_rows, features), F32), ((trade_rows, features), F32)],
        own_adjoint, *basis_terms, *weight_terms,
        name="sums",
    )
    return (loss[0, :1], basis_adjoint, weight_adjoint)


def solution(mesh):
    placed = (
        P(("groups", "paths"), None),
        P(("groups", "paths"), None),
        P(("groups", "paths")),
        P("groups"),
        P("groups"),
        P("groups"),
        P("groups"),
    )
    return jax.shard_map(
        shards,
        mesh=mesh,
        in_specs=placed,
        out_specs=(P("groups"), P(("groups", "paths"), None), P(("groups", "paths"), None)),
        check_vma=False,
    )
```

```python
import math
from functools import partial

import jax
import jax.numpy as jnp
from jax import lax
from jax.experimental import pallas as pl
from jax.experimental.pallas import tpu as pltpu
from jax.sharding import PartitionSpec as P

REGRESSORS = 32
RIDGE_SCALE = 0.01
PRECISE = lax.Precision.HIGHEST
F32 = jnp.float32
BF16 = jnp.bfloat16
LANES = 128
SUBLANES = 8
CHUNK = 256
VMEM_BYTES = 48 * 1024 * 1024
LOG2_E = math.log2(math.e)
SHARES = 2
CONSTANT = REGRESSORS - 1


def split_bits(size):
    count = size.bit_length() - 1
    half = count // 2
    return list(range(1, half + 1)), list(range(count - 1, half, -1)) + [0]


def dot(a, b, ca=1, cb=0, precision=None):
    return lax.dot_general(
        a, b, (((ca,), (cb,)), ((), ())), precision=precision, preferred_element_type=F32
    )


def three(x, axis):
    high = x.astype(BF16)
    rest = x - high.astype(F32)
    middle = rest.astype(BF16)
    low = (rest - middle.astype(F32)).astype(BF16)
    return jnp.concatenate([high, middle, low], axis=axis)


def three_rows(x):
    blank = jnp.zeros((LANES - 3 * REGRESSORS, x.shape[1]), BF16)
    return jnp.concatenate([three(x, 0), blank], axis=0)


def lanes(shape):
    return lax.broadcasted_iota(jnp.int32, shape, len(shape) - 1)


def rows(shape):
    return lax.broadcasted_iota(jnp.int32, shape, len(shape) - 2)


def softplus(x):
    return jnp.maximum(x, 0.0) + jnp.log1p(jnp.exp(-jnp.abs(x)))


def sigmoid(x):
    small = jnp.exp(-jnp.abs(x))
    return jnp.where(x >= 0.0, 1.0, small) / (1.0 + small)


def each_chunk(size, step, first):
    count = size // CHUNK

    def body(i, carry):
        return step(carry, pl.ds(pl.multiple_of(i * CHUNK, CHUNK), CHUNK))

    return lax.fori_loop(0, count, body, first, unroll=count <= 8)


def invert(matrix):
    size = matrix.shape[0]
    work = jnp.concatenate([matrix, jnp.eye(size, dtype=F32)], axis=1)
    shape = (SUBLANES, 2 * size)
    blocks = [work[i : i + SUBLANES] for i in range(0, size, SUBLANES)]
    row = rows(shape)

    def row_of(block, k):
        return jnp.broadcast_to(block[k : k + 1], shape)

    for k in range(0, size, 4):
        at, here = k // SUBLANES, k % SUBLANES
        columns = [
            [jnp.broadcast_to(block[:, k + j : k + j + 1], shape) for block in blocks]
            for j in range(4)
        ]
        p = [[row_of(columns[j][at], here + i) for j in range(4)] for i in range(4)]
        r = [row_of(blocks[at], here + i) for i in range(4)]
        for i in range(4):
            scale = 1.0 / p[i][i]
            r[i] = r[i] * scale
            p[i] = [entry * scale for entry in p[i]]
            for m in range(4):
                if m != i:
                    r[m] = r[m] - p[m][i] * r[i]
                    p[m] = [x - p[m][i] * y if j > i else x for j, (x, y) in enumerate(zip(p[m], p[i]))]
        for i, block in enumerate(blocks):
            for j in range(4):
                block = block - columns[j][i] * r[j]
            if i == at:
                for j in range(4):
                    block = jnp.where(row == here + j, r[j], block)
            blocks[i] = block
    return jnp.concatenate(blocks, axis=0)[:, size:]


def lead_kernel(*refs):
    x_refs, lead_ref = refs[:-1], refs[-1]
    start = 0
    for x in x_refs:
        turned = x[:, :LANES].astype(F32).T[:REGRESSORS]
        turned = jnp.where(rows(turned.shape) == CONSTANT, 1.0, turned)
        lead_ref[:, start : start + x.shape[0]] = turned.astype(BF16)
        start += x.shape[0]


def tables_kernel(
    trade_masks, me_ref, level_ref, set_ref, index_ref, rate_ref, x_ref, w_ref,
    notional_ref, member_ref, thresh_out_ref, rate_out_ref, x_out_ref, w_out_ref, notional_out_ref,
):
    notional_out_ref[...] = notional_ref[...]
    x_out_ref[...] = x_ref[...]
    w_out_ref[...] = w_ref[...]
    me = me_ref[0]
    shares = index_ref.shape[0]
    place = me & (shares - 1)
    size = member_ref.shape[0] // shares
    trades = set_ref.shape[-1]
    for m in range(shares):
        here = slice(m * size, (m + 1) * size)
        label = (place ^ m) * size + rows((size, 1))
        for j, mask in enumerate(trade_masks):
            member_ref[here, j * trades : (j + 1) * trades] = jnp.where(
                set_ref[me ^ mask] == label, 1.0, 0.0
            ).astype(BF16)
        index = index_ref[place ^ m]
        thresh = jnp.zeros(index.shape, F32)
        for k in range(level_ref.shape[0]):
            thresh = jnp.where(index == k, level_ref[k], thresh)
        thresh_out_ref[:, here] = thresh
        rate_out_ref[:, here] = rate_ref[place ^ m]


def design_kernel(small_ref, design_ref, rows_ref):
    size = small_ref.shape[2]
    for d in range(small_ref.shape[0]):
        here = slice(d * size, (d + 1) * size)
        design_ref[:, here] = small_ref[d]
        turned = small_ref[d].astype(F32).T
        blank = jnp.zeros((size, LANES - 3 * REGRESSORS), F32)
        rows_ref[here] = jnp.concatenate([turned] * 3 + [blank], axis=1).astype(BF16)


def inverse_kernel(ridge, small_ref, inverse_ref):
    square = (REGRESSORS, REGRESSORS)
    gram = jnp.where(rows(square) == lanes(square), ridge, 0.0)
    for d in range(small_ref.shape[0]):
        gram = gram + dot(small_ref[d], small_ref[d], 1, 1)
    inverse_ref[...] = invert(gram)


def joined_weights(refs):
    return jnp.concatenate([ref[...] for ref in refs], axis=0)


def one_row(ref):
    wide = ref[...].astype(F32)
    return jnp.concatenate([wide[k : k + 1] for k in range(wide.shape[0])], axis=1)


def forward_kernel(paths, trades, *refs):
    x_refs, refs = refs[:paths], refs[paths:]
    weights, notional = joined_weights(refs[:trades]), one_row(refs[trades])
    lead_ref, member_ref, value_ref, *moment_refs = refs[trades + 1 :]
    start = 0
    for x in x_refs:
        pre_act = dot(x[...], weights, 1, 1)
        value_ref[start : start + x.shape[0]] = (notional * softplus(pre_act)).astype(BF16)
        start += x.shape[0]
    trade_moment = dot(lead_ref[...], value_ref[...])
    parts = dot(three(trade_moment, 0), member_ref[...], 1, 1)
    moment = parts[:REGRESSORS] + parts[REGRESSORS : 2 * REGRESSORS] + parts[2 * REGRESSORS :]
    size = moment.shape[1] // len(moment_refs)
    for m, moment_ref in enumerate(moment_refs):
        moment_ref[...] = moment[:, m * size : (m + 1) * size]


def slope_kernel(paths, trades, *refs):
    x_refs, refs, slope_ref = refs[:paths], refs[paths:], refs[-1]
    weights, notional = joined_weights(refs[:trades]), one_row(refs[trades])
    start = 0
    for x in x_refs:
        slope_ref[start : start + x.shape[0]] = notional * sigmoid(dot(x[...], weights, 1, 1))
        start += x.shape[0]


def solve_kernel(
    terms, inverse_ref, design_ref, rows_ref, thresh_ref, rate_ref, *refs
):
    solved_ref, turn_ref = refs[terms:]
    moment = refs[0][...]
    for ref in refs[1:terms]:
        moment = moment + ref[...]
    size = moment.shape[1]
    inverse = inverse_ref[...]
    coeffs = dot(inverse, moment, precision=PRECISE)
    solved_ref[REGRESSORS:] = coeffs
    is_constant = rows(coeffs.shape) == CONSTANT
    shifted = coeffs - jnp.where(is_constant, thresh_ref[:, :size], 0.0)
    turn_ref[...] = three_rows(-LOG2_E * shifted)

    def seeds(total, here):
        power = jnp.exp2(jnp.minimum(dot(rows_ref[here], turn_ref[...]), 126.0))
        below = 1.0 + power
        seed = pl.reciprocal(below, approx=True)
        seed = (seed * (2.0 - below * seed)).astype(BF16)
        return total + dot(design_ref[:, here], seed)

    total = each_chunk(rows_ref.shape[0], seeds, jnp.zeros((REGRESSORS, size), F32))
    solved_ref[:REGRESSORS] = dot(inverse, total * rate_ref[:, :size], precision=PRECISE)


def joined(refs, part):
    here = slice(part * REGRESSORS, (part + 1) * REGRESSORS)
    return jnp.concatenate([ref[here] for ref in refs], axis=1)


def weight_side_kernel(scale, shares, paths, member_ref, rows_ref, slope_ref, *refs):
    solved_refs, refs = refs[:shares], refs[shares:]
    x_refs, (traded_ref, slopes_ref, *weight_refs) = refs[:paths], refs[paths:]
    traded = dot(three_rows(joined(solved_refs, 0)), member_ref[...]).astype(BF16)
    traded_ref[...] = traded
    group = slopes_ref.shape[0]
    spread = dot(rows_ref[:group], traded).astype(BF16).astype(F32)
    slopes_ref[...] = (slope_ref[...] * spread).astype(BF16)
    basis = jnp.concatenate([x[...] for x in x_refs], axis=0)
    weight = (dot(slopes_ref[...], basis, 0, 0) * scale).astype(BF16)
    start = 0
    for part in weight_refs:
        part[...] = weight[start : start + part.shape[0]]
        start += part.shape[0]


def basis_side_kernel(trades, value_ref, traded_ref, slopes_ref, *refs):
    w_refs, basis_refs = refs[:trades], refs[trades:]
    weights = joined_weights(w_refs)
    start = 0
    for part in basis_refs:
        here = slice(start, start + part.shape[0])
        total = dot(slopes_ref[here], weights)
        wide = dot(value_ref[here], traded_ref[...], 1, 1)
        design = wide
        for k in range(1, 3):
            design = design + pltpu.roll(wide, LANES - k * REGRESSORS, 1)
        design = jnp.where(lanes(design.shape) < CONSTANT, design, 0.0)
        part[:, :LANES] = (total[:, :LANES] + design).astype(BF16)
        part[:, LANES:] = total[:, LANES:].astype(BF16)
        start += part.shape[0]


def loss_kernel(rows_ref, thresh_ref, rate_ref, *refs):
    solved_refs, (loss_ref, own_ref, split_ref) = refs[:-3], refs[-3:]
    adjoint = joined(solved_refs, 0)
    coeffs = joined(solved_refs, 1)
    thresh = thresh_ref[...]
    rate = rate_ref[...]
    split_ref[...] = three_rows(coeffs)

    def losses(total, here):
        loss = softplus(dot(rows_ref[here], split_ref[...]) - thresh)
        return total + jnp.sum(loss.reshape(-1, *total.shape), axis=0)

    total = each_chunk(rows_ref.shape[0], losses, jnp.zeros((SUBLANES, coeffs.shape[1]), F32))
    summed = jnp.sum(jnp.sum(total * rate, axis=0, keepdims=True), axis=1, keepdims=True)
    loss_ref[...] = jnp.broadcast_to(
        summed / (rows_ref.shape[0] * coeffs.shape[1]), loss_ref.shape
    )
    own = rows_ref[: own_ref.shape[0]]
    fitted = dot(own, split_ref[...])
    seed = rate * sigmoid(fitted - thresh)
    rest = seed - dot(own, three_rows(adjoint))
    design = dot(rest, coeffs, 1, 1, PRECISE) - dot(fitted, adjoint, 1, 1, PRECISE)
    blank = jnp.zeros((design.shape[0], LANES - REGRESSORS), F32)
    design = jnp.concatenate([design, blank], axis=1)
    own_ref[...] = jnp.where(lanes(design.shape) < CONSTANT, design, 0.0)


def sum_kernel(first, own_ref, *refs):
    *terms, basis_ref, weight_ref, basis_scratch, weight_scratch, sems = refs

    def total(refs, here):
        out = refs[0][here].astype(F32)
        for ref in refs[1:]:
            out = out + ref[here].astype(F32)
        return out

    copies = []

    def send(source, target, here):
        copy = pltpu.make_async_copy(source.at[here], target.at[here], sems.at[len(copies)])
        copy.start()
        copies.append(copy)

    parts = sems.shape[0] // 2
    for k in range(parts):
        size = weight_ref.shape[0] // parts
        here = slice(k * size, (k + 1) * size)
        weight_scratch[here] = total(terms[first:], here)
        send(weight_scratch, weight_ref, pl.ds(k * size, size))
    for k in range(parts):
        size = basis_ref.shape[0] // parts
        here = slice(k * size, (k + 1) * size)
        basis = total(terms[:first], here)
        basis_scratch[here, :LANES] = basis[:, :LANES] + own_ref[here]
        basis_scratch[here, LANES:] = basis[:, LANES:]
        send(basis_scratch, basis_ref, pl.ds(k * size, size))
    for copy in copies:
        copy.wait()


def call(kernel, outs, *args, name, flops=0, scratch=(), scalars=0, far=False):
    size = sum(a.size * a.dtype.itemsize for a in args) + sum(
        math.prod(s) * jnp.dtype(d).itemsize for s, d in outs
    )
    return pl.pallas_call(
        kernel,
        out_shape=[jax.ShapeDtypeStruct(s, d) for s, d in outs],
        in_specs=[pl.BlockSpec(memory_space=pltpu.SMEM)] * scalars
        + [pl.BlockSpec(memory_space=pltpu.VMEM)] * (len(args) - scalars),
        out_specs=[pl.BlockSpec(memory_space=pl.ANY if far else pltpu.VMEM)] * len(outs),
        scratch_shapes=scratch,
        compiler_params=pltpu.CompilerParams(vmem_limit_bytes=VMEM_BYTES),
        cost_estimate=pl.CostEstimate(flops=int(flops), bytes_accessed=int(size), transcendentals=0),
        name=name,
    )(*args)


def shards(
    path_basis, proxy_weight, notional, set_of, threshold_index, threshold_levels, loss_rate
):
    n = lax.axis_size("paths")
    me = lax.axis_index("paths")
    inner_bits, outer_bits = split_bits(n)
    inner, outer = 1 << len(inner_bits), 1 << len(outer_bits)
    path_rows, features = path_basis.shape
    trade_rows = proxy_weight.shape[0]
    paths_all = path_rows * n
    sets = loss_rate.shape[0]
    share = sets // SHARES
    group_paths, group_trades = inner * path_rows, outer * trade_rows

    def swap(x, mask):
        return lax.ppermute(x, "paths", [(d, d ^ mask) for d in range(n)])

    def masks(bits):
        return [
            sum(((m >> j) & 1) << bit for j, bit in enumerate(bits)) for m in range(1 << len(bits))
        ]

    def after(x, *others):
        return lax.optimization_barrier((x, *others))[0]

    def direct(slots, masks):
        return [swap(x, mask) for x, mask in zip(slots[1:], masks[1:])]

    outer_masks = masks(outer_bits)
    inner_masks = [0] + masks(inner_bits)[:0:-1]
    first_bit = outer_bits[0]
    weights = [proxy_weight, swap(proxy_weight, 1 << first_bit)]
    basis = [path_basis] + direct([path_basis] * inner, inner_masks)
    notionals = [notional[None, :], swap(notional, 1 << first_bit)[None, :]]

    member, thresh, rate, basis[0], own_weight, notionals[0] = call(
        partial(tables_kernel, outer_masks),
        [
            ((sets, group_trades), BF16),
            ((1, sets), F32),
            ((1, sets), F32),
            (path_basis.shape, BF16),
            (proxy_weight.shape, BF16),
            ((1, trade_rows), BF16),
        ],
        me.astype(jnp.int32).reshape(1),
        threshold_levels,
        set_of.reshape(n, 1, trade_rows),
        threshold_index.reshape(SHARES, 1, share),
        loss_rate.reshape(SHARES, 1, share),
        path_basis,
        proxy_weight,
        notionals[0],
        name="tables",
        scalars=2,
    )
    notionals = after(jnp.concatenate(notionals, axis=0), basis[-1])
    for bit in outer_bits[1:]:
        weights = weights + [
            swap(w if k else after(w, member), 1 << bit) for k, w in enumerate(weights)
        ]
        notionals = jnp.concatenate([notionals, swap(notionals, 1 << bit)], axis=0)
    weights[0] = own_weight
    (lead,) = call(lead_kernel, [((REGRESSORS, group_paths), BF16)], *basis, name="lead")
    value, *moments = call(
        partial(forward_kernel, inner, outer),
        [((group_paths, group_trades), BF16)] + [((REGRESSORS, share), F32)] * SHARES,
        *basis, *weights, notionals, lead, member,
        name="forward",
    )
    moment = moments[0] + swap(moments[1], SHARES - 1)
    lead = after(lead, moment)
    leads = [lead] + direct([lead] * outer, outer_masks)
    for bit in outer_bits[:-1]:
        there = swap(moment, 1 << bit)
        moment = moment + there
    small = jnp.stack(leads)
    moments = [moment] + direct([moment] * inner, inner_masks)
    (inverse,) = call(
        partial(inverse_kernel, RIDGE_SCALE * paths_all),
        [((REGRESSORS, REGRESSORS), F32)],
        small,
        name="inverse",
    )
    design_all, design_rows = call(
        design_kernel,
        [((REGRESSORS, paths_all), BF16), ((paths_all, LANES), BF16)],
        small,
        name="design",
    )
    (solved,) = call(
        partial(solve_kernel, len(moments)),
        [((2 * REGRESSORS, share), F32)],
        inverse, design_all, design_rows, thresh, rate, *moments,
        name="solve",
        scratch=[pltpu.VMEM((LANES, share), BF16)],
    )
    solved = [solved, swap(solved, SHARES - 1)]
    (slope,) = call(
        partial(slope_kernel, inner, outer),
        [((group_paths, group_trades), F32)],
        *basis, *weights, notionals,
        name="slope",
    )
    traded, slopes, *weight_parts = call(
        partial(weight_side_kernel, 1.0 / math.sqrt(paths_all), SHARES, inner),
        [((LANES, group_trades), BF16), ((group_paths, group_trades), BF16)]
        + [((trade_rows, features), BF16)] * outer,
        member, design_rows, slope, *solved, *basis,
        name="weight_side",
    )
    basis_parts = list(
        call(
            partial(basis_side_kernel, outer),
            [((path_rows, features), BF16)] * inner,
            value, traded, slopes, *weights,
            name="basis_side",
        )
    )
    terms = [[part] for part in weight_parts]
    for bit in reversed(outer_bits):
        count = len(terms) // 2
        arrived = None
        for k in reversed(range(count)):
            gone = terms[count + k]
            gone = gone[0] if len(gone) == 1 else sum(g.astype(F32) for g in gone).astype(BF16)
            if arrived is not None:
                gone = after(gone, arrived)
            arrived = swap(gone, 1 << bit)
            terms[k].append(arrived)
            if bit == outer_bits[-1] and k == count - 1:
                basis_parts[-1] = after(basis_parts[-1], arrived)
        terms = terms[:count]
    weight_terms = terms[0]
    basis_terms = [basis_parts[0]] + direct(basis_parts, inner_masks)
    loss, own_adjoint = call(
        loss_kernel,
        [((8, LANES), F32), ((path_rows, LANES), F32)],
        design_rows, thresh, rate, *solved,
        name="loss",
        scratch=[pltpu.VMEM((LANES, sets), BF16)],
    )
    parts = 4 if trade_rows % (4 * SUBLANES * 2) == 0 else 1
    basis_adjoint, weight_adjoint = call(
        partial(sum_kernel, len(basis_terms)),
        [((path_rows, features), F32), ((trade_rows, features), F32)],
        own_adjoint, *basis_terms, *weight_terms,
        name="sums",
        scratch=[
            pltpu.VMEM((path_rows, features), F32),
            pltpu.VMEM((trade_rows, features), F32),
            pltpu.SemaphoreType.DMA((2 * parts,)),
        ],
        far=True,
    )
    return (loss[0, :1], basis_adjoint, weight_adjoint)


def solution(mesh):
    placed = (
        P(("groups", "paths"), None),
        P(("groups", "paths"), None),
        P(("groups", "paths")),
        P("groups"),
        P("groups"),
        P("groups"),
        P("groups"),
    )
    return jax.shard_map(
        shards,
        mesh=mesh,
        in_specs=placed,
        out_specs=(P("groups"), P(("groups", "paths"), None), P(("groups", "paths"), None)),
        check_vma=False,
    )
```

```python
import math
from functools import partial

import jax
import jax.numpy as jnp
from jax import lax
from jax.experimental import pallas as pl
from jax.experimental.pallas import tpu as pltpu
from jax.sharding import PartitionSpec as P

REGRESSORS = 32
RIDGE_SCALE = 0.01
PRECISE = lax.Precision.HIGHEST
F32 = jnp.float32
BF16 = jnp.bfloat16
LANES = 128
SUBLANES = 8
CHUNK = 256
VMEM_BYTES = 48 * 1024 * 1024
LOG2_E = math.log2(math.e)
SHARES = 2
CONSTANT = REGRESSORS - 1


def split_bits(size):
    count = size.bit_length() - 1
    half = count // 2
    return list(range(1, half + 1)), list(range(count - 1, half, -1)) + [0]


def dot(a, b, ca=1, cb=0, precision=None):
    return lax.dot_general(
        a, b, (((ca,), (cb,)), ((), ())), precision=precision, preferred_element_type=F32
    )


def three(x, axis):
    high = x.astype(BF16)
    rest = x - high.astype(F32)
    middle = rest.astype(BF16)
    low = (rest - middle.astype(F32)).astype(BF16)
    return jnp.concatenate([high, middle, low], axis=axis)


def three_rows(x):
    blank = jnp.zeros((LANES - 3 * REGRESSORS, x.shape[1]), BF16)
    return jnp.concatenate([three(x, 0), blank], axis=0)


def lanes(shape):
    return lax.broadcasted_iota(jnp.int32, shape, len(shape) - 1)


def rows(shape):
    return lax.broadcasted_iota(jnp.int32, shape, len(shape) - 2)


def softplus(x):
    return jnp.maximum(x, 0.0) + jnp.log1p(jnp.exp(-jnp.abs(x)))


def sigmoid(x):
    small = jnp.exp(-jnp.abs(x))
    return jnp.where(x >= 0.0, 1.0, small) / (1.0 + small)


def each_chunk(size, step, first):
    count = size // CHUNK

    def body(i, carry):
        return step(carry, pl.ds(pl.multiple_of(i * CHUNK, CHUNK), CHUNK))

    return lax.fori_loop(0, count, body, first, unroll=count <= 8)


def invert(matrix):
    size = matrix.shape[0]
    work = jnp.concatenate([matrix, jnp.eye(size, dtype=F32)], axis=1)
    shape = (SUBLANES, 2 * size)
    blocks = [work[i : i + SUBLANES] for i in range(0, size, SUBLANES)]
    row = rows(shape)

    def row_of(block, k):
        return jnp.broadcast_to(block[k : k + 1], shape)

    for k in range(0, size, 4):
        at, here = k // SUBLANES, k % SUBLANES
        columns = [
            [jnp.broadcast_to(block[:, k + j : k + j + 1], shape) for block in blocks]
            for j in range(4)
        ]
        p = [[row_of(columns[j][at], here + i) for j in range(4)] for i in range(4)]
        r = [row_of(blocks[at], here + i) for i in range(4)]
        for i in range(4):
            scale = 1.0 / p[i][i]
            r[i] = r[i] * scale
            p[i] = [entry * scale for entry in p[i]]
            for m in range(4):
                if m != i:
                    r[m] = r[m] - p[m][i] * r[i]
                    p[m] = [x - p[m][i] * y if j > i else x for j, (x, y) in enumerate(zip(p[m], p[i]))]
        for i, block in enumerate(blocks):
            for j in range(4):
                block = block - columns[j][i] * r[j]
            if i == at:
                for j in range(4):
                    block = jnp.where(row == here + j, r[j], block)
            blocks[i] = block
    return jnp.concatenate(blocks, axis=0)[:, size:]


def lead_kernel(*refs):
    x_refs, lead_ref = refs[:-1], refs[-1]
    start = 0
    for x in x_refs:
        turned = x[:, :LANES].astype(F32).T[:REGRESSORS]
        turned = jnp.where(rows(turned.shape) == CONSTANT, 1.0, turned)
        lead_ref[:, start : start + x.shape[0]] = turned.astype(BF16)
        start += x.shape[0]


def tables_kernel(
    trade_masks, me_ref, level_ref, set_ref, index_ref, rate_ref, x_ref, w_ref,
    notional_ref, member_ref, thresh_out_ref, rate_out_ref, x_out_ref, w_out_ref, notional_out_ref,
):
    notional_out_ref[...] = notional_ref[...]
    x_out_ref[...] = x_ref[...]
    w_out_ref[...] = w_ref[...]
    me = me_ref[0]
    shares = index_ref.shape[0]
    place = me & (shares - 1)
    size = member_ref.shape[0] // shares
    trades = set_ref.shape[-1]
    for m in range(shares):
        here = slice(m * size, (m + 1) * size)
        label = (place ^ m) * size + rows((size, 1))
        for j, mask in enumerate(trade_masks):
            member_ref[here, j * trades : (j + 1) * trades] = jnp.where(
                set_ref[me ^ mask] == label, 1.0, 0.0
            ).astype(BF16)
        index = index_ref[place ^ m]
        thresh = jnp.zeros(index.shape, F32)
        for k in range(level_ref.shape[0]):
            thresh = jnp.where(index == k, level_ref[k], thresh)
        thresh_out_ref[:, here] = thresh
        rate_out_ref[:, here] = rate_ref[place ^ m]


def design_kernel(small_ref, design_ref, rows_ref):
    size = small_ref.shape[2]
    for d in range(small_ref.shape[0]):
        here = slice(d * size, (d + 1) * size)
        design_ref[:, here] = small_ref[d]
        turned = small_ref[d].astype(F32).T
        blank = jnp.zeros((size, LANES - 3 * REGRESSORS), F32)
        rows_ref[here] = jnp.concatenate([turned] * 3 + [blank], axis=1).astype(BF16)


def inverse_kernel(ridge, small_ref, inverse_ref):
    square = (REGRESSORS, REGRESSORS)
    gram = jnp.where(rows(square) == lanes(square), ridge, 0.0)
    for d in range(small_ref.shape[0]):
        gram = gram + dot(small_ref[d], small_ref[d], 1, 1)
    inverse_ref[...] = invert(gram)


def joined_weights(refs):
    return jnp.concatenate([ref[...] for ref in refs], axis=0)


def one_row(ref):
    wide = ref[...].astype(F32)
    return jnp.concatenate([wide[k : k + 1] for k in range(wide.shape[0])], axis=1)


def forward_kernel(paths, trades, *refs):
    x_refs, refs = refs[:paths], refs[paths:]
    weights, notional = joined_weights(refs[:trades]), one_row(refs[trades])
    lead_ref, member_ref, value_ref, *moment_refs = refs[trades + 1 :]
    start = 0
    for x in x_refs:
        pre_act = dot(x[...], weights, 1, 1)
        value_ref[start : start + x.shape[0]] = (notional * softplus(pre_act)).astype(BF16)
        start += x.shape[0]
    trade_moment = dot(lead_ref[...], value_ref[...])
    parts = dot(three(trade_moment, 0), member_ref[...], 1, 1)
    moment = parts[:REGRESSORS] + parts[REGRESSORS : 2 * REGRESSORS] + parts[2 * REGRESSORS :]
    size = moment.shape[1] // len(moment_refs)
    for m, moment_ref in enumerate(moment_refs):
        moment_ref[...] = moment[:, m * size : (m + 1) * size]


def slope_kernel(paths, trades, *refs):
    x_refs, refs, slope_ref = refs[:paths], refs[paths:], refs[-1]
    weights, notional = joined_weights(refs[:trades]), one_row(refs[trades])
    start = 0
    for x in x_refs:
        slope_ref[start : start + x.shape[0]] = notional * sigmoid(dot(x[...], weights, 1, 1))
        start += x.shape[0]


def solve_kernel(
    terms, inverse_ref, design_ref, rows_ref, thresh_ref, rate_ref, *refs
):
    solved_ref, turn_ref = refs[terms:]
    moment = refs[0][...]
    for ref in refs[1:terms]:
        moment = moment + ref[...]
    size = moment.shape[1]
    inverse = inverse_ref[...]
    coeffs = dot(inverse, moment, precision=PRECISE)
    solved_ref[REGRESSORS:] = coeffs
    is_constant = rows(coeffs.shape) == CONSTANT
    shifted = coeffs - jnp.where(is_constant, thresh_ref[:, :size], 0.0)
    turn_ref[...] = three_rows(-LOG2_E * shifted)

    def seeds(total, here):
        power = jnp.exp2(jnp.minimum(dot(rows_ref[here], turn_ref[...]), 126.0))
        below = 1.0 + power
        seed = pl.reciprocal(below, approx=True)
        seed = (seed * (2.0 - below * seed)).astype(BF16)
        return total + dot(design_ref[:, here], seed)

    total = each_chunk(rows_ref.shape[0], seeds, jnp.zeros((REGRESSORS, size), F32))
    solved_ref[:REGRESSORS] = dot(inverse, total * rate_ref[:, :size], precision=PRECISE)


def joined(refs, part):
    here = slice(part * REGRESSORS, (part + 1) * REGRESSORS)
    return jnp.concatenate([ref[here] for ref in refs], axis=1)


def weight_side_kernel(scale, shares, paths, member_ref, rows_ref, slope_ref, *refs):
    solved_refs, refs = refs[:shares], refs[shares:]
    x_refs, (traded_ref, slopes_ref, *weight_refs) = refs[:paths], refs[paths:]
    traded = dot(three_rows(joined(solved_refs, 0)), member_ref[...]).astype(BF16)
    traded_ref[...] = traded
    group = slopes_ref.shape[0]
    spread = dot(rows_ref[:group], traded).astype(BF16).astype(F32)
    slopes_ref[...] = (slope_ref[...] * spread).astype(BF16)
    basis = jnp.concatenate([x[...] for x in x_refs], axis=0)
    weight = (dot(slopes_ref[...], basis, 0, 0) * scale).astype(BF16)
    start = 0
    for part in weight_refs:
        part[...] = weight[start : start + part.shape[0]]
        start += part.shape[0]


def basis_side_kernel(trades, first, value_ref, traded_ref, slopes_ref, *refs):
    w_refs, basis_refs = refs[:trades], refs[trades:]
    weights = joined_weights(w_refs)
    start = first
    for part in basis_refs:
        here = slice(start, start + part.shape[0])
        total = dot(slopes_ref[here], weights)
        wide = dot(value_ref[here], traded_ref[...], 1, 1)
        design = wide
        for k in range(1, 3):
            design = design + pltpu.roll(wide, LANES - k * REGRESSORS, 1)
        design = jnp.where(lanes(design.shape) < CONSTANT, design, 0.0)
        part[:, :LANES] = (total[:, :LANES] + design).astype(BF16)
        part[:, LANES:] = total[:, LANES:].astype(BF16)
        start += part.shape[0]


def loss_kernel(rows_ref, thresh_ref, rate_ref, *refs):
    solved_refs, (loss_ref, own_ref, split_ref) = refs[:-3], refs[-3:]
    adjoint = joined(solved_refs, 0)
    coeffs = joined(solved_refs, 1)
    thresh = thresh_ref[...]
    rate = rate_ref[...]
    split_ref[...] = three_rows(coeffs)

    def losses(total, here):
        loss = softplus(dot(rows_ref[here], split_ref[...]) - thresh)
        return total + jnp.sum(loss.reshape(-1, *total.shape), axis=0)

    total = each_chunk(rows_ref.shape[0], losses, jnp.zeros((SUBLANES, coeffs.shape[1]), F32))
    summed = jnp.sum(jnp.sum(total * rate, axis=0, keepdims=True), axis=1, keepdims=True)
    loss_ref[...] = jnp.broadcast_to(
        summed / (rows_ref.shape[0] * coeffs.shape[1]), loss_ref.shape
    )
    own = rows_ref[: own_ref.shape[0]]
    fitted = dot(own, split_ref[...])
    seed = rate * sigmoid(fitted - thresh)
    rest = seed - dot(own, three_rows(adjoint))
    design = dot(rest, coeffs, 1, 1, PRECISE) - dot(fitted, adjoint, 1, 1, PRECISE)
    blank = jnp.zeros((design.shape[0], LANES - REGRESSORS), F32)
    design = jnp.concatenate([design, blank], axis=1)
    own_ref[...] = jnp.where(lanes(design.shape) < CONSTANT, design, 0.0)


def sum_kernel(first, own_ref, *refs):
    *terms, basis_ref, weight_ref, basis_scratch, weight_scratch, sems = refs

    def total(refs, here):
        out = refs[0][here].astype(F32)
        for ref in refs[1:]:
            out = out + ref[here].astype(F32)
        return out

    copies = []

    def send(source, target, here):
        copy = pltpu.make_async_copy(source.at[here], target.at[here], sems.at[len(copies)])
        copy.start()
        copies.append(copy)

    parts = sems.shape[0] // 2
    for k in range(parts):
        size = weight_ref.shape[0] // parts
        here = slice(k * size, (k + 1) * size)
        weight_scratch[here] = total(terms[first:], here)
        send(weight_scratch, weight_ref, pl.ds(k * size, size))
    for k in range(parts):
        size = basis_ref.shape[0] // parts
        here = slice(k * size, (k + 1) * size)
        basis = total(terms[:first], here)
        basis_scratch[here, :LANES] = basis[:, :LANES] + own_ref[here]
        basis_scratch[here, LANES:] = basis[:, LANES:]
        send(basis_scratch, basis_ref, pl.ds(k * size, size))
    for copy in copies:
        copy.wait()


def call(kernel, outs, *args, name, flops=0, scratch=(), scalars=0, far=False):
    size = sum(a.size * a.dtype.itemsize for a in args) + sum(
        math.prod(s) * jnp.dtype(d).itemsize for s, d in outs
    )
    return pl.pallas_call(
        kernel,
        out_shape=[jax.ShapeDtypeStruct(s, d) for s, d in outs],
        in_specs=[pl.BlockSpec(memory_space=pltpu.SMEM)] * scalars
        + [pl.BlockSpec(memory_space=pltpu.VMEM)] * (len(args) - scalars),
        out_specs=[pl.BlockSpec(memory_space=pl.ANY if far else pltpu.VMEM)] * len(outs),
        scratch_shapes=scratch,
        compiler_params=pltpu.CompilerParams(vmem_limit_bytes=VMEM_BYTES),
        cost_estimate=pl.CostEstimate(flops=int(flops), bytes_accessed=int(size), transcendentals=0),
        name=name,
    )(*args)


def shards(
    path_basis, proxy_weight, notional, set_of, threshold_index, threshold_levels, loss_rate
):
    n = lax.axis_size("paths")
    me = lax.axis_index("paths")
    inner_bits, outer_bits = split_bits(n)
    inner, outer = 1 << len(inner_bits), 1 << len(outer_bits)
    path_rows, features = path_basis.shape
    trade_rows = proxy_weight.shape[0]
    paths_all = path_rows * n
    sets = loss_rate.shape[0]
    share = sets // SHARES
    group_paths, group_trades = inner * path_rows, outer * trade_rows

    def swap(x, mask):
        return lax.ppermute(x, "paths", [(d, d ^ mask) for d in range(n)])

    def masks(bits):
        return [
            sum(((m >> j) & 1) << bit for j, bit in enumerate(bits)) for m in range(1 << len(bits))
        ]

    def after(x, *others):
        return lax.optimization_barrier((x, *others))[0]

    def direct(slots, masks):
        return [swap(x, mask) for x, mask in zip(slots[1:], masks[1:])]

    outer_masks = masks(outer_bits)
    inner_masks = [0] + masks(inner_bits)[:0:-1]
    first_bit = outer_bits[0]
    weights = [proxy_weight, swap(proxy_weight, 1 << first_bit)]
    basis = [path_basis] + direct([path_basis] * inner, inner_masks)
    notionals = [notional[None, :], swap(notional, 1 << first_bit)[None, :]]

    member, thresh, rate, basis[0], own_weight, notionals[0] = call(
        partial(tables_kernel, outer_masks),
        [
            ((sets, group_trades), BF16),
            ((1, sets), F32),
            ((1, sets), F32),
            (path_basis.shape, BF16),
            (proxy_weight.shape, BF16),
            ((1, trade_rows), BF16),
        ],
        me.astype(jnp.int32).reshape(1),
        threshold_levels,
        set_of.reshape(n, 1, trade_rows),
        threshold_index.reshape(SHARES, 1, share),
        loss_rate.reshape(SHARES, 1, share),
        path_basis,
        proxy_weight,
        notionals[0],
        name="tables",
        scalars=2,
    )
    notionals = after(jnp.concatenate(notionals, axis=0), weights[1])
    for bit in outer_bits[1:]:
        weights = weights + [
            swap(w if k else after(w, member), 1 << bit) for k, w in enumerate(weights)
        ]
        notionals = jnp.concatenate([notionals, swap(notionals, 1 << bit)], axis=0)
    weights[0] = own_weight
    (lead,) = call(lead_kernel, [((REGRESSORS, group_paths), BF16)], *basis, name="lead")
    value, *moments = call(
        partial(forward_kernel, inner, outer),
        [((group_paths, group_trades), BF16)] + [((REGRESSORS, share), F32)] * SHARES,
        *basis, *weights, notionals, lead, member,
        name="forward",
    )
    moment = moments[0] + swap(moments[1], SHARES - 1)
    lead = after(lead, moment)
    leads = [lead] + direct([lead] * outer, outer_masks)
    for bit in outer_bits[:-1]:
        there = swap(moment, 1 << bit)
        moment = moment + there
    small = jnp.stack(leads)
    moments = [moment] + direct([moment] * inner, inner_masks)
    (inverse,) = call(
        partial(inverse_kernel, RIDGE_SCALE * paths_all),
        [((REGRESSORS, REGRESSORS), F32)],
        small,
        name="inverse",
    )
    design_all, design_rows = call(
        design_kernel,
        [((REGRESSORS, paths_all), BF16), ((paths_all, LANES), BF16)],
        small,
        name="design",
    )
    (solved,) = call(
        partial(solve_kernel, len(moments)),
        [((2 * REGRESSORS, share), F32)],
        inverse, design_all, design_rows, thresh, rate, *moments,
        name="solve",
        scratch=[pltpu.VMEM((LANES, share), BF16)],
    )
    solved = [solved, swap(solved, SHARES - 1)]
    (slope,) = call(
        partial(slope_kernel, inner, outer),
        [((group_paths, group_trades), F32)],
        *basis, *weights, notionals,
        name="slope",
    )
    traded, slopes, *weight_parts = call(
        partial(weight_side_kernel, 1.0 / math.sqrt(paths_all), SHARES, inner),
        [((LANES, group_trades), BF16), ((group_paths, group_trades), BF16)]
        + [((trade_rows, features), BF16)] * outer,
        member, design_rows, slope, *solved, *basis,
        name="weight_side",
    )
    terms = [[part] for part in weight_parts]
    core_step = None
    for bit in reversed(outer_bits):
        count = len(terms) // 2
        arrived = None
        for k in reversed(range(count)):
            gone = terms[count + k]
            gone = gone[0] if len(gone) == 1 else sum(g.astype(F32) for g in gone).astype(BF16)
            if arrived is not None:
                gone = after(gone, arrived)
            arrived = swap(gone, 1 << bit)
            terms[k].append(arrived)
            if core_step is None:
                core_step = arrived
        terms = terms[:count]
    weight_terms = terms[0]

    def basis_side(first, last, slopes):
        return call(
            partial(basis_side_kernel, outer, first * path_rows),
            [((path_rows, features), BF16)] * (last - first),
            value, traded, slopes, *weights,
            name="basis_side",
        )

    far = list(basis_side(1, inner - 1, slopes))
    late = after(slopes, core_step)
    own, near = basis_side(0, 1, late)[0], basis_side(inner - 1, inner, late)[0]
    basis_terms = [own] + direct([own] + far + [near], inner_masks)
    loss, own_adjoint = call(
        loss_kernel,
        [((8, LANES), F32), ((path_rows, LANES), F32)],
        design_rows, thresh, rate, *solved,
        name="loss",
        scratch=[pltpu.VMEM((LANES, sets), BF16)],
    )
    parts = 4 if trade_rows % (4 * SUBLANES * 2) == 0 else 1
    basis_adjoint, weight_adjoint = call(
        partial(sum_kernel, len(basis_terms)),
        [((path_rows, features), F32), ((trade_rows, features), F32)],
        own_adjoint, *basis_terms, *weight_terms,
        name="sums",
        scratch=[
            pltpu.VMEM((path_rows, features), F32),
            pltpu.VMEM((trade_rows, features), F32),
            pltpu.SemaphoreType.DMA((2 * parts,)),
        ],
        far=True,
    )
    return (loss[0, :1], basis_adjoint, weight_adjoint)


def solution(mesh):
    placed = (
        P(("groups", "paths"), None),
        P(("groups", "paths"), None),
        P(("groups", "paths")),
        P("groups"),
        P("groups"),
        P("groups"),
        P("groups"),
    )
    return jax.shard_map(
        shards,
        mesh=mesh,
        in_specs=placed,
        out_specs=(P("groups"), P(("groups", "paths"), None), P(("groups", "paths"), None)),
        check_vma=False,
    )
```

```python
import math
from functools import partial

import jax
import jax.numpy as jnp
from jax import lax
from jax.experimental import pallas as pl
from jax.experimental.pallas import tpu as pltpu
from jax.sharding import PartitionSpec as P

REGRESSORS = 32
RIDGE_SCALE = 0.01
PRECISE = lax.Precision.HIGHEST
F32 = jnp.float32
BF16 = jnp.bfloat16
LANES = 128
SUBLANES = 8
CHUNK = 256
VMEM_BYTES = 48 * 1024 * 1024
LOG2_E = math.log2(math.e)
SHARES = 2
CONSTANT = REGRESSORS - 1


def split_bits(size):
    count = size.bit_length() - 1
    half = count // 2
    return list(range(1, half + 1)), list(range(count - 1, half, -1)) + [0]


def dot(a, b, ca=1, cb=0, precision=None):
    return lax.dot_general(
        a, b, (((ca,), (cb,)), ((), ())), precision=precision, preferred_element_type=F32
    )


def three(x, axis):
    high = x.astype(BF16)
    rest = x - high.astype(F32)
    middle = rest.astype(BF16)
    low = (rest - middle.astype(F32)).astype(BF16)
    return jnp.concatenate([high, middle, low], axis=axis)


def three_rows(x):
    blank = jnp.zeros((LANES - 3 * REGRESSORS, x.shape[1]), BF16)
    return jnp.concatenate([three(x, 0), blank], axis=0)


def lanes(shape):
    return lax.broadcasted_iota(jnp.int32, shape, len(shape) - 1)


def rows(shape):
    return lax.broadcasted_iota(jnp.int32, shape, len(shape) - 2)


def softplus(x):
    return jnp.maximum(x, 0.0) + jnp.log1p(jnp.exp(-jnp.abs(x)))


def sigmoid(x):
    small = jnp.exp(-jnp.abs(x))
    return jnp.where(x >= 0.0, 1.0, small) / (1.0 + small)


def each_chunk(size, step, first):
    count = size // CHUNK

    def body(i, carry):
        return step(carry, pl.ds(pl.multiple_of(i * CHUNK, CHUNK), CHUNK))

    return lax.fori_loop(0, count, body, first, unroll=count <= 8)


def invert(matrix):
    size = matrix.shape[0]
    work = jnp.concatenate([matrix, jnp.eye(size, dtype=F32)], axis=1)
    shape = (SUBLANES, 2 * size)
    blocks = [work[i : i + SUBLANES] for i in range(0, size, SUBLANES)]
    row = rows(shape)

    def row_of(block, k):
        return jnp.broadcast_to(block[k : k + 1], shape)

    for k in range(0, size, 4):
        at, here = k // SUBLANES, k % SUBLANES
        columns = [
            [jnp.broadcast_to(block[:, k + j : k + j + 1], shape) for block in blocks]
            for j in range(4)
        ]
        p = [[row_of(columns[j][at], here + i) for j in range(4)] for i in range(4)]
        r = [row_of(blocks[at], here + i) for i in range(4)]
        for i in range(4):
            scale = 1.0 / p[i][i]
            r[i] = r[i] * scale
            p[i] = [entry * scale for entry in p[i]]
            for m in range(4):
                if m != i:
                    r[m] = r[m] - p[m][i] * r[i]
                    p[m] = [x - p[m][i] * y if j > i else x for j, (x, y) in enumerate(zip(p[m], p[i]))]
        for i, block in enumerate(blocks):
            for j in range(4):
                block = block - columns[j][i] * r[j]
            if i == at:
                for j in range(4):
                    block = jnp.where(row == here + j, r[j], block)
            blocks[i] = block
    return jnp.concatenate(blocks, axis=0)[:, size:]


def lead_kernel(*refs):
    x_refs, lead_ref = refs[:-1], refs[-1]
    start = 0
    for x in x_refs:
        turned = x[:, :LANES].astype(F32).T[:REGRESSORS]
        turned = jnp.where(rows(turned.shape) == CONSTANT, 1.0, turned)
        lead_ref[:, start : start + x.shape[0]] = turned.astype(BF16)
        start += x.shape[0]


def tables_kernel(
    trade_masks, me_ref, level_ref, set_ref, index_ref, rate_ref, x_ref, w_ref,
    notional_ref, member_ref, thresh_out_ref, rate_out_ref, x_out_ref, w_out_ref, notional_out_ref,
):
    notional_out_ref[...] = notional_ref[...]
    x_out_ref[...] = x_ref[...]
    w_out_ref[...] = w_ref[...]
    me = me_ref[0]
    shares = index_ref.shape[0]
    place = me & (shares - 1)
    size = member_ref.shape[0] // shares
    trades = set_ref.shape[-1]
    for m in range(shares):
        here = slice(m * size, (m + 1) * size)
        label = (place ^ m) * size + rows((size, 1))
        for j, mask in enumerate(trade_masks):
            member_ref[here, j * trades : (j + 1) * trades] = jnp.where(
                set_ref[me ^ mask] == label, 1.0, 0.0
            ).astype(BF16)
        index = index_ref[place ^ m]
        thresh = jnp.zeros(index.shape, F32)
        for k in range(level_ref.shape[0]):
            thresh = jnp.where(index == k, level_ref[k], thresh)
        thresh_out_ref[:, here] = thresh
        rate_out_ref[:, here] = rate_ref[place ^ m]


def design_kernel(small_ref, design_ref, rows_ref):
    size = small_ref.shape[2]
    for d in range(small_ref.shape[0]):
        here = slice(d * size, (d + 1) * size)
        design_ref[:, here] = small_ref[d]
        turned = small_ref[d].astype(F32).T
        blank = jnp.zeros((size, LANES - 3 * REGRESSORS), F32)
        rows_ref[here] = jnp.concatenate([turned] * 3 + [blank], axis=1).astype(BF16)


def inverse_kernel(ridge, small_ref, inverse_ref):
    square = (REGRESSORS, REGRESSORS)
    gram = jnp.where(rows(square) == lanes(square), ridge, 0.0)
    for d in range(small_ref.shape[0]):
        gram = gram + dot(small_ref[d], small_ref[d], 1, 1)
    inverse_ref[...] = invert(gram)


def joined_weights(refs):
    return jnp.concatenate([ref[...] for ref in refs], axis=0)


def one_row(ref):
    wide = ref[...].astype(F32)
    return jnp.concatenate([wide[k : k + 1] for k in range(wide.shape[0])], axis=1)


def forward_kernel(paths, trades, *refs):
    x_refs, refs = refs[:paths], refs[paths:]
    weights, notional = joined_weights(refs[:trades]), one_row(refs[trades])
    lead_ref, member_ref, value_ref, *moment_refs = refs[trades + 1 :]
    start = 0
    for x in x_refs:
        pre_act = dot(x[...], weights, 1, 1)
        value_ref[start : start + x.shape[0]] = (notional * softplus(pre_act)).astype(BF16)
        start += x.shape[0]
    trade_moment = dot(lead_ref[...], value_ref[...])
    parts = dot(three(trade_moment, 0), member_ref[...], 1, 1)
    moment = parts[:REGRESSORS] + parts[REGRESSORS : 2 * REGRESSORS] + parts[2 * REGRESSORS :]
    size = moment.shape[1] // len(moment_refs)
    for m, moment_ref in enumerate(moment_refs):
        moment_ref[...] = moment[:, m * size : (m + 1) * size]


def slope_kernel(paths, trades, *refs):
    x_refs, refs, slope_ref = refs[:paths], refs[paths:], refs[-1]
    weights, notional = joined_weights(refs[:trades]), one_row(refs[trades])
    start = 0
    for x in x_refs:
        slope_ref[start : start + x.shape[0]] = notional * sigmoid(dot(x[...], weights, 1, 1))
        start += x.shape[0]


def solve_kernel(
    terms, inverse_ref, design_ref, rows_ref, thresh_ref, rate_ref, *refs
):
    solved_ref, turn_ref = refs[terms:]
    moment = refs[0][...]
    for ref in refs[1:terms]:
        moment = moment + ref[...]
    size = moment.shape[1]
    inverse = inverse_ref[...]
    coeffs = dot(inverse, moment, precision=PRECISE)
    solved_ref[REGRESSORS:] = coeffs
    is_constant = rows(coeffs.shape) == CONSTANT
    shifted = coeffs - jnp.where(is_constant, thresh_ref[:, :size], 0.0)
    turn_ref[...] = three_rows(-LOG2_E * shifted)

    def seeds(total, here):
        power = jnp.exp2(jnp.minimum(dot(rows_ref[here], turn_ref[...]), 126.0))
        below = 1.0 + power
        seed = pl.reciprocal(below, approx=True)
        seed = (seed * (2.0 - below * seed)).astype(BF16)
        return total + dot(design_ref[:, here], seed)

    total = each_chunk(rows_ref.shape[0], seeds, jnp.zeros((REGRESSORS, size), F32))
    solved_ref[:REGRESSORS] = dot(inverse, total * rate_ref[:, :size], precision=PRECISE)


def joined(refs, part):
    here = slice(part * REGRESSORS, (part + 1) * REGRESSORS)
    return jnp.concatenate([ref[here] for ref in refs], axis=1)


def weight_side_kernel(scale, shares, paths, member_ref, rows_ref, slope_ref, *refs):
    solved_refs, refs = refs[:shares], refs[shares:]
    x_refs, (traded_ref, slopes_ref, *weight_refs) = refs[:paths], refs[paths:]
    traded = dot(three_rows(joined(solved_refs, 0)), member_ref[...]).astype(BF16)
    traded_ref[...] = traded
    group = slopes_ref.shape[0]
    spread = dot(rows_ref[:group], traded).astype(BF16).astype(F32)
    slopes_ref[...] = (slope_ref[...] * spread).astype(BF16)
    basis = jnp.concatenate([x[...] for x in x_refs], axis=0)
    weight = (dot(slopes_ref[...], basis, 0, 0) * scale).astype(BF16)
    start = 0
    for part in weight_refs:
        part[...] = weight[start : start + part.shape[0]]
        start += part.shape[0]


def basis_side_kernel(trades, first, value_ref, traded_ref, slopes_ref, *refs):
    w_refs, basis_refs = refs[:trades], refs[trades:]
    weights = joined_weights(w_refs)
    start = first
    for part in basis_refs:
        here = slice(start, start + part.shape[0])
        total = dot(slopes_ref[here], weights)
        wide = dot(value_ref[here], traded_ref[...], 1, 1)
        design = wide
        for k in range(1, 3):
            design = design + pltpu.roll(wide, LANES - k * REGRESSORS, 1)
        design = jnp.where(lanes(design.shape) < CONSTANT, design, 0.0)
        part[:, :LANES] = (total[:, :LANES] + design).astype(BF16)
        part[:, LANES:] = total[:, LANES:].astype(BF16)
        start += part.shape[0]


def loss_kernel(rows_ref, thresh_ref, rate_ref, *refs):
    solved_refs, (loss_ref, own_ref, split_ref) = refs[:-3], refs[-3:]
    adjoint = joined(solved_refs, 0)
    coeffs = joined(solved_refs, 1)
    thresh = thresh_ref[...]
    rate = rate_ref[...]
    split_ref[...] = three_rows(coeffs)

    def losses(total, here):
        loss = softplus(dot(rows_ref[here], split_ref[...]) - thresh)
        return total + jnp.sum(loss.reshape(-1, *total.shape), axis=0)

    total = each_chunk(rows_ref.shape[0], losses, jnp.zeros((SUBLANES, coeffs.shape[1]), F32))
    summed = jnp.sum(jnp.sum(total * rate, axis=0, keepdims=True), axis=1, keepdims=True)
    loss_ref[...] = jnp.broadcast_to(
        summed / (rows_ref.shape[0] * coeffs.shape[1]), loss_ref.shape
    )
    own = rows_ref[: own_ref.shape[0]]
    fitted = dot(own, split_ref[...])
    seed = rate * sigmoid(fitted - thresh)
    rest = seed - dot(own, three_rows(adjoint))
    design = dot(rest, coeffs, 1, 1, PRECISE) - dot(fitted, adjoint, 1, 1, PRECISE)
    blank = jnp.zeros((design.shape[0], LANES - REGRESSORS), F32)
    design = jnp.concatenate([design, blank], axis=1)
    own_ref[...] = jnp.where(lanes(design.shape) < CONSTANT, design, 0.0)


def sum_kernel(first, own_ref, *refs):
    *terms, basis_ref, weight_ref, basis_scratch, weight_scratch, sems = refs

    def total(refs, here):
        out = refs[0][here].astype(F32)
        for ref in refs[1:]:
            out = out + ref[here].astype(F32)
        return out

    copies = []

    def send(source, target, here):
        copy = pltpu.make_async_copy(source.at[here], target.at[here], sems.at[len(copies)])
        copy.start()
        copies.append(copy)

    parts = sems.shape[0] // 2
    for k in range(parts):
        size = weight_ref.shape[0] // parts
        here = slice(k * size, (k + 1) * size)
        weight_scratch[here] = total(terms[first:], here)
        send(weight_scratch, weight_ref, pl.ds(k * size, size))
    for k in range(parts):
        size = basis_ref.shape[0] // parts
        here = slice(k * size, (k + 1) * size)
        basis = total(terms[:first], here)
        basis_scratch[here, :LANES] = basis[:, :LANES] + own_ref[here]
        basis_scratch[here, LANES:] = basis[:, LANES:]
        send(basis_scratch, basis_ref, pl.ds(k * size, size))
    for copy in copies:
        copy.wait()


def call(kernel, outs, *args, name, flops=0, scratch=(), scalars=0, far=False):
    size = sum(a.size * a.dtype.itemsize for a in args) + sum(
        math.prod(s) * jnp.dtype(d).itemsize for s, d in outs
    )
    return pl.pallas_call(
        kernel,
        out_shape=[jax.ShapeDtypeStruct(s, d) for s, d in outs],
        in_specs=[pl.BlockSpec(memory_space=pltpu.SMEM)] * scalars
        + [pl.BlockSpec(memory_space=pltpu.VMEM)] * (len(args) - scalars),
        out_specs=[pl.BlockSpec(memory_space=pl.ANY if far else pltpu.VMEM)] * len(outs),
        scratch_shapes=scratch,
        compiler_params=pltpu.CompilerParams(vmem_limit_bytes=VMEM_BYTES),
        cost_estimate=pl.CostEstimate(flops=int(flops), bytes_accessed=int(size), transcendentals=0),
        name=name,
    )(*args)


def shards(
    path_basis, proxy_weight, notional, set_of, threshold_index, threshold_levels, loss_rate
):
    n = lax.axis_size("paths")
    me = lax.axis_index("paths")
    inner_bits, outer_bits = split_bits(n)
    inner, outer = 1 << len(inner_bits), 1 << len(outer_bits)
    path_rows, features = path_basis.shape
    trade_rows = proxy_weight.shape[0]
    paths_all = path_rows * n
    sets = loss_rate.shape[0]
    share = sets // SHARES
    group_paths, group_trades = inner * path_rows, outer * trade_rows

    def swap(x, mask):
        return lax.ppermute(x, "paths", [(d, d ^ mask) for d in range(n)])

    def masks(bits):
        return [
            sum(((m >> j) & 1) << bit for j, bit in enumerate(bits)) for m in range(1 << len(bits))
        ]

    def after(x, *others):
        return lax.optimization_barrier((x, *others))[0]

    def direct(slots, masks):
        return [swap(x, mask) for x, mask in zip(slots[1:], masks[1:])]

    outer_masks = masks(outer_bits)
    inner_masks = [0] + masks(inner_bits)[:0:-1]
    first_bit = outer_bits[0]
    weights = [proxy_weight, swap(proxy_weight, 1 << first_bit)]
    basis = [path_basis] + direct([path_basis] * inner, inner_masks)
    notionals = [notional[None, :], swap(notional, 1 << first_bit)[None, :]]

    member, thresh, rate, basis[0], own_weight, notionals[0] = call(
        partial(tables_kernel, outer_masks),
        [
            ((sets, group_trades), BF16),
            ((1, sets), F32),
            ((1, sets), F32),
            (path_basis.shape, BF16),
            (proxy_weight.shape, BF16),
            ((1, trade_rows), BF16),
        ],
        me.astype(jnp.int32).reshape(1),
        threshold_levels,
        set_of.reshape(n, 1, trade_rows),
        threshold_index.reshape(SHARES, 1, share),
        loss_rate.reshape(SHARES, 1, share),
        path_basis,
        proxy_weight,
        notionals[0],
        name="tables",
        scalars=2,
    )
    notionals = after(jnp.concatenate(notionals, axis=0), weights[1])
    for bit in outer_bits[1:]:
        weights = weights + [
            swap(w if k else after(w, member), 1 << bit) for k, w in enumerate(weights)
        ]
        notionals = jnp.concatenate([notionals, swap(notionals, 1 << bit)], axis=0)
    weights[0] = own_weight
    (lead,) = call(lead_kernel, [((REGRESSORS, group_paths), BF16)], *basis, name="lead")
    value, *moments = call(
        partial(forward_kernel, inner, outer),
        [((group_paths, group_trades), BF16)] + [((REGRESSORS, share), F32)] * SHARES,
        *basis, *weights, notionals, lead, member,
        name="forward",
    )
    sent = [moments[mask & (SHARES - 1)] for mask in outer_masks]
    moment = sum(direct(sent, outer_masks), moments[0])
    lead = after(lead, value)
    small = jnp.stack([lead] + direct([lead] * outer, outer_masks))
    moments = [moment] + direct([moment] * inner, inner_masks)
    (inverse,) = call(
        partial(inverse_kernel, RIDGE_SCALE * paths_all),
        [((REGRESSORS, REGRESSORS), F32)],
        small,
        name="inverse",
    )
    design_all, design_rows = call(
        design_kernel,
        [((REGRESSORS, paths_all), BF16), ((paths_all, LANES), BF16)],
        small,
        name="design",
    )
    (solved,) = call(
        partial(solve_kernel, len(moments)),
        [((2 * REGRESSORS, share), F32)],
        inverse, design_all, design_rows, thresh, rate, *moments,
        name="solve",
        scratch=[pltpu.VMEM((LANES, share), BF16)],
    )
    solved = [solved, swap(solved, SHARES - 1)]
    (slope,) = call(
        partial(slope_kernel, inner, outer),
        [((group_paths, group_trades), F32)],
        *basis, *weights, notionals,
        name="slope",
    )
    traded, slopes, *weight_parts = call(
        partial(weight_side_kernel, 1.0 / math.sqrt(paths_all), SHARES, inner),
        [((LANES, group_trades), BF16), ((group_paths, group_trades), BF16)]
        + [((trade_rows, features), BF16)] * outer,
        member, design_rows, slope, *solved, *basis,
        name="weight_side",
    )
    terms = [[part] for part in weight_parts]
    core_step = None
    for bit in reversed(outer_bits):
        count = len(terms) // 2
        arrived = None
        for k in reversed(range(count)):
            gone = terms[count + k]
            gone = gone[0] if len(gone) == 1 else sum(g.astype(F32) for g in gone).astype(BF16)
            if arrived is not None:
                gone = after(gone, arrived)
            arrived = swap(gone, 1 << bit)
            terms[k].append(arrived)
            if core_step is None:
                core_step = arrived
        terms = terms[:count]
    weight_terms = terms[0]

    def basis_side(first, last, slopes):
        return call(
            partial(basis_side_kernel, outer, first * path_rows),
            [((path_rows, features), BF16)] * (last - first),
            value, traded, slopes, *weights,
            name="basis_side",
        )

    far = list(basis_side(1, inner - 1, slopes))
    late = after(slopes, core_step)
    own, near = basis_side(0, 1, late)[0], basis_side(inner - 1, inner, late)[0]
    basis_terms = [own] + direct([own] + far + [near], inner_masks)
    loss, own_adjoint = call(
        loss_kernel,
        [((8, LANES), F32), ((path_rows, LANES), F32)],
        design_rows, thresh, rate, *solved,
        name="loss",
        scratch=[pltpu.VMEM((LANES, sets), BF16)],
    )
    parts = 4 if trade_rows % (4 * SUBLANES * 2) == 0 else 1
    basis_adjoint, weight_adjoint = call(
        partial(sum_kernel, len(basis_terms)),
        [((path_rows, features), F32), ((trade_rows, features), F32)],
        own_adjoint, *basis_terms, *weight_terms,
        name="sums",
        scratch=[
            pltpu.VMEM((path_rows, features), F32),
            pltpu.VMEM((trade_rows, features), F32),
            pltpu.SemaphoreType.DMA((2 * parts,)),
        ],
        far=True,
    )
    return (loss[0, :1], basis_adjoint, weight_adjoint)


def solution(mesh):
    placed = (
        P(("groups", "paths"), None),
        P(("groups", "paths"), None),
        P(("groups", "paths")),
        P("groups"),
        P("groups"),
        P("groups"),
        P("groups"),
    )
    return jax.shard_map(
        shards,
        mesh=mesh,
        in_specs=placed,
        out_specs=(P("groups"), P(("groups", "paths"), None), P(("groups", "paths"), None)),
        check_vma=False,
    )
```

```python
import math
from functools import partial

import jax
import jax.numpy as jnp
from jax import lax
from jax.experimental import pallas as pl
from jax.experimental.pallas import tpu as pltpu
from jax.sharding import PartitionSpec as P

REGRESSORS = 32
RIDGE_SCALE = 0.01
PRECISE = lax.Precision.HIGHEST
F32 = jnp.float32
BF16 = jnp.bfloat16
LANES = 128
SUBLANES = 8
CHUNK = 256
VMEM_BYTES = 48 * 1024 * 1024
LOG2_E = math.log2(math.e)
SHARES = 2
CONSTANT = REGRESSORS - 1


def split_bits(size):
    count = size.bit_length() - 1
    half = count // 2
    return list(range(1, half + 1)), list(range(count - 1, half, -1)) + [0]


def dot(a, b, ca=1, cb=0, precision=None):
    return lax.dot_general(
        a, b, (((ca,), (cb,)), ((), ())), precision=precision, preferred_element_type=F32
    )


def three(x, axis):
    high = x.astype(BF16)
    rest = x - high.astype(F32)
    middle = rest.astype(BF16)
    low = (rest - middle.astype(F32)).astype(BF16)
    return jnp.concatenate([high, middle, low], axis=axis)


def three_rows(x):
    blank = jnp.zeros((LANES - 3 * REGRESSORS, x.shape[1]), BF16)
    return jnp.concatenate([three(x, 0), blank], axis=0)


def lanes(shape):
    return lax.broadcasted_iota(jnp.int32, shape, len(shape) - 1)


def rows(shape):
    return lax.broadcasted_iota(jnp.int32, shape, len(shape) - 2)


def softplus(x):
    return jnp.maximum(x, 0.0) + jnp.log1p(jnp.exp(-jnp.abs(x)))


def sigmoid(x):
    small = jnp.exp(-jnp.abs(x))
    return jnp.where(x >= 0.0, 1.0, small) / (1.0 + small)


def each_chunk(size, step, first):
    count = size // CHUNK

    def body(i, carry):
        return step(carry, pl.ds(pl.multiple_of(i * CHUNK, CHUNK), CHUNK))

    return lax.fori_loop(0, count, body, first, unroll=count <= 8)


def invert(matrix):
    size = matrix.shape[0]
    work = jnp.concatenate([matrix, jnp.eye(size, dtype=F32)], axis=1)
    shape = (SUBLANES, 2 * size)
    blocks = [work[i : i + SUBLANES] for i in range(0, size, SUBLANES)]
    row = rows(shape)

    def row_of(block, k):
        return jnp.broadcast_to(block[k : k + 1], shape)

    for k in range(0, size, 4):
        at, here = k // SUBLANES, k % SUBLANES
        columns = [
            [jnp.broadcast_to(block[:, k + j : k + j + 1], shape) for block in blocks]
            for j in range(4)
        ]
        p = [[row_of(columns[j][at], here + i) for j in range(4)] for i in range(4)]
        r = [row_of(blocks[at], here + i) for i in range(4)]
        for i in range(4):
            scale = 1.0 / p[i][i]
            r[i] = r[i] * scale
            p[i] = [entry * scale for entry in p[i]]
            for m in range(4):
                if m != i:
                    r[m] = r[m] - p[m][i] * r[i]
                    p[m] = [x - p[m][i] * y if j > i else x for j, (x, y) in enumerate(zip(p[m], p[i]))]
        for i, block in enumerate(blocks):
            for j in range(4):
                block = block - columns[j][i] * r[j]
            if i == at:
                for j in range(4):
                    block = jnp.where(row == here + j, r[j], block)
            blocks[i] = block
    return jnp.concatenate(blocks, axis=0)[:, size:]


def lead_kernel(*refs):
    x_refs, lead_ref = refs[:-1], refs[-1]
    start = 0
    for x in x_refs:
        turned = x[:, :LANES].astype(F32).T[:REGRESSORS]
        turned = jnp.where(rows(turned.shape) == CONSTANT, 1.0, turned)
        lead_ref[:, start : start + x.shape[0]] = turned.astype(BF16)
        start += x.shape[0]


def tables_kernel(
    trade_masks, me_ref, level_ref, set_ref, index_ref, rate_ref, x_ref, w_ref,
    notional_ref, member_ref, thresh_out_ref, rate_out_ref, x_out_ref, w_out_ref, notional_out_ref,
):
    notional_out_ref[...] = notional_ref[...]
    x_out_ref[...] = x_ref[...]
    w_out_ref[...] = w_ref[...]
    me = me_ref[0]
    shares = index_ref.shape[0]
    place = me & (shares - 1)
    size = member_ref.shape[0] // shares
    trades = set_ref.shape[-1]
    for m in range(shares):
        here = slice(m * size, (m + 1) * size)
        label = (place ^ m) * size + rows((size, 1))
        for j, mask in enumerate(trade_masks):
            member_ref[here, j * trades : (j + 1) * trades] = jnp.where(
                set_ref[me ^ mask] == label, 1.0, 0.0
            ).astype(BF16)
        index = index_ref[place ^ m]
        thresh = jnp.zeros(index.shape, F32)
        for k in range(level_ref.shape[0]):
            thresh = jnp.where(index == k, level_ref[k], thresh)
        thresh_out_ref[:, here] = thresh
        rate_out_ref[:, here] = rate_ref[place ^ m]


def design_kernel(small_ref, design_ref, rows_ref):
    size = small_ref.shape[2]
    for d in range(small_ref.shape[0]):
        here = slice(d * size, (d + 1) * size)
        design_ref[:, here] = small_ref[d]
        turned = small_ref[d].astype(F32).T
        blank = jnp.zeros((size, LANES - 3 * REGRESSORS), F32)
        rows_ref[here] = jnp.concatenate([turned] * 3 + [blank], axis=1).astype(BF16)


def inverse_kernel(ridge, small_ref, inverse_ref):
    square = (REGRESSORS, REGRESSORS)
    gram = jnp.where(rows(square) == lanes(square), ridge, 0.0)
    for d in range(small_ref.shape[0]):
        gram = gram + dot(small_ref[d], small_ref[d], 1, 1)
    inverse_ref[...] = invert(gram)


def joined_weights(refs):
    return jnp.concatenate([ref[...] for ref in refs], axis=0)


def one_row(ref):
    wide = ref[...].astype(F32)
    return jnp.concatenate([wide[k : k + 1] for k in range(wide.shape[0])], axis=1)


def forward_kernel(paths, trades, *refs):
    x_refs, refs = refs[:paths], refs[paths:]
    weights, notional = joined_weights(refs[:trades]), one_row(refs[trades])
    lead_ref, member_ref, value_ref, *moment_refs = refs[trades + 1 :]
    start = 0
    for x in x_refs:
        pre_act = dot(x[...], weights, 1, 1)
        value_ref[start : start + x.shape[0]] = (notional * softplus(pre_act)).astype(BF16)
        start += x.shape[0]
    trade_moment = dot(lead_ref[...], value_ref[...])
    parts = dot(three(trade_moment, 0), member_ref[...], 1, 1)
    moment = parts[:REGRESSORS] + parts[REGRESSORS : 2 * REGRESSORS] + parts[2 * REGRESSORS :]
    size = moment.shape[1] // len(moment_refs)
    for m, moment_ref in enumerate(moment_refs):
        moment_ref[...] = moment[:, m * size : (m + 1) * size]


def slope_kernel(paths, trades, *refs):
    x_refs, refs, slope_ref = refs[:paths], refs[paths:], refs[-1]
    weights, notional = joined_weights(refs[:trades]), one_row(refs[trades])
    start = 0
    for x in x_refs:
        slope_ref[start : start + x.shape[0]] = notional * sigmoid(dot(x[...], weights, 1, 1))
        start += x.shape[0]


def solve_kernel(
    terms, inverse_ref, design_ref, rows_ref, thresh_ref, rate_ref, *refs
):
    solved_ref, turn_ref = refs[terms:]
    moment = refs[0][...]
    for ref in refs[1:terms]:
        moment = moment + ref[...]
    size = moment.shape[1]
    inverse = inverse_ref[...]
    coeffs = dot(inverse, moment, precision=PRECISE)
    solved_ref[REGRESSORS:] = coeffs
    is_constant = rows(coeffs.shape) == CONSTANT
    shifted = coeffs - jnp.where(is_constant, thresh_ref[:, :size], 0.0)
    turn_ref[...] = three_rows(-LOG2_E * shifted)

    def seeds(total, here):
        power = jnp.exp2(jnp.minimum(dot(rows_ref[here], turn_ref[...]), 126.0))
        below = 1.0 + power
        seed = pl.reciprocal(below, approx=True)
        seed = (seed * (2.0 - below * seed)).astype(BF16)
        return total + dot(design_ref[:, here], seed)

    total = each_chunk(rows_ref.shape[0], seeds, jnp.zeros((REGRESSORS, size), F32))
    solved_ref[:REGRESSORS] = dot(inverse, total * rate_ref[:, :size], precision=PRECISE)


def joined(refs, part):
    here = slice(part * REGRESSORS, (part + 1) * REGRESSORS)
    return jnp.concatenate([ref[here] for ref in refs], axis=1)


def weight_side_kernel(scale, shares, paths, member_ref, rows_ref, slope_ref, *refs):
    solved_refs, refs = refs[:shares], refs[shares:]
    x_refs, (traded_ref, slopes_ref, *weight_refs) = refs[:paths], refs[paths:]
    traded = dot(three_rows(joined(solved_refs, 0)), member_ref[...]).astype(BF16)
    traded_ref[...] = traded
    group = slopes_ref.shape[0]
    spread = dot(rows_ref[:group], traded).astype(BF16).astype(F32)
    slopes_ref[...] = (slope_ref[...] * spread).astype(BF16)
    basis = jnp.concatenate([x[...] for x in x_refs], axis=0)
    weight = (dot(slopes_ref[...], basis, 0, 0) * scale).astype(BF16)
    start = 0
    for part in weight_refs:
        part[...] = weight[start : start + part.shape[0]]
        start += part.shape[0]


def basis_side_kernel(trades, first, value_ref, traded_ref, slopes_ref, *refs):
    w_refs, basis_refs = refs[:trades], refs[trades:]
    weights = joined_weights(w_refs)
    start = first
    for part in basis_refs:
        here = slice(start, start + part.shape[0])
        total = dot(slopes_ref[here], weights)
        wide = dot(value_ref[here], traded_ref[...], 1, 1)
        design = wide
        for k in range(1, 3):
            design = design + pltpu.roll(wide, LANES - k * REGRESSORS, 1)
        design = jnp.where(lanes(design.shape) < CONSTANT, design, 0.0)
        part[:, :LANES] = (total[:, :LANES] + design).astype(BF16)
        part[:, LANES:] = total[:, LANES:].astype(BF16)
        start += part.shape[0]


def loss_kernel(rows_ref, thresh_ref, rate_ref, *refs):
    solved_refs, (loss_ref, own_ref, split_ref) = refs[:-3], refs[-3:]
    adjoint = joined(solved_refs, 0)
    coeffs = joined(solved_refs, 1)
    thresh = thresh_ref[...]
    rate = rate_ref[...]
    split_ref[...] = three_rows(coeffs)

    def losses(total, here):
        loss = softplus(dot(rows_ref[here], split_ref[...]) - thresh)
        return total + jnp.sum(loss.reshape(-1, *total.shape), axis=0)

    total = each_chunk(rows_ref.shape[0], losses, jnp.zeros((SUBLANES, coeffs.shape[1]), F32))
    summed = jnp.sum(jnp.sum(total * rate, axis=0, keepdims=True), axis=1, keepdims=True)
    loss_ref[...] = jnp.broadcast_to(
        summed / (rows_ref.shape[0] * coeffs.shape[1]), loss_ref.shape
    )
    own = rows_ref[: own_ref.shape[0]]
    fitted = dot(own, split_ref[...])
    seed = rate * sigmoid(fitted - thresh)
    rest = seed - dot(own, three_rows(adjoint))
    design = dot(rest, coeffs, 1, 1, PRECISE) - dot(fitted, adjoint, 1, 1, PRECISE)
    blank = jnp.zeros((design.shape[0], LANES - REGRESSORS), F32)
    design = jnp.concatenate([design, blank], axis=1)
    own_ref[...] = jnp.where(lanes(design.shape) < CONSTANT, design, 0.0)


def sum_kernel(first, own_ref, *refs):
    *terms, basis_ref, weight_ref, basis_scratch, weight_scratch, sems = refs

    def total(refs, here):
        out = refs[0][here].astype(F32)
        for ref in refs[1:]:
            out = out + ref[here].astype(F32)
        return out

    copies = []

    def send(source, target, here):
        copy = pltpu.make_async_copy(source.at[here], target.at[here], sems.at[len(copies)])
        copy.start()
        copies.append(copy)

    parts = sems.shape[0] // 2
    for k in range(parts):
        size = weight_ref.shape[0] // parts
        here = slice(k * size, (k + 1) * size)
        weight_scratch[here] = total(terms[first:], here)
        send(weight_scratch, weight_ref, pl.ds(k * size, size))
    for k in range(parts):
        size = basis_ref.shape[0] // parts
        here = slice(k * size, (k + 1) * size)
        basis = total(terms[:first], here)
        basis_scratch[here, :LANES] = basis[:, :LANES] + own_ref[here]
        basis_scratch[here, LANES:] = basis[:, LANES:]
        send(basis_scratch, basis_ref, pl.ds(k * size, size))
    for copy in copies:
        copy.wait()


def call(kernel, outs, *args, name, flops=0, scratch=(), scalars=0, far=False):
    size = sum(a.size * a.dtype.itemsize for a in args) + sum(
        math.prod(s) * jnp.dtype(d).itemsize for s, d in outs
    )
    return pl.pallas_call(
        kernel,
        out_shape=[jax.ShapeDtypeStruct(s, d) for s, d in outs],
        in_specs=[pl.BlockSpec(memory_space=pltpu.SMEM)] * scalars
        + [pl.BlockSpec(memory_space=pltpu.VMEM)] * (len(args) - scalars),
        out_specs=[pl.BlockSpec(memory_space=pl.ANY if far else pltpu.VMEM)] * len(outs),
        scratch_shapes=scratch,
        compiler_params=pltpu.CompilerParams(vmem_limit_bytes=VMEM_BYTES),
        cost_estimate=pl.CostEstimate(flops=int(flops), bytes_accessed=int(size), transcendentals=0),
        name=name,
    )(*args)


def shards(
    path_basis, proxy_weight, notional, set_of, threshold_index, threshold_levels, loss_rate
):
    n = lax.axis_size("paths")
    me = lax.axis_index("paths")
    inner_bits, outer_bits = split_bits(n)
    inner, outer = 1 << len(inner_bits), 1 << len(outer_bits)
    path_rows, features = path_basis.shape
    trade_rows = proxy_weight.shape[0]
    paths_all = path_rows * n
    sets = loss_rate.shape[0]
    share = sets // SHARES
    group_paths, group_trades = inner * path_rows, outer * trade_rows

    def swap(x, mask):
        return lax.ppermute(x, "paths", [(d, d ^ mask) for d in range(n)])

    def masks(bits):
        return [
            sum(((m >> j) & 1) << bit for j, bit in enumerate(bits)) for m in range(1 << len(bits))
        ]

    def after(x, *others):
        return lax.optimization_barrier((x, *others))[0]

    def direct(slots, masks):
        return [swap(x, mask) for x, mask in zip(slots[1:], masks[1:])]

    outer_masks = masks(outer_bits)
    inner_masks = [0] + masks(inner_bits)[:0:-1]
    first_bit = outer_bits[0]
    weights = [proxy_weight, swap(proxy_weight, 1 << first_bit)]
    basis = [path_basis] + direct([path_basis] * inner, inner_masks)
    notionals = [notional[None, :], swap(notional, 1 << first_bit)[None, :]]

    member, thresh, rate, basis[0], own_weight, notionals[0] = call(
        partial(tables_kernel, outer_masks),
        [
            ((sets, group_trades), BF16),
            ((1, sets), F32),
            ((1, sets), F32),
            (path_basis.shape, BF16),
            (proxy_weight.shape, BF16),
            ((1, trade_rows), BF16),
        ],
        me.astype(jnp.int32).reshape(1),
        threshold_levels,
        set_of.reshape(n, 1, trade_rows),
        threshold_index.reshape(SHARES, 1, share),
        loss_rate.reshape(SHARES, 1, share),
        path_basis,
        proxy_weight,
        notionals[0],
        name="tables",
        scalars=2,
    )
    notionals = after(jnp.concatenate(notionals, axis=0), weights[1])
    for bit in outer_bits[1:]:
        weights = weights + [
            swap(after(w, basis[-2] if k else member), 1 << bit) for k, w in enumerate(weights)
        ]
        notionals = jnp.concatenate([notionals, swap(notionals, 1 << bit)], axis=0)
    weights[0] = own_weight
    (lead,) = call(lead_kernel, [((REGRESSORS, group_paths), BF16)], *basis, name="lead")
    value, *moments = call(
        partial(forward_kernel, inner, outer),
        [((group_paths, group_trades), BF16)] + [((REGRESSORS, share), F32)] * SHARES,
        *basis, *weights, notionals, lead, member,
        name="forward",
    )
    moment = moments[0] + swap(moments[1], SHARES - 1)
    lead = after(lead, moment)
    leads = [lead] + direct([lead] * outer, outer_masks)
    for bit in outer_bits[:-1]:
        there = swap(moment, 1 << bit)
        moment = moment + there
    small = jnp.stack(leads)
    moments = [moment] + direct([moment] * inner, inner_masks)
    (inverse,) = call(
        partial(inverse_kernel, RIDGE_SCALE * paths_all),
        [((REGRESSORS, REGRESSORS), F32)],
        small,
        name="inverse",
    )
    design_all, design_rows = call(
        design_kernel,
        [((REGRESSORS, paths_all), BF16), ((paths_all, LANES), BF16)],
        small,
        name="design",
    )
    (solved,) = call(
        partial(solve_kernel, len(moments)),
        [((2 * REGRESSORS, share), F32)],
        inverse, design_all, design_rows, thresh, rate, *moments,
        name="solve",
        scratch=[pltpu.VMEM((LANES, share), BF16)],
    )
    solved = [solved, swap(solved, SHARES - 1)]
    (slope,) = call(
        partial(slope_kernel, inner, outer),
        [((group_paths, group_trades), F32)],
        *basis, *weights, notionals,
        name="slope",
    )
    traded, slopes, *weight_parts = call(
        partial(weight_side_kernel, 1.0 / math.sqrt(paths_all), SHARES, inner),
        [((LANES, group_trades), BF16), ((group_paths, group_trades), BF16)]
        + [((trade_rows, features), BF16)] * outer,
        member, design_rows, slope, *solved, *basis,
        name="weight_side",
    )
    terms = [[part] for part in weight_parts]
    core_step = None
    for bit in reversed(outer_bits):
        count = len(terms) // 2
        arrived = None
        for k in reversed(range(count)):
            gone = terms[count + k]
            gone = gone[0] if len(gone) == 1 else sum(g.astype(F32) for g in gone).astype(BF16)
            if arrived is not None:
                gone = after(gone, arrived)
            arrived = swap(gone, 1 << bit)
            terms[k].append(arrived)
            if core_step is None:
                core_step = arrived
        terms = terms[:count]
    weight_terms = terms[0]

    def basis_side(first, last, slopes):
        return call(
            partial(basis_side_kernel, outer, first * path_rows),
            [((path_rows, features), BF16)] * (last - first),
            value, traded, slopes, *weights,
            name="basis_side",
        )

    far = list(basis_side(1, inner - 1, slopes))
    late = after(slopes, core_step)
    own, near = basis_side(0, 1, late)[0], basis_side(inner - 1, inner, late)[0]
    basis_terms = [own] + direct([own] + far + [near], inner_masks)
    loss, own_adjoint = call(
        loss_kernel,
        [((8, LANES), F32), ((path_rows, LANES), F32)],
        design_rows, thresh, rate, *solved,
        name="loss",
        scratch=[pltpu.VMEM((LANES, sets), BF16)],
    )
    parts = 4 if trade_rows % (4 * SUBLANES * 2) == 0 else 1
    basis_adjoint, weight_adjoint = call(
        partial(sum_kernel, len(basis_terms)),
        [((path_rows, features), F32), ((trade_rows, features), F32)],
        own_adjoint, *basis_terms, *weight_terms,
        name="sums",
        scratch=[
            pltpu.VMEM((path_rows, features), F32),
            pltpu.VMEM((trade_rows, features), F32),
            pltpu.SemaphoreType.DMA((2 * parts,)),
        ],
        far=True,
    )
    return (loss[0, :1], basis_adjoint, weight_adjoint)


def solution(mesh):
    placed = (
        P(("groups", "paths"), None),
        P(("groups", "paths"), None),
        P(("groups", "paths")),
        P("groups"),
        P("groups"),
        P("groups"),
        P("groups"),
    )
    return jax.shard_map(
        shards,
        mesh=mesh,
        in_specs=placed,
        out_specs=(P("groups"), P(("groups", "paths"), None), P(("groups", "paths"), None)),
        check_vma=False,
    )
```

```python
import math
from functools import partial

import jax
import jax.numpy as jnp
from jax import lax
from jax.experimental import pallas as pl
from jax.experimental.pallas import tpu as pltpu
from jax.sharding import PartitionSpec as P

REGRESSORS = 32
RIDGE_SCALE = 0.01
PRECISE = lax.Precision.HIGHEST
F32 = jnp.float32
BF16 = jnp.bfloat16
LANES = 128
SUBLANES = 8
CHUNK = 256
VMEM_BYTES = 48 * 1024 * 1024
LOG2_E = math.log2(math.e)
SHARES = 2
CONSTANT = REGRESSORS - 1


def split_bits(size):
    count = size.bit_length() - 1
    half = count // 2
    return list(range(1, half + 1)), list(range(count - 1, half, -1)) + [0]


def dot(a, b, ca=1, cb=0, precision=None):
    return lax.dot_general(
        a, b, (((ca,), (cb,)), ((), ())), precision=precision, preferred_element_type=F32
    )


def three(x, axis):
    high = x.astype(BF16)
    rest = x - high.astype(F32)
    middle = rest.astype(BF16)
    low = (rest - middle.astype(F32)).astype(BF16)
    return jnp.concatenate([high, middle, low], axis=axis)


def three_rows(x):
    blank = jnp.zeros((LANES - 3 * REGRESSORS, x.shape[1]), BF16)
    return jnp.concatenate([three(x, 0), blank], axis=0)


def lanes(shape):
    return lax.broadcasted_iota(jnp.int32, shape, len(shape) - 1)


def rows(shape):
    return lax.broadcasted_iota(jnp.int32, shape, len(shape) - 2)


def softplus(x):
    return jnp.maximum(x, 0.0) + jnp.log1p(jnp.exp(-jnp.abs(x)))


def sigmoid(x):
    small = jnp.exp(-jnp.abs(x))
    return jnp.where(x >= 0.0, 1.0, small) / (1.0 + small)


def each_chunk(size, step, first):
    count = size // CHUNK

    def body(i, carry):
        return step(carry, pl.ds(pl.multiple_of(i * CHUNK, CHUNK), CHUNK))

    return lax.fori_loop(0, count, body, first, unroll=count <= 8)


def invert(matrix):
    size = matrix.shape[0]
    work = jnp.concatenate([matrix, jnp.eye(size, dtype=F32)], axis=1)
    shape = (SUBLANES, 2 * size)
    blocks = [work[i : i + SUBLANES] for i in range(0, size, SUBLANES)]
    row = rows(shape)

    def row_of(block, k):
        return jnp.broadcast_to(block[k : k + 1], shape)

    for k in range(0, size, 4):
        at, here = k // SUBLANES, k % SUBLANES
        columns = [
            [jnp.broadcast_to(block[:, k + j : k + j + 1], shape) for block in blocks]
            for j in range(4)
        ]
        p = [[row_of(columns[j][at], here + i) for j in range(4)] for i in range(4)]
        r = [row_of(blocks[at], here + i) for i in range(4)]
        for i in range(4):
            scale = 1.0 / p[i][i]
            r[i] = r[i] * scale
            p[i] = [entry * scale for entry in p[i]]
            for m in range(4):
                if m != i:
                    r[m] = r[m] - p[m][i] * r[i]
                    p[m] = [x - p[m][i] * y if j > i else x for j, (x, y) in enumerate(zip(p[m], p[i]))]
        for i, block in enumerate(blocks):
            for j in range(4):
                block = block - columns[j][i] * r[j]
            if i == at:
                for j in range(4):
                    block = jnp.where(row == here + j, r[j], block)
            blocks[i] = block
    return jnp.concatenate(blocks, axis=0)[:, size:]


def lead_kernel(*refs):
    x_refs, lead_ref = refs[:-1], refs[-1]
    start = 0
    for x in x_refs:
        turned = x[:, :LANES].astype(F32).T[:REGRESSORS]
        turned = jnp.where(rows(turned.shape) == CONSTANT, 1.0, turned)
        lead_ref[:, start : start + x.shape[0]] = turned.astype(BF16)
        start += x.shape[0]


def tables_kernel(
    trade_masks, me_ref, level_ref, set_ref, index_ref, rate_ref, x_ref, w_ref,
    notional_ref, member_ref, thresh_out_ref, rate_out_ref, x_out_ref, w_out_ref, notional_out_ref,
):
    notional_out_ref[...] = notional_ref[...]
    x_out_ref[...] = x_ref[...]
    w_out_ref[...] = w_ref[...]
    me = me_ref[0]
    shares = index_ref.shape[0]
    place = me & (shares - 1)
    size = member_ref.shape[0] // shares
    trades = set_ref.shape[-1]
    for m in range(shares):
        here = slice(m * size, (m + 1) * size)
        label = (place ^ m) * size + rows((size, 1))
        for j, mask in enumerate(trade_masks):
            member_ref[here, j * trades : (j + 1) * trades] = jnp.where(
                set_ref[me ^ mask] == label, 1.0, 0.0
            ).astype(BF16)
        index = index_ref[place ^ m]
        thresh = jnp.zeros(index.shape, F32)
        for k in range(level_ref.shape[0]):
            thresh = jnp.where(index == k, level_ref[k], thresh)
        thresh_out_ref[:, here] = thresh
        rate_out_ref[:, here] = rate_ref[place ^ m]


def design_kernel(small_ref, design_ref, rows_ref):
    size = small_ref.shape[2]
    for d in range(small_ref.shape[0]):
        here = slice(d * size, (d + 1) * size)
        design_ref[:, here] = small_ref[d]
        turned = small_ref[d].astype(F32).T
        blank = jnp.zeros((size, LANES - 3 * REGRESSORS), F32)
        rows_ref[here] = jnp.concatenate([turned] * 3 + [blank], axis=1).astype(BF16)


def inverse_kernel(ridge, small_ref, inverse_ref):
    square = (REGRESSORS, REGRESSORS)
    gram = jnp.where(rows(square) == lanes(square), ridge, 0.0)
    for d in range(small_ref.shape[0]):
        gram = gram + dot(small_ref[d], small_ref[d], 1, 1)
    inverse_ref[...] = invert(gram)


def joined_weights(refs):
    return jnp.concatenate([ref[...] for ref in refs], axis=0)


def one_row(ref):
    wide = ref[...].astype(F32)
    return jnp.concatenate([wide[k : k + 1] for k in range(wide.shape[0])], axis=1)


def forward_kernel(paths, trades, *refs):
    x_refs, refs = refs[:paths], refs[paths:]
    weights, notional = joined_weights(refs[:trades]), one_row(refs[trades])
    lead_ref, member_ref, value_ref, *moment_refs = refs[trades + 1 :]
    start = 0
    for x in x_refs:
        pre_act = dot(x[...], weights, 1, 1)
        value_ref[start : start + x.shape[0]] = (notional * softplus(pre_act)).astype(BF16)
        start += x.shape[0]
    trade_moment = dot(lead_ref[...], value_ref[...])
    parts = dot(three(trade_moment, 0), member_ref[...], 1, 1)
    moment = parts[:REGRESSORS] + parts[REGRESSORS : 2 * REGRESSORS] + parts[2 * REGRESSORS :]
    size = moment.shape[1] // len(moment_refs)
    for m, moment_ref in enumerate(moment_refs):
        moment_ref[...] = moment[:, m * size : (m + 1) * size]


def slope_kernel(paths, trades, *refs):
    x_refs, refs, slope_ref = refs[:paths], refs[paths:], refs[-1]
    weights, notional = joined_weights(refs[:trades]), one_row(refs[trades])
    start = 0
    for x in x_refs:
        slope_ref[start : start + x.shape[0]] = notional * sigmoid(dot(x[...], weights, 1, 1))
        start += x.shape[0]


def solve_kernel(
    terms, inverse_ref, design_ref, rows_ref, thresh_ref, rate_ref, *refs
):
    solved_ref, turn_ref = refs[terms:]
    moment = refs[0][...]
    for ref in refs[1:terms]:
        moment = moment + ref[...]
    size = moment.shape[1]
    inverse = inverse_ref[...]
    coeffs = dot(inverse, moment, precision=PRECISE)
    solved_ref[REGRESSORS:] = coeffs
    is_constant = rows(coeffs.shape) == CONSTANT
    shifted = coeffs - jnp.where(is_constant, thresh_ref[:, :size], 0.0)
    turn_ref[...] = three_rows(-LOG2_E * shifted)

    def seeds(total, here):
        power = jnp.exp2(jnp.minimum(dot(rows_ref[here], turn_ref[...]), 126.0))
        below = 1.0 + power
        seed = pl.reciprocal(below, approx=True)
        seed = (seed * (2.0 - below * seed)).astype(BF16)
        return total + dot(design_ref[:, here], seed)

    total = each_chunk(rows_ref.shape[0], seeds, jnp.zeros((REGRESSORS, size), F32))
    solved_ref[:REGRESSORS] = dot(inverse, total * rate_ref[:, :size], precision=PRECISE)


def joined(refs, part):
    here = slice(part * REGRESSORS, (part + 1) * REGRESSORS)
    return jnp.concatenate([ref[here] for ref in refs], axis=1)


def weight_side_kernel(scale, shares, paths, member_ref, rows_ref, slope_ref, *refs):
    solved_refs, refs = refs[:shares], refs[shares:]
    x_refs, (traded_ref, slopes_ref, *weight_refs) = refs[:paths], refs[paths:]
    traded = dot(three_rows(joined(solved_refs, 0)), member_ref[...]).astype(BF16)
    traded_ref[...] = traded
    group = slopes_ref.shape[0]
    spread = dot(rows_ref[:group], traded).astype(BF16).astype(F32)
    slopes_ref[...] = (slope_ref[...] * spread).astype(BF16)
    basis = jnp.concatenate([x[...] for x in x_refs], axis=0)
    weight = (dot(slopes_ref[...], basis, 0, 0) * scale).astype(BF16)
    start = 0
    for part in weight_refs:
        part[...] = weight[start : start + part.shape[0]]
        start += part.shape[0]


def basis_side_kernel(trades, first, value_ref, traded_ref, slopes_ref, *refs):
    w_refs, basis_refs = refs[:trades], refs[trades:]
    weights = joined_weights(w_refs)
    start = first
    for part in basis_refs:
        here = slice(start, start + part.shape[0])
        total = dot(slopes_ref[here], weights)
        wide = dot(value_ref[here], traded_ref[...], 1, 1)
        design = wide
        for k in range(1, 3):
            design = design + pltpu.roll(wide, LANES - k * REGRESSORS, 1)
        design = jnp.where(lanes(design.shape) < CONSTANT, design, 0.0)
        part[:, :LANES] = (total[:, :LANES] + design).astype(BF16)
        part[:, LANES:] = total[:, LANES:].astype(BF16)
        start += part.shape[0]


def loss_kernel(rows_ref, thresh_ref, rate_ref, *refs):
    solved_refs, (loss_ref, own_ref, split_ref) = refs[:-3], refs[-3:]
    adjoint = joined(solved_refs, 0)
    coeffs = joined(solved_refs, 1)
    thresh = thresh_ref[...]
    rate = rate_ref[...]
    split_ref[...] = three_rows(coeffs)

    def losses(total, here):
        loss = softplus(dot(rows_ref[here], split_ref[...]) - thresh)
        return total + jnp.sum(loss.reshape(-1, *total.shape), axis=0)

    total = each_chunk(rows_ref.shape[0], losses, jnp.zeros((SUBLANES, coeffs.shape[1]), F32))
    summed = jnp.sum(jnp.sum(total * rate, axis=0, keepdims=True), axis=1, keepdims=True)
    loss_ref[...] = jnp.broadcast_to(
        summed / (rows_ref.shape[0] * coeffs.shape[1]), loss_ref.shape
    )
    own = rows_ref[: own_ref.shape[0]]
    fitted = dot(own, split_ref[...])
    seed = rate * sigmoid(fitted - thresh)
    rest = seed - dot(own, three_rows(adjoint))
    design = dot(rest, coeffs, 1, 1, PRECISE) - dot(fitted, adjoint, 1, 1, PRECISE)
    blank = jnp.zeros((design.shape[0], LANES - REGRESSORS), F32)
    design = jnp.concatenate([design, blank], axis=1)
    own_ref[...] = jnp.where(lanes(design.shape) < CONSTANT, design, 0.0)


def sum_kernel(first, own_ref, *refs):
    *terms, basis_ref, weight_ref, basis_scratch, weight_scratch, sems = refs

    def total(refs, here):
        out = refs[0][here].astype(F32)
        for ref in refs[1:]:
            out = out + ref[here].astype(F32)
        return out

    copies = []

    def send(source, target, here):
        copy = pltpu.make_async_copy(source.at[here], target.at[here], sems.at[len(copies)])
        copy.start()
        copies.append(copy)

    parts = sems.shape[0] // 2
    for k in range(parts):
        size = weight_ref.shape[0] // parts
        here = slice(k * size, (k + 1) * size)
        weight_scratch[here] = total(terms[first:], here)
        send(weight_scratch, weight_ref, pl.ds(k * size, size))
    for k in range(parts):
        size = basis_ref.shape[0] // parts
        here = slice(k * size, (k + 1) * size)
        basis = total(terms[:first], here)
        basis_scratch[here, :LANES] = basis[:, :LANES] + own_ref[here]
        basis_scratch[here, LANES:] = basis[:, LANES:]
        send(basis_scratch, basis_ref, pl.ds(k * size, size))
    for copy in copies:
        copy.wait()


def call(kernel, outs, *args, name, flops=0, scratch=(), scalars=0, far=False):
    size = sum(a.size * a.dtype.itemsize for a in args) + sum(
        math.prod(s) * jnp.dtype(d).itemsize for s, d in outs
    )
    return pl.pallas_call(
        kernel,
        out_shape=[jax.ShapeDtypeStruct(s, d) for s, d in outs],
        in_specs=[pl.BlockSpec(memory_space=pltpu.SMEM)] * scalars
        + [pl.BlockSpec(memory_space=pltpu.VMEM)] * (len(args) - scalars),
        out_specs=[pl.BlockSpec(memory_space=pl.ANY if far else pltpu.VMEM)] * len(outs),
        scratch_shapes=scratch,
        compiler_params=pltpu.CompilerParams(vmem_limit_bytes=VMEM_BYTES),
        cost_estimate=pl.CostEstimate(flops=int(flops), bytes_accessed=int(size), transcendentals=0),
        name=name,
    )(*args)


def shards(
    path_basis, proxy_weight, notional, set_of, threshold_index, threshold_levels, loss_rate
):
    n = lax.axis_size("paths")
    me = lax.axis_index("paths")
    inner_bits, outer_bits = split_bits(n)
    inner, outer = 1 << len(inner_bits), 1 << len(outer_bits)
    path_rows, features = path_basis.shape
    trade_rows = proxy_weight.shape[0]
    paths_all = path_rows * n
    sets = loss_rate.shape[0]
    share = sets // SHARES
    group_paths, group_trades = inner * path_rows, outer * trade_rows

    def swap(x, mask):
        return lax.ppermute(x, "paths", [(d, d ^ mask) for d in range(n)])

    def masks(bits):
        return [
            sum(((m >> j) & 1) << bit for j, bit in enumerate(bits)) for m in range(1 << len(bits))
        ]

    def after(x, *others):
        return lax.optimization_barrier((x, *others))[0]

    def direct(slots, masks):
        return [swap(x, mask) for x, mask in zip(slots[1:], masks[1:])]

    outer_masks = masks(outer_bits)
    inner_masks = [0] + masks(inner_bits)[:0:-1]
    first_bit = outer_bits[0]
    weights = [proxy_weight, swap(proxy_weight, 1 << first_bit)]
    basis = [path_basis] + direct([path_basis] * inner, inner_masks)
    notionals = [notional[None, :], swap(notional, 1 << first_bit)[None, :]]

    member, thresh, rate, basis[0], own_weight, notionals[0] = call(
        partial(tables_kernel, outer_masks),
        [
            ((sets, group_trades), BF16),
            ((1, sets), F32),
            ((1, sets), F32),
            (path_basis.shape, BF16),
            (proxy_weight.shape, BF16),
            ((1, trade_rows), BF16),
        ],
        me.astype(jnp.int32).reshape(1),
        threshold_levels,
        set_of.reshape(n, 1, trade_rows),
        threshold_index.reshape(SHARES, 1, share),
        loss_rate.reshape(SHARES, 1, share),
        path_basis,
        proxy_weight,
        notionals[0],
        name="tables",
        scalars=2,
    )
    notionals = after(jnp.concatenate(notionals, axis=0), weights[1])
    for bit in outer_bits[1:]:
        weights = weights + [
            swap(after(w, basis[-2] if k else member), 1 << bit) for k, w in enumerate(weights)
        ]
        notionals = jnp.concatenate([notionals, swap(notionals, 1 << bit)], axis=0)
    weights[0] = own_weight
    (lead,) = call(lead_kernel, [((REGRESSORS, group_paths), BF16)], *basis, name="lead")
    value, *moments = call(
        partial(forward_kernel, inner, outer),
        [((group_paths, group_trades), BF16)] + [((REGRESSORS, share), F32)] * SHARES,
        *basis, *weights, notionals, lead, member,
        name="forward",
    )
    moment = moments[0] + swap(moments[1], SHARES - 1)
    lead = after(lead, moment)
    leads = [lead] + direct([lead] * outer, outer_masks)
    for bit in outer_bits[:-1]:
        there = swap(moment, 1 << bit)
        moment = moment + there
    small = jnp.stack(leads)
    moments = [moment] + direct([moment] * inner, inner_masks)
    (inverse,) = call(
        partial(inverse_kernel, RIDGE_SCALE * paths_all),
        [((REGRESSORS, REGRESSORS), F32)],
        small,
        name="inverse",
    )
    design_all, design_rows = call(
        design_kernel,
        [((REGRESSORS, paths_all), BF16), ((paths_all, LANES), BF16)],
        small,
        name="design",
    )
    (solved,) = call(
        partial(solve_kernel, len(moments)),
        [((2 * REGRESSORS, share), F32)],
        inverse, design_all, design_rows, thresh, rate, *moments,
        name="solve",
        scratch=[pltpu.VMEM((LANES, share), BF16)],
    )
    solved = [solved, swap(solved, SHARES - 1)]
    (slope,) = call(
        partial(slope_kernel, inner, outer),
        [((group_paths, group_trades), F32)],
        *basis, *weights, notionals,
        name="slope",
    )
    traded, slopes, *weight_parts = call(
        partial(weight_side_kernel, 1.0 / math.sqrt(paths_all), SHARES, inner),
        [((LANES, group_trades), BF16), ((group_paths, group_trades), BF16)]
        + [((trade_rows, features), BF16)] * outer,
        member, design_rows, slope, *solved, *basis,
        name="weight_side",
    )
    terms = [[part] for part in weight_parts]
    core_step = None
    for bit in reversed(outer_bits):
        count = len(terms) // 2
        arrived = None
        for k in reversed(range(count)):
            gone = terms[count + k]
            gone = gone[0] if len(gone) == 1 else sum(g.astype(F32) for g in gone).astype(BF16)
            if arrived is not None:
                gone = after(gone, arrived)
            arrived = swap(gone, 1 << bit)
            terms[k].append(arrived)
            if core_step is None:
                core_step = arrived
        terms = terms[:count]
    weight_terms = terms[0]

    def basis_side(first, last, slopes):
        return call(
            partial(basis_side_kernel, outer, first * path_rows),
            [((path_rows, features), BF16)] * (last - first),
            value, traded, slopes, *weights,
            name="basis_side",
        )

    far = list(basis_side(1, inner - 1, slopes))
    late = after(slopes, core_step)
    own, near = basis_side(0, 1, late)[0], basis_side(inner - 1, inner, late)[0]
    arrived = direct([own] + far + [near], inner_masks)
    hops = [bin(mask).count("1") for mask in inner_masks[1:]]
    basis_terms = [own] + [arrived[k] for k in sorted(range(len(hops)), key=lambda k: hops[k])]
    loss, own_adjoint = call(
        loss_kernel,
        [((8, LANES), F32), ((path_rows, LANES), F32)],
        design_rows, thresh, rate, *solved,
        name="loss",
        scratch=[pltpu.VMEM((LANES, sets), BF16)],
    )
    parts = 4 if trade_rows % (4 * SUBLANES * 2) == 0 else 1
    basis_adjoint, weight_adjoint = call(
        partial(sum_kernel, len(basis_terms)),
        [((path_rows, features), F32), ((trade_rows, features), F32)],
        own_adjoint, *basis_terms, *weight_terms,
        name="sums",
        scratch=[
            pltpu.VMEM((path_rows, features), F32),
            pltpu.VMEM((trade_rows, features), F32),
            pltpu.SemaphoreType.DMA((2 * parts,)),
        ],
        far=True,
    )
    return (loss[0, :1], basis_adjoint, weight_adjoint)


def solution(mesh):
    placed = (
        P(("groups", "paths"), None),
        P(("groups", "paths"), None),
        P(("groups", "paths")),
        P("groups"),
        P("groups"),
        P("groups"),
        P("groups"),
    )
    return jax.shard_map(
        shards,
        mesh=mesh,
        in_specs=placed,
        out_specs=(P("groups"), P(("groups", "paths"), None), P(("groups", "paths"), None)),
        check_vma=False,
    )
```

```python
import math
from functools import partial

import jax
import jax.numpy as jnp
from jax import lax
from jax.experimental import pallas as pl
from jax.experimental.pallas import tpu as pltpu
from jax.sharding import PartitionSpec as P

REGRESSORS = 32
RIDGE_SCALE = 0.01
PRECISE = lax.Precision.HIGHEST
F32 = jnp.float32
BF16 = jnp.bfloat16
LANES = 128
SUBLANES = 8
CHUNK = 256
VMEM_BYTES = 48 * 1024 * 1024
LOG2_E = math.log2(math.e)
SHARES = 2
CONSTANT = REGRESSORS - 1


def split_bits(size):
    count = size.bit_length() - 1
    half = count // 2
    return list(range(1, half + 1)), list(range(count - 1, half, -1)) + [0]


def dot(a, b, ca=1, cb=0, precision=None):
    return lax.dot_general(
        a, b, (((ca,), (cb,)), ((), ())), precision=precision, preferred_element_type=F32
    )


def three(x, axis):
    high = x.astype(BF16)
    rest = x - high.astype(F32)
    middle = rest.astype(BF16)
    low = (rest - middle.astype(F32)).astype(BF16)
    return jnp.concatenate([high, middle, low], axis=axis)


def three_rows(x):
    blank = jnp.zeros((LANES - 3 * REGRESSORS, x.shape[1]), BF16)
    return jnp.concatenate([three(x, 0), blank], axis=0)


def lanes(shape):
    return lax.broadcasted_iota(jnp.int32, shape, len(shape) - 1)


def rows(shape):
    return lax.broadcasted_iota(jnp.int32, shape, len(shape) - 2)


def softplus(x):
    return jnp.maximum(x, 0.0) + jnp.log1p(jnp.exp(-jnp.abs(x)))


def sigmoid(x):
    small = jnp.exp(-jnp.abs(x))
    return jnp.where(x >= 0.0, 1.0, small) / (1.0 + small)


def each_chunk(size, step, first):
    count = size // CHUNK

    def body(i, carry):
        return step(carry, pl.ds(pl.multiple_of(i * CHUNK, CHUNK), CHUNK))

    return lax.fori_loop(0, count, body, first, unroll=count <= 8)


def invert(matrix):
    size = matrix.shape[0]
    work = jnp.concatenate([matrix, jnp.eye(size, dtype=F32)], axis=1)
    shape = (SUBLANES, 2 * size)
    blocks = [work[i : i + SUBLANES] for i in range(0, size, SUBLANES)]
    row = rows(shape)

    def row_of(block, k):
        return jnp.broadcast_to(block[k : k + 1], shape)

    for k in range(0, size, 4):
        at, here = k // SUBLANES, k % SUBLANES
        columns = [
            [jnp.broadcast_to(block[:, k + j : k + j + 1], shape) for block in blocks]
            for j in range(4)
        ]
        p = [[row_of(columns[j][at], here + i) for j in range(4)] for i in range(4)]
        r = [row_of(blocks[at], here + i) for i in range(4)]
        for i in range(4):
            scale = 1.0 / p[i][i]
            r[i] = r[i] * scale
            p[i] = [entry * scale for entry in p[i]]
            for m in range(4):
                if m != i:
                    r[m] = r[m] - p[m][i] * r[i]
                    p[m] = [x - p[m][i] * y if j > i else x for j, (x, y) in enumerate(zip(p[m], p[i]))]
        for i, block in enumerate(blocks):
            for j in range(4):
                block = block - columns[j][i] * r[j]
            if i == at:
                for j in range(4):
                    block = jnp.where(row == here + j, r[j], block)
            blocks[i] = block
    return jnp.concatenate(blocks, axis=0)[:, size:]


def tables_kernel(
    trade_masks, me_ref, level_ref, set_ref, index_ref, rate_ref, x_ref, w_ref,
    notional_ref, member_ref, thresh_out_ref, rate_out_ref, x_out_ref, w_out_ref, notional_out_ref,
):
    notional_out_ref[...] = notional_ref[...]
    x_out_ref[...] = x_ref[...]
    w_out_ref[...] = w_ref[...]
    me = me_ref[0]
    shares = index_ref.shape[0]
    place = me & (shares - 1)
    size = member_ref.shape[0] // shares
    trades = set_ref.shape[-1]
    for m in range(shares):
        here = slice(m * size, (m + 1) * size)
        label = (place ^ m) * size + rows((size, 1))
        for j, mask in enumerate(trade_masks):
            member_ref[here, j * trades : (j + 1) * trades] = jnp.where(
                set_ref[me ^ mask] == label, 1.0, 0.0
            ).astype(BF16)
        index = index_ref[place ^ m]
        thresh = jnp.zeros(index.shape, F32)
        for k in range(level_ref.shape[0]):
            thresh = jnp.where(index == k, level_ref[k], thresh)
        thresh_out_ref[:, here] = thresh
        rate_out_ref[:, here] = rate_ref[place ^ m]


def design_kernel(small_ref, design_ref, rows_ref):
    size = small_ref.shape[2]
    for d in range(small_ref.shape[0]):
        here = slice(d * size, (d + 1) * size)
        design_ref[:, here] = small_ref[d]
        turned = small_ref[d].astype(F32).T
        blank = jnp.zeros((size, LANES - 3 * REGRESSORS), F32)
        rows_ref[here] = jnp.concatenate([turned] * 3 + [blank], axis=1).astype(BF16)


def inverse_kernel(ridge, small_ref, inverse_ref):
    square = (REGRESSORS, REGRESSORS)
    gram = jnp.where(rows(square) == lanes(square), ridge, 0.0)
    for d in range(small_ref.shape[0]):
        gram = gram + dot(small_ref[d], small_ref[d], 1, 1)
    inverse_ref[...] = invert(gram)


def joined_weights(refs):
    return jnp.concatenate([ref[...] for ref in refs], axis=0)


def one_row(ref):
    wide = ref[...].astype(F32)
    return jnp.concatenate([wide[k : k + 1] for k in range(wide.shape[0])], axis=1)


def forward_kernel(paths, trades, *refs):
    x_refs, refs = refs[:paths], refs[paths:]
    weights, notional = joined_weights(refs[:trades]), one_row(refs[trades])
    member_ref, value_ref, lead_ref, *moment_refs = refs[trades + 1 :]
    start = 0
    for x in x_refs:
        pre_act = dot(x[...], weights, 1, 1)
        value_ref[start : start + x.shape[0]] = (notional * softplus(pre_act)).astype(BF16)
        turned = x[:, :LANES].astype(F32).T[:REGRESSORS]
        turned = jnp.where(rows(turned.shape) == CONSTANT, 1.0, turned)
        lead_ref[:, start : start + x.shape[0]] = turned.astype(BF16)
        start += x.shape[0]
    trade_moment = dot(lead_ref[...], value_ref[...])
    parts = dot(three(trade_moment, 0), member_ref[...], 1, 1)
    moment = parts[:REGRESSORS] + parts[REGRESSORS : 2 * REGRESSORS] + parts[2 * REGRESSORS :]
    size = moment.shape[1] // len(moment_refs)
    for m, moment_ref in enumerate(moment_refs):
        moment_ref[...] = moment[:, m * size : (m + 1) * size]


def slope_kernel(paths, trades, *refs):
    x_refs, refs, slope_ref = refs[:paths], refs[paths:], refs[-1]
    weights, notional = joined_weights(refs[:trades]), one_row(refs[trades])
    start = 0
    for x in x_refs:
        slope_ref[start : start + x.shape[0]] = notional * sigmoid(dot(x[...], weights, 1, 1))
        start += x.shape[0]


def solve_kernel(
    terms, inverse_ref, design_ref, rows_ref, thresh_ref, rate_ref, *refs
):
    solved_ref, turn_ref = refs[terms:]
    moment = refs[0][...]
    for ref in refs[1:terms]:
        moment = moment + ref[...]
    size = moment.shape[1]
    inverse = inverse_ref[...]
    coeffs = dot(inverse, moment, precision=PRECISE)
    solved_ref[REGRESSORS:] = coeffs
    is_constant = rows(coeffs.shape) == CONSTANT
    shifted = coeffs - jnp.where(is_constant, thresh_ref[:, :size], 0.0)
    turn_ref[...] = three_rows(-LOG2_E * shifted)

    def seeds(total, here):
        power = jnp.exp2(jnp.minimum(dot(rows_ref[here], turn_ref[...]), 126.0))
        below = 1.0 + power
        seed = pl.reciprocal(below, approx=True)
        seed = (seed * (2.0 - below * seed)).astype(BF16)
        return total + dot(design_ref[:, here], seed)

    total = each_chunk(rows_ref.shape[0], seeds, jnp.zeros((REGRESSORS, size), F32))
    solved_ref[:REGRESSORS] = dot(inverse, total * rate_ref[:, :size], precision=PRECISE)


def joined(refs, part):
    here = slice(part * REGRESSORS, (part + 1) * REGRESSORS)
    return jnp.concatenate([ref[here] for ref in refs], axis=1)


def weight_side_kernel(scale, shares, paths, member_ref, rows_ref, slope_ref, *refs):
    solved_refs, refs = refs[:shares], refs[shares:]
    x_refs, (traded_ref, slopes_ref, *weight_refs) = refs[:paths], refs[paths:]
    traded = dot(three_rows(joined(solved_refs, 0)), member_ref[...]).astype(BF16)
    traded_ref[...] = traded
    group = slopes_ref.shape[0]
    spread = dot(rows_ref[:group], traded).astype(BF16).astype(F32)
    slopes_ref[...] = (slope_ref[...] * spread).astype(BF16)
    basis = jnp.concatenate([x[...] for x in x_refs], axis=0)
    weight = (dot(slopes_ref[...], basis, 0, 0) * scale).astype(BF16)
    start = 0
    for part in weight_refs:
        part[...] = weight[start : start + part.shape[0]]
        start += part.shape[0]


def basis_side_kernel(trades, first, value_ref, traded_ref, slopes_ref, *refs):
    w_refs, basis_refs = refs[:trades], refs[trades:]
    weights = joined_weights(w_refs)
    start = first
    for part in basis_refs:
        here = slice(start, start + part.shape[0])
        total = dot(slopes_ref[here], weights)
        wide = dot(value_ref[here], traded_ref[...], 1, 1)
        design = wide
        for k in range(1, 3):
            design = design + pltpu.roll(wide, LANES - k * REGRESSORS, 1)
        design = jnp.where(lanes(design.shape) < CONSTANT, design, 0.0)
        part[:, :LANES] = (total[:, :LANES] + design).astype(BF16)
        part[:, LANES:] = total[:, LANES:].astype(BF16)
        start += part.shape[0]


def loss_kernel(rows_ref, thresh_ref, rate_ref, *refs):
    solved_refs, (loss_ref, own_ref, split_ref) = refs[:-3], refs[-3:]
    adjoint = joined(solved_refs, 0)
    coeffs = joined(solved_refs, 1)
    thresh = thresh_ref[...]
    rate = rate_ref[...]
    split_ref[...] = three_rows(coeffs)

    def losses(total, here):
        loss = softplus(dot(rows_ref[here], split_ref[...]) - thresh)
        return total + jnp.sum(loss.reshape(-1, *total.shape), axis=0)

    total = each_chunk(rows_ref.shape[0], losses, jnp.zeros((SUBLANES, coeffs.shape[1]), F32))
    summed = jnp.sum(jnp.sum(total * rate, axis=0, keepdims=True), axis=1, keepdims=True)
    loss_ref[...] = jnp.broadcast_to(
        summed / (rows_ref.shape[0] * coeffs.shape[1]), loss_ref.shape
    )
    own = rows_ref[: own_ref.shape[0]]
    fitted = dot(own, split_ref[...])
    seed = rate * sigmoid(fitted - thresh)
    rest = seed - dot(own, three_rows(adjoint))
    design = dot(rest, coeffs, 1, 1, PRECISE) - dot(fitted, adjoint, 1, 1, PRECISE)
    blank = jnp.zeros((design.shape[0], LANES - REGRESSORS), F32)
    design = jnp.concatenate([design, blank], axis=1)
    own_ref[...] = jnp.where(lanes(design.shape) < CONSTANT, design, 0.0)


def sum_kernel(first, own_ref, *refs):
    *terms, basis_ref, weight_ref, basis_scratch, weight_scratch, sems = refs

    def total(refs, here):
        out = refs[0][here].astype(F32)
        for ref in refs[1:]:
            out = out + ref[here].astype(F32)
        return out

    copies = []

    def send(source, target, here):
        copy = pltpu.make_async_copy(source.at[here], target.at[here], sems.at[len(copies)])
        copy.start()
        copies.append(copy)

    parts = sems.shape[0] // 2
    for k in range(parts):
        size = weight_ref.shape[0] // parts
        here = slice(k * size, (k + 1) * size)
        weight_scratch[here] = total(terms[first:], here)
        send(weight_scratch, weight_ref, pl.ds(k * size, size))
    for k in range(parts):
        size = basis_ref.shape[0] // parts
        here = slice(k * size, (k + 1) * size)
        basis = total(terms[:first], here)
        basis_scratch[here, :LANES] = basis[:, :LANES] + own_ref[here]
        basis_scratch[here, LANES:] = basis[:, LANES:]
        send(basis_scratch, basis_ref, pl.ds(k * size, size))
    for copy in copies:
        copy.wait()


def call(kernel, outs, *args, name, flops=0, scratch=(), scalars=0, far=False):
    size = sum(a.size * a.dtype.itemsize for a in args) + sum(
        math.prod(s) * jnp.dtype(d).itemsize for s, d in outs
    )
    return pl.pallas_call(
        kernel,
        out_shape=[jax.ShapeDtypeStruct(s, d) for s, d in outs],
        in_specs=[pl.BlockSpec(memory_space=pltpu.SMEM)] * scalars
        + [pl.BlockSpec(memory_space=pltpu.VMEM)] * (len(args) - scalars),
        out_specs=[pl.BlockSpec(memory_space=pl.ANY if far else pltpu.VMEM)] * len(outs),
        scratch_shapes=scratch,
        compiler_params=pltpu.CompilerParams(vmem_limit_bytes=VMEM_BYTES),
        cost_estimate=pl.CostEstimate(flops=int(flops), bytes_accessed=int(size), transcendentals=0),
        name=name,
    )(*args)


def shards(
    path_basis, proxy_weight, notional, set_of, threshold_index, threshold_levels, loss_rate
):
    n = lax.axis_size("paths")
    me = lax.axis_index("paths")
    inner_bits, outer_bits = split_bits(n)
    inner, outer = 1 << len(inner_bits), 1 << len(outer_bits)
    path_rows, features = path_basis.shape
    trade_rows = proxy_weight.shape[0]
    paths_all = path_rows * n
    sets = loss_rate.shape[0]
    share = sets // SHARES
    group_paths, group_trades = inner * path_rows, outer * trade_rows

    def swap(x, mask):
        return lax.ppermute(x, "paths", [(d, d ^ mask) for d in range(n)])

    def masks(bits):
        return [
            sum(((m >> j) & 1) << bit for j, bit in enumerate(bits)) for m in range(1 << len(bits))
        ]

    def after(x, *others):
        return lax.optimization_barrier((x, *others))[0]

    def direct(slots, masks):
        return [swap(x, mask) for x, mask in zip(slots[1:], masks[1:])]

    outer_masks = masks(outer_bits)
    inner_masks = [0] + masks(inner_bits)[:0:-1]
    first_bit = outer_bits[0]
    weights = [proxy_weight, swap(proxy_weight, 1 << first_bit)]
    basis = [path_basis] + direct([path_basis] * inner, inner_masks)
    notionals = [notional[None, :], swap(notional, 1 << first_bit)[None, :]]

    member, thresh, rate, basis[0], own_weight, notionals[0] = call(
        partial(tables_kernel, outer_masks),
        [
            ((sets, group_trades), BF16),
            ((1, sets), F32),
            ((1, sets), F32),
            (path_basis.shape, BF16),
            (proxy_weight.shape, BF16),
            ((1, trade_rows), BF16),
        ],
        me.astype(jnp.int32).reshape(1),
        threshold_levels,
        set_of.reshape(n, 1, trade_rows),
        threshold_index.reshape(SHARES, 1, share),
        loss_rate.reshape(SHARES, 1, share),
        path_basis,
        proxy_weight,
        notionals[0],
        name="tables",
        scalars=2,
    )
    notionals = after(jnp.concatenate(notionals, axis=0), weights[1])
    for bit in outer_bits[1:]:
        weights = weights + [
            swap(after(w, basis[-2] if k else member), 1 << bit) for k, w in enumerate(weights)
        ]
        notionals = jnp.concatenate([notionals, swap(notionals, 1 << bit)], axis=0)
    weights[0] = own_weight
    value, lead, *moments = call(
        partial(forward_kernel, inner, outer),
        [((group_paths, group_trades), BF16), ((REGRESSORS, group_paths), BF16)]
        + [((REGRESSORS, share), F32)] * SHARES,
        *basis, *weights, notionals, member,
        name="forward",
    )
    moment = moments[0] + swap(moments[1], SHARES - 1)
    lead = after(lead, moment)
    leads = [lead] + direct([lead] * outer, outer_masks)
    for bit in outer_bits[:-1]:
        there = swap(moment, 1 << bit)
        moment = moment + there
    small = jnp.stack(leads)
    moments = [moment] + direct([moment] * inner, inner_masks)
    (inverse,) = call(
        partial(inverse_kernel, RIDGE_SCALE * paths_all),
        [((REGRESSORS, REGRESSORS), F32)],
        small,
        name="inverse",
    )
    design_all, design_rows = call(
        design_kernel,
        [((REGRESSORS, paths_all), BF16), ((paths_all, LANES), BF16)],
        small,
        name="design",
    )
    (solved,) = call(
        partial(solve_kernel, len(moments)),
        [((2 * REGRESSORS, share), F32)],
        inverse, design_all, design_rows, thresh, rate, *moments,
        name="solve",
        scratch=[pltpu.VMEM((LANES, share), BF16)],
    )
    solved = [solved, swap(solved, SHARES - 1)]
    (slope,) = call(
        partial(slope_kernel, inner, outer),
        [((group_paths, group_trades), F32)],
        *basis, *weights, notionals,
        name="slope",
    )
    traded, slopes, *weight_parts = call(
        partial(weight_side_kernel, 1.0 / math.sqrt(paths_all), SHARES, inner),
        [((LANES, group_trades), BF16), ((group_paths, group_trades), BF16)]
        + [((trade_rows, features), BF16)] * outer,
        member, design_rows, slope, *solved, *basis,
        name="weight_side",
    )
    terms = [[part] for part in weight_parts]
    core_step = None
    for bit in reversed(outer_bits):
        count = len(terms) // 2
        arrived = None
        for k in reversed(range(count)):
            gone = terms[count + k]
            gone = gone[0] if len(gone) == 1 else sum(g.astype(F32) for g in gone).astype(BF16)
            if arrived is not None:
                gone = after(gone, arrived)
            arrived = swap(gone, 1 << bit)
            terms[k].append(arrived)
            if core_step is None:
                core_step = arrived
        terms = terms[:count]
    weight_terms = terms[0]

    def basis_side(first, last, slopes):
        return call(
            partial(basis_side_kernel, outer, first * path_rows),
            [((path_rows, features), BF16)] * (last - first),
            value, traded, slopes, *weights,
            name="basis_side",
        )

    far = list(basis_side(1, inner - 1, slopes))
    late = after(slopes, core_step)
    own, near = basis_side(0, 1, late)[0], basis_side(inner - 1, inner, late)[0]
    basis_terms = [own] + direct([own] + far + [near], inner_masks)
    loss, own_adjoint = call(
        loss_kernel,
        [((8, LANES), F32), ((path_rows, LANES), F32)],
        design_rows, thresh, rate, *solved,
        name="loss",
        scratch=[pltpu.VMEM((LANES, sets), BF16)],
    )
    parts = 4 if trade_rows % (4 * SUBLANES * 2) == 0 else 1
    basis_adjoint, weight_adjoint = call(
        partial(sum_kernel, len(basis_terms)),
        [((path_rows, features), F32), ((trade_rows, features), F32)],
        own_adjoint, *basis_terms, *weight_terms,
        name="sums",
        scratch=[
            pltpu.VMEM((path_rows, features), F32),
            pltpu.VMEM((trade_rows, features), F32),
            pltpu.SemaphoreType.DMA((2 * parts,)),
        ],
        far=True,
    )
    return (loss[0, :1], basis_adjoint, weight_adjoint)


def solution(mesh):
    placed = (
        P(("groups", "paths"), None),
        P(("groups", "paths"), None),
        P(("groups", "paths")),
        P("groups"),
        P("groups"),
        P("groups"),
        P("groups"),
    )
    return jax.shard_map(
        shards,
        mesh=mesh,
        in_specs=placed,
        out_specs=(P("groups"), P(("groups", "paths"), None), P(("groups", "paths"), None)),
        check_vma=False,
    )
```

```python
import math
from functools import partial

import jax
import jax.numpy as jnp
from jax import lax
from jax.experimental import pallas as pl
from jax.experimental.pallas import tpu as pltpu
from jax.sharding import PartitionSpec as P

REGRESSORS = 32
RIDGE_SCALE = 0.01
PRECISE = lax.Precision.HIGHEST
F32 = jnp.float32
BF16 = jnp.bfloat16
LANES = 128
SUBLANES = 8
CHUNK = 512
VMEM_BYTES = 48 * 1024 * 1024
LOG2_E = math.log2(math.e)
SHARES = 2
CONSTANT = REGRESSORS - 1


def split_bits(size):
    count = size.bit_length() - 1
    half = count // 2
    return list(range(1, half + 1)), list(range(count - 1, half, -1)) + [0]


def dot(a, b, ca=1, cb=0, precision=None):
    return lax.dot_general(
        a, b, (((ca,), (cb,)), ((), ())), precision=precision, preferred_element_type=F32
    )


def three(x, axis):
    high = x.astype(BF16)
    rest = x - high.astype(F32)
    middle = rest.astype(BF16)
    low = (rest - middle.astype(F32)).astype(BF16)
    return jnp.concatenate([high, middle, low], axis=axis)


def three_rows(x):
    blank = jnp.zeros((LANES - 3 * REGRESSORS, x.shape[1]), BF16)
    return jnp.concatenate([three(x, 0), blank], axis=0)


def lanes(shape):
    return lax.broadcasted_iota(jnp.int32, shape, len(shape) - 1)


def rows(shape):
    return lax.broadcasted_iota(jnp.int32, shape, len(shape) - 2)


def softplus(x):
    return jnp.maximum(x, 0.0) + jnp.log1p(jnp.exp(-jnp.abs(x)))


def sigmoid(x):
    small = jnp.exp(-jnp.abs(x))
    return jnp.where(x >= 0.0, 1.0, small) / (1.0 + small)


def each_chunk(size, step, first):
    count = size // CHUNK

    def body(i, carry):
        return step(carry, pl.ds(pl.multiple_of(i * CHUNK, CHUNK), CHUNK))

    return lax.fori_loop(0, count, body, first, unroll=count <= 8)


def invert(matrix):
    size = matrix.shape[0]
    work = jnp.concatenate([matrix, jnp.eye(size, dtype=F32)], axis=1)
    shape = (SUBLANES, 2 * size)
    blocks = [work[i : i + SUBLANES] for i in range(0, size, SUBLANES)]
    row = rows(shape)

    def row_of(block, k):
        return jnp.broadcast_to(block[k : k + 1], shape)

    for k in range(0, size, 4):
        at, here = k // SUBLANES, k % SUBLANES
        columns = [
            [jnp.broadcast_to(block[:, k + j : k + j + 1], shape) for block in blocks]
            for j in range(4)
        ]
        p = [[row_of(columns[j][at], here + i) for j in range(4)] for i in range(4)]
        r = [row_of(blocks[at], here + i) for i in range(4)]
        for i in range(4):
            scale = 1.0 / p[i][i]
            r[i] = r[i] * scale
            p[i] = [entry * scale for entry in p[i]]
            for m in range(4):
                if m != i:
                    r[m] = r[m] - p[m][i] * r[i]
                    p[m] = [x - p[m][i] * y if j > i else x for j, (x, y) in enumerate(zip(p[m], p[i]))]
        for i, block in enumerate(blocks):
            for j in range(4):
                block = block - columns[j][i] * r[j]
            if i == at:
                for j in range(4):
                    block = jnp.where(row == here + j, r[j], block)
            blocks[i] = block
    return jnp.concatenate(blocks, axis=0)[:, size:]


def tables_kernel(
    trade_masks, me_ref, level_ref, set_ref, index_ref, rate_ref, x_ref, w_ref,
    notional_ref, member_ref, thresh_out_ref, rate_out_ref, x_out_ref, w_out_ref, notional_out_ref,
):
    notional_out_ref[...] = notional_ref[...]
    x_out_ref[...] = x_ref[...]
    w_out_ref[...] = w_ref[...]
    me = me_ref[0]
    shares = index_ref.shape[0]
    place = me & (shares - 1)
    size = member_ref.shape[0] // shares
    trades = set_ref.shape[-1]
    for m in range(shares):
        here = slice(m * size, (m + 1) * size)
        label = (place ^ m) * size + rows((size, 1))
        for j, mask in enumerate(trade_masks):
            member_ref[here, j * trades : (j + 1) * trades] = jnp.where(
                set_ref[me ^ mask] == label, 1.0, 0.0
            ).astype(BF16)
        index = index_ref[place ^ m]
        thresh = jnp.zeros(index.shape, F32)
        for k in range(level_ref.shape[0]):
            thresh = jnp.where(index == k, level_ref[k], thresh)
        thresh_out_ref[:, here] = thresh
        rate_out_ref[:, here] = rate_ref[place ^ m]


def design_kernel(small_ref, design_ref, rows_ref):
    size = small_ref.shape[2]
    for d in range(small_ref.shape[0]):
        here = slice(d * size, (d + 1) * size)
        design_ref[:, here] = small_ref[d]
        turned = small_ref[d].astype(F32).T
        blank = jnp.zeros((size, LANES - 3 * REGRESSORS), F32)
        rows_ref[here] = jnp.concatenate([turned] * 3 + [blank], axis=1).astype(BF16)


def inverse_kernel(ridge, small_ref, inverse_ref):
    square = (REGRESSORS, REGRESSORS)
    gram = jnp.where(rows(square) == lanes(square), ridge, 0.0)
    for d in range(small_ref.shape[0]):
        gram = gram + dot(small_ref[d], small_ref[d], 1, 1)
    inverse_ref[...] = invert(gram)


def joined_weights(refs):
    return jnp.concatenate([ref[...] for ref in refs], axis=0)


def one_row(ref):
    wide = ref[...].astype(F32)
    return jnp.concatenate([wide[k : k + 1] for k in range(wide.shape[0])], axis=1)


def forward_kernel(paths, trades, *refs):
    x_refs, refs = refs[:paths], refs[paths:]
    weights, notional = joined_weights(refs[:trades]), one_row(refs[trades])
    member_ref, value_ref, lead_ref, *moment_refs = refs[trades + 1 :]
    start = 0
    for x in x_refs:
        pre_act = dot(x[...], weights, 1, 1)
        value_ref[start : start + x.shape[0]] = (notional * softplus(pre_act)).astype(BF16)
        turned = x[:, :LANES].astype(F32).T[:REGRESSORS]
        turned = jnp.where(rows(turned.shape) == CONSTANT, 1.0, turned)
        lead_ref[:, start : start + x.shape[0]] = turned.astype(BF16)
        start += x.shape[0]
    trade_moment = dot(lead_ref[...], value_ref[...])
    parts = dot(three(trade_moment, 0), member_ref[...], 1, 1)
    moment = parts[:REGRESSORS] + parts[REGRESSORS : 2 * REGRESSORS] + parts[2 * REGRESSORS :]
    size = moment.shape[1] // len(moment_refs)
    for m, moment_ref in enumerate(moment_refs):
        moment_ref[...] = moment[:, m * size : (m + 1) * size]


def slope_kernel(paths, trades, *refs):
    x_refs, refs, slope_ref = refs[:paths], refs[paths:], refs[-1]
    weights, notional = joined_weights(refs[:trades]), one_row(refs[trades])
    start = 0
    for x in x_refs:
        slope_ref[start : start + x.shape[0]] = notional * sigmoid(dot(x[...], weights, 1, 1))
        start += x.shape[0]


def solve_kernel(
    terms, inverse_ref, design_ref, rows_ref, thresh_ref, rate_ref, *refs
):
    solved_ref, turn_ref = refs[terms:]
    moment = refs[0][...]
    for ref in refs[1:terms]:
        moment = moment + ref[...]
    size = moment.shape[1]
    inverse = inverse_ref[...]
    coeffs = dot(inverse, moment, precision=PRECISE)
    solved_ref[REGRESSORS:] = coeffs
    is_constant = rows(coeffs.shape) == CONSTANT
    shifted = coeffs - jnp.where(is_constant, thresh_ref[:, :size], 0.0)
    turn_ref[...] = three_rows(-LOG2_E * shifted)

    def seeds(total, here):
        power = jnp.exp2(jnp.minimum(dot(rows_ref[here], turn_ref[...]), 126.0))
        below = 1.0 + power
        seed = pl.reciprocal(below, approx=True)
        seed = (seed * (2.0 - below * seed)).astype(BF16)
        return total + dot(design_ref[:, here], seed)

    total = each_chunk(rows_ref.shape[0], seeds, jnp.zeros((REGRESSORS, size), F32))
    solved_ref[:REGRESSORS] = dot(inverse, total * rate_ref[:, :size], precision=PRECISE)


def joined(refs, part):
    here = slice(part * REGRESSORS, (part + 1) * REGRESSORS)
    return jnp.concatenate([ref[here] for ref in refs], axis=1)


def weight_side_kernel(scale, shares, paths, member_ref, rows_ref, slope_ref, *refs):
    solved_refs, refs = refs[:shares], refs[shares:]
    x_refs, (traded_ref, slopes_ref, *weight_refs) = refs[:paths], refs[paths:]
    traded = dot(three_rows(joined(solved_refs, 0)), member_ref[...]).astype(BF16)
    traded_ref[...] = traded
    group = slopes_ref.shape[0]
    spread = dot(rows_ref[:group], traded).astype(BF16).astype(F32)
    slopes_ref[...] = (slope_ref[...] * spread).astype(BF16)
    basis = jnp.concatenate([x[...] for x in x_refs], axis=0)
    weight = (dot(slopes_ref[...], basis, 0, 0) * scale).astype(BF16)
    start = 0
    for part in weight_refs:
        part[...] = weight[start : start + part.shape[0]]
        start += part.shape[0]


def basis_side_kernel(trades, first, value_ref, traded_ref, slopes_ref, *refs):
    w_refs, basis_refs = refs[:trades], refs[trades:]
    weights = joined_weights(w_refs)
    start = first
    for part in basis_refs:
        here = slice(start, start + part.shape[0])
        total = dot(slopes_ref[here], weights)
        wide = dot(value_ref[here], traded_ref[...], 1, 1)
        design = wide
        for k in range(1, 3):
            design = design + pltpu.roll(wide, LANES - k * REGRESSORS, 1)
        design = jnp.where(lanes(design.shape) < CONSTANT, design, 0.0)
        part[:, :LANES] = (total[:, :LANES] + design).astype(BF16)
        part[:, LANES:] = total[:, LANES:].astype(BF16)
        start += part.shape[0]


def loss_kernel(rows_ref, thresh_ref, rate_ref, *refs):
    solved_refs, (loss_ref, own_ref, split_ref) = refs[:-3], refs[-3:]
    adjoint = joined(solved_refs, 0)
    coeffs = joined(solved_refs, 1)
    thresh = thresh_ref[...]
    rate = rate_ref[...]
    split_ref[...] = three_rows(coeffs)

    def losses(total, here):
        loss = softplus(dot(rows_ref[here], split_ref[...]) - thresh)
        return total + jnp.sum(loss.reshape(-1, *total.shape), axis=0)

    total = each_chunk(rows_ref.shape[0], losses, jnp.zeros((SUBLANES, coeffs.shape[1]), F32))
    summed = jnp.sum(jnp.sum(total * rate, axis=0, keepdims=True), axis=1, keepdims=True)
    loss_ref[...] = jnp.broadcast_to(
        summed / (rows_ref.shape[0] * coeffs.shape[1]), loss_ref.shape
    )
    own = rows_ref[: own_ref.shape[0]]
    fitted = dot(own, split_ref[...])
    seed = rate * sigmoid(fitted - thresh)
    rest = seed - dot(own, three_rows(adjoint))
    design = dot(rest, coeffs, 1, 1, PRECISE) - dot(fitted, adjoint, 1, 1, PRECISE)
    blank = jnp.zeros((design.shape[0], LANES - REGRESSORS), F32)
    design = jnp.concatenate([design, blank], axis=1)
    own_ref[...] = jnp.where(lanes(design.shape) < CONSTANT, design, 0.0)


def sum_kernel(first, own_ref, *refs):
    *terms, basis_ref, weight_ref, basis_scratch, weight_scratch, sems = refs

    def total(refs, here):
        out = refs[0][here].astype(F32)
        for ref in refs[1:]:
            out = out + ref[here].astype(F32)
        return out

    copies = []

    def send(source, target, here):
        copy = pltpu.make_async_copy(source.at[here], target.at[here], sems.at[len(copies)])
        copy.start()
        copies.append(copy)

    parts = sems.shape[0] // 2
    for k in range(parts):
        size = weight_ref.shape[0] // parts
        here = slice(k * size, (k + 1) * size)
        weight_scratch[here] = total(terms[first:], here)
        send(weight_scratch, weight_ref, pl.ds(k * size, size))
    for k in range(parts):
        size = basis_ref.shape[0] // parts
        here = slice(k * size, (k + 1) * size)
        basis = total(terms[:first], here)
        basis_scratch[here, :LANES] = basis[:, :LANES] + own_ref[here]
        basis_scratch[here, LANES:] = basis[:, LANES:]
        send(basis_scratch, basis_ref, pl.ds(k * size, size))
    for copy in copies:
        copy.wait()


def call(kernel, outs, *args, name, flops=0, scratch=(), scalars=0, far=False):
    size = sum(a.size * a.dtype.itemsize for a in args) + sum(
        math.prod(s) * jnp.dtype(d).itemsize for s, d in outs
    )
    return pl.pallas_call(
        kernel,
        out_shape=[jax.ShapeDtypeStruct(s, d) for s, d in outs],
        in_specs=[pl.BlockSpec(memory_space=pltpu.SMEM)] * scalars
        + [pl.BlockSpec(memory_space=pltpu.VMEM)] * (len(args) - scalars),
        out_specs=[pl.BlockSpec(memory_space=pl.ANY if far else pltpu.VMEM)] * len(outs),
        scratch_shapes=scratch,
        compiler_params=pltpu.CompilerParams(vmem_limit_bytes=VMEM_BYTES),
        cost_estimate=pl.CostEstimate(flops=int(flops), bytes_accessed=int(size), transcendentals=0),
        name=name,
    )(*args)


def shards(
    path_basis, proxy_weight, notional, set_of, threshold_index, threshold_levels, loss_rate
):
    n = lax.axis_size("paths")
    me = lax.axis_index("paths")
    inner_bits, outer_bits = split_bits(n)
    inner, outer = 1 << len(inner_bits), 1 << len(outer_bits)
    path_rows, features = path_basis.shape
    trade_rows = proxy_weight.shape[0]
    paths_all = path_rows * n
    sets = loss_rate.shape[0]
    share = sets // SHARES
    group_paths, group_trades = inner * path_rows, outer * trade_rows

    def swap(x, mask):
        return lax.ppermute(x, "paths", [(d, d ^ mask) for d in range(n)])

    def masks(bits):
        return [
            sum(((m >> j) & 1) << bit for j, bit in enumerate(bits)) for m in range(1 << len(bits))
        ]

    def after(x, *others):
        return lax.optimization_barrier((x, *others))[0]

    def direct(slots, masks):
        return [swap(x, mask) for x, mask in zip(slots[1:], masks[1:])]

    outer_masks = masks(outer_bits)
    inner_masks = [0] + masks(inner_bits)[:0:-1]
    first_bit = outer_bits[0]
    weights = [proxy_weight, swap(proxy_weight, 1 << first_bit)]
    basis = [path_basis] + direct([path_basis] * inner, inner_masks)
    notionals = [notional[None, :], swap(notional, 1 << first_bit)[None, :]]

    member, thresh, rate, basis[0], own_weight, notionals[0] = call(
        partial(tables_kernel, outer_masks),
        [
            ((sets, group_trades), BF16),
            ((1, sets), F32),
            ((1, sets), F32),
            (path_basis.shape, BF16),
            (proxy_weight.shape, BF16),
            ((1, trade_rows), BF16),
        ],
        me.astype(jnp.int32).reshape(1),
        threshold_levels,
        set_of.reshape(n, 1, trade_rows),
        threshold_index.reshape(SHARES, 1, share),
        loss_rate.reshape(SHARES, 1, share),
        path_basis,
        proxy_weight,
        notionals[0],
        name="tables",
        scalars=2,
    )
    notionals = after(jnp.concatenate(notionals, axis=0), weights[1])
    for bit in outer_bits[1:]:
        weights = weights + [
            swap(after(w, basis[-2] if k else member), 1 << bit) for k, w in enumerate(weights)
        ]
        notionals = jnp.concatenate([notionals, swap(notionals, 1 << bit)], axis=0)
    weights[0] = own_weight
    value, lead, *moments = call(
        partial(forward_kernel, inner, outer),
        [((group_paths, group_trades), BF16), ((REGRESSORS, group_paths), BF16)]
        + [((REGRESSORS, share), F32)] * SHARES,
        *basis, *weights, notionals, member,
        name="forward",
    )
    moment = moments[0] + swap(moments[1], SHARES - 1)
    lead = after(lead, moment)
    leads = [lead] + direct([lead] * outer, outer_masks)
    for bit in outer_bits[:-1]:
        there = swap(moment, 1 << bit)
        moment = moment + there
    small = jnp.stack(leads)
    moments = [moment] + direct([moment] * inner, inner_masks)
    (inverse,) = call(
        partial(inverse_kernel, RIDGE_SCALE * paths_all),
        [((REGRESSORS, REGRESSORS), F32)],
        small,
        name="inverse",
    )
    design_all, design_rows = call(
        design_kernel,
        [((REGRESSORS, paths_all), BF16), ((paths_all, LANES), BF16)],
        small,
        name="design",
    )
    (solved,) = call(
        partial(solve_kernel, len(moments)),
        [((2 * REGRESSORS, share), F32)],
        inverse, design_all, design_rows, thresh, rate, *moments,
        name="solve",
        scratch=[pltpu.VMEM((LANES, share), BF16)],
    )
    solved = [solved, swap(solved, SHARES - 1)]
    (slope,) = call(
        partial(slope_kernel, inner, outer),
        [((group_paths, group_trades), F32)],
        *basis, *weights, notionals,
        name="slope",
    )
    traded, slopes, *weight_parts = call(
        partial(weight_side_kernel, 1.0 / math.sqrt(paths_all), SHARES, inner),
        [((LANES, group_trades), BF16), ((group_paths, group_trades), BF16)]
        + [((trade_rows, features), BF16)] * outer,
        member, design_rows, slope, *solved, *basis,
        name="weight_side",
    )
    terms = [[part] for part in weight_parts]
    core_step = None
    for bit in reversed(outer_bits):
        count = len(terms) // 2
        arrived = None
        for k in reversed(range(count)):
            gone = terms[count + k]
            gone = gone[0] if len(gone) == 1 else sum(g.astype(F32) for g in gone).astype(BF16)
            if arrived is not None:
                gone = after(gone, arrived)
            arrived = swap(gone, 1 << bit)
            terms[k].append(arrived)
            if core_step is None:
                core_step = arrived
        terms = terms[:count]
    weight_terms = terms[0]

    def basis_side(first, last, slopes):
        return call(
            partial(basis_side_kernel, outer, first * path_rows),
            [((path_rows, features), BF16)] * (last - first),
            value, traded, slopes, *weights,
            name="basis_side",
        )

    far = list(basis_side(1, inner - 1, slopes))
    late = after(slopes, core_step)
    own, near = basis_side(0, 1, late)[0], basis_side(inner - 1, inner, late)[0]
    basis_terms = [own] + direct([own] + far + [near], inner_masks)
    loss, own_adjoint = call(
        loss_kernel,
        [((8, LANES), F32), ((path_rows, LANES), F32)],
        design_rows, thresh, rate, *solved,
        name="loss",
        scratch=[pltpu.VMEM((LANES, sets), BF16)],
    )
    parts = 4 if trade_rows % (4 * SUBLANES * 2) == 0 else 1
    basis_adjoint, weight_adjoint = call(
        partial(sum_kernel, len(basis_terms)),
        [((path_rows, features), F32), ((trade_rows, features), F32)],
        own_adjoint, *basis_terms, *weight_terms,
        name="sums",
        scratch=[
            pltpu.VMEM((path_rows, features), F32),
            pltpu.VMEM((trade_rows, features), F32),
            pltpu.SemaphoreType.DMA((2 * parts,)),
        ],
        far=True,
    )
    return (loss[0, :1], basis_adjoint, weight_adjoint)


def solution(mesh):
    placed = (
        P(("groups", "paths"), None),
        P(("groups", "paths"), None),
        P(("groups", "paths")),
        P("groups"),
        P("groups"),
        P("groups"),
        P("groups"),
    )
    return jax.shard_map(
        shards,
        mesh=mesh,
        in_specs=placed,
        out_specs=(P("groups"), P(("groups", "paths"), None), P(("groups", "paths"), None)),
        check_vma=False,
    )
```
